32 devices in a mesh: rep: 4 (over z), fsdp: 4 (over y, x), seq: 2 (over core).
Axes of the slice: x: 2, y: 2, z: 4, core: 2. Of those that a mesh axis runs over, the one named last changes fastest.
Arguments:
- tokens: bfloat16 [2, 16, 1024, 768], P(None, ('rep', 'fsdp'), 'seq'), may hold values from -6 to 6
- cotangent: bfloat16 [2, 16, 1024, 768], P(None, ('rep', 'fsdp'), 'seq'), may hold values from -6 to 6
- segments: int32 [2, 16, 1024], P(None, ('rep', 'fsdp')), may hold values from 0 to 3, as said below
- input_weight: float32 [768, 3328], P(('fsdp', 'seq')), may hold values from -0.21875 to 0.21875
- output_weight: float32 [1536, 768], P(('fsdp', 'seq')), may hold values from -0.15625 to 0.15625
- small_values: float32 [29768], replicated, may hold values from -12 to 2, as said below
- input_momentum: float32 [768, 3328], P(('fsdp', 'seq')), may hold values from -160 to 160
- output_momentum: float32 [1536, 768], P(('fsdp', 'seq')), may hold values from -160 to 160
- small_momentum: float32 [29768], replicated, may hold values from -16 to 16
- input_error: float32 [4, 768, 3328], P('rep', ('fsdp', 'seq')), may hold values from -1357.645 to 1357.645
- output_error: float32 [4, 1536, 768], P('rep', ('fsdp', 'seq')), may hold values from -1357.645 to 1357.645
- input_start: float32 [3328, 8], replicated, may hold values from -6 to 6
- output_start: float32 [768, 8], replicated, may hold values from -6 to 6
Outputs:
- output: bfloat16 [2, 16, 1024, 768], P(None, ('rep', 'fsdp'), 'seq')
- input_grad: bfloat16 [2, 16, 1024, 768], P(None, ('rep', 'fsdp'), 'seq')
- new_input_weight: float32 [768, 3328], P(('fsdp', 'seq'))
- new_output_weight: float32 [1536, 768], P(('fsdp', 'seq'))
- new_input_momentum: float32 [768, 3328], P(('fsdp', 'seq'))
- new_output_momentum: float32 [1536, 768], P(('fsdp', 'seq'))
- new_small_values: float32 [29768], replicated
- new_small_momentum: float32 [29768], replicated
- input_left: float32 [768, 8], P(('fsdp', 'seq'))
- input_right: float32 [3328, 8], replicated
- output_left: float32 [1536, 8], P(('fsdp', 'seq'))
- output_right: float32 [768, 8], replicated
- new_input_error: float32 [4, 768, 3328], P('rep', ('fsdp', 'seq'))
- new_output_error: float32 [4, 1536, 768], P('rep', ('fsdp', 'seq'))
The draws below stay inside these ranges and needn't reach their ends.
Inputs may be any that keep to these rules, and one draw needn't show every extreme that they name: `segments`: within each sequence the ids never fall and run from 0 to 3: every sequence holds exactly 4 documents of 1 to 512 tokens, one of them exactly 512 tokens. `small_values`: the small parameters lie within this range.
All inputs are finite; a program needn't handle non-finite values.
Results may differ from the reference program's by a relative error of at most 0.012.
Values may be sent and summed in bfloat16 or wider, within the bound.
A program may use at most 192 MiB of HBM per device.

```python
import math
from functools import partial
import jax
import jax.numpy as jnp
from jax import lax

D = 768
INNER = 1536
HEADS = 24
HEADDIM = 64
STATE = 128
CONV = 4
GROUP = 256
RANK = 8
MICRO = 2
PROJ = 3328
XBC = 1792
NVEC = 29768
SEQLEN = 1024
DOCS = 4
BATCH = 16
TOKREP = 8192
N_REP = 4
N_FSDP = 4


def scaled_error(base_values, row_count):
    rising = 1.0 + 2.0 * jnp.arange(row_count, dtype=jnp.float32) / max(row_count - 1, 1)
    replica_scale = 1.0 + jnp.arange(N_REP, dtype=jnp.float32) / max(N_REP - 1, 1)
    return base_values * rising[None, :, None] * replica_scale[:, None, None] * (0.5 * math.sqrt(TOKREP))


def draw_input_error(key, part):
    key = jax.random.fold_in(key, 21)
    base_values = jnp.clip(jax.random.normal(key, (N_REP, D, PROJ), jnp.float32), -5.0, 5.0)
    return scaled_error(base_values, D)


def draw_output_error(key, part):
    key = jax.random.fold_in(key, 31)
    base_values = jnp.clip(jax.random.normal(key, (N_REP, INNER, D), jnp.float32), -5.0, 5.0)
    return scaled_error(base_values, INNER)


def draw_segments(key, part):
    key = jax.random.fold_in(key, 41)
    subkeys = jax.random.split(key, 5)
    row_count = MICRO * BATCH
    longest = SEQLEN // 2
    spare_room = SEQLEN - longest
    any_start = jax.random.randint(subkeys[0], (MICRO, BATCH), 0, spare_room + 1)
    cross_start = jax.random.randint(subkeys[1], (MICRO, BATCH), 1, spare_room)
    snapping = jax.random.randint(subkeys[2], (MICRO, BATCH), 0, 2) == 0
    chosen = jax.random.randint(subkeys[3], (BATCH,), 0, MICRO)
    crossing = jnp.arange(MICRO, dtype=jnp.int32)[:, None] == chosen[None, :]
    snapped = any_start - any_start % GROUP
    long_start = jnp.where(crossing, cross_start, jnp.where(snapping, snapped, any_start)).reshape(row_count)
    finish = long_start + longest
    position = jnp.arange(SEQLEN, dtype=jnp.int32)[None, :]
    allowed = (position >= 1) & (position < long_start[:, None]) | (position > finish[:, None])
    scores = jax.random.randint(subkeys[4], (row_count, SEQLEN), 0, 65536) * SEQLEN + position
    scores = jnp.where(allowed, scores, -1)
    picked_scores, picked = lax.top_k(scores, DOCS - 1)
    extra_cuts = DOCS - 1 - (long_start > 0).astype(jnp.int32) - (finish < SEQLEN).astype(jnp.int32)
    in_use = jnp.arange(DOCS - 1, dtype=jnp.int32)[None, :] < extra_cuts[:, None]
    doc_marks = jnp.sum(((picked[:, :, None] == position[:, None, :]) & in_use[:, :, None]).astype(jnp.int32), axis=1)
    doc_marks = doc_marks + ((position == long_start[:, None]) & (long_start[:, None] > 0)).astype(jnp.int32)
    doc_marks = doc_marks + (position == finish[:, None]).astype(jnp.int32)
    return jnp.cumsum(doc_marks, axis=1).reshape(MICRO, BATCH, SEQLEN)


def draw_small_values(key, part):
    key = jax.random.fold_in(key, 11)
    subkeys = jax.random.split(key, 10)
    norm_gain = jax.random.uniform(subkeys[0], (D,), jnp.float32, 0.6, 1.4)
    delta_weight = jnp.clip(jax.random.normal(subkeys[1], (D * HEADS,), jnp.float32), -4.0, 4.0) * D ** (-0.5)
    conv_weight = jnp.clip(jax.random.normal(subkeys[2], (CONV * XBC,), jnp.float32), -4.0, 4.0) * 0.5
    conv_bias = jnp.clip(jax.random.normal(subkeys[3], (XBC,), jnp.float32), -4.0, 4.0) * 0.3
    gate_gain = jax.random.uniform(subkeys[4], (INNER,), jnp.float32, 0.6, 1.4)
    percent = 35
    quick = jax.random.randint(subkeys[5], (HEADS,), 0, 100) < percent
    slow_delta = jnp.exp(jax.random.uniform(subkeys[6], (HEADS,), jnp.float32, math.log(0.3 / SEQLEN), math.log(1.1 / SEQLEN)))
    quick_delta = jnp.exp(jax.random.uniform(subkeys[7], (HEADS,), jnp.float32, math.log(0.015), math.log(0.04)))
    delta_init = jnp.where(quick, quick_delta, slow_delta)
    dt_bias = jnp.log(jnp.expm1(delta_init))
    log_rate = jnp.log(jax.random.uniform(subkeys[8], (HEADS,), jnp.float32, 1.0, 2.0))
    skip_gain = jax.random.uniform(subkeys[9], (HEADS,), jnp.float32, 0.5, 1.5)
    return jnp.concatenate([norm_gain, delta_weight, conv_weight, conv_bias, gate_gain, dt_bias, log_rate, skip_gain])


def shard_levels(own_key, shape, cuts, least, high):
    def one(dim, shards_of):
        draws = jax.random.uniform(jax.random.fold_in(jax.random.fold_in(own_key, 6), dim), (shards_of,), jnp.float32, least / len(cuts), high / len(cuts))
        return jnp.repeat(jnp.exp(draws), shape[dim] // shards_of).reshape((-1,) + (1,) * (len(shape) - dim - 1))

    level = one(*cuts[0])
    for cut in cuts[1:]:
        level = level * one(*cut)
    return level


def noise(own_key, shape, deviation, bound, cuts=(), kind=jnp.bfloat16):
    factor_of = shard_levels(own_key, shape, cuts, -0.22, 0.18) if cuts else 1.0
    values = jax.random.normal(own_key, shape, jnp.float32) * deviation * factor_of
    return jnp.minimum(jnp.maximum(values, -bound), bound).astype(kind)


def setup_inputs(seed: int = 0) -> dict:
    splits = jax.random.split(jax.random.key(seed), 14)
    return {
        "tokens": noise(splits[0], (MICRO, BATCH, SEQLEN, D), 1.0, 6.0, ((1, 16), (2, 2))),
        "cotangent": noise(splits[1], (MICRO, BATCH, SEQLEN, D), 1.0, 6.0, ((1, 16), (2, 2))),
        "segments": draw_segments(jax.random.fold_in(splits[13], 71), 0),
        "input_weight": noise(splits[3], (D, PROJ), D ** -0.5, 0.21875, ((0, 8),), jnp.float32),
        "output_weight": noise(splits[4], (INNER, D), INNER ** -0.5, 0.15625, ((0, 8),), jnp.float32),
        "small_values": draw_small_values(jax.random.fold_in(splits[13], 71), 0),
        "input_momentum": noise(splits[6], (D, PROJ), (0.3 * TOKREP ** 0.5), 160.0, ((0, 8),), jnp.float32),
        "output_momentum": noise(splits[7], (INNER, D), (0.3 * TOKREP ** 0.5), 160.0, ((0, 8),), jnp.float32),
        "small_momentum": noise(splits[8], (NVEC,), (0.03 * TOKREP ** 0.5), 16.0, (), jnp.float32),
        "input_error": draw_input_error(jax.random.fold_in(splits[13], 71), 0),
        "output_error": draw_output_error(jax.random.fold_in(splits[13], 71), 0),
        "input_start": noise(splits[11], (PROJ, RANK), 1.0, 6.0, (), jnp.float32),
        "output_start": noise(splits[12], (D, RANK), 1.0, 6.0, (), jnp.float32),
    }


@jax.custom_vjp
def low(v):
    return lax.optimization_barrier(v.astype(jnp.bfloat16)).astype(jnp.float32)

@jax.custom_vjp
def low_back(v):
    return v

def low_keep(v):
    return (low(v), None)

def low_pass(kept, grad):
    return (grad,)

def back_keep(v):
    return (v, None)

def back_low(kept, grad):
    return (low(grad),)
low.defvjp(low_keep, low_pass)
low_back.defvjp(back_keep, back_low)
EPS = 1e-05
MOMENTUM = 0.9
HIGH = lax.Precision.HIGHEST

def split_small(small_values):
    pieces = []
    offset = 0
    for amount in (D, D * HEADS, CONV * XBC, XBC, INNER, HEADS, HEADS, HEADS):
        pieces.append(small_values[offset:offset + amount])
        offset = offset + amount
    return (pieces[0], pieces[1].reshape(D, HEADS), pieces[2].reshape(CONV, XBC), pieces[3], pieces[4], pieces[5], pieces[6], pieces[7])

def rms_scale(values, weights):
    return values * lax.rsqrt(lax.optimization_barrier(jnp.mean(values * values, axis=-1, keepdims=True)) + EPS) * weights

def step_rates(tokens_replica):
    grad_scale = 0.3 * math.sqrt(tokens_replica)
    return (0.5 / (math.sqrt(D) * grad_scale), 0.5 / (math.sqrt(INNER) * grad_scale), 0.1 / grad_scale)

def convolve(documents, halo_documents, raw_rows, halo_rows, conv_weight, conv_bias):
    extended = jnp.concatenate([halo_rows, raw_rows], axis=0)
    wider_segments = jnp.concatenate([halo_documents, documents])
    extent = documents.shape[0]
    summed = jnp.zeros(raw_rows.shape, jnp.float32) + conv_bias[None, :]
    for offset in range(CONV):
        same_doc = jnp.where(wider_segments[offset:offset + extent] == documents, 1.0, 0.0)
        summed = summed + conv_weight[offset][None, :] * extended[offset:offset + extent] * same_doc[:, None]
    return jax.nn.silu(summed)

def group_output(value_block, write_block, read_block, delta_block, decay_block, segment_block, before, carried, skip_gain):
    extent = segment_block.shape[0]
    totals = jnp.cumsum(decay_block, axis=0)
    row_index = lax.broadcasted_iota(jnp.int32, (extent, extent), 0)
    col_index = lax.broadcasted_iota(jnp.int32, (extent, extent), 1)
    allowed = ((segment_block[:, None] == segment_block[None, :]) & (row_index >= col_index))[:, :, None]
    spread = totals[:, None, :] - totals[None, :, :]
    decay_matrix = jnp.where(allowed, jnp.exp(jnp.where(allowed, spread, 0.0)), 0.0)
    scores = jnp.dot(read_block, write_block.T, precision=HIGH)
    mixing = decay_matrix * scores[:, :, None] * delta_block[None, :, :]
    inside = jnp.einsum('tsh,shp->thp', mixing, value_block, precision=HIGH)
    linked = jnp.where(segment_block == before, 1.0, 0.0)
    reading = jnp.einsum('tn,hpn->thp', read_block, carried, precision=HIGH)
    fading = jnp.exp(totals) * linked[:, None]
    return inside + fading[:, :, None] * reading + skip_gain[None, :, None] * value_block

def group_state(value_block, write_block, delta_block, decay_block, segment_block, before):
    totals = jnp.cumsum(decay_block, axis=0)
    keeping = jnp.where(segment_block == segment_block[-1], 1.0, 0.0)
    to_end = jnp.exp(totals[-1][None, :] - totals) * keeping[:, None] * delta_block
    fresh_state = jnp.einsum('shp,sn->hpn', value_block * to_end[:, :, None], write_block, precision=HIGH)
    passing = jnp.exp(totals[-1]) * jnp.where(segment_block[-1] == before, 1.0, 0.0)
    return (fresh_state, passing)

def run_groups(documents, first_before, values, writers, readers, deltas, log_decay, start_state, skip_gain):
    blocks = documents.shape[0] // GROUP
    segment_blocks = documents.reshape(blocks, GROUP)
    befores = jnp.concatenate([jnp.reshape(first_before, (1,)).astype(jnp.int32), segment_blocks[:-1, -1].astype(jnp.int32)])
    current_all = (values.reshape(blocks, GROUP, HEADS, HEADDIM), writers.reshape(blocks, GROUP, STATE), readers.reshape(blocks, GROUP, STATE), deltas.reshape(blocks, GROUP, HEADS), log_decay.reshape(blocks, GROUP, HEADS), segment_blocks, befores)

    def advance(carried, current):
        value_block, write_block, read_block, delta_block, decay_block, segment_block, before = current
        produced = group_output(value_block, write_block, read_block, delta_block, decay_block, segment_block, before, carried, skip_gain)
        fresh_state, passing = group_state(value_block, write_block, delta_block, decay_block, segment_block, before)
        return (passing[:, None, None] * carried + fresh_state, produced)
    final_state, produced = lax.scan(jax.checkpoint(advance), start_state, current_all)
    return (produced.reshape(documents.shape[0], HEADS, HEADDIM), final_state)

def sequence_forward(tokens_row, documents, input_low, output_low, delta_low, norm_gain, conv_weight, conv_bias, gate_gain, dt_bias, log_rate, skip_gain):
    normed_in = low(rms_scale(tokens_row, norm_gain))
    projected = low_back(low(jnp.dot(normed_in, input_low, precision=HIGH)))
    delta_raw = low_back(jnp.dot(normed_in, delta_low, precision=HIGH))
    gate_rows = projected[:, :INNER]
    raw_rows = projected[:, INNER:]
    halo_rows = jnp.zeros((CONV - 1, XBC), jnp.float32)
    halo_documents = jnp.full((CONV - 1,), -1, jnp.int32)
    activated = low(convolve(documents, halo_documents, raw_rows, halo_rows, conv_weight, conv_bias))
    values = activated[:, :INNER].reshape(-1, HEADS, HEADDIM)
    writers = activated[:, INNER:INNER + STATE]
    readers = activated[:, INNER + STATE:]
    deltas = jax.nn.softplus(delta_raw + dt_bias)
    log_decay = deltas * -jnp.exp(log_rate)
    mixed, final_state = run_groups(documents, jnp.array(-1, jnp.int32), values, writers, readers, deltas, log_decay, jnp.zeros((HEADS, HEADDIM, STATE), jnp.float32), skip_gain)
    gated = mixed.reshape(-1, INNER) * jax.nn.silu(gate_rows)
    gated_out = low(rms_scale(gated, gate_gain))
    return tokens_row + jnp.dot(gated_out, output_low, precision=HIGH)

def replica_forward(replica_documents, replica_tokens, input_weight, output_weight, small_values):
    norm_gain, delta_weight, conv_weight, conv_bias, gate_gain, dt_bias, log_rate, skip_gain = split_small(small_values)
    input_low = low(input_weight)
    output_low = low(output_weight)
    delta_low = low(delta_weight)

    def one_sequence(carry_none, current):
        tokens_row, documents = current
        produced = sequence_forward(tokens_row, documents, input_low, output_low, delta_low, norm_gain, conv_weight, conv_bias, gate_gain, dt_bias, log_rate, skip_gain)
        return (carry_none, produced)
    unused, outputs = lax.scan(jax.checkpoint(one_sequence), jnp.zeros((), jnp.float32), (replica_tokens, replica_documents))
    return outputs

def orthonormal(factor):
    gram = jnp.dot(factor.T, factor, precision=HIGH)
    lower = jnp.linalg.cholesky(gram)
    return lax.linalg.triangular_solve(lower, factor, left_side=False, lower=True, transpose_a=True)

def compress(gradients, errors, start_factor, momentum, weight, rate):
    combined = gradients + errors
    left = jnp.einsum('rij,jk->ik', combined, start_factor, precision=HIGH) / N_REP
    left_hat = orthonormal(left)
    right = jnp.einsum('rij,ik->jk', combined, left_hat, precision=HIGH) / N_REP
    approx = jnp.dot(left_hat, right.T, precision=HIGH)
    new_momentum = MOMENTUM * momentum + approx
    return (weight - rate * new_momentum, new_momentum, left_hat, right, combined - approx[None])

def regroup(array):
    shaped = array.reshape((MICRO, N_REP, N_FSDP) + array.shape[2:])
    shaped = jnp.moveaxis(shaped, 1, 0)
    return shaped.reshape((N_REP, MICRO * N_FSDP) + array.shape[2:])

def ungroup(array):
    shaped = array.reshape((N_REP, MICRO, N_FSDP) + array.shape[2:])
    shaped = jnp.moveaxis(shaped, 0, 1)
    return shaped.reshape((MICRO, N_REP * N_FSDP) + array.shape[2:])

def reference(tokens, cotangent, segments, input_weight, output_weight, small_values, input_momentum, output_momentum, small_momentum, input_error, output_error, input_start, output_start):

    def replica_pass(current):
        replica_tokens, replica_documents, replica_cotangent = current
        outputs, backward = jax.vjp(partial(replica_forward, replica_documents), replica_tokens, input_weight, output_weight, small_values)
        gradients = backward(replica_cotangent)
        return (outputs,) + tuple(gradients)
    outputs, token_grads, input_grads, output_grads, small_grads = lax.map(replica_pass, (regroup(tokens.astype(jnp.float32)), regroup(segments), regroup(cotangent.astype(jnp.float32))))
    rate_in, rate_out, rate_small = step_rates(TOKREP)
    new_input_weight, new_input_momentum, input_left, input_right, new_input_error = compress(input_grads, input_error, input_start, input_momentum, input_weight, rate_in)
    new_output_weight, new_output_momentum, output_left, output_right, new_output_error = compress(output_grads, output_error, output_start, output_momentum, output_weight, rate_out)
    new_small_momentum = MOMENTUM * small_momentum + lax.optimization_barrier(jnp.sum(small_grads, axis=0)) / N_REP
    new_small_values = small_values - rate_small * new_small_momentum
    output = ungroup(outputs).astype(jnp.bfloat16)
    input_grad = ungroup(token_grads).astype(jnp.bfloat16)
    return (output, input_grad, new_input_weight, new_output_weight, new_input_momentum, new_output_momentum, new_small_values, new_small_momentum, input_left, input_right, output_left, output_right, new_input_error, new_output_error)
```

```python
from functools import partial
import math

import jax
import jax.numpy as jnp
from jax import lax
from jax.experimental import pallas as pl
from jax.experimental.pallas import tpu as pltpu
from jax.sharding import PartitionSpec as P

D = 768
INNER = 1536
HEADS = 24
HEADDIM = 64
STATE = 128
CONV = 4
PROJ = 3328
XBC = 1792

EPS = 1e-05
MOMENTUM = 0.9
HIGH = lax.Precision.HIGHEST
F32 = jnp.float32
BF16 = jnp.bfloat16
HP = 32
CH = 128
HALO = 16
TILE = 256
NEG = -1e30
VMEM_LIMIT = 58 * 2**20


def nn(a, b):
    return lax.dot_general(a, b, (((1,), (0,)), ((), ())), preferred_element_type=F32)


def nt(a, b):
    return lax.dot_general(a, b, (((1,), (1,)), ((), ())), preferred_element_type=F32)


def tn(a, b):
    return lax.dot_general(a, b, (((0,), (0,)), ((), ())), preferred_element_type=F32)


def nn_high(a, b):
    return lax.dot_general(
        a, b, (((1,), (0,)), ((), ())), precision=HIGH, preferred_element_type=F32
    )


def softplus(v):
    return jnp.maximum(v, 0.0) + jnp.log1p(jnp.exp(-jnp.abs(v)))


def triangle(extent):
    return jnp.where(
        lax.broadcasted_iota(jnp.int32, (extent, extent), 0)
        <= lax.broadcasted_iota(jnp.int32, (extent, extent), 1),
        1.0,
        0.0,
    )


def params(semantics, **more):
    return pltpu.CompilerParams(
        dimension_semantics=semantics, vmem_limit_bytes=VMEM_LIMIT, **more
    )


def enter_kernel(
    tok_ref, halo_ref, gain_ref, wraw_ref, dlow_ref, cw_ref, cb_ref, same_ref,
    bias_ref, rate_ref, segrow_ref,
    normed_ref, raw_ref, dsilu_ref, val_ref, wr_ref, draw_ref, delta_ref, send_ref,
    ext, rawbuf, act, mask, weight,
):
    length = tok_ref.shape[1]
    gain = gain_ref[...]
    for start, rows, src in ((0, HALO, halo_ref), (HALO, length, tok_ref)):
        for b in range(0, rows, 128):
            n = min(128, rows - b)
            x = src[0, b : b + n, :].astype(F32)
            scale = lax.rsqrt(jnp.mean(x * x, axis=-1, keepdims=True) + EPS)
            ext[start + b : start + b + n, :] = (x * scale * gain).astype(BF16)
    normed_ref[0] = ext[HALO:, :]
    for k in range(1, CONV):
        mask[k - 1] = jnp.broadcast_to(same_ref[0, :, k : k + 1], (length, 128))

    def tile(c):
        cols = pl.ds(pl.multiple_of(c * TILE, TILE), TILE)
        low = nn(ext[...], wraw_ref[:, cols]).astype(BF16)
        raw_ref[0, :, cols] = low
        rawbuf[...] = low.astype(F32)
        for half in range(0, TILE, 128):
            hc = pl.ds(pl.multiple_of(c * TILE + half, 128), 128)
            w = cw_ref[:, hc]
            bias = cb_ref[:, hc]
            for b in range(0, length, 64):
                z = bias + w[3:4] * rawbuf[HALO + b : HALO + b + 64, half : half + 128]
                for j in range(1, CONV):
                    moved = rawbuf[HALO + b - j : HALO + b - j + 64, half : half + 128]
                    z = z + w[3 - j : 4 - j] * (moved * mask[j - 1, b : b + 64, :])
                sig = 1.0 / (1.0 + jnp.exp(-z))
                act[b : b + 64, half : half + 128] = z * sig
                dsilu_ref[0, b : b + 64, hc] = (sig * (1.0 + z * (1.0 - sig))).astype(BF16)

    def value_tile(c, carry):
        tile(c)
        val_ref[0, pl.ds(pl.multiple_of(c * TILE, TILE), TILE), :] = act[...].T.astype(BF16)
        return carry

    lax.fori_loop(0, INNER // TILE, value_tile, 0)
    tile(INNER // TILE)
    wr_ref[0] = act[...].astype(BF16)

    draw = nt(dlow_ref[...], ext[HALO:, :]) + bias_ref[...]
    delta = softplus(draw)
    draw_ref[0] = draw
    delta_ref[0] = delta
    totals = nn_high(-jnp.exp(rate_ref[...]) * delta, triangle(length))
    seg = segrow_ref[0]
    keep = jnp.where(seg == seg[:, length - 1 :], 1.0, 0.0)
    weight[...] = jnp.exp(totals[:, length - 1 :] - totals) * keep * delta
    writers = wr_ref[0, :, :STATE]

    def state_tile(c, carry):
        for h in range(4):
            rows = pl.ds(pl.multiple_of(c * TILE + h * HEADDIM, HEADDIM), HEADDIM)
            act_t = val_ref[0, rows, :].astype(F32) * weight[pl.ds(c * 4 + h, 1), :]
            send_ref[0, rows, :] = nn(act_t.astype(BF16), writers).astype(BF16)
        return carry

    lax.fori_loop(0, INNER // TILE, state_tile, 0)


def enter(tokens, halo, gain, wraw, dlow, cw, cb, same, bias, rate, segrow):
    n, length, _ = tokens.shape
    one = lambda *shape: pl.BlockSpec((1,) + shape, lambda i: (i, 0, 0))
    whole = lambda a: pl.BlockSpec(a.shape, lambda i: (0,) * a.ndim)
    outs = [
        ((n, length, D), BF16),
        ((n, length + HALO, XBC), BF16),
        ((n, length, XBC), BF16),
        ((n, INNER, length), BF16),
        ((n, length, 2 * STATE), BF16),
        ((n, HP, length), F32),
        ((n, HP, length), F32),
        ((n, INNER, STATE), BF16),
    ]
    return pl.pallas_call(
        enter_kernel,
        grid=(n,),
        in_specs=[
            one(length, D), one(HALO, D), whole(gain), whole(wraw), whole(dlow), whole(cw),
            whole(cb), one(length, 8), whole(bias), whole(rate), one(1, length),
        ],
        out_specs=[one(*s[1:]) for s, _ in outs],
        out_shape=[jax.ShapeDtypeStruct(s, t) for s, t in outs],
        scratch_shapes=[
            pltpu.VMEM((length + HALO, D), BF16),
            pltpu.VMEM((length + HALO, TILE), F32),
            pltpu.VMEM((length, TILE), F32),
            pltpu.VMEM((CONV - 1, length, 128), F32),
            pltpu.VMEM((HP, length), F32),
        ],
        compiler_params=params(("arbitrary",)),
        name="enter",
    )(tokens, halo, gain, wraw, dlow, cw, cb, same, bias, rate, segrow)


def chunk_terms(delta, rate_ref, segrow, segcol, before, last):
    decay = -jnp.exp(rate_ref[...]) * delta
    totals = nn_high(decay, triangle(CH))
    end = totals[:, CH - 1 :]
    fade = jnp.exp(totals) * jnp.where(segrow == before, 1.0, 0.0)
    to_end = jnp.exp(end - totals) * jnp.where(segrow == last, 1.0, 0.0)
    passing = jnp.exp(end) * jnp.where(last == before, 1.0, 0.0)
    allowed = (segcol == segrow) & (
        lax.broadcasted_iota(jnp.int32, (CH, CH), 0)
        <= lax.broadcasted_iota(jnp.int32, (CH, CH), 1)
    )
    return decay, totals, fade, to_end, passing, jnp.where(allowed, 0.0, NEG)


def forward_kernel(
    marks_ref, val_ref, w_ref, r_ref, delta_ref, rate_ref, segrow_ref, segcol_ref, in_ref,
    y_ref, start_ref,
    state, off, fresh,
):
    n, k = pl.program_id(0), pl.program_id(1)

    @pl.when(k == 0)
    def _():
        state[...] = in_ref[0].astype(F32)

    writers, readers = w_ref[0], r_ref[0]
    delta = delta_ref[0]
    _, totals, fade, to_end, passing, barred = chunk_terms(
        delta, rate_ref, segrow_ref[0], segcol_ref[0], marks_ref[n, k, 0], marks_ref[n, k, 1]
    )
    columns = totals.T
    scores = nt(writers, readers)
    low_state = state[...].astype(BF16)
    start_ref[0, 0] = low_state
    off[...] = nt(low_state, readers)
    for h in range(HEADS):
        rows = slice(h * HEADDIM, (h + 1) * HEADDIM)
        mixing = jnp.exp(totals[h : h + 1, :] - columns[:, h : h + 1] + barred) * scores
        scaled = val_ref[0, rows, :].astype(F32) * delta[h : h + 1, :]
        fresh[rows, :] = (scaled * to_end[h : h + 1, :]).astype(BF16)
        inside = nn(scaled.astype(BF16), mixing.astype(BF16))
        y_ref[0, rows, :] = inside + off[rows, :] * fade[h : h + 1, :]
    off[...] = nn(fresh[...], writers)
    for h in range(HEADS):
        rows = slice(h * HEADDIM, (h + 1) * HEADDIM)
        state[rows, :] = passing[h : h + 1, :] * state[rows, :] + off[rows, :]


def forward_scan(marks, values, wr, delta, rate, segrow, segcol, incoming):
    n, _, length = values.shape
    chunks = length // CH
    return pl.pallas_call(
        forward_kernel,
        grid_spec=pltpu.PrefetchScalarGridSpec(
            num_scalar_prefetch=1,
            grid=(n, chunks),
            in_specs=[
                pl.BlockSpec((1, INNER, CH), lambda i, k, m: (i, 0, k)),
                pl.BlockSpec((1, CH, STATE), lambda i, k, m: (i, k, 0)),
                pl.BlockSpec((1, CH, STATE), lambda i, k, m: (i, k, 1)),
                pl.BlockSpec((1, HP, CH), lambda i, k, m: (i, 0, k)),
                pl.BlockSpec((HP, 1), lambda i, k, m: (0, 0)),
                pl.BlockSpec((1, 1, CH), lambda i, k, m: (i, 0, k)),
                pl.BlockSpec((1, CH, 1), lambda i, k, m: (i, k, 0)),
                pl.BlockSpec((1, INNER, STATE), lambda i, k, m: (i, 0, 0)),
            ],
            out_specs=[
                pl.BlockSpec((1, INNER, CH), lambda i, k, m: (i, 0, k)),
                pl.BlockSpec((1, 1, INNER, STATE), lambda i, k, m: (i, k, 0, 0)),
            ],
            scratch_shapes=[
                pltpu.VMEM((INNER, STATE), F32),
                pltpu.VMEM((INNER, CH), F32),
                pltpu.VMEM((INNER, CH), BF16),
            ],
        ),
        out_shape=[
            jax.ShapeDtypeStruct((n, INNER, length), F32),
            jax.ShapeDtypeStruct((n, chunks, INNER, STATE), BF16),
        ],
        compiler_params=params(("arbitrary", "arbitrary")),
        name="forward_scan",
    )(marks, values, wr, wr, delta, rate, segrow, segcol, incoming)


def backward_kernel(
    marks_ref, val_ref, w_ref, r_ref, delta_ref, draw_ref, rate_ref, skip_ref, segrow_ref,
    segcol_ref, gy_ref, first_ref, start_ref, in_ref, carry_ref,
    gval_ref, gwr_ref, gdraw_ref, gbias_ref, grate_ref,
    grad, link, off, fresh, faded, gdelta, paid,
):
    n, step = pl.program_id(0), pl.program_id(1)
    k = pl.num_programs(1) - 1 - step

    @pl.when(step == 0)
    def _():
        grad[...] = in_ref[0].astype(F32)
        link[...] = carry_ref[0]

    @pl.when((n == 0) & (step == 0))
    def _():
        gbias_ref[...] = jnp.zeros_like(gbias_ref)
        grate_ref[...] = jnp.zeros_like(grate_ref)

    writers, readers = w_ref[0], r_ref[0]
    delta = delta_ref[0]
    segrow, segcol = segrow_ref[0], segcol_ref[0]
    decay, totals, fade, to_end, passing, barred = chunk_terms(
        delta, rate_ref, segrow, segcol, marks_ref[n, k, 0], marks_ref[n, k, 1]
    )
    columns = totals.T
    scores = nt(writers, readers)
    low_grad = grad[...].astype(BF16)
    off[...] = nt(low_grad, writers)
    gscores = jnp.zeros((CH, CH), F32)
    gdelta[...] = jnp.zeros_like(gdelta)
    paid[...] = jnp.zeros_like(paid)
    for h in range(HEADS):
        rows = slice(h * HEADDIM, (h + 1) * HEADDIM)
        spread = jnp.exp(totals[h : h + 1, :] - columns[:, h : h + 1] + barred)
        values = val_ref[0, rows, :].astype(F32)
        gy = gy_ref[0, rows, :]
        gy32 = gy.astype(F32)
        scaled = values * delta[h : h + 1, :]
        fresh[rows, :] = (scaled * to_end[h : h + 1, :]).astype(BF16)
        faded[rows, :] = (gy32 * fade[h : h + 1, :]).astype(BF16)
        gscaled = nt(gy, (spread * scores).astype(BF16)) + off[rows, :] * to_end[h : h + 1, :]
        low = scaled.astype(BF16)
        gscores = gscores + tn(low, gy) * spread
        paid[h : h + 1, :] = jnp.sum(low.astype(F32) * gscaled, axis=0, keepdims=True)
        gdelta[h : h + 1, :] = jnp.sum(values * gscaled, axis=0, keepdims=True)
        gval_ref[0, rows, :] = (
            gscaled * delta[h : h + 1, :] + gy32 * skip_ref[h : h + 1, :]
        ).astype(BF16)
    low_scores = gscores.astype(BF16)
    gwr_ref[0, :, :STATE] = nn(low_scores, readers) + tn(fresh[...], low_grad)
    gwr_ref[0, :, STATE:] = tn(low_scores, writers) + tn(faded[...], start_ref[0, 0])
    off[...] = nn(faded[...], readers)
    for h in range(HEADS):
        rows = slice(h * HEADDIM, (h + 1) * HEADDIM)
        grad[rows, :] = passing[h : h + 1, :] * grad[rows, :] + off[rows, :]
    difference = first_ref[0] - paid[...]
    reach = jnp.where(
        (segcol == segrow)
        & (
            lax.broadcasted_iota(jnp.int32, (CH, CH), 0)
            >= lax.broadcasted_iota(jnp.int32, (CH, CH), 1)
        ),
        1.0,
        0.0,
    )
    following = jnp.where(segrow == marks_ref[n, k, 2], 1.0, 0.0)
    gdecay = nn_high(difference, reach) + following * link[...]
    link[...] = gdecay[:, :1]
    gtotal = gdelta[...] - jnp.exp(rate_ref[...]) * gdecay
    gdraw = gtotal / (1.0 + jnp.exp(-draw_ref[0]))
    gdraw_ref[0] = gdraw
    gbias_ref[...] += jnp.sum(gdraw, axis=1, keepdims=True)
    grate_ref[...] += jnp.sum(gdecay * decay, axis=1, keepdims=True)


def backward_scan(
    marks, values, wr, delta, draw, rate, skip, segrow, segcol, gy, first, starts, incoming, carry
):
    n, _, length = values.shape
    chunks = length // CH
    back = lambda k: chunks - 1 - k
    lanes = lambda rows: pl.BlockSpec((1, rows, CH), lambda i, k, m: (i, 0, back(k)))
    column = pl.BlockSpec((HP, 1), lambda i, k, m: (0, 0))
    return pl.pallas_call(
        backward_kernel,
        grid_spec=pltpu.PrefetchScalarGridSpec(
            num_scalar_prefetch=1,
            grid=(n, chunks),
            in_specs=[
                lanes(INNER),
                pl.BlockSpec((1, CH, STATE), lambda i, k, m: (i, back(k), 0)),
                pl.BlockSpec((1, CH, STATE), lambda i, k, m: (i, back(k), 1)),
                lanes(HP),
                lanes(HP),
                column,
                column,
                lanes(1),
                pl.BlockSpec((1, CH, 1), lambda i, k, m: (i, back(k), 0)),
                lanes(INNER),
                lanes(HP),
                pl.BlockSpec((1, 1, INNER, STATE), lambda i, k, m: (i, back(k), 0, 0)),
                pl.BlockSpec((1, INNER, STATE), lambda i, k, m: (i, 0, 0)),
                pl.BlockSpec((1, HP, 1), lambda i, k, m: (i, 0, 0)),
            ],
            out_specs=[
                lanes(INNER),
                pl.BlockSpec((1, CH, 2 * STATE), lambda i, k, m: (i, back(k), 0)),
                lanes(HP),
                column,
                column,
            ],
            scratch_shapes=[
                pltpu.VMEM((INNER, STATE), F32),
                pltpu.VMEM((HP, 1), F32),
                pltpu.VMEM((INNER, CH), F32),
                pltpu.VMEM((INNER, CH), BF16),
                pltpu.VMEM((INNER, CH), BF16),
                pltpu.VMEM((HP, CH), F32),
                pltpu.VMEM((HP, CH), F32),
            ],
        ),
        out_shape=[
            jax.ShapeDtypeStruct((n, INNER, length), BF16),
            jax.ShapeDtypeStruct((n, length, 2 * STATE), F32),
            jax.ShapeDtypeStruct((n, HP, length), F32),
            jax.ShapeDtypeStruct((HP, 1), F32),
            jax.ShapeDtypeStruct((HP, 1), F32),
        ],
        compiler_params=params(("arbitrary", "arbitrary")),
        name="backward_scan",
    )(
        marks, values, wr, wr, delta, draw, rate, skip, segrow, segcol, gy, first, starts,
        incoming, carry,
    )


def leave_kernel(
    marks_ref, normed_ref, wgate_ref, wout_ref, cot_ref, tok_ref, y_ref, val_ref, r_ref,
    gain_ref, skip_ref, delta_ref, rate_ref, segrow_ref,
    out_ref, gy_ref, ggate_ref, first_ref, gstate_ref, gout_ref, ggain_ref, gskip_ref,
    gate, gated, upward, lifted, flat, fade, total, products, skips,
):
    n = pl.program_id(0)
    length = normed_ref.shape[1]
    tiles = INNER // TILE
    lanes = range(0, length, 128)

    @pl.when(n == 0)
    def _():
        total[...] = jnp.zeros_like(total)
        ggain_ref[...] = jnp.zeros_like(ggain_ref)
        skips[...] = jnp.zeros_like(skips)

    totals = nn_high(-jnp.exp(rate_ref[...]) * delta_ref[0], triangle(length))
    fade[...] = jnp.exp(totals) * jnp.where(segrow_ref[0] == marks_ref[n, 0, 0], 1.0, 0.0)

    def fold(v):
        return jnp.sum(v.reshape(HEADDIM // 8, 8, 128), axis=0)

    def span(c):
        return pl.ds(pl.multiple_of(c * TILE, TILE), TILE)

    def head_rows(c, h):
        return pl.ds(pl.multiple_of(c * TILE + h * HEADDIM, HEADDIM), HEADDIM)

    def gate_tile(c, squares):
        gate[span(c), :] = nn(normed_ref[0], wgate_ref[:, span(c)]).T.astype(BF16)
        parts = list(squares)
        for h in range(4):
            rows = head_rows(c, h)
            skip = skip_ref[pl.ds(c * 4 + h, 1), :]
            for i, b in enumerate(lanes):
                g = gate[rows, b : b + 128].astype(F32)
                values = val_ref[0, rows, b : b + 128].astype(F32)
                v = (y_ref[0, rows, b : b + 128] + skip * values) * (g / (1.0 + jnp.exp(-g)))
                gated[rows, b : b + 128] = v
                parts[i] = parts[i] + fold(v * v)
        return tuple(parts)

    zero = tuple(jnp.zeros((8, 128), F32) for _ in lanes)
    down = lambda s: jnp.sum(s, axis=0, keepdims=True)
    squares = lax.fori_loop(0, tiles, gate_tile, zero)
    scale = [lax.rsqrt(down(s) * (1.0 / INNER) + EPS) for s in squares]

    def norm_tile(c, dots):
        upward[span(c), :] = nt(wout_ref[span(c), :], cot_ref[0])
        parts = list(dots)
        for h in range(4):
            rows = head_rows(c, h)
            gain = gain_ref[rows, :]
            sums = jnp.zeros((HEADDIM, 128), F32)
            for i, b in enumerate(lanes):
                v = gated[rows, b : b + 128]
                normal = v * scale[i]
                lifted[rows, b : b + 128] = (normal * gain).astype(BF16)
                u = upward[rows, b : b + 128]
                sums = sums + u * normal
                u = u * gain
                upward[rows, b : b + 128] = u
                parts[i] = parts[i] + fold(u * v)
            ggain_ref[rows, :] += jnp.sum(sums, axis=1, keepdims=True)
        low = lifted[span(c), :]
        flat[:, span(c)] = low.T
        total[span(c), :] += nn(low, cot_ref[0])
        return tuple(parts)

    dots = lax.fori_loop(0, tiles, norm_tile, zero)
    pull = [s * s * s * down(d) * (1.0 / INNER) for s, d in zip(scale, dots)]
    def back_tile(c, carry):
        for h in range(4):
            rows = head_rows(c, h)
            head = pl.ds(c * 4 + h, 1)
            eight = pl.ds(pl.multiple_of((c * 4 + h) * 8, 8), 8)
            skip = skip_ref[head, :]
            fading = fade[head, :]
            sums = jnp.zeros((8, 128), F32)
            for i, b in enumerate(lanes):
                gv = scale[i] * upward[rows, b : b + 128] - pull[i] * gated[rows, b : b + 128]
                g = gate[rows, b : b + 128].astype(F32)
                sig = 1.0 / (1.0 + jnp.exp(-g))
                silu = g * sig
                values = val_ref[0, rows, b : b + 128].astype(F32)
                y = y_ref[0, rows, b : b + 128]
                low = (gv * silu).astype(BF16)
                gm = low.astype(F32)
                ggate_ref[0, rows, b : b + 128] = (
                    gv * (y + skip * values) * (sig + silu * (1.0 - sig))
                ).astype(BF16)
                gy_ref[0, rows, b : b + 128] = low
                products[eight, b : b + 128] = fold(gm * y)
                sums = sums + fold(gm * values)
                lifted[rows, b : b + 128] = (gm * fading[:, b : b + 128]).astype(BF16)
            skips[eight, :] += sums
        gstate_ref[0, span(c), :] = nn(lifted[span(c), :], r_ref[0]).astype(BF16)
        return carry

    lax.fori_loop(0, tiles, back_tile, 0)
    first_ref[0, 0:HEADS, :] = jnp.sum(products[...].reshape(HEADS, 8, length), axis=1)
    first_ref[0, HEADS:, :] = jnp.zeros((HP - HEADS, length), F32)
    for b in range(0, D, TILE):
        branch = nn(flat[...], wout_ref[:, b : b + TILE])
        out_ref[0, :, b : b + TILE] = (tok_ref[0, :, b : b + TILE].astype(F32) + branch).astype(BF16)

    @pl.when(n == pl.num_programs(0) - 1)
    def _():
        gout_ref[...] = total[...].astype(BF16)
        gskip_ref[0:HEADS, :] = jnp.sum(skips[...].reshape(HEADS, 8, 128), axis=1)
        gskip_ref[HEADS:, :] = jnp.zeros((HP - HEADS, 128), F32)


def leave(
    marks, normed, wgate, wout, cot, tokens, y, values, wr, gain, skip, delta, rate, segrow
):
    n, length, _ = normed.shape
    one = lambda *shape: pl.BlockSpec((1,) + shape, lambda i, m: (i, 0, 0))
    whole = lambda a: pl.BlockSpec(a.shape, lambda i, m: (0,) * a.ndim)
    flat = lambda *shape: pl.BlockSpec(shape, lambda i, m: (0, 0))
    return pl.pallas_call(
        leave_kernel,
        grid_spec=pltpu.PrefetchScalarGridSpec(
            num_scalar_prefetch=1,
            grid=(n,),
            in_specs=[
                one(length, D), whole(wgate), whole(wout), one(length, D), one(length, D),
                one(INNER, length), one(INNER, length),
                pl.BlockSpec((1, length, STATE), lambda i, m: (i, 0, 1)),
                whole(gain), whole(skip), one(HP, length), whole(rate), one(1, length),
            ],
            out_specs=[
                one(length, D), one(INNER, length), one(INNER, length), one(HP, length),
                one(INNER, STATE), flat(INNER, D), flat(INNER, 1), flat(HP, 128),
            ],
            scratch_shapes=[
                pltpu.VMEM((INNER, length), BF16),
                pltpu.VMEM((INNER, length), F32),
                pltpu.VMEM((INNER, length), F32),
                pltpu.VMEM((INNER, length), BF16),
                pltpu.VMEM((length, INNER), BF16),
                pltpu.VMEM((HP, length), F32),
                pltpu.VMEM((INNER, D), F32),
                pltpu.VMEM((HEADS * 8, length), F32),
                pltpu.VMEM((HEADS * 8, 128), F32),
            ],
        ),
        out_shape=[
            jax.ShapeDtypeStruct((n, length, D), BF16),
            jax.ShapeDtypeStruct((n, INNER, length), BF16),
            jax.ShapeDtypeStruct((n, INNER, length), BF16),
            jax.ShapeDtypeStruct((n, HP, length), F32),
            jax.ShapeDtypeStruct((n, INNER, STATE), BF16),
            jax.ShapeDtypeStruct((INNER, D), BF16),
            jax.ShapeDtypeStruct((INNER, 1), F32),
            jax.ShapeDtypeStruct((HP, 128), F32),
        ],
        compiler_params=params(("arbitrary",)),
        name="leave",
    )(marks, normed, wgate, wout, cot, tokens, y, values, wr, gain, skip, delta, rate, segrow)


def conv_back_kernel(
    gval_ref, gwr_ref, dsilu_ref, raw_ref, near_ref, cw_ref,
    graw_ref, tail_ref, ghalo_ref, gconv_ref,
    pre, rawbuf, mask,
):
    c, n = pl.program_id(0), pl.program_id(1)
    length = dsilu_ref.shape[1]

    @pl.when(n == 0)
    def _():
        gconv_ref[...] = jnp.zeros_like(gconv_ref)

    for j in range(1, CONV):
        mask[j - 1] = jnp.broadcast_to(near_ref[0, :, j : j + 1], (length + 8, 128))
    pre[0:8, :] = jnp.zeros((8, TILE), F32)
    pre[length + 8 :, :] = jnp.zeros((8, TILE), F32)

    @pl.when(c < INNER // TILE)
    def _():
        pre[8 : length + 8, :] = gval_ref[0].astype(F32).T

    @pl.when(c == INNER // TILE)
    def _():
        pre[8 : length + 8, :] = gwr_ref[0]

    rawbuf[...] = raw_ref[0].astype(F32)
    for half in range(0, TILE, 128):
        cols = slice(half, half + 128)
        w = cw_ref[:, cols]
        for b in range(0, length, 64):
            pre[8 + b : 72 + b, cols] = pre[8 + b : 72 + b, cols] * dsilu_ref[0, b : b + 64, cols].astype(F32)
        sums = [jnp.zeros((8, 128), F32) for _ in range(CONV + 1)]
        for b, rows in [(0, 8)] + [(8 + 64 * i, 64) for i in range(length // 64)]:
            fold = lambda v: jnp.sum(v.reshape(rows // 8, 8, 128), axis=0)
            raw = rawbuf[HALO - 8 + b : HALO - 8 + b + rows, cols]
            here = pre[b : b + rows, cols]
            grad = w[3:4] * here
            sums[3] = sums[3] + fold(raw * here)
            sums[4] = sums[4] + fold(here)
            for j in range(1, CONV):
                term = pre[b + j : b + j + rows, cols] * mask[j - 1, b : b + rows, :]
                grad = grad + w[3 - j : 4 - j] * term
                sums[3 - j] = sums[3 - j] + fold(raw * term)
            if b == 0:
                ghalo_ref[0, :, cols] = grad
            else:
                graw_ref[0, b - 8 : b - 8 + rows, cols] = grad.astype(BF16)
        tail_ref[0, :, cols] = grad[48:]
        gconv_ref[0 : CONV + 1, cols] += jnp.concatenate(
            [jnp.sum(s, axis=0, keepdims=True) for s in sums], axis=0
        )


def conv_back(gval, gwr, dsilu, raw, near, cw):
    n, length, _ = dsilu.shape
    tiles = XBC // TILE
    rows = lambda r: pl.BlockSpec((1, r, TILE), lambda c, i: (i, 0, c))
    return pl.pallas_call(
        conv_back_kernel,
        grid=(tiles, n),
        in_specs=[
            pl.BlockSpec((1, TILE, length), lambda c, i: (i, jnp.minimum(c, INNER // TILE - 1), 0)),
            pl.BlockSpec((1, length, TILE), lambda c, i: (i, 0, 0)),
            rows(length),
            rows(length + HALO),
            pl.BlockSpec((1, length + 8, 8), lambda c, i: (i, 0, 0)),
            pl.BlockSpec((8, TILE), lambda c, i: (0, c)),
        ],
        out_specs=[
            rows(length), rows(16), rows(8), pl.BlockSpec((8, TILE), lambda c, i: (0, c)),
        ],
        out_shape=[
            jax.ShapeDtypeStruct((n, length, XBC), BF16),
            jax.ShapeDtypeStruct((n, 16, XBC), F32),
            jax.ShapeDtypeStruct((n, 8, XBC), F32),
            jax.ShapeDtypeStruct((8, XBC), F32),
        ],
        scratch_shapes=[
            pltpu.VMEM((length + 16, TILE), F32),
            pltpu.VMEM((length + HALO, TILE), F32),
            pltpu.VMEM((CONV - 1, length + 8, 128), F32),
        ],
        compiler_params=params(("arbitrary", "arbitrary")),
        name="conv_back",
    )(gval, gwr, dsilu, raw, near, cw)


MESH = pl.DeviceIdType.MESH


def sum_kernel(
    width, group, replicas, x_ref, o_ref, own, from_group, from_reps,
    send_a, recv_a, send_b, recv_b, send_c, recv_c,
):
    r, f, s = lax.axis_index("rep"), lax.axis_index("fsdp"), lax.axis_index("seq")
    me = f * 2 + s
    peers = []
    for j in range(1, group):
        p = lax.rem(me + j, group)
        peers.append((p, (r, lax.div(p, 2), lax.rem(p, 2))))
    others = [(lax.rem(r + j, replicas), f, s) for j in range(1, replicas)]
    barrier = pltpu.get_barrier_semaphore()
    for device in [d for _, d in peers] + others:
        pl.semaphore_signal(barrier, inc=1, device_id=device, device_id_type=MESH)
    pl.semaphore_wait(barrier, group + replicas - 2)

    sent = []
    for j, (p, device) in enumerate(peers):
        copy = pltpu.make_async_remote_copy(
            x_ref.at[pl.ds(p * width, width)], from_group.at[j], send_a.at[j], recv_a.at[j],
            device_id=device, device_id_type=MESH,
        )
        copy.start()
        sent.append(copy)
    total = x_ref[pl.ds(me * width, width)]
    for j in range(group - 1):
        sent[j].wait_recv()
        total = total + from_group[j]
    own[...] = total
    from_reps[pl.ds(r, 1)] = total[None]
    for j, device in enumerate(others):
        copy = pltpu.make_async_remote_copy(
            own, from_reps.at[r], send_b.at[j], recv_b.at[j], device_id=device, device_id_type=MESH
        )
        copy.start()
        sent.append(copy)
    for j in range(replicas - 1):
        sent[group - 1 + j].wait_recv()
    total = from_reps[0]
    for j in range(1, replicas):
        total = total + from_reps[j]
    mine = pl.ds(me * width, width)
    o_ref[mine] = total
    shared = []
    for j, (p, device) in enumerate(peers):
        copy = pltpu.make_async_remote_copy(
            o_ref.at[mine], o_ref.at[mine], send_c.at[j], recv_c.at[j],
            device_id=device, device_id_type=MESH,
        )
        copy.start()
        shared.append(copy)
    for copy in sent:
        copy.wait_send()
    for copy in shared:
        copy.wait()


def sum_everywhere(tiles, identity):
    group = lax.axis_size("fsdp") * lax.axis_size("seq")
    replicas = lax.axis_size("rep")
    width = tiles.shape[0] // group
    block = (width, 8, 128)
    dma = pltpu.SemaphoreType.DMA
    return pl.pallas_call(
        partial(sum_kernel, width, group, replicas),
        out_shape=jax.ShapeDtypeStruct(tiles.shape, F32),
        in_specs=[pl.BlockSpec(memory_space=pltpu.VMEM)],
        out_specs=pl.BlockSpec(memory_space=pltpu.VMEM),
        scratch_shapes=[
            pltpu.VMEM(block, F32),
            pltpu.VMEM((group - 1,) + block, F32),
            pltpu.VMEM((replicas,) + block, F32),
            dma((group - 1,)), dma((group - 1,)),
            dma((replicas - 1,)), dma((replicas - 1,)),
            dma((group - 1,)), dma((group - 1,)),
        ],
        compiler_params=pltpu.CompilerParams(collective_id=identity, has_side_effects=True),
        name="sum_everywhere",
    )(tiles)


def split_three(v):
    high = v.astype(BF16)
    rest = v - high.astype(F32)
    middle = rest.astype(BF16)
    return [high, middle, (rest - middle.astype(F32)).astype(BF16)]


def join_three(v):
    return v[0:8] + v[8:16] + v[16:24]


def tiles_of(extent):
    return -(-extent // 128)


def pieces_of(rows):
    return [(i, i * 128, min(128, rows - i * 128)) for i in range(tiles_of(rows))]


def left_kernel(me_ref, sin_ref, sout_ref, gate_ref, raw_ref, out_ref, err_ref, x_ref):
    group, rows_in, rows_out = gate_ref.shape[0], gate_ref.shape[1], out_ref.shape[1]
    ahead = tiles_of(rows_in)
    width = ahead + tiles_of(rows_out)
    x_ref[...] = jnp.zeros_like(x_ref)
    for p in range(group):
        left = join_three(nt(sin_ref[:, :INNER], gate_ref[p]) + nt(sin_ref[:, INNER:], raw_ref[p]))
        for i, at, n in pieces_of(rows_in):
            x_ref[p * width + i, :, :n] = left[:, at : at + n]
        left = join_three(nt(sout_ref[...], out_ref[p]))
        for i, at, n in pieces_of(rows_out):
            x_ref[p * width + ahead + i, :, :n] = left[:, at : at + n]
    mine = pl.ds(me_ref[0] * width, width)
    x_ref[mine] = x_ref[mine] + err_ref[...]


def inverse_factor(gram):
    rows = lax.broadcasted_iota(jnp.int32, (8, 8), 0)
    cols = lax.broadcasted_iota(jnp.int32, (8, 8), 1)
    left, right = gram, jnp.where(rows == cols, 1.0, 0.0)
    for j in range(7):
        factor = jnp.where(rows[:, :1] > j, left[:, j : j + 1] / left[j : j + 1, j : j + 1], 0.0)
        left, right = left - factor * left[j : j + 1, :], right - factor * right[j : j + 1, :]
    pivots = jnp.sum(jnp.where(rows == cols, left, 0.0), axis=1, keepdims=True)
    return right * lax.rsqrt(pivots)


def nt_high(a, b):
    return lax.dot_general(
        a, b, (((1,), (1,)), ((), ())), precision=HIGH, preferred_element_type=F32
    )


def tn_high(a, b):
    return lax.dot_general(
        a, b, (((0,), (0,)), ((), ())), precision=HIGH, preferred_element_type=F32
    )


def right_kernel(
    replicas, me_ref, left_ref, gate_ref, raw_ref, out_ref, ein_ref, eout_ref, small_ref,
    x_ref, own_ref,
    hat,
):
    group, rows_in, rows_out = gate_ref.shape[0], gate_ref.shape[1], out_ref.shape[1]
    ahead = tiles_of(rows_in)
    width = ahead + tiles_of(rows_out)
    for first, last in ((0, ahead), (ahead, width)):
        gram = jnp.zeros((8, 8), F32)
        for p in range(group):
            for i in range(first, last):
                tile = left_ref[p * width + i] * (1.0 / replicas)
                gram = gram + nt_high(tile, tile)
        inverse = inverse_factor(gram)
        for p in range(group):
            for i in range(first, last):
                hat[p * width + i] = nn_high(inverse, left_ref[p * width + i] * (1.0 / replicas))
    mine = pl.ds(me_ref[0] * width, width)
    own = hat[mine]
    own_ref[...] = own

    def product(matrices, rows, skipped, error, columns, at):
        spread = [
            jnp.concatenate(split_three(joined(hat, p * width + skipped, rows)), axis=0)
            for p in range(group)
        ]
        mixed = joined(own, skipped, rows)
        for ref, width_here in matrices:
            for b in range(0, width_here, TILE):
                total = jnp.zeros((24, TILE), F32)
                for p in range(group):
                    total = total + nn(spread[p], ref[p, :, b : b + TILE])
                right = join_three(total) + nn_high(mixed, error[:, columns + b : columns + b + TILE])
                for half in range(0, TILE, 128):
                    x_ref[at + (columns + b + half) // 128] = right[:, half : half + 128]
            columns += width_here

    def joined(tiles, start, rows):
        return jnp.concatenate([tiles[start + i][:, :n] for i, _, n in pieces_of(rows)], axis=1)

    product(((gate_ref, INNER), (raw_ref, XBC)), rows_in, 0, ein_ref, 0, 0)
    product(((out_ref, D),), rows_out, ahead, eout_ref, 0, PROJ // 128)
    after = (PROJ + D) // 128
    x_ref[after:] = jnp.zeros((x_ref.shape[0] - after, 8, 128), F32)
    x_ref[after : after + small_ref.shape[0]] = small_ref[...]


def update_kernel(
    rates, replicas, x_ref, own_ref, win_ref, wout_ref, min_ref, mout_ref,
    nwin_ref, nwout_ref, nmin_ref, nmout_ref,
):
    ahead = tiles_of(win_ref.shape[0])
    for w, m, nw, nm, first, columns, at, rate in (
        (win_ref, min_ref, nwin_ref, nmin_ref, 0, PROJ, 0, rates[0]),
        (wout_ref, mout_ref, nwout_ref, nmout_ref, ahead, D, PROJ // 128, rates[1]),
    ):
        for i, start, n in pieces_of(w.shape[0]):
            rows = slice(start, start + n)
            left = own_ref[first + i][:, :n]
            for b in range(0, columns, 128):
                approx = tn_high(left, x_ref[at + b // 128] * (1.0 / replicas))
                momentum = MOMENTUM * m[rows, b : b + 128] + approx
                nm[rows, b : b + 128] = momentum
                nw[rows, b : b + 128] = w[rows, b : b + 128] - rate * momentum


def residual_kernel(
    replicas, x_ref, own_ref, gate_ref, raw_ref, out_ref, ein_ref, eout_ref, nein_ref, neout_ref
):
    ahead = tiles_of(ein_ref.shape[0])
    for grad, error, new, first, columns, at, offset in (
        (gate_ref, ein_ref, nein_ref, 0, INNER, 0, 0),
        (raw_ref, ein_ref, nein_ref, 0, XBC, INNER // 128, INNER),
        (out_ref, eout_ref, neout_ref, ahead, D, PROJ // 128, 0),
    ):
        for i, start, n in pieces_of(error.shape[0]):
            rows = slice(start, start + n)
            left = own_ref[first + i][:, :n]
            for b in range(0, columns, 128):
                approx = tn_high(left, x_ref[at + b // 128] * (1.0 / replicas))
                here = slice(offset + b, offset + b + 128)
                new[rows, here] = (grad[rows, b : b + 128].astype(F32) + error[rows, here]) - approx


def local_call(kernel, outs, *arrays, scalars=0, scratch=(), name):
    spec = pl.BlockSpec(memory_space=pltpu.VMEM)
    return pl.pallas_call(
        kernel,
        out_shape=outs,
        in_specs=[pl.BlockSpec(memory_space=pltpu.SMEM)] * scalars + [spec] * (len(arrays) - scalars),
        out_specs=jax.tree.map(lambda _: spec, outs),
        scratch_shapes=list(scratch),
        compiler_params=pltpu.CompilerParams(vmem_limit_bytes=VMEM_LIMIT),
        name=name,
    )(*arrays)


def split_small(small_values):
    pieces = []
    offset = 0
    for amount in (D, D * HEADS, CONV * XBC, XBC, INNER, HEADS, HEADS, HEADS):
        pieces.append(small_values[offset : offset + amount])
        offset = offset + amount
    return (
        pieces[0],
        pieces[1].reshape(D, HEADS),
        pieces[2].reshape(CONV, XBC),
        pieces[3],
        pieces[4],
        pieces[5],
        pieces[6],
        pieces[7],
    )


def step_rates(tokens_replica):
    grad_scale = 0.3 * math.sqrt(tokens_replica)
    return (
        0.5 / (math.sqrt(D) * grad_scale),
        0.5 / (math.sqrt(INNER) * grad_scale),
        0.1 / grad_scale,
    )


def to_later(block):
    return lax.ppermute(block, "seq", [(i, i + 1) for i in range(lax.axis_size("seq") - 1)])


def to_earlier(block):
    return lax.ppermute(block, "seq", [(i + 1, i) for i in range(lax.axis_size("seq") - 1)])


def head_column(values):
    return jnp.pad(values, (0, HP - HEADS)).reshape(HP, 1)


def gather_rows(shard):
    return lax.all_gather(shard, ("fsdp", "seq"), axis=0, tiled=True)


def scatter_rows(total):
    return lax.psum_scatter(total, ("fsdp", "seq"), scatter_dimension=0, tiled=True)


def body(
    tokens,
    cotangent,
    segments,
    input_weight,
    output_weight,
    small_values,
    input_momentum,
    output_momentum,
    small_momentum,
    input_error,
    output_error,
    input_start,
    output_start,
):
    shape = tokens.shape
    pieces = shape[0] * shape[1]
    length = shape[2]
    chunks = length // CH
    replicas = lax.axis_size("rep")
    place = lax.axis_index("seq")
    whole_length = segments.shape[2]
    tokens_replica = pieces * length * lax.axis_size("fsdp") * lax.axis_size("seq")
    rate_in, rate_out, rate_small = step_rates(tokens_replica)
    norm_gain, delta_weight, conv_weight, conv_bias, gate_gain, dt_bias, log_rate, skip_gain = (
        split_small(small_values)
    )
    raw_low = input_weight[:, INNER:].astype(BF16)
    gate_low = input_weight[:, :INNER].astype(BF16)
    raw_full = gather_rows(raw_low)
    gate_full = gather_rows(gate_low)
    output_full = gather_rows(output_weight.astype(BF16))

    tokens = tokens.reshape(pieces, length, D)
    cotangent = cotangent.reshape(pieces, length, D)
    documents = segments.reshape(pieces, whole_length)
    padded = jnp.pad(documents, ((0, 0), (HALO, 1)), constant_values=-1)
    wider = lax.dynamic_slice_in_dim(padded, place * length, HALO + length + 1, 1)
    own = wider[:, HALO : HALO + length]
    ahead = jnp.pad(wider[:, HALO - 8 : HALO + length], ((0, 0), (0, 8)), constant_values=-3)
    same = jnp.stack(
        [
            jnp.where(wider[:, HALO - j : HALO - j + length] == own, 1.0, 0.0)
            for j in range(CONV)
        ]
        + [jnp.zeros(own.shape, F32)] * (8 - CONV),
        axis=2,
    )
    near = jnp.stack(
        [
            jnp.where(ahead[:, j : j + length + 8] == ahead[:, : length + 8], 1.0, 0.0)
            for j in range(CONV)
        ]
        + [jnp.zeros((pieces, length + 8), F32)] * (8 - CONV),
        axis=2,
    )
    edges = wider[:, HALO - 1 :]
    marks = jnp.stack(
        [edges[:, :-2:CH], edges[:, CH::CH][:, :chunks], edges[:, CH + 1 :: CH]], axis=2
    )
    segrow = own[:, None, :]
    segcol = own[:, :, None]
    delta_low = delta_weight.astype(BF16)
    delta_rows = jnp.pad(delta_low.T, ((0, HP - HEADS), (0, 0)))
    taps = jnp.pad(conv_weight, ((0, 8 - CONV), (0, 0)))
    bias, rate, skip = head_column(dt_bias), head_column(log_rate), head_column(skip_gain)
    halo = to_later(tokens[:, length - HALO :, :])

    def error_tiles(error, start):
        left = nt_high(start.T, error[0])
        amount = tiles_of(left.shape[1])
        left = jnp.pad(left, ((0, 0), (0, amount * 128 - left.shape[1])))
        return left.reshape(8, amount, 128).transpose(1, 0, 2)

    error_left = jnp.concatenate(
        [error_tiles(input_error, input_start), error_tiles(output_error, output_start)], axis=0
    )
    start_in = jnp.concatenate(split_three(input_start.T), axis=0)
    start_out = jnp.concatenate(split_three(output_start.T), axis=0)

    normed, raw, dsilu, values, wr, draw, delta, send = enter(
        tokens, halo, norm_gain[None], raw_full, delta_rows, taps, conv_bias[None], same, bias,
        rate, segrow,
    )
    incoming = to_later(send)
    y, starts = forward_scan(marks, values, wr, delta, rate, segrow, segcol, incoming)
    output, gy, ggate, first, gstate, grad_output, ggain, gskip = leave(
        marks, normed, gate_full, output_full, cotangent, tokens, y, values, wr,
        gate_gain[:, None], skip, delta, rate, segrow,
    )
    output_total = scatter_rows(grad_output)
    outgoing = to_earlier(gstate)
    grad_gate = jnp.einsum("nld,nkl->dk", normed, ggate, preferred_element_type=F32).astype(BF16)
    gate_total = scatter_rows(grad_gate)
    carry = jnp.sum(
        (outgoing.astype(F32) * send.astype(F32)).reshape(pieces, HEADS, HEADDIM * STATE), axis=2
    )
    carry = jnp.pad(carry, ((0, 0), (0, HP - HEADS)))[:, :, None]
    gval, gwr, gdraw, gbias, grate = backward_scan(
        marks, values, wr, delta, draw, rate, skip, segrow, segcol, gy, first, starts, outgoing,
        carry,
    )
    graw, tail, ghalo, gconv = conv_back(gval, gwr, dsilu, raw, near, taps)
    returned = to_earlier(ghalo)
    tail = tail + jnp.pad(returned, ((0, 0), (8, 0), (0, 0)))
    graw = lax.dynamic_update_slice_in_dim(graw, tail.astype(BF16), length - 16, 1)
    grad_raw = jnp.einsum("nld,nlk->dk", normed, graw, preferred_element_type=F32).astype(BF16)
    raw_total = scatter_rows(grad_raw)
    gdelta = gdraw[:, :HEADS].astype(BF16)
    delta_weight_grad = jnp.einsum("nld,nhl->dh", normed, gdelta, preferred_element_type=F32)
    normed_grad = (
        jnp.einsum("nkl,dk->nld", ggate, gate_full, preferred_element_type=F32)
        + jnp.einsum("nlk,dk->nld", graw, raw_full, preferred_element_type=F32)
        + jnp.einsum("nhl,dh->nld", gdelta, delta_low, preferred_element_type=F32)
    )
    rows_in = tokens.astype(F32)
    scale = lax.rsqrt(jnp.mean(rows_in * rows_in, axis=-1, keepdims=True) + EPS)
    lifted = normed_grad * norm_gain
    norm_gain_grad = jnp.sum(normed_grad * rows_in * scale, axis=(0, 1))
    rows_grad = scale * lifted - rows_in * (
        scale * scale * scale * jnp.mean(lifted * rows_in, axis=-1, keepdims=True)
    )
    input_grad = (cotangent.astype(F32) + rows_grad).astype(BF16)
    small_total = jnp.concatenate(
        [
            norm_gain_grad,
            delta_weight_grad.reshape(-1),
            gconv[:CONV].reshape(-1),
            gconv[CONV],
            ggain[:, 0],
            gbias[:HEADS, 0],
            grate[:HEADS, 0],
            jnp.sum(gskip[:HEADS], axis=1),
        ]
    )
    group = lax.axis_size("fsdp") * lax.axis_size("seq")
    me = (lax.axis_index("fsdp") * lax.axis_size("seq") + place).astype(jnp.int32).reshape(1)
    tall = lambda tiles: jax.ShapeDtypeStruct((tiles, 8, 128), F32)
    like = lambda a: jax.ShapeDtypeStruct(a.shape, a.dtype)
    by_owner = lambda a: a.reshape(group, a.shape[0] // group, a.shape[1])
    grads = (by_owner(grad_gate), by_owner(grad_raw), by_owner(grad_output))
    width = error_left.shape[0]
    lefts = local_call(
        left_kernel, tall(group * width), me, start_in, start_out, *grads, error_left, scalars=1,
        name="left",
    )
    lefts = sum_everywhere(lefts, 1)
    vectors = tiles_of(small_total.shape[0] * 128 // 1024)
    flat = lambda a: jnp.pad(a, (0, vectors * 1024 - a.shape[0])).reshape(vectors, 8, 128)
    per_owner = -(-((PROJ + D) // 128 + vectors) // group)
    rights, own_left = local_call(
        partial(right_kernel, replicas),
        (tall(group * per_owner), tall(width)),
        me, lefts, *grads, input_error[0], output_error[0], flat(small_total),
        scalars=1,
        scratch=[pltpu.VMEM((group * width, 8, 128), F32)],
        name="right",
    )
    rights = sum_everywhere(rights, 2)
    new_input_weight, new_output_weight, new_input_momentum, new_output_momentum = local_call(
        partial(update_kernel, (rate_in, rate_out), replicas),
        tuple(map(like, (input_weight, output_weight, input_momentum, output_momentum))),
        rights, own_left, input_weight, output_weight, input_momentum, output_momentum,
        name="update",
    )
    new_input_error, new_output_error = local_call(
        partial(residual_kernel, replicas),
        (like(input_error[0]), like(output_error[0])),
        rights, own_left, gate_total, raw_total, output_total, input_error[0], output_error[0],
        name="residual",
    )
    rows_of = lambda tiles, amount: tiles.transpose(0, 2, 1).reshape(-1, 8)[:amount]
    ahead = tiles_of(input_weight.shape[0])
    input_left = rows_of(own_left[:ahead], input_weight.shape[0])
    output_left = rows_of(own_left[ahead:], output_weight.shape[0])
    input_right = rows_of(rights[: PROJ // 128], PROJ) / replicas
    output_right = rows_of(rights[PROJ // 128 : (PROJ + D) // 128], D) / replicas
    small_sum = rights[(PROJ + D) // 128 :].reshape(-1)[: small_values.shape[0]]
    new_small_momentum = MOMENTUM * small_momentum + small_sum / replicas
    new_small_values = small_values - rate_small * new_small_momentum
    return (
        output.reshape(shape),
        input_grad.reshape(shape),
        new_input_weight,
        new_output_weight,
        new_input_momentum,
        new_output_momentum,
        new_small_values,
        new_small_momentum,
        input_left,
        input_right,
        output_left,
        output_right,
        new_input_error[None],
        new_output_error[None],
    )


def solution(mesh):
    return jax.shard_map(
        body,
        mesh=mesh,
        in_specs=(
            P(None, ("rep", "fsdp"), "seq", None),
            P(None, ("rep", "fsdp"), "seq", None),
            P(None, ("rep", "fsdp"), None),
            P(("fsdp", "seq"), None),
            P(("fsdp", "seq"), None),
            P(),
            P(("fsdp", "seq"), None),
            P(("fsdp", "seq"), None),
            P(),
            P("rep", ("fsdp", "seq"), None),
            P("rep", ("fsdp", "seq"), None),
            P(),
            P(),
        ),
        out_specs=(
            P(None, ("rep", "fsdp"), "seq", None),
            P(None, ("rep", "fsdp"), "seq", None),
            P(("fsdp", "seq"), None),
            P(("fsdp", "seq"), None),
            P(("fsdp", "seq"), None),
            P(("fsdp", "seq"), None),
            P(),
            P(),
            P(("fsdp", "seq"), None),
            P(),
            P(("fsdp", "seq"), None),
            P(),
            P("rep", ("fsdp", "seq"), None),
            P("rep", ("fsdp", "seq"), None),
        ),
        check_vma=False,
    )
```

```python
from functools import partial
import math

import jax
import jax.numpy as jnp
from jax import lax
from jax.experimental import pallas as pl
from jax.experimental.pallas import tpu as pltpu
from jax.sharding import PartitionSpec as P

D = 768
INNER = 1536
HEADS = 24
HEADDIM = 64
STATE = 128
CONV = 4
PROJ = 3328
XBC = 1792

EPS = 1e-05
MOMENTUM = 0.9
HIGH = lax.Precision.HIGHEST
F32 = jnp.float32
BF16 = jnp.bfloat16
HP = 32
CH = 128
HALO = 16
TILE = 256
NEG = -1e30
VMEM_LIMIT = 63 * 2**20
MESH = pl.DeviceIdType.MESH

BEFORE = 3
LEAD = 128
BIAS, RATE, SKIP = 0, 1, 2
AT_CONV = D + D * HEADS
AT_GATE = AT_CONV + (CONV + 1) * XBC
AT_HEADS = AT_GATE + INNER


def nn(a, b):
    return lax.dot_general(a, b, (((1,), (0,)), ((), ())), preferred_element_type=F32)


def nt(a, b):
    return lax.dot_general(a, b, (((1,), (1,)), ((), ())), preferred_element_type=F32)


def tn(a, b):
    return lax.dot_general(a, b, (((0,), (0,)), ((), ())), preferred_element_type=F32)


def nn_high(a, b):
    return lax.dot_general(
        a, b, (((1,), (0,)), ((), ())), precision=HIGH, preferred_element_type=F32
    )


def nt_high(a, b):
    return lax.dot_general(
        a, b, (((1,), (1,)), ((), ())), precision=HIGH, preferred_element_type=F32
    )


def tn_high(a, b):
    return lax.dot_general(
        a, b, (((0,), (0,)), ((), ())), precision=HIGH, preferred_element_type=F32
    )


def softplus(v):
    return jnp.maximum(v, 0.0) + jnp.log1p(jnp.exp(-jnp.abs(v)))


def sigmoid(v):
    return 0.5 + 0.5 * jnp.tanh(0.5 * v)


def triangle(extent):
    return jnp.where(
        lax.broadcasted_iota(jnp.int32, (extent, extent), 0)
        <= lax.broadcasted_iota(jnp.int32, (extent, extent), 1),
        1.0,
        0.0,
    )


def column(heads_ref, row):
    return heads_ref[...].T[:HP, row : row + 1]


def square_of(row):
    return jnp.broadcast_to(row, (128, 128)).T


def params(semantics, **more):
    return pltpu.CompilerParams(
        dimension_semantics=semantics, vmem_limit_bytes=VMEM_LIMIT, **more
    )


def piece(*shape):
    return pl.BlockSpec((1,) + shape, lambda i: (i,) + (0,) * len(shape))


def whole(shape, ranks=1):
    index = (lambda i: (0,) * len(shape)) if ranks == 1 else (lambda i, k: (0,) * len(shape))
    return pl.BlockSpec(shape, index, pipeline_mode=pl.Buffered(1))


def unpack_small(rows_ref, gain_ref, conv_ref, gate_ref, heads_ref):
    for q in range(D // 128):
        gain_ref[:, q * 128 : q * 128 + 128] = rows_ref[q : q + 1, :]
    at = AT_CONV // 128
    for k in range(CONV + 1):
        for q in range(XBC // 128):
            conv_ref[k : k + 1, q * 128 : q * 128 + 128] = rows_ref[at : at + 1, :]
            at += 1
    gate_ref[...] = rows_ref[at : at + INNER // 128, :]
    row = jnp.broadcast_to(rows_ref[at + INNER // 128 : at + INNER // 128 + 1, :], (8, 128))
    place = lax.broadcasted_iota(jnp.int32, (8, 128), 0)
    heads = jnp.zeros((8, 128), F32)
    for k in range(3):
        moved = row if k == 0 else pltpu.roll(row, 128 - k * HEADS, 1)
        heads = jnp.where(place == k, moved, heads)
    lane = lax.broadcasted_iota(jnp.int32, (8, 128), 1)
    heads_ref[...] = jnp.where(lane < HEADS, heads, 0.0)


def unpack_documents(seg_ref, docs_ref, later):
    n, _, extent = docs_ref.shape
    length = extent - LEAD
    place = lax.broadcasted_iota(jnp.int32, (8, extent), 0)
    for i in range(n):
        ids = jnp.broadcast_to(seg_ref[i].astype(F32), (8, seg_ref.shape[2]))
        ahead, behind = jnp.full((8, LEAD), -1.0, F32), jnp.full((8, LEAD), -3.0, F32)
        ids = jnp.concatenate([ahead, ids, behind], axis=1)
        total = ids.shape[1]
        docs = jnp.zeros((8, extent), F32)
        for row, offset in enumerate((0, 1, 2, 3, -1, -2, -3)):
            moved = ids if offset == 0 else pltpu.roll(ids, (-offset) % total, 1)
            here = jnp.where(later, moved[:, length : length + extent], moved[:, :extent])
            docs = jnp.where(place == row, here, docs)
        docs_ref[i] = docs


def gather_kernel(
    nf, w_ref, tok_ref, small_ref, seg_ref,
    o_ref, halo_ref, gain_ref, conv_ref, gate_ref, heads_ref, docs_ref,
    mine, near, local, send, recv,
):
    r, f, s = lax.axis_index("rep"), lax.axis_index("fsdp"), lax.axis_index("seq")
    other = (r, f, 1 - s)
    if nf == 4:
        fx, fy = f + 1 - 2 * lax.rem(f, 2), lax.rem(f + 2, 4)
        fd = lax.rem(fx + 2, 4)
        far = [(r, fx, s), (r, fy, s)]
    else:
        far = [(r, lax.rem(f + j, nf), s) for j in range(1, nf)]
    barrier = pltpu.get_barrier_semaphore()
    for device in far + [other]:
        pl.semaphore_signal(barrier, inc=1, device_id=device, device_id_type=MESH)
    mine[...] = w_ref[:, INNER:].astype(BF16)
    near[...] = tok_ref[:, tok_ref.shape[1] - HALO :, :]
    pl.semaphore_wait(barrier, len(far) + 1)
    copies = []

    def start(src, dst, device):
        k = len(copies)
        copy = pltpu.make_async_remote_copy(
            src, dst, send.at[k], recv.at[k], device_id=device, device_id_type=MESH
        )
        copy.start()
        copies.append(copy)
        return copy

    def block(owner):
        return o_ref.at[owner * 2 + s]

    own = pltpu.make_async_copy(mine, block(f), local)
    own.start()
    if nf == 4:
        x_dev, y_dev = far
        half = mine.shape[0] // 2
        low, high = pl.ds(0, half), pl.ds(half, half)
        from_x, from_y, from_d = block(fx), block(fy), block(fd)
        x_low = start(mine.at[low], block(f).at[low], x_dev)
        y_high = start(mine.at[high], block(f).at[high], y_dev)
        x_high = start(mine.at[high], block(f).at[high], x_dev)
        y_low = start(mine.at[low], block(f).at[low], y_dev)
        late = [start(mine, block(f), other), start(near, halo_ref, other)]
        unpack_small(small_ref, gain_ref, conv_ref, gate_ref, heads_ref)
        unpack_documents(seg_ref, docs_ref, s == 1)
        x_low.wait_recv()
        d_low = start(from_x.at[low], from_x.at[low], y_dev)
        y_high.wait_recv()
        d_high = start(from_y.at[high], from_y.at[high], x_dev)
        x_high.wait_recv()
        late.append(start(from_x, from_x, other))
        y_low.wait_recv()
        late.append(start(from_y, from_y, other))
        d_low.wait_recv()
        late.append(start(from_d.at[low], from_d.at[low], other))
        d_high.wait_recv()
        late.append(start(from_d.at[high], from_d.at[high], other))
    else:
        first = [start(mine, block(f), device) for device in far]
        late = [start(mine, block(f), other), start(near, halo_ref, other)]
        unpack_small(small_ref, gain_ref, conv_ref, gate_ref, heads_ref)
        unpack_documents(seg_ref, docs_ref, s == 1)
        for j, copy in enumerate(first):
            copy.wait_recv()
            source = block(lax.rem(f - 1 - j + nf, nf))
            late.append(start(source, source, other))
    for copy in late:
        copy.wait_recv()
    for copy in copies:
        copy.wait_send()
    own.wait()


def gather_raw(weight, tokens, small_rows, segments):
    nf = lax.axis_size("fsdp")
    rows = weight.shape[0]
    n, length, _ = tokens.shape
    vmem = pl.BlockSpec(memory_space=pltpu.VMEM)
    dma = pltpu.SemaphoreType.DMA
    count = 12 if nf == 4 else 2 * nf
    full, *rest = pl.pallas_call(
        partial(gather_kernel, nf),
        out_shape=[
            jax.ShapeDtypeStruct((2 * nf, rows, XBC), BF16),
            jax.ShapeDtypeStruct((n, HALO, D), BF16),
            jax.ShapeDtypeStruct((1, D), F32),
            jax.ShapeDtypeStruct((CONV + 1, XBC), F32),
            jax.ShapeDtypeStruct((INNER // 128, 128), F32),
            jax.ShapeDtypeStruct((8, 128), F32),
            jax.ShapeDtypeStruct((n, 8, LEAD + length), F32),
        ],
        in_specs=[vmem] * 4,
        out_specs=[pl.BlockSpec(memory_space=pl.ANY)] + [vmem] * 6,
        scratch_shapes=[
            pltpu.VMEM((rows, XBC), BF16),
            pltpu.VMEM((n, HALO, D), BF16),
            dma,
            dma((count,)),
            dma((count,)),
        ],
        compiler_params=pltpu.CompilerParams(
            collective_id=1, has_side_effects=True, vmem_limit_bytes=VMEM_LIMIT
        ),
        name="gather_raw",
    )(weight, tokens, small_rows, segments)
    return full.reshape(2 * nf * rows, XBC), *rest


def enter_kernel(
    tok_ref, halo_ref, gain_ref, wraw_ref, dlow_ref, conv_ref, heads_ref, docs_ref,
    normed_ref, turned_ref, raw_ref, dsilu_ref, val_ref, wr_ref, draw_ref, delta_ref, send_ref,
    ext, rawbuf, act, mask,
):
    length = tok_ref.shape[1]
    gain = gain_ref[...]
    for start, rows, src in ((0, HALO, halo_ref), (HALO, length, tok_ref)):
        for b in range(0, rows, 128):
            n = min(128, rows - b)
            x = src[0, b : b + n, :].astype(F32)
            scale = lax.rsqrt(jnp.mean(x * x, axis=-1, keepdims=True) + EPS)
            ext[start + b : start + b + n, :] = (x * scale * gain).astype(BF16)
    normed = ext[HALO:, :]
    normed_ref[0] = normed
    turned_ref[0] = normed.T
    own = docs_ref[0, 0:1, LEAD:]
    for j in range(1, CONV):
        same = jnp.where(docs_ref[0, BEFORE + j : BEFORE + j + 1, LEAD:] == own, 1.0, 0.0)
        for b in range(0, length, 128):
            mask[j - 1, b : b + 128, :] = square_of(same[:, b : b + 128])

    for c in range(XBC // TILE):
        cols = slice(c * TILE, (c + 1) * TILE)
        low = nn(ext[...], wraw_ref[:, cols]).astype(BF16)
        raw_ref[0, :, cols] = low
        rawbuf[c % 2] = low.astype(F32)
        for half in range(0, TILE, 128):
            hc = slice(c * TILE + half, c * TILE + half + 128)
            w = conv_ref[:, hc]
            for b in range(0, length, 64):
                z = w[4:5] + w[3:4] * rawbuf[c % 2, HALO + b : HALO + b + 64, half : half + 128]
                for j in range(1, CONV):
                    moved = rawbuf[c % 2, HALO + b - j : HALO + b - j + 64, half : half + 128]
                    z = z + w[3 - j : 4 - j] * (moved * mask[j - 1, b : b + 64, :])
                sig = sigmoid(z)
                silu = z * sig
                act[c % 2, b : b + 64, half : half + 128] = silu
                dsilu_ref[0, b : b + 64, hc] = (sig + silu * (1.0 - sig)).astype(BF16)
        if c < INNER // TILE:
            val_ref[0, cols, :] = act[c % 2].T.astype(BF16)
        else:
            wr_ref[0] = act[c % 2].astype(BF16)

    draw = nt(dlow_ref[...], normed) + column(heads_ref, BIAS)
    delta = softplus(draw)
    draw_ref[0] = draw
    delta_ref[0] = delta
    totals = nn_high(-jnp.exp(column(heads_ref, RATE)) * delta, triangle(length))
    keep = jnp.where(own == own[:, length - 1 :], 1.0, 0.0)
    weight = jnp.exp(totals[:, length - 1 :] - totals) * keep * delta
    writers = wr_ref[0, :, :STATE]
    for h in range(HEADS):
        rows = slice(h * HEADDIM, (h + 1) * HEADDIM)
        scaled = val_ref[0, rows, :].astype(F32) * weight[h : h + 1, :]
        send_ref[0, rows, :] = nn(scaled.astype(BF16), writers).astype(BF16)


def enter(tokens, halo, gain, wraw, dlow, conv, heads, docs):
    n, length, _ = tokens.shape
    outs = [
        ((n, length, D), BF16),
        ((n, D, length), BF16),
        ((n, length + HALO, XBC), BF16),
        ((n, length, XBC), BF16),
        ((n, INNER, length), BF16),
        ((n, length, 2 * STATE), BF16),
        ((n, HP, length), F32),
        ((n, HP, length), F32),
        ((n, INNER, STATE), BF16),
    ]
    return pl.pallas_call(
        enter_kernel,
        grid=(n,),
        in_specs=[
            piece(length, D), piece(HALO, D), whole(gain.shape), whole(wraw.shape),
            whole(dlow.shape), whole(conv.shape), whole(heads.shape), piece(*docs.shape[1:]),
        ],
        out_specs=[piece(*s[1:]) for s, _ in outs],
        out_shape=[jax.ShapeDtypeStruct(s, t) for s, t in outs],
        scratch_shapes=[
            pltpu.VMEM((length + HALO, D), BF16),
            pltpu.VMEM((2, length + HALO, TILE), F32),
            pltpu.VMEM((2, length, TILE), F32),
            pltpu.VMEM((CONV - 1, length, 128), F32),
        ],
        compiler_params=params(("arbitrary",)),
        name="enter",
    )(tokens, halo, gain, wraw, dlow, conv, heads, docs)


def chunk_terms(delta, rate, docs_ref):
    own = docs_ref[0, 0:1, :]
    before = docs_ref[0, BEFORE + 1 : BEFORE + 2, 0:1]
    last = docs_ref[0, 0:1, CH - 1 :]
    decay = -jnp.exp(rate) * delta
    totals = nn_high(decay, triangle(CH))
    end = totals[:, CH - 1 :]
    fade = jnp.exp(totals) * jnp.where(own == before, 1.0, 0.0)
    to_end = jnp.exp(end - totals) * jnp.where(own == last, 1.0, 0.0)
    passing = jnp.exp(end) * jnp.where(last == before, 1.0, 0.0)
    together = square_of(own) == own
    first = lax.broadcasted_iota(jnp.int32, (CH, CH), 0)
    second = lax.broadcasted_iota(jnp.int32, (CH, CH), 1)
    barred = jnp.where(together & (first <= second), 0.0, NEG)
    reach = jnp.where(together & (first >= second), 1.0, 0.0)
    return decay, totals, fade, to_end, passing, barred, reach


def forward_kernel(
    val_ref, w_ref, r_ref, delta_ref, heads_ref, docs_ref, in_ref,
    y_ref, start_ref,
    state, off, fresh,
):
    @pl.when(pl.program_id(1) == 0)
    def _():
        state[...] = in_ref[0].astype(F32)

    writers, readers = w_ref[0], r_ref[0]
    delta = delta_ref[0]
    _, totals, fade, to_end, passing, barred, _ = chunk_terms(
        delta, column(heads_ref, RATE), docs_ref
    )
    columns = totals.T
    scores = nt(writers, readers)
    low_state = state[...].astype(BF16)
    start_ref[0, 0] = low_state
    off[...] = nt(low_state, readers)
    for h in range(HEADS):
        rows = slice(h * HEADDIM, (h + 1) * HEADDIM)
        mixing = jnp.exp(totals[h : h + 1, :] - columns[:, h : h + 1] + barred) * scores
        scaled = val_ref[0, rows, :].astype(F32) * delta[h : h + 1, :]
        fresh[rows, :] = (scaled * to_end[h : h + 1, :]).astype(BF16)
        inside = nn(scaled.astype(BF16), mixing.astype(BF16))
        y_ref[0, rows, :] = inside + off[rows, :] * fade[h : h + 1, :]
    off[...] = nn(fresh[...], writers)
    for h in range(HEADS):
        rows = slice(h * HEADDIM, (h + 1) * HEADDIM)
        state[rows, :] = passing[h : h + 1, :] * state[rows, :] + off[rows, :]


def forward_scan(values, wr, delta, heads, docs, incoming):
    n, _, length = values.shape
    chunks = length // CH
    return pl.pallas_call(
        forward_kernel,
        grid=(n, chunks),
        in_specs=[
            pl.BlockSpec((1, INNER, CH), lambda i, k: (i, 0, k)),
            pl.BlockSpec((1, CH, STATE), lambda i, k: (i, k, 0)),
            pl.BlockSpec((1, CH, STATE), lambda i, k: (i, k, 1)),
            pl.BlockSpec((1, HP, CH), lambda i, k: (i, 0, k)),
            whole(heads.shape, 2),
            pl.BlockSpec((1, 8, CH), lambda i, k: (i, 0, k + LEAD // CH)),
            pl.BlockSpec((1, INNER, STATE), lambda i, k: (i, 0, 0)),
        ],
        out_specs=[
            pl.BlockSpec((1, INNER, CH), lambda i, k: (i, 0, k)),
            pl.BlockSpec((1, 1, INNER, STATE), lambda i, k: (i, k, 0, 0)),
        ],
        scratch_shapes=[
            pltpu.VMEM((INNER, STATE), F32),
            pltpu.VMEM((INNER, CH), F32),
            pltpu.VMEM((INNER, CH), BF16),
        ],
        out_shape=[
            jax.ShapeDtypeStruct((n, INNER, length), F32),
            jax.ShapeDtypeStruct((n, chunks, INNER, STATE), BF16),
        ],
        compiler_params=params(("arbitrary", "arbitrary")),
        name="forward_scan",
    )(values, wr, wr, delta, heads, docs, incoming)


def backward_kernel(
    val_ref, w_ref, r_ref, delta_ref, draw_ref, heads_ref, docs_ref, gy_ref, first_ref,
    start_ref, in_ref, final_ref, dsilu_ref, conv_ref, near_ref,
    gval_ref, gwr_ref, gdraw_ref, gheads_ref, ghalo_ref,
    grad, link, off, fresh, faded, gdelta, paid, sums,
):
    n, step = pl.program_id(0), pl.program_id(1)
    rate = column(heads_ref, RATE)

    @pl.when(step == 0)
    def _():
        grad[...] = in_ref[0].astype(F32)
        product = in_ref[0].astype(F32) * final_ref[0].astype(F32)
        by_head = jnp.sum(product.reshape(HEADS, HEADDIM, STATE), axis=1)
        link[0:HEADS, :] = jnp.sum(by_head, axis=1, keepdims=True)
        link[HEADS:, :] = jnp.zeros((HP - HEADS, 1), F32)

    @pl.when((n == 0) & (step == 0))
    def _():
        sums[...] = jnp.zeros_like(sums)

    writers, readers = w_ref[0], r_ref[0]
    delta = delta_ref[0]
    decay, totals, fade, to_end, passing, barred, reach = chunk_terms(delta, rate, docs_ref)
    columns = totals.T
    scores = nt(writers, readers)
    low_grad = grad[...].astype(BF16)
    off[...] = nt(low_grad, writers)
    gscores = jnp.zeros((CH, CH), F32)
    gdelta[HEADS:, :] = jnp.zeros((HP - HEADS, CH), F32)
    paid[HEADS:, :] = jnp.zeros((HP - HEADS, CH), F32)
    for h in range(HEADS):
        rows = slice(h * HEADDIM, (h + 1) * HEADDIM)
        spread = jnp.exp(totals[h : h + 1, :] - columns[:, h : h + 1] + barred)
        values = val_ref[0, rows, :].astype(F32)
        gy = gy_ref[0, rows, :]
        gy32 = gy.astype(F32)
        scaled = values * delta[h : h + 1, :]
        fresh[rows, :] = (scaled * to_end[h : h + 1, :]).astype(BF16)
        faded[rows, :] = (gy32 * fade[h : h + 1, :]).astype(BF16)
        gscaled = nt(gy, (spread * scores).astype(BF16)) + off[rows, :] * to_end[h : h + 1, :]
        low = scaled.astype(BF16)
        gscores = gscores + tn(low, gy) * spread
        paid[h : h + 1, :] = jnp.sum(low.astype(F32) * gscaled, axis=0, keepdims=True)
        gdelta[h : h + 1, :] = jnp.sum(values * gscaled, axis=0, keepdims=True)
        gval_ref[0, rows, :] = (
            gscaled * delta[h : h + 1, :] + gy32 * heads_ref[SKIP : SKIP + 1, h : h + 1]
        ).astype(BF16)
    low_scores = gscores.astype(BF16)
    gwr_ref[0, :, :STATE] = nn(low_scores, readers) + tn(fresh[...], low_grad)
    gwr_ref[0, :, STATE:] = tn(low_scores, writers) + tn(faded[...], start_ref[0, 0])
    off[...] = nn(faded[...], readers)
    for h in range(HEADS):
        rows = slice(h * HEADDIM, (h + 1) * HEADDIM)
        grad[rows, :] = passing[h : h + 1, :] * grad[rows, :] + off[rows, :]
    following = jnp.where(docs_ref[0, 0:1, :] == docs_ref[0, 1:2, CH - 1 :], 1.0, 0.0)
    gdecay = nn_high(first_ref[0] - paid[...], reach) + following * link[...]
    link[...] = gdecay[:, :1]
    gtotal = gdelta[...] - jnp.exp(rate) * gdecay
    gdraw = gtotal * sigmoid(draw_ref[0])
    gdraw_ref[0] = gdraw
    sums[0] += gdraw
    sums[1] += gdecay * decay

    @pl.when(step == pl.num_programs(1) - 1)
    def _():
        taps = conv_ref[...]
        near = [
            square_of(
                jnp.where(near_ref[0, j : j + 1, :] == near_ref[0, 0:1, :], 1.0, 0.0)
            )[120:, :]
            for j in range(CONV)
        ]
        for c in range(XBC // 128):
            cols = slice(c * 128, (c + 1) * 128)
            if c < INNER // 128:
                here = gval_ref[0, cols, :].astype(F32).T[:8, :]
            else:
                here = gwr_ref[0, 0:8, c * 128 - INNER : c * 128 - INNER + 128]
            pre = here * dsilu_ref[0, 0:8, cols].astype(F32)
            wide = jnp.concatenate([jnp.zeros((8, 128), F32), pre], axis=0)
            total = jnp.zeros((8, 128), F32)
            for j in range(1, CONV):
                total = total + taps[3 - j : 4 - j, cols] * wide[j : j + 8] * near[j]
            ghalo_ref[0, :, cols] = total

    @pl.when((n == pl.num_programs(0) - 1) & (step == pl.num_programs(1) - 1))
    def _():
        for i in range(2):
            both = jnp.concatenate([sums[i], jnp.zeros((128 - HP, CH), F32)], axis=0)
            gheads_ref[i : i + 1, :] = jnp.sum(both.T, axis=0, keepdims=True)
        gheads_ref[2:, :] = jnp.zeros((6, 128), F32)


def backward_scan(
    values, wr, delta, draw, heads, docs, gy, first, starts, incoming, final, dsilu, conv
):
    n, _, length = values.shape
    chunks = length // CH
    back = lambda k: chunks - 1 - k
    lanes = lambda rows: pl.BlockSpec((1, rows, CH), lambda i, k: (i, 0, back(k)))
    return pl.pallas_call(
        backward_kernel,
        grid=(n, chunks),
        in_specs=[
            lanes(INNER),
            pl.BlockSpec((1, CH, STATE), lambda i, k: (i, back(k), 0)),
            pl.BlockSpec((1, CH, STATE), lambda i, k: (i, back(k), 1)),
            lanes(HP),
            lanes(HP),
            whole(heads.shape, 2),
            pl.BlockSpec((1, 8, CH), lambda i, k: (i, 0, back(k) + LEAD // CH)),
            lanes(INNER),
            lanes(HP),
            pl.BlockSpec((1, 1, INNER, STATE), lambda i, k: (i, back(k), 0, 0)),
            pl.BlockSpec((1, INNER, STATE), lambda i, k: (i, 0, 0)),
            pl.BlockSpec((1, INNER, STATE), lambda i, k: (i, 0, 0)),
            pl.BlockSpec((1, 16, XBC), lambda i, k: (i, 0, 0)),
            whole(conv.shape, 2),
            pl.BlockSpec((1, 8, 128), lambda i, k: (i, 0, 0)),
        ],
        out_specs=[
            lanes(INNER),
            pl.BlockSpec((1, CH, 2 * STATE), lambda i, k: (i, back(k), 0)),
            lanes(HP),
            pl.BlockSpec((8, 128), lambda i, k: (0, 0)),
            pl.BlockSpec((1, 8, XBC), lambda i, k: (i, 0, 0)),
        ],
        scratch_shapes=[
            pltpu.VMEM((INNER, STATE), F32),
            pltpu.VMEM((HP, 1), F32),
            pltpu.VMEM((INNER, CH), F32),
            pltpu.VMEM((INNER, CH), BF16),
            pltpu.VMEM((INNER, CH), BF16),
            pltpu.VMEM((HP, CH), F32),
            pltpu.VMEM((HP, CH), F32),
            pltpu.VMEM((2, HP, CH), F32),
        ],
        out_shape=[
            jax.ShapeDtypeStruct((n, INNER, length), BF16),
            jax.ShapeDtypeStruct((n, length, 2 * STATE), F32),
            jax.ShapeDtypeStruct((n, HP, length), F32),
            jax.ShapeDtypeStruct((8, 128), F32),
            jax.ShapeDtypeStruct((n, 8, XBC), F32),
        ],
        compiler_params=params(("arbitrary", "arbitrary")),
        name="backward_scan",
    )(
        values, wr, wr, delta, draw, heads, docs, gy, first, starts, incoming, final, dsilu,
        conv, docs,
    )


def leave_kernel(
    normed_ref, turned_ref, wgate_ref, wout_ref, cot_ref, tok_ref, y_ref, val_ref, r_ref,
    gain_ref, delta_ref, heads_ref, docs_ref,
    out_ref, gy_ref, gnorm_ref, first_ref, gstate_ref, gout_ref, ggate_ref, ggain_ref, gskip_ref,
    gate, gated, upward, lifted, flat, total_out, total_gate, products, skips, gains, wide_gain,
):
    n = pl.program_id(0)
    length = normed_ref.shape[1]
    tiles = INNER // TILE
    lanes = range(0, length, 128)
    down = lambda s: jnp.sum(s, axis=0, keepdims=True)

    def fold(v):
        return jnp.sum(v.reshape(HEADDIM // 8, 8, 128), axis=0)

    @pl.when(n == 0)
    def _():
        total_out[...] = jnp.zeros_like(total_out)
        total_gate[...] = jnp.zeros_like(total_gate)
        skips[...] = jnp.zeros_like(skips)
        gains[...] = jnp.zeros_like(gains)
        for q in range(INNER // 128):
            wide_gain[q * 128 : (q + 1) * 128, :] = square_of(gain_ref[q : q + 1, :])

    own = docs_ref[0, 0:1, LEAD:]
    before = docs_ref[0, BEFORE + 1 : BEFORE + 2, LEAD : LEAD + 1]
    totals = nn_high(-jnp.exp(column(heads_ref, RATE)) * delta_ref[0], triangle(length))
    fade = jnp.exp(totals) * jnp.where(own == before, 1.0, 0.0)

    def span(c):
        return slice(c * TILE, (c + 1) * TILE)

    def head_rows(h):
        return slice(h * HEADDIM, (h + 1) * HEADDIM)

    parts = [jnp.zeros((8, 128), F32) for _ in lanes]
    for c in range(tiles):
        gate[span(c), :] = nn(normed_ref[0], wgate_ref[:, span(c)]).T.astype(BF16)
        for h in range(c * 4, c * 4 + 4):
            rows = head_rows(h)
            skip = heads_ref[SKIP : SKIP + 1, h : h + 1]
            for i, b in enumerate(lanes):
                g = gate[rows, b : b + 128].astype(F32)
                values = val_ref[0, rows, b : b + 128].astype(F32)
                v = (y_ref[0, rows, b : b + 128] + skip * values) * (g * sigmoid(g))
                gated[rows, b : b + 128] = v
                parts[i] = parts[i] + fold(v * v)
    scale = [lax.rsqrt(down(s) * (1.0 / INNER) + EPS) for s in parts]

    parts = [jnp.zeros((8, 128), F32) for _ in lanes]
    for c in range(tiles):
        upward[span(c), :] = nt(wout_ref[span(c), :], cot_ref[0])
        for h in range(c * 4, c * 4 + 4):
            rows = head_rows(h)
            gain = wide_gain[rows, :]
            sums = jnp.zeros((HEADDIM, 128), F32)
            for i, b in enumerate(lanes):
                v = gated[rows, b : b + 128]
                normal = v * scale[i]
                lifted[rows, b : b + 128] = (normal * gain).astype(BF16)
                u = upward[rows, b : b + 128]
                sums = sums + u * normal
                u = u * gain
                upward[rows, b : b + 128] = u
                parts[i] = parts[i] + fold(u * v)
            gains[rows, :] += sums
        low = lifted[span(c), :]
        flat[:, span(c)] = low.T
        total_out[span(c), :] += nn(low, cot_ref[0])
    pull = [s * s * s * down(d) * (1.0 / INNER) for s, d in zip(scale, parts)]

    for b in range(0, D, TILE):
        branch = nn(flat[...], wout_ref[:, b : b + TILE])
        out_ref[0, :, b : b + TILE] = (tok_ref[0, :, b : b + TILE].astype(F32) + branch).astype(BF16)

    for c in range(tiles):
        for h in range(c * 4, c * 4 + 4):
            rows = head_rows(h)
            eight = slice(h * 8, h * 8 + 8)
            skip = heads_ref[SKIP : SKIP + 1, h : h + 1]
            sums = jnp.zeros((8, 128), F32)
            for i, b in enumerate(lanes):
                gv = scale[i] * upward[rows, b : b + 128] - pull[i] * gated[rows, b : b + 128]
                g = gate[rows, b : b + 128].astype(F32)
                sig = sigmoid(g)
                silu = g * sig
                values = val_ref[0, rows, b : b + 128].astype(F32)
                y = y_ref[0, rows, b : b + 128]
                gate[rows, b : b + 128] = (
                    gv * (y + skip * values) * (sig + silu * (1.0 - sig))
                ).astype(BF16)
                low = (gv * silu).astype(BF16)
                gy_ref[0, rows, b : b + 128] = low
                gm = low.astype(F32)
                products[eight, b : b + 128] = fold(gm * y)
                sums = sums + fold(gm * values)
                lifted[rows, b : b + 128] = (gm * fade[h : h + 1, b : b + 128]).astype(BF16)
            skips[eight, :] += sums
        gstate_ref[0, span(c), :] = nn(lifted[span(c), :], r_ref[0]).astype(BF16)
        total_gate[:, span(c)] += nt(turned_ref[0], gate[span(c), :])
    gnorm_ref[0] = nn(wgate_ref[...], gate[...])
    first_ref[0, 0:HEADS, :] = jnp.sum(products[...].reshape(HEADS, 8, length), axis=1)
    first_ref[0, HEADS:, :] = jnp.zeros((HP - HEADS, length), F32)

    @pl.when(n == pl.num_programs(0) - 1)
    def _():
        gout_ref[...] = total_out[...].astype(BF16)
        ggate_ref[...] = total_gate[...].astype(BF16)
        for q in range(INNER // 128):
            ggain_ref[q : q + 1, :] = down(gains[q * 128 : (q + 1) * 128, :].T)
        ggain_ref[INNER // 128 :, :] = jnp.zeros((16 - INNER // 128, 128), F32)
        by_head = jnp.sum(skips[...].reshape(HEADS, 8, 128), axis=1)
        by_head = jnp.concatenate([by_head, jnp.zeros((128 - HEADS, 128), F32)], axis=0)
        gskip_ref[0:1, :] = down(by_head.T)
        gskip_ref[1:, :] = jnp.zeros((7, 128), F32)


def leave(normed, turned, wgate, wout, cot, tokens, y, values, wr, gain, delta, heads, docs):
    n, length, _ = normed.shape
    return pl.pallas_call(
        leave_kernel,
        grid=(n,),
        in_specs=[
            piece(length, D), piece(D, length), whole(wgate.shape), whole(wout.shape),
            piece(length, D), piece(length, D), piece(INNER, length), piece(INNER, length),
            pl.BlockSpec((1, length, STATE), lambda i: (i, 0, 1)),
            whole(gain.shape), piece(HP, length), whole(heads.shape), piece(*docs.shape[1:]),
        ],
        out_specs=[
            piece(length, D), piece(INNER, length), piece(D, length), piece(HP, length),
            piece(INNER, STATE), whole((INNER, D)), whole((D, INNER)), whole((16, 128)),
            whole((8, 128)),
        ],
        scratch_shapes=[
            pltpu.VMEM((INNER, length), BF16),
            pltpu.VMEM((INNER, length), F32),
            pltpu.VMEM((INNER, length), F32),
            pltpu.VMEM((INNER, length), BF16),
            pltpu.VMEM((length, INNER), BF16),
            pltpu.VMEM((INNER, D), F32),
            pltpu.VMEM((D, INNER), F32),
            pltpu.VMEM((HEADS * 8, length), F32),
            pltpu.VMEM((HEADS * 8, 128), F32),
            pltpu.VMEM((INNER, 128), F32),
            pltpu.VMEM((INNER, 128), F32),
        ],
        out_shape=[
            jax.ShapeDtypeStruct((n, length, D), BF16),
            jax.ShapeDtypeStruct((n, INNER, length), BF16),
            jax.ShapeDtypeStruct((n, D, length), F32),
            jax.ShapeDtypeStruct((n, HP, length), F32),
            jax.ShapeDtypeStruct((n, INNER, STATE), BF16),
            jax.ShapeDtypeStruct((INNER, D), BF16),
            jax.ShapeDtypeStruct((D, INNER), BF16),
            jax.ShapeDtypeStruct((16, 128), F32),
            jax.ShapeDtypeStruct((8, 128), F32),
        ],
        compiler_params=params(("arbitrary",)),
        name="leave",
    )(normed, turned, wgate, wout, cot, tokens, y, values, wr, gain, delta, heads, docs)


def exit_kernel(
    gval_ref, gwr_ref, dsilu_ref, raw_ref, docs_ref, conv_ref, back_ref, normed_ref, turned_ref,
    wraw_ref, gdraw_ref, dlow_ref, gnorm_ref, tok_ref, cot_ref, gain_ref,
    grad_ref, graw_ref, gdelta_ref, ggain_ref, gconv_ref,
    pre, rawbuf, mask, low, lifted, total, sums,
):
    n = pl.program_id(0)
    length = dsilu_ref.shape[1]
    last = n == pl.num_programs(0) - 1

    @pl.when(n == 0)
    def _():
        total[...] = jnp.zeros_like(total)
        sums[...] = jnp.zeros_like(sums)
        gdelta_ref[...] = jnp.zeros_like(gdelta_ref)
        ggain_ref[...] = jnp.zeros_like(ggain_ref)

    for j in range(1, CONV):
        near = jnp.where(docs_ref[0, j : j + 1, :] == docs_ref[0, 0:1, :], 1.0, 0.0)
        mask[j - 1, 0:8, :] = square_of(near[:, 0:128])[120:, :]
        for b in range(0, length, 128):
            mask[j - 1, 8 + b : 136 + b, :] = square_of(near[:, LEAD + b : LEAD + b + 128])

    for c in range(XBC // TILE):
        slot = c % 2
        pre[slot, 0:8, :] = jnp.zeros((8, TILE), F32)
        pre[slot, length + 8 :, :] = jnp.zeros((8, TILE), F32)
        span = slice(c * TILE, (c + 1) * TILE)
        if c < INNER // TILE:
            here = gval_ref[0, span, :].astype(F32).T
        else:
            here = gwr_ref[0]
        pre[slot, 8 : length + 8, :] = here * dsilu_ref[0, :, span].astype(F32)
        rawbuf[slot] = raw_ref[0, :, span].astype(F32)
        for half in range(0, TILE, 128):
            cols = slice(half, half + 128)
            wide = slice(c * TILE + half, c * TILE + half + 128)
            w = conv_ref[:, wide]
            folded = [sums[k, :, wide] for k in range(CONV + 1)]
            for b, rows in [(0, 8)] + [(8 + 64 * i, 64) for i in range(length // 64)]:
                fold = lambda v: jnp.sum(v.reshape(rows // 8, 8, 128), axis=0)
                raw = rawbuf[slot, HALO - 8 + b : HALO - 8 + b + rows, cols]
                now = pre[slot, b : b + rows, cols]
                grad = w[3:4] * now
                folded[3] = folded[3] + fold(raw * now)
                folded[4] = folded[4] + fold(now)
                for j in range(1, CONV):
                    term = pre[slot, b + j : b + j + rows, cols] * mask[j - 1, b : b + rows, :]
                    grad = grad + w[3 - j : 4 - j] * term
                    folded[3 - j] = folded[3 - j] + fold(raw * term)
                if b == length - 56:
                    grad = jnp.concatenate([grad[:56], grad[56:] + back_ref[0, :, wide]], axis=0)
                if b > 0:
                    low[slot, b - 8 : b - 8 + rows, cols] = grad.astype(BF16)
            for k in range(CONV + 1):
                sums[k, :, wide] = folded[k]
        total[:, span] += nn(turned_ref[0], low[slot])
        through = nt(low[slot], wraw_ref[:, span])
        if c == 0:
            lifted[...] = through
        else:
            lifted[...] += through

    gdraw = gdraw_ref[0].astype(BF16)
    gdelta_ref[...] += nn(gdraw, normed_ref[0])
    gain = gain_ref[...]
    gains = jnp.zeros((8, D), F32)
    for b in range(0, length, 128):
        rows = slice(b, b + 128)
        up = lifted[rows, :] + gnorm_ref[0, :, rows].T + tn(gdraw[:, rows], dlow_ref[...])
        x = tok_ref[0, rows, :].astype(F32)
        scale = lax.rsqrt(jnp.mean(x * x, axis=-1, keepdims=True) + EPS)
        normal = x * scale
        gains = gains + jnp.sum((up * normal).reshape(16, 8, D), axis=0)
        up = up * gain
        inner = jnp.mean(up * normal, axis=-1, keepdims=True)
        grad = cot_ref[0, rows, :].astype(F32) + scale * (up - normal * inner)
        grad_ref[0, rows, :] = grad.astype(BF16)
    ggain_ref[0:1, :] += jnp.sum(gains, axis=0, keepdims=True)

    @pl.when(last)
    def _():
        graw_ref[...] = total[...].astype(BF16)
        gconv_ref[0 : CONV + 1, :] = jnp.sum(sums[...], axis=1)


def leave_back(
    gval, gwr, dsilu, raw, docs, conv, back, normed, turned, wraw, gdraw, dlow, gnorm, tokens,
    cotangent, gain,
):
    n, length, _ = dsilu.shape
    return pl.pallas_call(
        exit_kernel,
        grid=(n,),
        in_specs=[
            piece(INNER, length), piece(length, 2 * STATE), piece(length, XBC),
            piece(length + HALO, XBC), piece(*docs.shape[1:]), whole(conv.shape), piece(8, XBC),
            piece(length, D), piece(D, length), whole(wraw.shape), piece(HP, length),
            whole(dlow.shape), piece(D, length), piece(length, D), piece(length, D),
            whole(gain.shape),
        ],
        out_specs=[
            piece(length, D), whole((D, XBC)), whole((HP, D)), whole((8, D)), whole((8, XBC)),
        ],
        out_shape=[
            jax.ShapeDtypeStruct((n, length, D), BF16),
            jax.ShapeDtypeStruct((D, XBC), BF16),
            jax.ShapeDtypeStruct((HP, D), F32),
            jax.ShapeDtypeStruct((8, D), F32),
            jax.ShapeDtypeStruct((8, XBC), F32),
        ],
        scratch_shapes=[
            pltpu.VMEM((2, length + 16, TILE), F32),
            pltpu.VMEM((2, length + HALO, TILE), F32),
            pltpu.VMEM((CONV - 1, length + 8, 128), F32),
            pltpu.VMEM((2, length, TILE), BF16),
            pltpu.VMEM((length, D), F32),
            pltpu.VMEM((D, XBC), F32),
            pltpu.VMEM((CONV + 1, 8, XBC), F32),
        ],
        compiler_params=params(("arbitrary",)),
        name="leave_back",
    )(
        gval, gwr, dsilu, raw, docs, conv, back, normed, turned, wraw, gdraw, dlow, gnorm, tokens,
        cotangent, gain,
    )


def tiles_of(extent):
    return -(-extent // 128)


def pieces_of(rows):
    return [(i, i * 128, min(128, rows - i * 128)) for i in range(tiles_of(rows))]


def split_three(v):
    high = v.astype(BF16)
    rest = v - high.astype(F32)
    middle = rest.astype(BF16)
    low = (rest - middle.astype(F32)).astype(BF16)
    return jnp.concatenate([high, middle, low], axis=0)


def join_three(v):
    return v[0:8] + v[8:16] + v[16:24]


def inverse_factor(gram):
    rows = lax.broadcasted_iota(jnp.int32, (8, 8), 0)
    cols = lax.broadcasted_iota(jnp.int32, (8, 8), 1)
    left, right = gram, jnp.where(rows == cols, 1.0, 0.0)
    for j in range(7):
        factor = jnp.where(rows[:, :1] > j, left[:, j : j + 1] / left[j : j + 1, j : j + 1], 0.0)
        left, right = left - factor * left[j : j + 1, :], right - factor * right[j : j + 1, :]
    pivots = jnp.sum(jnp.where(rows == cols, left, 0.0), axis=1, keepdims=True)
    return right * lax.rsqrt(pivots)


RIGHT_OUT = PROJ // 128
DELTA = RIGHT_OUT + D // 128
REST = DELTA + HEADS // 8 * (D // 128)
REST_ROWS = D // 128 + (CONV + 1) * (XBC // 128) + INNER // 128 + 3
SUMMED = REST + -(-REST_ROWS // 8)


class Scatter:
    def __init__(self, exchange, x_ref, from_core, pairs, from_far, send, recv):
        self.nf = exchange.group // 2
        self.x_ref, self.from_core, self.pairs, self.from_far = x_ref, from_core, pairs, from_far
        self.send, self.recv = send, recv
        self.r, self.f, self.s = (lax.axis_index(name) for name in ("rep", "fsdp", "seq"))
        self.copies = []

    def start(self, src, dst, device):
        k = len(self.copies)
        copy = pltpu.make_async_remote_copy(
            src, dst, self.send.at[k], self.recv.at[k], device_id=device, device_id_type=MESH
        )
        copy.start()
        self.copies.append(copy)
        return copy

    def begin(self):
        other = (self.r, self.f, 1 - self.s)
        self.near = []
        for j in range(self.nf):
            f = lax.rem(self.f + 1 + j, self.nf)
            self.near.append(self.start(self.x_ref.at[f * 2 + 1 - self.s], self.from_core.at[j], other))

    def cross(self):
        self.far = []
        for j in range(self.nf):
            f = lax.rem(self.f + 1 + j, self.nf)
            self.near[j].wait_recv()
            total = self.x_ref[f * 2 + self.s].astype(F32) + self.from_core[j].astype(F32)
            self.pairs[j] = total.astype(BF16)
            if j < self.nf - 1:
                self.far.append(
                    self.start(self.pairs.at[j], self.from_far.at[j], (self.r, f, self.s))
                )

    def end(self, o_ref):
        total = self.pairs[self.nf - 1].astype(F32)
        for j, copy in enumerate(self.far):
            copy.wait_recv()
            total = total + self.from_far[j].astype(F32)
        o_ref[...] = total
        for copy in self.copies:
            copy.wait_send()


class Exchange:
    def __init__(self, group, replicas):
        self.group, self.replicas = group, replicas
        r, f, s = lax.axis_index("rep"), lax.axis_index("fsdp"), lax.axis_index("seq")
        self.r, self.me = r, f * 2 + s
        self.peers = []
        for j in range(1, group):
            p = lax.rem(self.me + j, group)
            self.peers.append((p, (r, lax.div(p, 2), lax.rem(p, 2))))
        self.others = [(lax.rem(r + j, replicas), f, s) for j in range(1, replicas)]

    def greet(self):
        barrier = pltpu.get_barrier_semaphore()
        for device in [d for _, d in self.peers] + self.others:
            pl.semaphore_signal(barrier, inc=1, device_id=device, device_id_type=MESH)

    def met(self):
        pl.semaphore_wait(pltpu.get_barrier_semaphore(), self.group + self.replicas - 2)

    def sum(self, x_ref, o_ref, own, from_group, from_reps, send, recv, meanwhile=None):
        group, replicas, me = self.group, self.replicas, self.me
        width = own.shape[0]
        copies = []

        def start(src, dst, device):
            k = len(copies)
            copy = pltpu.make_async_remote_copy(
                src, dst, send.at[k], recv.at[k], device_id=device, device_id_type=MESH
            )
            copy.start()
            copies.append(copy)
            return copy

        arriving = [
            start(x_ref.at[pl.ds(p * width, width)], from_group.at[j], device)
            for j, (p, device) in enumerate(self.peers)
        ]
        total = x_ref[pl.ds(me * width, width)]
        for j, copy in enumerate(arriving):
            copy.wait_recv()
            total = total + from_group[j]
        own[...] = total
        from_reps[pl.ds(self.r, 1)] = total[None]
        arriving = [start(own, from_reps.at[self.r], device) for device in self.others]
        if meanwhile is not None:
            meanwhile()
        for copy in arriving:
            copy.wait_recv()
        total = from_reps[0]
        for j in range(1, replicas):
            total = total + from_reps[j]
        mine = pl.ds(me * width, width)
        o_ref[mine] = total
        arriving = [start(o_ref.at[mine], o_ref.at[mine], device) for _, device in self.peers]
        for copy in arriving:
            copy.wait_recv()
        for copy in copies:
            copy.wait_send()


def compress_kernel(
    group, replicas,
    sin_ref, sout_ref, gate_ref, raw_ref, out_ref, ein_ref, eout_ref, gdelta_ref, ggain_ref,
    gconv_ref, ggate_ref, gheads_ref, gskip_ref,
    sum_ref, left_in_ref, left_out_ref, turned_in_ref, turned_out_ref, raw_total_ref,
    lefts, left_sums, hat, rights,
    own_a, group_a, reps_a, own_b, group_b, reps_b, send_a, recv_a, send_b, recv_b,
    from_core, pairs, from_far, send_c, recv_c,
):
    rows_in, rows_out = gate_ref.shape[1], out_ref.shape[1]
    ahead = tiles_of(rows_in)
    width = ahead + tiles_of(rows_out)
    exchange = Exchange(group, replicas)
    exchange.greet()

    lefts[...] = jnp.zeros_like(lefts)
    mine = pl.ds(exchange.me * width, width)

    def place(index, values, rows, first):
        for i, at, n in pieces_of(rows):
            lefts[index + first + i, :, :n] = values[:, at : at + n]

    def place_own(values, rows, first):
        for i, at, n in pieces_of(rows):
            part = values[:, at : at + n]
            if n < 128:
                part = jnp.concatenate([part, jnp.zeros((8, 128 - n), F32)], axis=1)
            where = pl.ds(exchange.me * width + first + i, 1)
            lefts[where] = lefts[where] + part[None]

    s_in, s_out = split_three(sin_ref[...]), split_three(sout_ref[...])
    for p in range(group):
        product = nt(s_in[:, :INNER], gate_ref[p]) + nt(s_in[:, INNER:], raw_ref[p])
        place(p * width, join_three(product), rows_in, 0)
        place(p * width, join_three(nt(s_out, out_ref[p])), rows_out, ahead)
    place_own(nt_high(sin_ref[...], ein_ref[...]), rows_in, 0)
    place_own(nt_high(sout_ref[...], eout_ref[...]), rows_out, ahead)
    exchange.met()
    scatter = Scatter(exchange, raw_ref, from_core, pairs, from_far, send_c, recv_c)
    scatter.begin()
    exchange.sum(lefts, left_sums, own_a, group_a, reps_a, send_a, recv_a, scatter.cross)

    for first, last in ((0, ahead), (ahead, width)):
        gram = jnp.zeros((8, 8), F32)
        for p in range(group):
            for i in range(first, last):
                tile = left_sums[p * width + i] * (1.0 / replicas)
                gram = gram + nt_high(tile, tile)
        inverse = inverse_factor(gram)
        for p in range(group):
            for i in range(first, last):
                hat[p * width + i] = nn_high(inverse, left_sums[p * width + i] * (1.0 / replicas))
    own = hat[mine]
    for first, rows, left_ref, turned_ref in (
        (0, rows_in, left_in_ref, turned_in_ref), (ahead, rows_out, left_out_ref, turned_out_ref)
    ):
        for i, at, n in pieces_of(rows):
            turned_ref[:, at : at + n] = own[first + i][:, :n]
            left_ref[at : at + n, :] = own[first + i].T[:n, :]

    def joined(tiles, start, rows):
        return jnp.concatenate([tiles[start + i][:, :n] for i, _, n in pieces_of(rows)], axis=1)

    def product(matrices, rows, skipped, error, at):
        spread = [split_three(joined(hat, p * width + skipped, rows)) for p in range(group)]
        mixed = joined(own, skipped, rows)
        columns = 0
        for ref, extent in matrices:
            for b in range(0, extent, TILE):
                total = nn(spread[0], ref[0, :, b : b + TILE])
                for p in range(1, group):
                    total = total + nn(spread[p], ref[p, :, b : b + TILE])
                here = columns + b
                right = join_three(total) + nn_high(mixed, error[:, here : here + TILE])
                for half in range(0, TILE, 128):
                    rights[at + (here + half) // 128] = right[:, half : half + 128]
            columns += extent

    product(((gate_ref, INNER), (raw_ref, XBC)), rows_in, 0, ein_ref, 0)
    product(((out_ref, D),), rows_out, ahead, eout_ref, RIGHT_OUT)
    for g in range(HEADS // 8):
        for q in range(D // 128):
            rights[DELTA + g * (D // 128) + q] = gdelta_ref[
                g * 8 : g * 8 + 8, q * 128 : q * 128 + 128
            ]
    rights[REST:] = jnp.zeros((rights.shape[0] - REST, 8, 128), F32)
    rest = [ggain_ref[0:1, q * 128 : q * 128 + 128] for q in range(D // 128)]
    for k in range(CONV + 1):
        rest += [gconv_ref[k : k + 1, q * 128 : q * 128 + 128] for q in range(XBC // 128)]
    rest += [ggate_ref[q : q + 1, :] for q in range(INNER // 128)]
    rest += [gheads_ref[0:1, :], gheads_ref[1:2, :], gskip_ref[0:1, :]]
    for i in range(0, REST_ROWS, 8):
        eight = rest[i : i + 8]
        rights[REST + i // 8, : len(eight), :] = jnp.concatenate(eight, axis=0)
    exchange.sum(rights, sum_ref, own_b, group_b, reps_b, send_b, recv_b)
    scatter.end(raw_total_ref)


def compress(starts, grads, errors, smalls):
    group = lax.axis_size("fsdp") * lax.axis_size("seq")
    replicas = lax.axis_size("rep")
    grads = [a.reshape(group, a.shape[0] // group, a.shape[1]) for a in grads]
    rows_in, rows_out = grads[0].shape[1], grads[2].shape[1]
    width = tiles_of(rows_in) + tiles_of(rows_out)
    block = (rows_in, XBC)
    share = -(-SUMMED // group)
    dma = pltpu.SemaphoreType.DMA((2 * (group - 1) + replicas - 1,))
    tiles = lambda *n: pltpu.VMEM(n + (8, 128), F32)
    vmem = pl.BlockSpec(memory_space=pltpu.VMEM)
    arrays = [*starts, *grads, *errors, *smalls]
    return pl.pallas_call(
        partial(compress_kernel, group, replicas),
        out_shape=[
            jax.ShapeDtypeStruct((group * share, 8, 128), F32),
            jax.ShapeDtypeStruct((rows_in, 8), F32),
            jax.ShapeDtypeStruct((rows_out, 8), F32),
            jax.ShapeDtypeStruct((8, rows_in), F32),
            jax.ShapeDtypeStruct((8, rows_out), F32),
            jax.ShapeDtypeStruct((rows_in, XBC), F32),
        ],
        in_specs=[vmem] * len(arrays),
        out_specs=[vmem] * 6,
        scratch_shapes=[
            tiles(group * width), tiles(group * width), tiles(group * width),
            tiles(group * share),
            tiles(width), tiles(group - 1, width), tiles(replicas, width),
            tiles(share), tiles(group - 1, share), tiles(replicas, share),
            dma, dma, dma, dma,
            pltpu.VMEM((group // 2,) + block, BF16),
            pltpu.VMEM((group // 2,) + block, BF16),
            pltpu.VMEM((group // 2 - 1,) + block, BF16),
            pltpu.SemaphoreType.DMA((group - 1,)),
            pltpu.SemaphoreType.DMA((group - 1,)),
        ],
        compiler_params=pltpu.CompilerParams(
            collective_id=2, has_side_effects=True, vmem_limit_bytes=VMEM_LIMIT
        ),
        name="compress",
    )(*arrays)


def finish_kernel(
    rates, replicas, rights_ref, tin_ref, tout_ref, lin_ref, lout_ref,
    win_ref, min_ref, ein_ref, gate_ref, raw_ref, wout_ref, mout_ref, eout_ref, out_ref,
    nwin_ref, nmin_ref, nein_ref, nwout_ref, nmout_ref, neout_ref,
    rin_ref, rout_ref, ntin_ref, ntout_ref,
):
    @pl.when(pl.program_id(0) == 0)
    def _():
        for ref, at, extent in ((rin_ref, 0, PROJ), (rout_ref, RIGHT_OUT, D)):
            for q in range(extent // 128):
                ref[:, q * 128 : q * 128 + 128] = rights_ref[at + q] * (1.0 / replicas)
        ntin_ref[...] = tin_ref[...]
        ntout_ref[...] = tout_ref[...]

    def update(w, m, e, nw, nm, ne, left_ref, grads, at, rate):
        rows = w.shape[0]
        left = [jnp.broadcast_to(left_ref[:, k : k + 1], (rows, 128)) for k in range(8)]
        begin = 0
        for grad in grads:
            for b in range(0, grad.shape[1], 128):
                cols = slice(begin + b, begin + b + 128)
                right = rights_ref[at + (begin + b) // 128] * (1.0 / replicas)
                approx = left[0] * right[0:1]
                for k in range(1, 8):
                    approx = approx + left[k] * right[k : k + 1]
                momentum = MOMENTUM * m[:, cols] + approx
                nm[:, cols] = momentum
                nw[:, cols] = w[:, cols] - rate * momentum
                ne[:, cols] = (grad[:, b : b + 128].astype(F32) + e[:, cols]) - approx
            begin += grad.shape[1]

    update(
        win_ref, min_ref, ein_ref, nwin_ref, nmin_ref, nein_ref, lin_ref, (gate_ref, raw_ref), 0,
        rates[0],
    )
    update(
        wout_ref, mout_ref, eout_ref, nwout_ref, nmout_ref, neout_ref, lout_ref, (out_ref,),
        RIGHT_OUT, rates[1],
    )


def finish(rates, replicas, rights, turned_in, turned_out, left_in, left_out, wide, narrow):
    rows_in, rows_out = left_in.shape[0], left_out.shape[0]
    steps = 3 if rows_in % 48 == 0 else 1
    block = lambda a: pl.BlockSpec((a.shape[0] // steps, a.shape[1]), lambda i: (i, 0))
    like = lambda a: jax.ShapeDtypeStruct(a.shape, F32)
    arrays = [*wide, *narrow]
    outs = [*wide[:3], *narrow[:3]]
    extra = [(8, PROJ), (8, D), turned_in.shape, turned_out.shape]
    return pl.pallas_call(
        partial(finish_kernel, rates, replicas),
        grid=(steps,),
        in_specs=[
            whole(rights.shape), whole(turned_in.shape), whole(turned_out.shape),
            block(left_in), block(left_out), *map(block, arrays),
        ],
        out_specs=[*map(block, outs), *map(whole, extra)],
        out_shape=[*map(like, outs), *(jax.ShapeDtypeStruct(e, F32) for e in extra)],
        compiler_params=params(("arbitrary",)),
        name="finish",
    )(rights, turned_in, turned_out, left_in, left_out, *arrays)


def step_rates(tokens_replica):
    grad_scale = 0.3 * math.sqrt(tokens_replica)
    return (
        0.5 / (math.sqrt(D) * grad_scale),
        0.5 / (math.sqrt(INNER) * grad_scale),
        0.1 / grad_scale,
    )


def to_later(block):
    return lax.ppermute(block, "seq", [(i, i + 1) for i in range(lax.axis_size("seq") - 1)])


def to_earlier(block):
    return lax.ppermute(block, "seq", [(i + 1, i) for i in range(lax.axis_size("seq") - 1)])


def gather_rows(shard):
    return lax.all_gather(shard, ("fsdp", "seq"), axis=0, tiled=True)


def scatter_rows(total):
    return lax.psum_scatter(total, ("fsdp", "seq"), scatter_dimension=0, tiled=True)


def body(
    tokens,
    cotangent,
    segments,
    input_weight,
    output_weight,
    small_values,
    input_momentum,
    output_momentum,
    small_momentum,
    input_error,
    output_error,
    input_start,
    output_start,
):
    shape = tokens.shape
    pieces = shape[0] * shape[1]
    length = shape[2]
    replicas = lax.axis_size("rep")
    tokens_replica = pieces * length * lax.axis_size("fsdp") * lax.axis_size("seq")
    rate_in, rate_out, rate_small = step_rates(tokens_replica)

    tokens = tokens.reshape(pieces, length, D)
    cotangent = cotangent.reshape(pieces, length, D)
    small_rows = jnp.pad(small_values, (0, -small_values.shape[0] % 1024)).reshape(-1, 128)
    gate_full = gather_rows(input_weight[:, :INNER].astype(BF16))
    output_full = gather_rows(output_weight.astype(BF16))
    delta_rows = small_values[D:AT_CONV].reshape(D, HEADS).astype(BF16).T
    delta_rows = jnp.pad(delta_rows, ((0, HP - HEADS), (0, 0)))
    raw_full, halo, norm_gain, conv, gate_gain, heads, docs = gather_raw(
        input_weight, tokens, small_rows, segments.reshape(pieces, 1, segments.shape[2])
    )
    normed, turned, raw, dsilu, values, wr, draw, delta, send = enter(
        tokens, halo, norm_gain, raw_full, delta_rows, conv, heads, docs
    )
    y, starts = forward_scan(values, wr, delta, heads, docs, to_later(send))
    output, gy, gnorm, first, gstate, grad_output, grad_gate, ggate, gskip = leave(
        normed, turned, gate_full, output_full, cotangent, tokens, y, values, wr, gate_gain,
        delta, heads, docs,
    )
    output_total = scatter_rows(grad_output)
    gate_total = scatter_rows(grad_gate)
    gval, gwr, gdraw, gheads, ghalo = backward_scan(
        values, wr, delta, draw, heads, docs, gy, first, starts, to_earlier(gstate), send, dsilu,
        conv,
    )
    input_grad, grad_raw, gdelta, ggain, gconv = leave_back(
        gval, gwr, dsilu, raw, docs, conv, to_earlier(ghalo), normed, turned, raw_full, gdraw,
        delta_rows, gnorm, tokens, cotangent, norm_gain,
    )
    rights, left_in, left_out, turned_in, turned_out, raw_total = compress(
        (input_start.T, output_start.T),
        (grad_gate, grad_raw, grad_output),
        (input_error[0], output_error[0]),
        (gdelta, ggain, gconv, ggate, gheads, gskip),
    )
    (
        new_input_weight, new_input_momentum, new_input_error,
        new_output_weight, new_output_momentum, new_output_error,
        input_right, output_right, input_left, output_left,
    ) = finish(
        (rate_in, rate_out), replicas, rights, turned_in, turned_out, left_in, left_out,
        (input_weight, input_momentum, input_error[0], gate_total, raw_total),
        (output_weight, output_momentum, output_error[0], output_total),
    )
    rest = rights[REST:SUMMED].reshape(-1, 128)[:REST_ROWS]
    turned_delta = rights[DELTA:REST].reshape(HEADS // 8, D // 128, 8, 128)
    small_sum = jnp.concatenate(
        [
            rest[: D // 128].reshape(-1),
            turned_delta.transpose(1, 3, 0, 2).reshape(-1),
            rest[D // 128 : -3].reshape(-1),
            rest[-3:, :HEADS].reshape(-1),
        ]
    )
    new_small_momentum = MOMENTUM * small_momentum + small_sum / replicas
    new_small_values = small_values - rate_small * new_small_momentum
    return (
        output.reshape(shape),
        input_grad.reshape(shape),
        new_input_weight,
        new_output_weight,
        new_input_momentum,
        new_output_momentum,
        new_small_values,
        new_small_momentum,
        input_left.T,
        input_right.T,
        output_left.T,
        output_right.T,
        new_input_error[None],
        new_output_error[None],
    )


def solution(mesh):
    return jax.shard_map(
        body,
        mesh=mesh,
        in_specs=(
            P(None, ("rep", "fsdp"), "seq", None),
            P(None, ("rep", "fsdp"), "seq", None),
            P(None, ("rep", "fsdp"), None),
            P(("fsdp", "seq"), None),
            P(("fsdp", "seq"), None),
            P(),
            P(("fsdp", "seq"), None),
            P(("fsdp", "seq"), None),
            P(),
            P("rep", ("fsdp", "seq"), None),
            P("rep", ("fsdp", "seq"), None),
            P(),
            P(),
        ),
        out_specs=(
            P(None, ("rep", "fsdp"), "seq", None),
            P(None, ("rep", "fsdp"), "seq", None),
            P(("fsdp", "seq"), None),
            P(("fsdp", "seq"), None),
            P(("fsdp", "seq"), None),
            P(("fsdp", "seq"), None),
            P(),
            P(),
            P(("fsdp", "seq"), None),
            P(),
            P(("fsdp", "seq"), None),
            P(),
            P("rep", ("fsdp", "seq"), None),
            P("rep", ("fsdp", "seq"), None),
        ),
        check_vma=False,
    )
```

```python
from functools import partial
import math

import jax
import jax.numpy as jnp
from jax import lax
from jax.experimental import pallas as pl
from jax.experimental.pallas import tpu as pltpu
from jax.sharding import PartitionSpec as P

D = 768
INNER = 1536
HEADS = 24
HEADDIM = 64
STATE = 128
CONV = 4
PROJ = 3328
XBC = 1792

EPS = 1e-05
MOMENTUM = 0.9
HIGH = lax.Precision.HIGHEST
F32 = jnp.float32
BF16 = jnp.bfloat16
HP = 32
CH = 128
HALO = 16
TILE = 256
SUB = 16
ROWS = 256
SPAN = 128 + HALO
NEG = -1e30
VMEM_LIMIT = 63 * 2**20
MESH = pl.DeviceIdType.MESH

BEFORE = 3
LEAD = 128
BIAS, RATE, SKIP = 0, 1, 2
AT_CONV = D + D * HEADS
AT_GATE = AT_CONV + (CONV + 1) * XBC
AT_HEADS = AT_GATE + INNER


def nn(a, b):
    return lax.dot_general(a, b, (((1,), (0,)), ((), ())), preferred_element_type=F32)


def nt(a, b):
    return lax.dot_general(a, b, (((1,), (1,)), ((), ())), preferred_element_type=F32)


def tn(a, b):
    return lax.dot_general(a, b, (((0,), (0,)), ((), ())), preferred_element_type=F32)


def nn_high(a, b):
    return lax.dot_general(
        a, b, (((1,), (0,)), ((), ())), precision=HIGH, preferred_element_type=F32
    )


def nt_high(a, b):
    return lax.dot_general(
        a, b, (((1,), (1,)), ((), ())), precision=HIGH, preferred_element_type=F32
    )


def tn_high(a, b):
    return lax.dot_general(
        a, b, (((0,), (0,)), ((), ())), precision=HIGH, preferred_element_type=F32
    )


def softplus(v):
    return jnp.maximum(v, 0.0) + jnp.log1p(jnp.exp(-jnp.abs(v)))


def sigmoid(v):
    return 0.5 + 0.5 * jnp.tanh(0.5 * v)


def triangle(extent):
    return jnp.where(
        lax.broadcasted_iota(jnp.int32, (extent, extent), 0)
        <= lax.broadcasted_iota(jnp.int32, (extent, extent), 1),
        1.0,
        0.0,
    )


def column(heads_ref, row):
    return heads_ref[...].T[:HP, row : row + 1]


def square_of(row):
    return jnp.broadcast_to(row, (128, 128)).T


def params(semantics, **more):
    return pltpu.CompilerParams(
        dimension_semantics=semantics, vmem_limit_bytes=VMEM_LIMIT, **more
    )


def piece(*shape):
    return pl.BlockSpec((1,) + shape, lambda i: (i,) + (0,) * len(shape))


def whole(shape, ranks=1):
    index = (lambda i: (0,) * len(shape)) if ranks == 1 else (lambda i, k: (0,) * len(shape))
    return pl.BlockSpec(shape, index, pipeline_mode=pl.Buffered(1))


def unpack_small(rows_ref, gain_ref, conv_ref, gate_ref, heads_ref):
    for q in range(D // 128):
        gain_ref[:, q * 128 : q * 128 + 128] = rows_ref[q : q + 1, :]
    at = AT_CONV // 128
    for k in range(CONV + 1):
        for q in range(XBC // 128):
            conv_ref[k : k + 1, q * 128 : q * 128 + 128] = rows_ref[at : at + 1, :]
            at += 1
    gate_ref[...] = rows_ref[at : at + INNER // 128, :]
    row = jnp.broadcast_to(rows_ref[at + INNER // 128 : at + INNER // 128 + 1, :], (8, 128))
    place = lax.broadcasted_iota(jnp.int32, (8, 128), 0)
    heads = jnp.zeros((8, 128), F32)
    for k in range(3):
        moved = row if k == 0 else pltpu.roll(row, 128 - k * HEADS, 1)
        heads = jnp.where(place == k, moved, heads)
    lane = lax.broadcasted_iota(jnp.int32, (8, 128), 1)
    heads_ref[...] = jnp.where(lane < HEADS, heads, 0.0)


def unpack_documents(seg_ref, docs_ref, later):
    n, _, extent = docs_ref.shape
    length = extent - LEAD
    place = lax.broadcasted_iota(jnp.int32, (8, extent), 0)
    for i in range(n):
        ids = jnp.broadcast_to(seg_ref[i].astype(F32), (8, seg_ref.shape[2]))
        ahead, behind = jnp.full((8, LEAD), -1.0, F32), jnp.full((8, LEAD), -3.0, F32)
        ids = jnp.concatenate([ahead, ids, behind], axis=1)
        total = ids.shape[1]
        docs = jnp.zeros((8, extent), F32)
        for row, offset in enumerate((0, 1, 2, 3, -1, -2, -3)):
            moved = ids if offset == 0 else pltpu.roll(ids, (-offset) % total, 1)
            here = jnp.where(later, moved[:, length : length + extent], moved[:, :extent])
            docs = jnp.where(place == row, here, docs)
        docs_ref[i] = docs


def gather_kernel(
    nf, w_ref, tok_ref, small_ref, seg_ref,
    o_ref, halo_ref, gain_ref, conv_ref, gate_ref, heads_ref, docs_ref,
    mine, near, local, send, recv,
):
    r, f, s = lax.axis_index("rep"), lax.axis_index("fsdp"), lax.axis_index("seq")
    other = (r, f, 1 - s)
    if nf == 4:
        fx, fy = f + 1 - 2 * lax.rem(f, 2), lax.rem(f + 2, 4)
        fd = lax.rem(fx + 2, 4)
        far = [(r, fx, s), (r, fy, s)]
    else:
        far = [(r, lax.rem(f + j, nf), s) for j in range(1, nf)]
    barrier = pltpu.get_barrier_semaphore()
    for device in far + [other]:
        pl.semaphore_signal(barrier, inc=1, device_id=device, device_id_type=MESH)
    mine[...] = w_ref[:, INNER:].astype(BF16)
    near[...] = tok_ref[:, tok_ref.shape[1] - HALO :, :]
    pl.semaphore_wait(barrier, len(far) + 1)
    copies = []

    def start(src, dst, device):
        k = len(copies)
        copy = pltpu.make_async_remote_copy(
            src, dst, send.at[k], recv.at[k], device_id=device, device_id_type=MESH
        )
        copy.start()
        copies.append(copy)
        return copy

    def block(owner):
        return o_ref.at[owner * 2 + s]

    own = pltpu.make_async_copy(mine, block(f), local)
    own.start()
    if nf == 4:
        x_dev, y_dev = far
        half = mine.shape[0] // 2
        low, high = pl.ds(0, half), pl.ds(half, half)
        from_x, from_y, from_d = block(fx), block(fy), block(fd)
        x_low = start(mine.at[low], block(f).at[low], x_dev)
        y_high = start(mine.at[high], block(f).at[high], y_dev)
        x_high = start(mine.at[high], block(f).at[high], x_dev)
        y_low = start(mine.at[low], block(f).at[low], y_dev)
        late = [start(mine, block(f), other), start(near, halo_ref, other)]
        unpack_small(small_ref, gain_ref, conv_ref, gate_ref, heads_ref)
        unpack_documents(seg_ref, docs_ref, s == 1)
        x_low.wait_recv()
        d_low = start(from_x.at[low], from_x.at[low], y_dev)
        y_high.wait_recv()
        d_high = start(from_y.at[high], from_y.at[high], x_dev)
        x_high.wait_recv()
        late.append(start(from_x, from_x, other))
        y_low.wait_recv()
        late.append(start(from_y, from_y, other))
        d_low.wait_recv()
        late.append(start(from_d.at[low], from_d.at[low], other))
        d_high.wait_recv()
        late.append(start(from_d.at[high], from_d.at[high], other))
    else:
        first = [start(mine, block(f), device) for device in far]
        late = [start(mine, block(f), other), start(near, halo_ref, other)]
        unpack_small(small_ref, gain_ref, conv_ref, gate_ref, heads_ref)
        unpack_documents(seg_ref, docs_ref, s == 1)
        for j, copy in enumerate(first):
            copy.wait_recv()
            source = block(lax.rem(f - 1 - j + nf, nf))
            late.append(start(source, source, other))
    for copy in late:
        copy.wait_recv()
    for copy in copies:
        copy.wait_send()
    own.wait()


def gather_raw(weight, tokens, small_rows, segments):
    nf = lax.axis_size("fsdp")
    rows = weight.shape[0]
    n, length, _ = tokens.shape
    vmem = pl.BlockSpec(memory_space=pltpu.VMEM)
    dma = pltpu.SemaphoreType.DMA
    count = 12 if nf == 4 else 2 * nf
    full, *rest = pl.pallas_call(
        partial(gather_kernel, nf),
        out_shape=[
            jax.ShapeDtypeStruct((2 * nf, rows, XBC), BF16),
            jax.ShapeDtypeStruct((n, HALO, D), BF16),
            jax.ShapeDtypeStruct((1, D), F32),
            jax.ShapeDtypeStruct((CONV + 1, XBC), F32),
            jax.ShapeDtypeStruct((INNER // 128, 128), F32),
            jax.ShapeDtypeStruct((8, 128), F32),
            jax.ShapeDtypeStruct((n, 8, LEAD + length), F32),
        ],
        in_specs=[vmem] * 4,
        out_specs=[pl.BlockSpec(memory_space=pl.ANY)] + [vmem] * 6,
        scratch_shapes=[
            pltpu.VMEM((rows, XBC), BF16),
            pltpu.VMEM((n, HALO, D), BF16),
            dma,
            dma((count,)),
            dma((count,)),
        ],
        compiler_params=pltpu.CompilerParams(
            collective_id=1, has_side_effects=True, vmem_limit_bytes=VMEM_LIMIT
        ),
        name="gather_raw",
    )(weight, tokens, small_rows, segments)
    return full.reshape(2 * nf * rows, XBC), *rest


def enter_kernel(
    tok_ref, halo_ref, gain_ref, wraw_ref, dlow_ref, conv_ref, heads_ref, docs_ref,
    normed_ref, turned_ref, raw_ref, dsilu_ref, val_ref, wr_ref, draw_ref, delta_ref, send_ref,
    ext, moved, act, shift,
):
    length = tok_ref.shape[1]
    gain = gain_ref[...]
    for start, rows, src in ((0, HALO, halo_ref), (HALO, length, tok_ref)):
        for b in range(0, rows, 128):
            n = min(128, rows - b)
            x = src[0, b : b + n, :].astype(F32)
            scale = lax.rsqrt(jnp.mean(x * x, axis=-1, keepdims=True) + EPS)
            ext[start + b : start + b + n, :] = (x * scale * gain).astype(BF16)
    normed = ext[HALO:, :]
    normed_ref[0] = normed
    turned_ref[0] = normed.T
    own = docs_ref[0, 0:1, LEAD:]
    rows = lax.broadcasted_iota(jnp.int32, (128, SPAN), 0)
    cols = lax.broadcasted_iota(jnp.int32, (128, SPAN), 1)
    for j in range(1, CONV):
        same = jnp.where(docs_ref[0, BEFORE + j : BEFORE + j + 1, LEAD:] == own, 1.0, 0.0)
        for b in range(0, length, 128):
            here = square_of(same[:, b : b + 128])
            here = jnp.concatenate([here, here[:, : SPAN - 128]], axis=1)
            shift[b // 128, (j - 1) * 128 : j * 128, :] = jnp.where(
                cols == rows + (HALO - j), here, 0.0
            ).astype(BF16)

    draw = nt(dlow_ref[...], normed) + column(heads_ref, BIAS)
    delta = softplus(draw)
    draw_ref[0] = draw
    delta_ref[0] = delta
    totals = nn_high(-jnp.exp(column(heads_ref, RATE)) * delta, triangle(length))
    keep = jnp.where(own == own[:, length - 1 :], 1.0, 0.0)
    weight = jnp.exp(totals[:, length - 1 :] - totals) * keep * delta
    tiles = XBC // TILE
    blocks = length // 128

    def span_of(c):
        return slice(c * TILE, (c + 1) * TILE)

    def project(c):
        if c < tiles:
            raw_ref[0, :, span_of(c)] = nn(ext[...], wraw_ref[:, span_of(c)]).astype(BF16)

    def move(c):
        if c < tiles:
            for i in range(blocks):
                moved[c % 2 * blocks + i] = nn(
                    shift[i], raw_ref[0, i * 128 : i * 128 + SPAN, span_of(c)]
                )

    project(0)
    project(1)
    move(0)
    for c in range(tiles):
        span = span_of(c)
        project(c + 2)
        move(c + 1)
        for b in range(0, length, 128):
            slot = c % 2 * blocks + b // 128
            for half in range(0, TILE, 128):
                hc = slice(c * TILE + half, c * TILE + half + 128)
                lanes = slice(half, half + 128)
                w = conv_ref[:, hc]
                for q in range(0, 128, 64):
                    z = w[4:5] + w[3:4] * raw_ref[0, HALO + b + q : HALO + b + q + 64, hc].astype(F32)
                    for j in range(1, CONV):
                        at = (j - 1) * 128 + q
                        z = z + w[3 - j : 4 - j] * moved[slot, at : at + 64, lanes]
                    sig = sigmoid(z)
                    silu = z * sig
                    act[c % 2, b + q : b + q + 64, lanes] = silu
                    dsilu_ref[0, b + q : b + q + 64, hc] = (sig + silu * (1.0 - sig)).astype(BF16)
        if c < INNER // TILE:
            val_ref[0, span, :] = act[c % 2].T.astype(BF16)
        else:
            wr_ref[0] = act[c % 2].astype(BF16)

    writers = wr_ref[0, :, :STATE]
    for h in range(HEADS):
        rows = slice(h * HEADDIM, (h + 1) * HEADDIM)
        scaled = val_ref[0, rows, :].astype(F32) * weight[h : h + 1, :]
        send_ref[0, rows, :] = nn(scaled.astype(BF16), writers).astype(BF16)


def enter(tokens, halo, gain, wraw, dlow, conv, heads, docs):
    n, length, _ = tokens.shape
    outs = [
        ((n, length, D), BF16),
        ((n, D, length), BF16),
        ((n, length + HALO, XBC), BF16),
        ((n, length, XBC), BF16),
        ((n, INNER, length), BF16),
        ((n, length, 2 * STATE), BF16),
        ((n, HP, length), F32),
        ((n, HP, length), F32),
        ((n, INNER, STATE), BF16),
    ]
    return pl.pallas_call(
        enter_kernel,
        grid=(n,),
        in_specs=[
            piece(length, D), piece(HALO, D), whole(gain.shape), whole(wraw.shape),
            whole(dlow.shape), whole(conv.shape), whole(heads.shape), piece(*docs.shape[1:]),
        ],
        out_specs=[piece(*s[1:]) for s, _ in outs],
        out_shape=[jax.ShapeDtypeStruct(s, t) for s, t in outs],
        scratch_shapes=[
            pltpu.VMEM((length + HALO, D), BF16),
            pltpu.VMEM((2 * (length // 128), (CONV - 1) * 128, TILE), F32),
            pltpu.VMEM((2, length, TILE), F32),
            pltpu.VMEM((length // 128, (CONV - 1) * 128, SPAN), BF16),
        ],
        compiler_params=params(("arbitrary",)),
        name="enter",
    )(tokens, halo, gain, wraw, dlow, conv, heads, docs)


def chunk_terms(delta, rate, docs):
    own = docs[0:1, :]
    before = docs[BEFORE + 1 : BEFORE + 2, 0:1]
    last = docs[0:1, CH - 1 :]
    decay = -jnp.exp(rate) * delta
    totals = nn_high(decay, triangle(CH))
    end = totals[:, CH - 1 :]
    fade = jnp.exp(totals) * jnp.where(own == before, 1.0, 0.0)
    to_end = jnp.exp(end - totals) * jnp.where(own == last, 1.0, 0.0)
    passing = jnp.exp(end) * jnp.where(last == before, 1.0, 0.0)
    together = square_of(own) == own
    first = lax.broadcasted_iota(jnp.int32, (CH, CH), 0)
    second = lax.broadcasted_iota(jnp.int32, (CH, CH), 1)
    barred = jnp.where(together & (first <= second), 0.0, NEG)
    reach = jnp.where(together & (first >= second), 1.0, 0.0)
    return decay, totals, fade, to_end, passing, barred, reach


def forward_kernel(
    val_ref, w_ref, r_ref, delta_ref, heads_ref, docs_ref, in_ref,
    y_ref, start_ref,
    state, off, fresh,
):
    state[...] = in_ref[0].astype(F32)
    rate = column(heads_ref, RATE)
    for k in range(val_ref.shape[2] // CH):
        lanes = slice(k * CH, (k + 1) * CH)
        writers, readers = w_ref[0, lanes, :], r_ref[0, lanes, :]
        delta = delta_ref[0, :, lanes]
        _, totals, fade, to_end, passing, barred, _ = chunk_terms(
            delta, rate, docs_ref[0, :, LEAD + k * CH : LEAD + (k + 1) * CH]
        )
        columns = totals.T
        scores = nt(writers, readers)
        low_state = state[...].astype(BF16)
        start_ref[0, k] = low_state
        off[...] = nt(low_state, readers)
        for h in range(HEADS):
            rows = slice(h * HEADDIM, (h + 1) * HEADDIM)
            mixing = jnp.exp(totals[h : h + 1, :] - columns[:, h : h + 1] + barred) * scores
            scaled = val_ref[0, rows, lanes].astype(F32) * delta[h : h + 1, :]
            fresh[rows, :] = (scaled * to_end[h : h + 1, :]).astype(BF16)
            inside = nn(scaled.astype(BF16), mixing.astype(BF16))
            y_ref[0, rows, lanes] = inside + off[rows, :] * fade[h : h + 1, :]
        gained = nn(fresh[...], writers)
        for h in range(HEADS):
            rows = slice(h * HEADDIM, (h + 1) * HEADDIM)
            state[rows, :] = passing[h : h + 1, :] * state[rows, :] + gained[rows, :]


def forward_scan(values, wr, delta, heads, docs, incoming):
    n, _, length = values.shape
    chunks = length // CH
    return pl.pallas_call(
        forward_kernel,
        grid=(n,),
        in_specs=[
            piece(INNER, length),
            pl.BlockSpec((1, length, STATE), lambda i: (i, 0, 0)),
            pl.BlockSpec((1, length, STATE), lambda i: (i, 0, 1)),
            piece(HP, length),
            whole(heads.shape),
            piece(*docs.shape[1:]),
            piece(INNER, STATE),
        ],
        out_specs=[piece(INNER, length), piece(chunks, INNER, STATE)],
        scratch_shapes=[
            pltpu.VMEM((INNER, STATE), F32),
            pltpu.VMEM((INNER, CH), F32),
            pltpu.VMEM((INNER, CH), BF16),
        ],
        out_shape=[
            jax.ShapeDtypeStruct((n, INNER, length), F32),
            jax.ShapeDtypeStruct((n, chunks, INNER, STATE), BF16),
        ],
        compiler_params=params(("arbitrary",)),
        name="forward_scan",
    )(values, wr, wr, delta, heads, docs, incoming)


def backward_kernel(
    val_ref, w_ref, r_ref, delta_ref, draw_ref, heads_ref, docs_ref, gy_ref, first_ref,
    start_ref, in_ref, final_ref, dsilu_ref, conv_ref, near_ref,
    gval_ref, gwr_ref, gdraw_ref, gheads_ref, ghalo_ref,
    grad, link, off, fresh, faded, gdelta, paid, sums,
):
    n, step = pl.program_id(0), pl.program_id(1)
    rate = column(heads_ref, RATE)

    @pl.when(step == 0)
    def _():
        grad[...] = in_ref[0].astype(F32)
        product = in_ref[0].astype(F32) * final_ref[0].astype(F32)
        by_head = jnp.sum(product.reshape(HEADS, HEADDIM, STATE), axis=1)
        link[0:HEADS, :] = jnp.sum(by_head, axis=1, keepdims=True)
        link[HEADS:, :] = jnp.zeros((HP - HEADS, 1), F32)

    @pl.when((n == 0) & (step == 0))
    def _():
        sums[...] = jnp.zeros_like(sums)

    writers, readers = w_ref[0], r_ref[0]
    delta = delta_ref[0]
    decay, totals, fade, to_end, passing, barred, reach = chunk_terms(delta, rate, docs_ref[0])
    columns = totals.T
    scores = nt(writers, readers)
    low_grad = grad[...].astype(BF16)
    off[...] = nt(low_grad, writers)
    gscores = jnp.zeros((CH, CH), F32)
    gdelta[HEADS:, :] = jnp.zeros((HP - HEADS, CH), F32)
    paid[HEADS:, :] = jnp.zeros((HP - HEADS, CH), F32)
    for h in range(HEADS):
        rows = slice(h * HEADDIM, (h + 1) * HEADDIM)
        spread = jnp.exp(totals[h : h + 1, :] - columns[:, h : h + 1] + barred)
        values = val_ref[0, rows, :].astype(F32)
        gy = gy_ref[0, rows, :]
        gy32 = gy.astype(F32)
        scaled = values * delta[h : h + 1, :]
        fresh[rows, :] = (scaled * to_end[h : h + 1, :]).astype(BF16)
        faded[rows, :] = (gy32 * fade[h : h + 1, :]).astype(BF16)
        gscaled = nt(gy, (spread * scores).astype(BF16)) + off[rows, :] * to_end[h : h + 1, :]
        low = scaled.astype(BF16)
        gscores = gscores + tn(low, gy) * spread
        paid[h : h + 1, :] = jnp.sum(low.astype(F32) * gscaled, axis=0, keepdims=True)
        gdelta[h : h + 1, :] = jnp.sum(values * gscaled, axis=0, keepdims=True)
        gval_ref[0, rows, :] = (
            gscaled * delta[h : h + 1, :] + gy32 * heads_ref[SKIP : SKIP + 1, h : h + 1]
        ).astype(BF16)
    low_scores = gscores.astype(BF16)
    gwr_ref[0, :, :STATE] = nn(low_scores, readers) + tn(fresh[...], low_grad)
    gwr_ref[0, :, STATE:] = tn(low_scores, writers) + tn(faded[...], start_ref[0, 0])
    off[:, :STATE] = nn(faded[...], readers)
    for h in range(HEADS):
        rows = slice(h * HEADDIM, (h + 1) * HEADDIM)
        grad[rows, :] = passing[h : h + 1, :] * grad[rows, :] + off[rows, :STATE]
    following = jnp.where(docs_ref[0, 0:1, :] == docs_ref[0, 1:2, CH - 1 :], 1.0, 0.0)
    gdecay = nn_high(first_ref[0] - paid[...], reach) + following * link[...]
    link[...] = gdecay[:, :1]
    gtotal = gdelta[...] - jnp.exp(rate) * gdecay
    gdraw = gtotal * sigmoid(draw_ref[0])
    gdraw_ref[0] = gdraw
    sums[0] += gdraw
    sums[1] += gdecay * decay

    @pl.when(step == pl.num_programs(1) - 1)
    def _():
        taps = conv_ref[...]
        near = [
            square_of(
                jnp.where(near_ref[0, j : j + 1, :] == near_ref[0, 0:1, :], 1.0, 0.0)
            )[120:, :]
            for j in range(CONV)
        ]
        for c in range(XBC // 128):
            cols = slice(c * 128, (c + 1) * 128)
            if c < INNER // 128:
                here = gval_ref[0, cols, :].astype(F32).T[:8, :]
            else:
                here = gwr_ref[0, 0:8, c * 128 - INNER : c * 128 - INNER + 128]
            pre = here * dsilu_ref[0, 0:8, cols].astype(F32)
            wide = jnp.concatenate([jnp.zeros((8, 128), F32), pre], axis=0)
            total = jnp.zeros((8, 128), F32)
            for j in range(1, CONV):
                total = total + taps[3 - j : 4 - j, cols] * wide[j : j + 8] * near[j]
            ghalo_ref[0, :, cols] = total

    @pl.when((n == pl.num_programs(0) - 1) & (step == pl.num_programs(1) - 1))
    def _():
        for i in range(2):
            both = jnp.concatenate([sums[i], jnp.zeros((128 - HP, CH), F32)], axis=0)
            gheads_ref[i : i + 1, :] = jnp.sum(both.T, axis=0, keepdims=True)
        gheads_ref[2:, :] = jnp.zeros((6, 128), F32)


def backward_scan(
    values, wr, delta, draw, heads, docs, gy, first, starts, incoming, final, dsilu, conv
):
    n, _, length = values.shape
    chunks = length // CH
    back = lambda k: chunks - 1 - k
    lanes = lambda rows: pl.BlockSpec((1, rows, CH), lambda i, k: (i, 0, back(k)))
    return pl.pallas_call(
        backward_kernel,
        grid=(n, chunks),
        in_specs=[
            lanes(INNER),
            pl.BlockSpec((1, CH, STATE), lambda i, k: (i, back(k), 0)),
            pl.BlockSpec((1, CH, STATE), lambda i, k: (i, back(k), 1)),
            lanes(HP),
            lanes(HP),
            whole(heads.shape, 2),
            pl.BlockSpec((1, 8, CH), lambda i, k: (i, 0, back(k) + LEAD // CH)),
            lanes(INNER),
            lanes(HP),
            pl.BlockSpec((1, 1, INNER, STATE), lambda i, k: (i, back(k), 0, 0)),
            pl.BlockSpec((1, INNER, STATE), lambda i, k: (i, 0, 0)),
            pl.BlockSpec((1, INNER, STATE), lambda i, k: (i, 0, 0)),
            pl.BlockSpec((1, 16, XBC), lambda i, k: (i, 0, 0)),
            whole(conv.shape, 2),
            pl.BlockSpec((1, 8, 128), lambda i, k: (i, 0, 0)),
        ],
        out_specs=[
            lanes(INNER),
            pl.BlockSpec((1, CH, 2 * STATE), lambda i, k: (i, back(k), 0)),
            lanes(HP),
            pl.BlockSpec((8, 128), lambda i, k: (0, 0)),
            pl.BlockSpec((1, 8, XBC), lambda i, k: (i, 0, 0)),
        ],
        scratch_shapes=[
            pltpu.VMEM((INNER, STATE), F32),
            pltpu.VMEM((HP, 1), F32),
            pltpu.VMEM((INNER, CH), F32),
            pltpu.VMEM((INNER, CH), BF16),
            pltpu.VMEM((INNER, CH), BF16),
            pltpu.VMEM((HP, CH), F32),
            pltpu.VMEM((HP, CH), F32),
            pltpu.VMEM((2, HP, CH), F32),
        ],
        out_shape=[
            jax.ShapeDtypeStruct((n, INNER, length), BF16),
            jax.ShapeDtypeStruct((n, length, 2 * STATE), F32),
            jax.ShapeDtypeStruct((n, HP, length), F32),
            jax.ShapeDtypeStruct((8, 128), F32),
            jax.ShapeDtypeStruct((n, 8, XBC), F32),
        ],
        compiler_params=params(("arbitrary", "arbitrary")),
        name="backward_scan",
    )(
        values, wr, wr, delta, draw, heads, docs, gy, first, starts, incoming, final, dsilu,
        conv, docs,
    )


def leave_kernel(group, packed, *refs):
    if packed:
        weights_ref, *refs = refs
        *refs, wgate_ref, wout_ref, loaded = refs
    else:
        wgate_ref, wout_ref, *refs = refs
    (
        normed_ref, turned_ref, cot_ref, tok_ref, y_ref, val_ref, r_ref, gain_ref, delta_ref,
        heads_ref, docs_ref,
        out_ref, gy_ref, gnorm_ref, first_ref, gstate_ref, grads_ref, ggain_ref, gskip_ref,
        gate, gated, upward, lifted, faded, flat, total_out, total_gate, products, skips, gains,
        wide_gain, fade, total_state,
    ) = refs
    n, k = pl.program_id(0), pl.program_id(1)
    begin = (n == 0) & (k == 0)
    end = (n == pl.num_programs(0) - 1) & (k == pl.num_programs(1) - 1)
    length = delta_ref.shape[2]
    rows_out, rows_in = INNER // group, D // group
    tiles = INNER // TILE
    lanes = range(0, ROWS, 128)
    down = lambda s: jnp.sum(s, axis=0, keepdims=True)

    def fold(v):
        return jnp.sum(v.reshape(v.shape[0] // 8, 8, 128), axis=0)

    def loads():
        copies = []
        for p in range(group):
            for q, ref, at, left in (
                (2, wgate_ref, p * rows_in, 0), (3, wgate_ref, p * rows_in, D),
                (0, wout_ref, p * rows_out, 0), (1, wout_ref, p * rows_out + rows_in, 0),
            ):
                copies.append(
                    pltpu.make_async_copy(
                        weights_ref.at[p, q],
                        ref.at[pl.ds(at, rows_in), pl.ds(left, D)],
                        loaded.at[len(copies)],
                    )
                )
        return copies

    @pl.when(begin)
    def _():
        if packed:
            for copy in loads():
                copy.start()
        total_out[...] = jnp.zeros_like(total_out)
        total_gate[...] = jnp.zeros_like(total_gate)
        skips[...] = jnp.zeros_like(skips)
        gains[...] = jnp.zeros_like(gains)
        for q in range(INNER // 128):
            wide_gain[q * 128 : (q + 1) * 128, :] = square_of(gain_ref[q : q + 1, :])

    @pl.when(k == 0)
    def _():
        own = docs_ref[0, 0:1, LEAD:]
        before = docs_ref[0, BEFORE + 1 : BEFORE + 2, LEAD : LEAD + 1]
        totals = nn_high(-jnp.exp(column(heads_ref, RATE)) * delta_ref[0], triangle(length))
        fade[...] = jnp.exp(totals) * jnp.where(own == before, 1.0, 0.0)
        total_state[...] = jnp.zeros_like(total_state)

    if packed:

        @pl.when(begin)
        def _():
            for copy in loads():
                copy.wait()

    here = pl.ds(pl.multiple_of(k * ROWS, ROWS), ROWS)

    def span(c):
        return slice(c * TILE, (c + 1) * TILE)

    def head_rows(h):
        return slice(h * HEADDIM, (h + 1) * HEADDIM)

    def open_tile(c):
        if c < tiles:
            gate[span(c), :] = nn(normed_ref[0], wgate_ref[:, span(c)]).T.astype(BF16)
            upward[span(c), :] = nt(wout_ref[span(c), :], cot_ref[0])

    squares = [jnp.zeros((8, 128), F32) for _ in lanes]
    dots = [jnp.zeros((8, 128), F32) for _ in lanes]
    open_tile(0)
    for c in range(tiles):
        open_tile(c + 1)
        for h in range(c * 4, c * 4 + 4):
            rows = head_rows(h)
            skip = heads_ref[SKIP : SKIP + 1, h : h + 1]
            gain = wide_gain[rows, :]
            for i, b in enumerate(lanes):
                g = gate[rows, b : b + 128].astype(F32)
                values = val_ref[0, rows, b : b + 128].astype(F32)
                v = (y_ref[0, rows, b : b + 128] + skip * values) * (g * sigmoid(g))
                gated[rows, b : b + 128] = v
                squares[i] = squares[i] + fold(v * v)
                dots[i] = dots[i] + fold(upward[rows, b : b + 128] * gain * v)
    scale = [lax.rsqrt(down(s) * (1.0 / INNER) + EPS) for s in squares]
    pull = [s * s * s * down(d) * (1.0 / INNER) for s, d in zip(scale, dots)]

    def close_tile(c):
        low = lifted[span(c), :]
        flat[:, span(c)] = low.T
        total_out[span(c), :] += nn(low, cot_ref[0])
        total_gate[:, span(c)] += nt(turned_ref[0], gate[span(c), :])
        total_state[span(c), :] += nn(faded[c % 2], r_ref[0])

    for c in range(tiles):
        if c > 0:
            close_tile(c - 1)
        for h in range(c * 4, c * 4 + 4):
            eight = slice(h * 8, h * 8 + 8)
            skip = heads_ref[SKIP : SKIP + 1, h : h + 1]
            fading = fade[h : h + 1, here]
            sums = jnp.zeros((8, 128), F32)
            product = [jnp.zeros((8, 128), F32) for _ in lanes]
            for at in range(h * HEADDIM, (h + 1) * HEADDIM, SUB):
                rows = slice(at, at + SUB)
                inner = slice(at - c * TILE, at - c * TILE + SUB)
                gain = wide_gain[rows, :]
                gain_sums = gains[rows, :]
                for i, b in enumerate(lanes):
                    v = gated[rows, b : b + 128]
                    u = upward[rows, b : b + 128]
                    normal = v * scale[i]
                    lifted[rows, b : b + 128] = (normal * gain).astype(BF16)
                    gain_sums = gain_sums + u * normal
                    gv = scale[i] * (u * gain) - pull[i] * v
                    g = gate[rows, b : b + 128].astype(F32)
                    sig = sigmoid(g)
                    silu = g * sig
                    low = (gv * silu).astype(BF16)
                    gy_ref[0, rows, b : b + 128] = low
                    gm = low.astype(F32)
                    faded[c % 2, inner, b : b + 128] = (gm * fading[:, b : b + 128]).astype(BF16)
                    values = val_ref[0, rows, b : b + 128].astype(F32)
                    sums = sums + fold(gm * values)
                    y = y_ref[0, rows, b : b + 128]
                    product[i] = product[i] + fold(gm * y)
                    gate[rows, b : b + 128] = (
                        gv * (y + skip * values) * (sig + silu * (1.0 - sig))
                    ).astype(BF16)
                gains[rows, :] = gain_sums
            for i, b in enumerate(lanes):
                products[eight, b : b + 128] = product[i]
            skips[eight, :] += sums
    close_tile(tiles - 1)
    for b in range(0, D, TILE):
        branch = nn(flat[...], wout_ref[:, b : b + TILE])
        out_ref[0, :, b : b + TILE] = (tok_ref[0, :, b : b + TILE].astype(F32) + branch).astype(BF16)
    for b in range(0, D, TILE):
        gnorm_ref[0, b : b + TILE, :] = nn(wgate_ref[b : b + TILE, :], gate[...]).astype(BF16)
    first_ref[0, 0:HEADS, :] = jnp.sum(products[...].reshape(HEADS, 8, ROWS), axis=1)
    first_ref[0, HEADS:, :] = jnp.zeros((HP - HEADS, ROWS), F32)

    @pl.when(k == pl.num_programs(1) - 1)
    def _():
        gstate_ref[0] = total_state[...].astype(BF16)

    @pl.when(end)
    def _():
        for p in range(group):
            grads_ref[p, :rows_out, :] = total_out[p * rows_out : (p + 1) * rows_out, :].astype(BF16)
            for half in range(2):
                at = rows_out + half * rows_in
                grads_ref[p, at : at + rows_in, :] = total_gate[
                    p * rows_in : (p + 1) * rows_in, half * D : (half + 1) * D
                ].astype(BF16)
        for q in range(INNER // 128):
            ggain_ref[q : q + 1, :] = down(gains[q * 128 : (q + 1) * 128, :].T)
        ggain_ref[INNER // 128 :, :] = jnp.zeros((16 - INNER // 128, 128), F32)
        by_head = jnp.sum(skips[...].reshape(HEADS, 8, 128), axis=1)
        by_head = jnp.concatenate([by_head, jnp.zeros((128 - HEADS, 128), F32)], axis=0)
        gskip_ref[0:1, :] = down(by_head.T)
        gskip_ref[1:, :] = jnp.zeros((7, 128), F32)


def leave(weights, normed, turned, cot, tokens, y, values, wr, gain, delta, heads, docs):
    n, length, _ = normed.shape
    group, _, rows_in, _ = weights.shape
    packed = rows_in % 16 == 0
    if packed:
        weights, loaded = [weights], [pl.BlockSpec(memory_space=pl.ANY)]
        scratch = [
            pltpu.VMEM((D, INNER), BF16),
            pltpu.VMEM((INNER, D), BF16),
            pltpu.SemaphoreType.DMA((4 * group,)),
        ]
    else:
        gate = jnp.concatenate([weights[:, 2], weights[:, 3]], axis=-1).reshape(D, INNER)
        weights = [gate, weights[:, :2].reshape(INNER, D)]
        loaded, scratch = [whole(a.shape, 2) for a in weights], []
    grads = (group, 4 * rows_in, D)
    rows = lambda width: pl.BlockSpec((1, ROWS, width), lambda i, k: (i, k, 0))
    lanes = lambda height: pl.BlockSpec((1, height, ROWS), lambda i, k: (i, 0, k))
    each = lambda *shape: pl.BlockSpec((1,) + shape, lambda i, k: (i, 0, 0))
    return pl.pallas_call(
        partial(leave_kernel, group, packed),
        grid=(n, length // ROWS),
        in_specs=loaded + [
            rows(D), lanes(D), rows(D), rows(D), lanes(INNER), lanes(INNER),
            pl.BlockSpec((1, ROWS, STATE), lambda i, k: (i, k, 1)),
            whole(gain.shape, 2), each(HP, length), whole(heads.shape, 2), each(*docs.shape[1:]),
        ],
        out_specs=[
            rows(D), lanes(INNER), lanes(D), lanes(HP), each(INNER, STATE), whole(grads, 2),
            whole((16, 128), 2), whole((8, 128), 2),
        ],
        scratch_shapes=[
            pltpu.VMEM((INNER, ROWS), BF16),
            pltpu.VMEM((INNER, ROWS), F32),
            pltpu.VMEM((INNER, ROWS), F32),
            pltpu.VMEM((INNER, ROWS), BF16),
            pltpu.VMEM((2, TILE, ROWS), BF16),
            pltpu.VMEM((ROWS, INNER), BF16),
            pltpu.VMEM((INNER, D), F32),
            pltpu.VMEM((D, INNER), F32),
            pltpu.VMEM((HEADS * 8, ROWS), F32),
            pltpu.VMEM((HEADS * 8, 128), F32),
            pltpu.VMEM((INNER, 128), F32),
            pltpu.VMEM((INNER, 128), F32),
            pltpu.VMEM((HP, length), F32),
            pltpu.VMEM((INNER, STATE), F32),
        ] + scratch,
        out_shape=[
            jax.ShapeDtypeStruct((n, length, D), BF16),
            jax.ShapeDtypeStruct((n, INNER, length), BF16),
            jax.ShapeDtypeStruct((n, D, length), BF16),
            jax.ShapeDtypeStruct((n, HP, length), F32),
            jax.ShapeDtypeStruct((n, INNER, STATE), BF16),
            jax.ShapeDtypeStruct(grads, BF16),
            jax.ShapeDtypeStruct((16, 128), F32),
            jax.ShapeDtypeStruct((8, 128), F32),
        ],
        compiler_params=params(("arbitrary", "arbitrary")),
        name="leave",
    )(*weights, normed, turned, cot, tokens, y, values, wr, gain, delta, heads, docs)


def exit_kernel(
    gval_ref, gwr_ref, dsilu_ref, raw_ref, docs_ref, conv_ref, back_ref, normed_ref, turned_ref,
    wraw_ref, gdraw_ref, dlow_ref, gnorm_ref, tok_ref, cot_ref, gain_ref,
    grad_ref, graw_ref, gdelta_ref, ggain_ref, gconv_ref,
    pre, low_pre, moved, halo_terms, shift, low, lifted, total, sums,
):
    n = pl.program_id(0)
    length = dsilu_ref.shape[1]
    last = n == pl.num_programs(0) - 1

    @pl.when(n == 0)
    def _():
        total[...] = jnp.zeros_like(total)
        sums[...] = jnp.zeros_like(sums)
        gdelta_ref[...] = jnp.zeros_like(gdelta_ref)
        ggain_ref[...] = jnp.zeros_like(ggain_ref)

    def shifts(rows, extent, near):
        first = lax.broadcasted_iota(jnp.int32, (rows, extent), 0)
        second = lax.broadcasted_iota(jnp.int32, (rows, extent), 1)
        return [
            jnp.where(second == first + j, near[j - 1], 0.0).astype(BF16) for j in range(1, CONV)
        ]

    near = [
        jnp.where(docs_ref[0, j : j + 1, :] == docs_ref[0, 0:1, :], 1.0, 0.0)
        for j in range(1, CONV)
    ]
    for i in range(length // 128):
        square = [square_of(v[:, LEAD + i * 128 : LEAD + i * 128 + 128]) for v in near]
        square = [jnp.concatenate([v, v[:, : SPAN - 128]], axis=1) for v in square]
        shift[i] = jnp.concatenate(shifts(128, SPAN, square), axis=0)
    square = [square_of(v[:, LEAD - 128 : LEAD])[128 - HALO :, : 2 * HALO] for v in near]
    ahead = jnp.concatenate(shifts(HALO, 2 * HALO, square), axis=0)
    for slot in range(2):
        low_pre[slot, :HALO, :] = jnp.zeros((HALO, TILE), BF16)
        low_pre[slot, HALO + length :, :] = jnp.zeros((HALO, TILE), BF16)
    tiles = XBC // TILE
    blocks = length // 128

    def span_of(c):
        return slice(c * TILE, (c + 1) * TILE)

    def open_tile(c):
        if c == tiles:
            return
        if c < INNER // TILE:
            here = gval_ref[0, span_of(c), :].astype(F32).T
        else:
            here = gwr_ref[0]
        here = here * dsilu_ref[0, :, span_of(c)].astype(F32)
        pre[c % 2] = here
        low_pre[c % 2, HALO : HALO + length, :] = here.astype(BF16)
        halo_terms[c % 2] = nn(ahead, low_pre[c % 2, : 2 * HALO, :])
        for i in range(blocks):
            moved[c % 2 * blocks + i] = nn(
                shift[i], low_pre[c % 2, HALO + i * 128 : HALO + i * 128 + SPAN, :]
            )

    def close_tile(c):
        total[:, span_of(c)] += nn(turned_ref[0], low[c % 2])
        through = nt(low[c % 2], wraw_ref[:, span_of(c)])
        if c == 0:
            lifted[...] = through
        else:
            lifted[...] += through

    def fold(v):
        return jnp.sum(v.reshape(v.shape[0] // 8, 8, 128), axis=0)

    open_tile(0)
    for c in range(tiles):
        slot = c % 2
        open_tile(c + 1)
        if c > 0:
            close_tile(c - 1)
        for half in range(0, TILE, 128):
            cols = slice(half, half + 128)
            wide = slice(c * TILE + half, c * TILE + half + 128)
            w = conv_ref[:, wide]
            folded = [sums[k, :, wide] for k in range(CONV + 1)]
            raw = raw_ref[0, :HALO, wide].astype(F32)
            for j in range(1, CONV):
                term = halo_terms[slot, (j - 1) * HALO : j * HALO, cols]
                folded[3 - j] = folded[3 - j] + fold(raw * term)
            for b in range(0, length, 64):
                raw = raw_ref[0, HALO + b : HALO + b + 64, wide].astype(F32)
                now = pre[slot, b : b + 64, cols]
                grad = w[3:4] * now
                folded[3] = folded[3] + fold(raw * now)
                folded[4] = folded[4] + fold(now)
                for j in range(1, CONV):
                    at = (j - 1) * 128 + b % 128
                    term = moved[slot * blocks + b // 128, at : at + 64, cols]
                    grad = grad + w[3 - j : 4 - j] * term
                    folded[3 - j] = folded[3 - j] + fold(raw * term)
                if b == length - 64:
                    grad = jnp.concatenate([grad[:56], grad[56:] + back_ref[0, :, wide]], axis=0)
                low[slot, b : b + 64, cols] = grad.astype(BF16)
            for k in range(CONV + 1):
                sums[k, :, wide] = folded[k]
    close_tile(tiles - 1)

    gdraw = gdraw_ref[0].astype(BF16)
    gdelta_ref[...] += nn(gdraw, normed_ref[0])
    gain = gain_ref[...]
    gains = jnp.zeros((8, D), F32)
    for b in range(0, length, 128):
        rows = slice(b, b + 128)
        up = lifted[rows, :] + gnorm_ref[0, :, rows].astype(F32).T + tn(gdraw[:, rows], dlow_ref[...])
        x = tok_ref[0, rows, :].astype(F32)
        scale = lax.rsqrt(jnp.mean(x * x, axis=-1, keepdims=True) + EPS)
        normal = x * scale
        gains = gains + jnp.sum((up * normal).reshape(16, 8, D), axis=0)
        up = up * gain
        inner = jnp.mean(up * normal, axis=-1, keepdims=True)
        grad = cot_ref[0, rows, :].astype(F32) + scale * (up - normal * inner)
        grad_ref[0, rows, :] = grad.astype(BF16)
    ggain_ref[0:1, :] += jnp.sum(gains, axis=0, keepdims=True)

    @pl.when(last)
    def _():
        graw_ref[...] = total[...].astype(BF16)
        gconv_ref[0 : CONV + 1, :] = jnp.sum(sums[...], axis=1)


def leave_back(
    gval, gwr, dsilu, raw, docs, conv, back, normed, turned, wraw, gdraw, dlow, gnorm, tokens,
    cotangent, gain,
):
    n, length, _ = dsilu.shape
    return pl.pallas_call(
        exit_kernel,
        grid=(n,),
        in_specs=[
            piece(INNER, length), piece(length, 2 * STATE), piece(length, XBC),
            piece(length + HALO, XBC), piece(*docs.shape[1:]), whole(conv.shape), piece(8, XBC),
            piece(length, D), piece(D, length), whole(wraw.shape), piece(HP, length),
            whole(dlow.shape), piece(D, length), piece(length, D), piece(length, D),
            whole(gain.shape),
        ],
        out_specs=[
            piece(length, D), whole((D, XBC)), whole((HP, D)), whole((8, D)), whole((8, XBC)),
        ],
        out_shape=[
            jax.ShapeDtypeStruct((n, length, D), BF16),
            jax.ShapeDtypeStruct((D, XBC), BF16),
            jax.ShapeDtypeStruct((HP, D), F32),
            jax.ShapeDtypeStruct((8, D), F32),
            jax.ShapeDtypeStruct((8, XBC), F32),
        ],
        scratch_shapes=[
            pltpu.VMEM((2, length, TILE), F32),
            pltpu.VMEM((2, length + 2 * HALO, TILE), BF16),
            pltpu.VMEM((2 * (length // 128), (CONV - 1) * 128, TILE), F32),
            pltpu.VMEM((2, (CONV - 1) * HALO, TILE), F32),
            pltpu.VMEM((length // 128, (CONV - 1) * 128, SPAN), BF16),
            pltpu.VMEM((2, length, TILE), BF16),
            pltpu.VMEM((length, D), F32),
            pltpu.VMEM((D, XBC), F32),
            pltpu.VMEM((CONV + 1, 8, XBC), F32),
        ],
        compiler_params=params(("arbitrary",)),
        name="leave_back",
    )(
        gval, gwr, dsilu, raw, docs, conv, back, normed, turned, wraw, gdraw, dlow, gnorm, tokens,
        cotangent, gain,
    )


def tiles_of(extent):
    return -(-extent // 128)


def pieces_of(rows):
    return [(i, i * 128, min(128, rows - i * 128)) for i in range(tiles_of(rows))]


def split_three(v):
    high = v.astype(BF16)
    rest = v - high.astype(F32)
    middle = rest.astype(BF16)
    low = (rest - middle.astype(F32)).astype(BF16)
    return jnp.concatenate([high, middle, low], axis=0)


def join_three(v):
    return v[0:8] + v[8:16] + v[16:24]


def inverse_factor(gram):
    rows = lax.broadcasted_iota(jnp.int32, (8, 8), 0)
    cols = lax.broadcasted_iota(jnp.int32, (8, 8), 1)
    left, right = gram, jnp.where(rows == cols, 1.0, 0.0)
    for j in range(7):
        factor = jnp.where(rows[:, :1] > j, left[:, j : j + 1] / left[j : j + 1, j : j + 1], 0.0)
        left, right = left - factor * left[j : j + 1, :], right - factor * right[j : j + 1, :]
    pivots = jnp.sum(jnp.where(rows == cols, left, 0.0), axis=1, keepdims=True)
    return right * lax.rsqrt(pivots)


RIGHT_OUT = PROJ // 128
DELTA = RIGHT_OUT + D // 128
REST = DELTA + HEADS // 8 * (D // 128)
REST_ROWS = D // 128 + (CONV + 1) * (XBC // 128) + INNER // 128 + 3
SUMMED = REST + -(-REST_ROWS // 8)


class Scatter:
    def __init__(self, group, x_ref, from_core, pairs, from_far, joint, send, recv):
        self.nf = group // 2
        self.x_ref, self.from_core, self.pairs, self.from_far = x_ref, from_core, pairs, from_far
        self.joint, self.send, self.recv = joint, send, recv
        self.r, self.f, self.s = (lax.axis_index(name) for name in ("rep", "fsdp", "seq"))
        self.copies = []
        half = x_ref.shape[1] // 2
        self.parts = [slice(0, half), slice(half, 2 * half)]
        f = self.f
        if self.nf == 4:
            x, y = f + 1 - 2 * lax.rem(f, 2), lax.rem(f + 2, 4)
            self.order = [lax.rem(x + 2, 4), x, y, f]
        else:
            self.order = [lax.rem(f + 1 + j, self.nf) for j in range(self.nf)]

    def start(self, src, dst, device):
        k = len(self.copies)
        copy = pltpu.make_async_remote_copy(
            src, dst, self.send.at[k], self.recv.at[k], device_id=device, device_id_type=MESH
        )
        copy.start()
        self.copies.append(copy)
        return copy

    def begin(self):
        other = (self.r, self.f, 1 - self.s)
        self.near = [
            self.start(self.x_ref.at[f * 2 + 1 - self.s], self.from_core.at[j], other)
            for j, f in enumerate(self.order)
        ]

    def device(self, j):
        return (self.r, self.order[j], self.s)

    def cross(self):
        self.far = []
        for j, f in enumerate(self.order):
            self.near[j].wait_recv()
            total = self.x_ref[f * 2 + self.s].astype(F32) + self.from_core[j].astype(F32)
            self.pairs[j] = total.astype(BF16)
            if self.nf != 4 and j < self.nf - 1:
                self.far.append(self.start(self.pairs.at[j], self.from_far.at[j], self.device(j)))
            if self.nf == 4 and j < 3:
                for half, part in enumerate(self.parts):
                    if j == 0 or half == j - 1:
                        to = half + 1 if j == 0 else j
                        self.far.append(
                            self.start(
                                self.pairs.at[j, part], self.from_far.at[j, part], self.device(to)
                            )
                        )

    def turn(self):
        if self.nf != 4:
            return
        for half, part in enumerate(self.parts):
            self.far[half].wait_recv()
            to = 2 - half
            total = self.pairs[to, part].astype(F32) + self.from_far[0, part].astype(F32)
            self.joint[half] = total.astype(BF16)
            self.far.append(
                self.start(self.joint.at[half], self.from_far.at[to, part], self.device(to))
            )

    def end(self, o_ref):
        if self.nf == 4:
            for copy in self.far[2:]:
                copy.wait_recv()
            total = self.pairs[3].astype(F32)
            for j in (1, 2):
                total = total + self.from_far[j].astype(F32)
        else:
            total = self.pairs[self.nf - 1].astype(F32)
            for j, copy in enumerate(self.far):
                copy.wait_recv()
                total = total + self.from_far[j].astype(F32)
        o_ref[...] = total
        for copy in self.copies:
            copy.wait_send()


class Exchange:
    def __init__(self, group, replicas):
        self.group, self.replicas = group, replicas
        r, f, s = lax.axis_index("rep"), lax.axis_index("fsdp"), lax.axis_index("seq")
        self.r, self.me = r, f * 2 + s
        self.peers = []
        for j in range(1, group):
            p = lax.rem(self.me + j, group)
            self.peers.append((p, (r, lax.div(p, 2), lax.rem(p, 2))))
        self.others = [(lax.rem(r + j, replicas), f, s) for j in range(1, replicas)]

    def greet(self):
        barrier = pltpu.get_barrier_semaphore()
        for device in [d for _, d in self.peers] + self.others:
            pl.semaphore_signal(barrier, inc=1, device_id=device, device_id_type=MESH)

    def met(self):
        pl.semaphore_wait(pltpu.get_barrier_semaphore(), self.group + self.replicas - 2)

    def sum(self, x_ref, o_ref, own, from_group, from_reps, send, recv, second=None, third=None):
        group, replicas, me = self.group, self.replicas, self.me
        width = own.shape[0]
        copies = []

        def start(src, dst, device):
            k = len(copies)
            copy = pltpu.make_async_remote_copy(
                src, dst, send.at[k], recv.at[k], device_id=device, device_id_type=MESH
            )
            copy.start()
            copies.append(copy)
            return copy

        arriving = [
            start(x_ref.at[pl.ds(p * width, width)], from_group.at[j], device)
            for j, (p, device) in enumerate(self.peers)
        ]
        total = x_ref[pl.ds(me * width, width)]
        for j, copy in enumerate(arriving):
            copy.wait_recv()
            total = total + from_group[j]
        own[...] = total
        from_reps[pl.ds(self.r, 1)] = total[None]
        arriving = [start(own, from_reps.at[self.r], device) for device in self.others]
        if second is not None:
            second()
        for copy in arriving:
            copy.wait_recv()
        total = from_reps[0]
        for j in range(1, replicas):
            total = total + from_reps[j]
        mine = pl.ds(me * width, width)
        o_ref[mine] = total
        arriving = [start(o_ref.at[mine], o_ref.at[mine], device) for _, device in self.peers]
        if third is not None:
            third()
        for copy in arriving:
            copy.wait_recv()
        for copy in copies:
            copy.wait_send()


def compress_kernel(
    group, replicas,
    sin_ref, sout_ref, grads_ref, raw_ref, ein_ref, eout_ref, gdelta_ref, ggain_ref,
    gconv_ref, ggate_ref, gheads_ref, gskip_ref,
    sum_ref, left_in_ref, left_out_ref, turned_in_ref, turned_out_ref, raw_total_ref,
    lefts, left_sums, hat, rights,
    own_a, group_a, reps_a, own_b, group_b, reps_b, send_a, recv_a, send_b, recv_b,
    from_core, pairs, from_far, joint, send_c, recv_c, held_raw, held_grads, held_in, held_out,
    split_in, split_out, load,
):
    rows_in, rows_out = ein_ref.shape[0], eout_ref.shape[0]
    out_part = slice(0, rows_out)
    gate_parts = [slice(rows_out + i * rows_in, rows_out + (i + 1) * rows_in) for i in range(2)]
    ahead = tiles_of(rows_in)
    width = ahead + tiles_of(rows_out)
    exchange = Exchange(group, replicas)
    exchange.greet()
    loads = [
        pltpu.make_async_copy(src, dst, load.at[k])
        for k, (src, dst) in enumerate(
            ((ein_ref, held_in), (eout_ref, held_out), (grads_ref, held_grads), (raw_ref, held_raw))
        )
    ]
    for copy in loads:
        copy.start()
    raw_ref, grads_ref = held_raw, held_grads

    lefts[...] = jnp.zeros_like(lefts)
    mine = pl.ds(exchange.me * width, width)

    def place(index, values, rows, first):
        for i, at, n in pieces_of(rows):
            lefts[index + first + i, :, :n] += values[:, at : at + n]

    def place_own(values, rows, first):
        for i, at, n in pieces_of(rows):
            part = values[:, at : at + n]
            if n < 128:
                part = jnp.concatenate([part, jnp.zeros((8, 128 - n), F32)], axis=1)
            where = pl.ds(exchange.me * width + first + i, 1)
            lefts[where] = lefts[where] + part[None]

    s_in, s_out = split_three(sin_ref[...]), split_three(sout_ref[...])
    for k, (held, split, start, rows, first) in enumerate(
        ((held_in, split_in, s_in, rows_in, 0), (held_out, split_out, s_out, rows_out, ahead))
    ):
        loads[k].wait()
        high = held[...].astype(BF16)
        split[0] = high
        split[1] = (held[...] - high.astype(F32)).astype(BF16)
        place_own(join_three(nt(start, split[0]) + nt(start, split[1])), rows, first)
    loads[2].wait()
    for p in range(group):
        product = nt(s_in[:, :D], grads_ref[p, gate_parts[0]])
        product = product + nt(s_in[:, D:INNER], grads_ref[p, gate_parts[1]])
        place(p * width, join_three(product), rows_in, 0)
        place(p * width, join_three(nt(s_out, grads_ref[p, out_part])), rows_out, ahead)
    loads[3].wait()
    exchange.met()
    scatter = Scatter(group, raw_ref, from_core, pairs, from_far, joint, send_c, recv_c)
    scatter.begin()
    for p in range(group):
        place(p * width, join_three(nt(s_in[:, INNER:], raw_ref[p])), rows_in, 0)
    exchange.sum(
        lefts, left_sums, own_a, group_a, reps_a, send_a, recv_a, scatter.cross, scatter.turn
    )

    for first, last in ((0, ahead), (ahead, width)):
        gram = jnp.zeros((8, 8), F32)
        for p in range(group):
            for i in range(first, last):
                tile = left_sums[p * width + i] * (1.0 / replicas)
                gram = gram + nt_high(tile, tile)
        inverse = inverse_factor(gram)
        for p in range(group):
            for i in range(first, last):
                hat[p * width + i] = nn_high(inverse, left_sums[p * width + i] * (1.0 / replicas))
    own = hat[mine]
    for first, rows, left_ref, turned_ref in (
        (0, rows_in, left_in_ref, turned_in_ref), (ahead, rows_out, left_out_ref, turned_out_ref)
    ):
        for i, at, n in pieces_of(rows):
            turned_ref[:, at : at + n] = own[first + i][:, :n]
            left_ref[at : at + n, :] = own[first + i].T[:n, :]

    def joined(tiles, start, rows):
        return jnp.concatenate([tiles[start + i][:, :n] for i, _, n in pieces_of(rows)], axis=1)

    def product(matrices, rows, skipped, error, at):
        spread = [split_three(joined(hat, p * width + skipped, rows)) for p in range(group)]
        mixed = split_three(joined(own, skipped, rows))
        columns = 0
        for ref, part, extent in matrices:
            for b in range(0, extent, TILE):
                total = nn(spread[0], ref[0, part, b : b + TILE])
                for p in range(1, group):
                    total = total + nn(spread[p], ref[p, part, b : b + TILE])
                here = columns + b
                total = total + nn(mixed, error[0, :, here : here + TILE])
                total = total + nn(mixed, error[1, :, here : here + TILE])
                right = join_three(total)
                for half in range(0, TILE, 128):
                    rights[at + (here + half) // 128] = right[:, half : half + 128]
            columns += extent

    every = slice(0, rows_in)
    product(
        [(grads_ref, part, D) for part in gate_parts] + [(raw_ref, every, XBC)],
        rows_in, 0, split_in, 0,
    )
    product([(grads_ref, out_part, D)], rows_out, ahead, split_out, RIGHT_OUT)
    for g in range(HEADS // 8):
        for q in range(D // 128):
            rights[DELTA + g * (D // 128) + q] = gdelta_ref[
                g * 8 : g * 8 + 8, q * 128 : q * 128 + 128
            ]
    rights[REST:] = jnp.zeros((rights.shape[0] - REST, 8, 128), F32)
    rest = [ggain_ref[0:1, q * 128 : q * 128 + 128] for q in range(D // 128)]
    for k in range(CONV + 1):
        rest += [gconv_ref[k : k + 1, q * 128 : q * 128 + 128] for q in range(XBC // 128)]
    rest += [ggate_ref[q : q + 1, :] for q in range(INNER // 128)]
    rest += [gheads_ref[0:1, :], gheads_ref[1:2, :], gskip_ref[0:1, :]]
    for i in range(0, REST_ROWS, 8):
        eight = rest[i : i + 8]
        rights[REST + i // 8, : len(eight), :] = jnp.concatenate(eight, axis=0)
    exchange.sum(rights, sum_ref, own_b, group_b, reps_b, send_b, recv_b)
    scatter.end(raw_total_ref)


def compress(starts, grads, raw, errors, smalls):
    group = grads.shape[0]
    replicas = lax.axis_size("rep")
    raw = raw.reshape(group, D // group, XBC)
    rows_in, rows_out = errors[0].shape[0], errors[1].shape[0]
    width = tiles_of(rows_in) + tiles_of(rows_out)
    block = (rows_in, XBC)
    share = -(-SUMMED // group)
    dma = pltpu.SemaphoreType.DMA((2 * (group - 1) + replicas - 1,))
    tiles = lambda *n: pltpu.VMEM(n + (8, 128), F32)
    vmem = pl.BlockSpec(memory_space=pltpu.VMEM)
    arrays = [*starts, grads, raw, *errors, *smalls]
    return pl.pallas_call(
        partial(compress_kernel, group, replicas),
        out_shape=[
            jax.ShapeDtypeStruct((group * share, 8, 128), F32),
            jax.ShapeDtypeStruct((rows_in, 8), F32),
            jax.ShapeDtypeStruct((rows_out, 8), F32),
            jax.ShapeDtypeStruct((8, rows_in), F32),
            jax.ShapeDtypeStruct((8, rows_out), F32),
            jax.ShapeDtypeStruct((rows_in, XBC), F32),
        ],
        in_specs=[vmem] * 2 + [pl.BlockSpec(memory_space=pl.ANY)] * 4 + [vmem] * len(smalls),
        out_specs=[vmem] * 6,
        scratch_shapes=[
            tiles(group * width), tiles(group * width), tiles(group * width),
            tiles(group * share),
            tiles(width), tiles(group - 1, width), tiles(replicas, width),
            tiles(share), tiles(group - 1, share), tiles(replicas, share),
            dma, dma, dma, dma,
            pltpu.VMEM((group // 2,) + block, BF16),
            pltpu.VMEM((group // 2,) + block, BF16),
            pltpu.VMEM((group // 2 - 1,) + block, BF16),
            pltpu.VMEM((2, rows_in // 2, XBC), BF16),
            pltpu.SemaphoreType.DMA((group + 2,)),
            pltpu.SemaphoreType.DMA((group + 2,)),
            pltpu.VMEM(raw.shape, BF16),
            pltpu.VMEM(grads.shape, BF16),
            pltpu.VMEM(errors[0].shape, F32),
            pltpu.VMEM(errors[1].shape, F32),
            pltpu.VMEM((2,) + errors[0].shape, BF16),
            pltpu.VMEM((2,) + errors[1].shape, BF16),
            pltpu.SemaphoreType.DMA((4,)),
        ],
        compiler_params=pltpu.CompilerParams(
            collective_id=2, has_side_effects=True, vmem_limit_bytes=VMEM_LIMIT
        ),
        name="compress",
    )(*arrays)


def finish_kernel(
    rates, replicas, rights_ref, tin_ref, tout_ref, lin_ref, lout_ref,
    win_ref, min_ref, ein_ref, raw_ref, wout_ref, mout_ref, eout_ref, out_ref, low_ref, high_ref,
    nwin_ref, nmin_ref, nein_ref, nwout_ref, nmout_ref, neout_ref,
    rin_ref, rout_ref, ntin_ref, ntout_ref,
):
    @pl.when(pl.program_id(0) == 0)
    def _():
        for ref, at, extent in ((rin_ref, 0, PROJ), (rout_ref, RIGHT_OUT, D)):
            for q in range(extent // 128):
                ref[:, q * 128 : q * 128 + 128] = rights_ref[at + q] * (1.0 / replicas)
        ntin_ref[...] = tin_ref[...]
        ntout_ref[...] = tout_ref[...]

    def update(w, m, e, nw, nm, ne, left_ref, grads, at, rate):
        rows = w.shape[0]
        left = [jnp.broadcast_to(left_ref[:, k : k + 1], (rows, 128)) for k in range(8)]
        begin = 0
        for grad in grads:
            for b in range(0, grad.shape[1], 128):
                cols = slice(begin + b, begin + b + 128)
                right = rights_ref[at + (begin + b) // 128] * (1.0 / replicas)
                approx = left[0] * right[0:1]
                for k in range(1, 8):
                    approx = approx + left[k] * right[k : k + 1]
                momentum = MOMENTUM * m[:, cols] + approx
                nm[:, cols] = momentum
                nw[:, cols] = w[:, cols] - rate * momentum
                ne[:, cols] = (grad[:, b : b + 128].astype(F32) + e[:, cols]) - approx
            begin += grad.shape[1]

    update(
        win_ref, min_ref, ein_ref, nwin_ref, nmin_ref, nein_ref, lin_ref, (low_ref, high_ref, raw_ref), 0,
        rates[0],
    )
    update(
        wout_ref, mout_ref, eout_ref, nwout_ref, nmout_ref, neout_ref, lout_ref, (out_ref,),
        RIGHT_OUT, rates[1],
    )


def finish(rates, replicas, rights, turned_in, turned_out, left_in, left_out, wide, narrow, grads):
    rows_in, rows_out = left_in.shape[0], left_out.shape[0]
    steps = 3 if rows_in % 48 == 0 else 1
    block = lambda a: pl.BlockSpec((a.shape[0] // steps, a.shape[1]), lambda i: (i, 0))
    like = lambda a: jax.ShapeDtypeStruct(a.shape, F32)
    step_in, step_out = rows_in // steps, rows_out // steps
    parts = [pl.BlockSpec((step_out, D), lambda i: (i, 0))] + [
        pl.BlockSpec((step_in, D), lambda i, k=k: ((rows_out + k * rows_in) // step_in + i, 0))
        for k in range(2)
    ]
    arrays = [*wide, *narrow]
    outs = [*wide[:3], *narrow[:3]]
    extra = [(8, PROJ), (8, D), turned_in.shape, turned_out.shape]
    return pl.pallas_call(
        partial(finish_kernel, rates, replicas),
        grid=(steps,),
        in_specs=[
            whole(rights.shape), whole(turned_in.shape), whole(turned_out.shape),
            block(left_in), block(left_out), *map(block, arrays), *parts,
        ],
        out_specs=[*map(block, outs), *map(whole, extra)],
        out_shape=[*map(like, outs), *(jax.ShapeDtypeStruct(e, F32) for e in extra)],
        compiler_params=params(("arbitrary",)),
        name="finish",
    )(rights, turned_in, turned_out, left_in, left_out, *arrays, grads, grads, grads)


def step_rates(tokens_replica):
    grad_scale = 0.3 * math.sqrt(tokens_replica)
    return (
        0.5 / (math.sqrt(D) * grad_scale),
        0.5 / (math.sqrt(INNER) * grad_scale),
        0.1 / grad_scale,
    )


def to_later(block):
    return lax.ppermute(block, "seq", [(i, i + 1) for i in range(lax.axis_size("seq") - 1)])


def to_earlier(block):
    return lax.ppermute(block, "seq", [(i + 1, i) for i in range(lax.axis_size("seq") - 1)])


def gather_rows(shard):
    return lax.all_gather(shard, ("fsdp", "seq"), axis=0, tiled=True)


def scatter_rows(total):
    return lax.psum_scatter(total, ("fsdp", "seq"), scatter_dimension=0, tiled=True)


def body(
    tokens,
    cotangent,
    segments,
    input_weight,
    output_weight,
    small_values,
    input_momentum,
    output_momentum,
    small_momentum,
    input_error,
    output_error,
    input_start,
    output_start,
):
    shape = tokens.shape
    pieces = shape[0] * shape[1]
    length = shape[2]
    replicas = lax.axis_size("rep")
    tokens_replica = pieces * length * lax.axis_size("fsdp") * lax.axis_size("seq")
    rate_in, rate_out, rate_small = step_rates(tokens_replica)

    tokens = tokens.reshape(pieces, length, D)
    cotangent = cotangent.reshape(pieces, length, D)
    small_rows = jnp.pad(small_values, (0, -small_values.shape[0] % 1024)).reshape(-1, 128)
    group = lax.axis_size("fsdp") * lax.axis_size("seq")
    weights = jnp.concatenate(
        [output_weight, input_weight[:, :D], input_weight[:, D:INNER]], axis=0
    ).astype(BF16)
    weights = gather_rows(weights).reshape(group, 4, -1, D)
    delta_rows = small_values[D:AT_CONV].reshape(D, HEADS).astype(BF16).T
    delta_rows = jnp.pad(delta_rows, ((0, HP - HEADS), (0, 0)))
    raw_full, halo, norm_gain, conv, gate_gain, heads, docs = gather_raw(
        input_weight, tokens, small_rows, segments.reshape(pieces, 1, segments.shape[2])
    )
    normed, turned, raw, dsilu, values, wr, draw, delta, send = enter(
        tokens, halo, norm_gain, raw_full, delta_rows, conv, heads, docs
    )
    y, starts = forward_scan(values, wr, delta, heads, docs, to_later(send))
    output, gy, gnorm, first, gstate, grads, ggate, gskip = leave(
        weights, normed, turned, cotangent, tokens, y, values, wr, gate_gain, delta, heads, docs
    )
    total = scatter_rows(grads.reshape(-1, D))
    gval, gwr, gdraw, gheads, ghalo = backward_scan(
        values, wr, delta, draw, heads, docs, gy, first, starts, to_earlier(gstate), send, dsilu,
        conv,
    )
    input_grad, grad_raw, gdelta, ggain, gconv = leave_back(
        gval, gwr, dsilu, raw, docs, conv, to_earlier(ghalo), normed, turned, raw_full, gdraw,
        delta_rows, gnorm, tokens, cotangent, norm_gain,
    )
    rights, left_in, left_out, turned_in, turned_out, raw_total = compress(
        (input_start.T, output_start.T),
        grads,
        grad_raw,
        (input_error[0], output_error[0]),
        (gdelta, ggain, gconv, ggate, gheads, gskip),
    )
    (
        new_input_weight, new_input_momentum, new_input_error,
        new_output_weight, new_output_momentum, new_output_error,
        input_right, output_right, input_left, output_left,
    ) = finish(
        (rate_in, rate_out), replicas, rights, turned_in, turned_out, left_in, left_out,
        (input_weight, input_momentum, input_error[0], raw_total),
        (output_weight, output_momentum, output_error[0]),
        total,
    )
    rest = rights[REST:SUMMED].reshape(-1, 128)[:REST_ROWS]
    turned_delta = rights[DELTA:REST].reshape(HEADS // 8, D // 128, 8, 128)
    small_sum = jnp.concatenate(
        [
            rest[: D // 128].reshape(-1),
            turned_delta.transpose(1, 3, 0, 2).reshape(-1),
            rest[D // 128 : -3].reshape(-1),
            rest[-3:, :HEADS].reshape(-1),
        ]
    )
    new_small_momentum = MOMENTUM * small_momentum + small_sum / replicas
    new_small_values = small_values - rate_small * new_small_momentum
    return (
        output.reshape(shape),
        input_grad.reshape(shape),
        new_input_weight,
        new_output_weight,
        new_input_momentum,
        new_output_momentum,
        new_small_values,
        new_small_momentum,
        input_left.T,
        input_right.T,
        output_left.T,
        output_right.T,
        new_input_error[None],
        new_output_error[None],
    )


def solution(mesh):
    return jax.shard_map(
        body,
        mesh=mesh,
        in_specs=(
            P(None, ("rep", "fsdp"), "seq", None),
            P(None, ("rep", "fsdp"), "seq", None),
            P(None, ("rep", "fsdp"), None),
            P(("fsdp", "seq"), None),
            P(("fsdp", "seq"), None),
            P(),
            P(("fsdp", "seq"), None),
            P(("fsdp", "seq"), None),
            P(),
            P("rep", ("fsdp", "seq"), None),
            P("rep", ("fsdp", "seq"), None),
            P(),
            P(),
        ),
        out_specs=(
            P(None, ("rep", "fsdp"), "seq", None),
            P(None, ("rep", "fsdp"), "seq", None),
            P(("fsdp", "seq"), None),
            P(("fsdp", "seq"), None),
            P(("fsdp", "seq"), None),
            P(("fsdp", "seq"), None),
            P(),
            P(),
            P(("fsdp", "seq"), None),
            P(),
            P(("fsdp", "seq"), None),
            P(),
            P("rep", ("fsdp", "seq"), None),
            P("rep", ("fsdp", "seq"), None),
        ),
        check_vma=False,
    )
```

```python
from functools import partial
import math

import jax
import jax.numpy as jnp
from jax import lax
from jax.experimental import pallas as pl
from jax.experimental.pallas import tpu as pltpu
from jax.sharding import PartitionSpec as P

D = 768
INNER = 1536
HEADS = 24
HEADDIM = 64
STATE = 128
CONV = 4
PROJ = 3328
XBC = 1792

EPS = 1e-05
MOMENTUM = 0.9
HIGH = lax.Precision.HIGHEST
F32 = jnp.float32
BF16 = jnp.bfloat16
HP = 32
CH = 128
HALO = 16
TILE = 256
SUB = 16
ROWS = 256
SPAN = 128 + HALO
NEG = -1e30
VMEM_LIMIT = 63 * 2**20
MESH = pl.DeviceIdType.MESH

BEFORE = 3
LEAD = 128
BIAS, RATE, SKIP = 0, 1, 2
AT_CONV = D + D * HEADS
AT_GATE = AT_CONV + (CONV + 1) * XBC
AT_HEADS = AT_GATE + INNER


def nn(a, b):
    return lax.dot_general(a, b, (((1,), (0,)), ((), ())), preferred_element_type=F32)


def nt(a, b):
    return lax.dot_general(a, b, (((1,), (1,)), ((), ())), preferred_element_type=F32)


def tn(a, b):
    return lax.dot_general(a, b, (((0,), (0,)), ((), ())), preferred_element_type=F32)


def nn_high(a, b):
    return lax.dot_general(
        a, b, (((1,), (0,)), ((), ())), precision=HIGH, preferred_element_type=F32
    )


def nt_high(a, b):
    return lax.dot_general(
        a, b, (((1,), (1,)), ((), ())), precision=HIGH, preferred_element_type=F32
    )


def tn_high(a, b):
    return lax.dot_general(
        a, b, (((0,), (0,)), ((), ())), precision=HIGH, preferred_element_type=F32
    )


def softplus(v):
    return jnp.maximum(v, 0.0) + jnp.log1p(jnp.exp(-jnp.abs(v)))


def sigmoid(v):
    return 0.5 + 0.5 * jnp.tanh(0.5 * v)


def triangle(extent):
    return jnp.where(
        lax.broadcasted_iota(jnp.int32, (extent, extent), 0)
        <= lax.broadcasted_iota(jnp.int32, (extent, extent), 1),
        1.0,
        0.0,
    )


def column(heads_ref, row):
    return heads_ref[...].T[:HP, row : row + 1]


def square_of(row):
    return jnp.broadcast_to(row, (128, 128)).T


def params(semantics, **more):
    return pltpu.CompilerParams(
        dimension_semantics=semantics, vmem_limit_bytes=VMEM_LIMIT, **more
    )


def piece(*shape):
    return pl.BlockSpec((1,) + shape, lambda i: (i,) + (0,) * len(shape))


def whole(shape, ranks=1):
    index = (lambda i: (0,) * len(shape)) if ranks == 1 else (lambda i, k: (0,) * len(shape))
    return pl.BlockSpec(shape, index, pipeline_mode=pl.Buffered(1))


def unpack_small(rows_ref, gain_ref, conv_ref, gate_ref, heads_ref):
    for q in range(D // 128):
        gain_ref[:, q * 128 : q * 128 + 128] = rows_ref[q : q + 1, :]
    at = AT_CONV // 128
    for k in range(CONV + 1):
        for q in range(XBC // 128):
            conv_ref[k : k + 1, q * 128 : q * 128 + 128] = rows_ref[at : at + 1, :]
            at += 1
    gate_ref[...] = rows_ref[at : at + INNER // 128, :]
    row = jnp.broadcast_to(rows_ref[at + INNER // 128 : at + INNER // 128 + 1, :], (8, 128))
    place = lax.broadcasted_iota(jnp.int32, (8, 128), 0)
    heads = jnp.zeros((8, 128), F32)
    for k in range(3):
        moved = row if k == 0 else pltpu.roll(row, 128 - k * HEADS, 1)
        heads = jnp.where(place == k, moved, heads)
    lane = lax.broadcasted_iota(jnp.int32, (8, 128), 1)
    heads_ref[...] = jnp.where(lane < HEADS, heads, 0.0)


def unpack_documents(seg_ref, docs_ref, later):
    n, _, extent = docs_ref.shape
    length = extent - LEAD
    place = lax.broadcasted_iota(jnp.int32, (8, extent), 0)
    for i in range(n):
        ids = jnp.broadcast_to(seg_ref[i].astype(F32), (8, seg_ref.shape[2]))
        ahead, behind = jnp.full((8, LEAD), -1.0, F32), jnp.full((8, LEAD), -3.0, F32)
        ids = jnp.concatenate([ahead, ids, behind], axis=1)
        total = ids.shape[1]
        docs = jnp.zeros((8, extent), F32)
        for row, offset in enumerate((0, 1, 2, 3, -1, -2, -3)):
            moved = ids if offset == 0 else pltpu.roll(ids, (-offset) % total, 1)
            here = jnp.where(later, moved[:, length : length + extent], moved[:, :extent])
            docs = jnp.where(place == row, here, docs)
        docs_ref[i] = docs


def gather_kernel(
    nf, w_ref, tok_ref, small_ref, seg_ref,
    o_ref, halo_ref, gain_ref, conv_ref, gate_ref, heads_ref, docs_ref,
    mine, near, local, send, recv,
):
    r, f, s = lax.axis_index("rep"), lax.axis_index("fsdp"), lax.axis_index("seq")
    other = (r, f, 1 - s)
    if nf == 4:
        fx, fy = f + 1 - 2 * lax.rem(f, 2), lax.rem(f + 2, 4)
        fd = lax.rem(fx + 2, 4)
        far = [(r, fx, s), (r, fy, s)]
    else:
        far = [(r, lax.rem(f + j, nf), s) for j in range(1, nf)]
    barrier = pltpu.get_barrier_semaphore()
    for device in far + [other]:
        pl.semaphore_signal(barrier, inc=1, device_id=device, device_id_type=MESH)
    mine[...] = w_ref[:, INNER:].astype(BF16)
    near[...] = tok_ref[:, tok_ref.shape[1] - HALO :, :]
    pl.semaphore_wait(barrier, len(far) + 1)
    copies = []

    def start(src, dst, device):
        k = len(copies)
        copy = pltpu.make_async_remote_copy(
            src, dst, send.at[k], recv.at[k], device_id=device, device_id_type=MESH
        )
        copy.start()
        copies.append(copy)
        return copy

    def block(owner):
        return o_ref.at[owner * 2 + s]

    own = pltpu.make_async_copy(mine, block(f), local)
    own.start()
    if nf == 4:
        x_dev, y_dev = far
        half = mine.shape[0] // 2
        low, high = pl.ds(0, half), pl.ds(half, half)
        from_x, from_y, from_d = block(fx), block(fy), block(fd)
        x_low = start(mine.at[low], block(f).at[low], x_dev)
        y_high = start(mine.at[high], block(f).at[high], y_dev)
        x_high = start(mine.at[high], block(f).at[high], x_dev)
        y_low = start(mine.at[low], block(f).at[low], y_dev)
        late = [start(mine, block(f), other), start(near, halo_ref, other)]
        unpack_small(small_ref, gain_ref, conv_ref, gate_ref, heads_ref)
        unpack_documents(seg_ref, docs_ref, s == 1)
        x_low.wait_recv()
        d_low = start(from_x.at[low], from_x.at[low], y_dev)
        y_high.wait_recv()
        d_high = start(from_y.at[high], from_y.at[high], x_dev)
        x_high.wait_recv()
        late.append(start(from_x, from_x, other))
        y_low.wait_recv()
        late.append(start(from_y, from_y, other))
        d_low.wait_recv()
        late.append(start(from_d.at[low], from_d.at[low], other))
        d_high.wait_recv()
        late.append(start(from_d.at[high], from_d.at[high], other))
    else:
        first = [start(mine, block(f), device) for device in far]
        late = [start(mine, block(f), other), start(near, halo_ref, other)]
        unpack_small(small_ref, gain_ref, conv_ref, gate_ref, heads_ref)
        unpack_documents(seg_ref, docs_ref, s == 1)
        for j, copy in enumerate(first):
            copy.wait_recv()
            source = block(lax.rem(f - 1 - j + nf, nf))
            late.append(start(source, source, other))
    for copy in late:
        copy.wait_recv()
    for copy in copies:
        copy.wait_send()
    own.wait()


def gather_raw(weight, tokens, small_rows, segments):
    nf = lax.axis_size("fsdp")
    rows = weight.shape[0]
    n, length, _ = tokens.shape
    vmem = pl.BlockSpec(memory_space=pltpu.VMEM)
    dma = pltpu.SemaphoreType.DMA
    count = 12 if nf == 4 else 2 * nf
    full, *rest = pl.pallas_call(
        partial(gather_kernel, nf),
        out_shape=[
            jax.ShapeDtypeStruct((2 * nf, rows, XBC), BF16),
            jax.ShapeDtypeStruct((n, HALO, D), BF16),
            jax.ShapeDtypeStruct((1, D), F32),
            jax.ShapeDtypeStruct((CONV + 1, XBC), F32),
            jax.ShapeDtypeStruct((INNER // 128, 128), F32),
            jax.ShapeDtypeStruct((8, 128), F32),
            jax.ShapeDtypeStruct((n, 8, LEAD + length), F32),
        ],
        in_specs=[vmem] * 4,
        out_specs=[pl.BlockSpec(memory_space=pl.ANY)] + [vmem] * 6,
        scratch_shapes=[
            pltpu.VMEM((rows, XBC), BF16),
            pltpu.VMEM((n, HALO, D), BF16),
            dma,
            dma((count,)),
            dma((count,)),
        ],
        compiler_params=pltpu.CompilerParams(
            collective_id=1, has_side_effects=True, vmem_limit_bytes=VMEM_LIMIT
        ),
        name="gather_raw",
    )(weight, tokens, small_rows, segments)
    return full.reshape(2 * nf * rows, XBC), *rest


def store_shift(shift, i, j, values):
    shift[i, (j - 1) * 128 : j * 128, :] = values


def shift_matrices(docs, store):
    own = docs[0:1, LEAD:]
    rows = lax.broadcasted_iota(jnp.int32, (128, SPAN), 0)
    cols = lax.broadcasted_iota(jnp.int32, (128, SPAN), 1)
    for j in range(1, CONV):
        same = jnp.where(docs[BEFORE + j : BEFORE + j + 1, LEAD:] == own, 1.0, 0.0)
        for i in range(own.shape[1] // 128):
            here = square_of(same[:, i * 128 : i * 128 + 128])
            here = jnp.concatenate([here, here[:, : SPAN - 128]], axis=1)
            store(i, j, jnp.where(cols == rows + (HALO - j), here, 0.0).astype(BF16))


def step_terms(normed, dlow, heads_ref, docs):
    length = normed.shape[0]
    own = docs[0:1, LEAD:]
    draw = nt(dlow, normed) + column(heads_ref, BIAS)
    delta = softplus(draw)
    totals = nn_high(-jnp.exp(column(heads_ref, RATE)) * delta, triangle(length))
    keep = jnp.where(own == own[:, length - 1 :], 1.0, 0.0)
    return draw, delta, jnp.exp(totals[:, length - 1 :] - totals) * keep * delta


def enter_kernel(
    tok_ref, halo_ref, gain_ref, wraw_ref, dlow_ref, conv_ref, heads_ref, docs_ref,
    normed_ref, turned_ref, raw_ref, dsilu_ref, val_ref, wr_ref, draw_ref, delta_ref, send_ref,
    ext, moved, act, shift,
):
    length = tok_ref.shape[1]
    gain = gain_ref[...]
    for start, rows, src in ((0, HALO, halo_ref), (HALO, length, tok_ref)):
        for b in range(0, rows, 128):
            n = min(128, rows - b)
            x = src[0, b : b + n, :].astype(F32)
            scale = lax.rsqrt(jnp.mean(x * x, axis=-1, keepdims=True) + EPS)
            ext[start + b : start + b + n, :] = (x * scale * gain).astype(BF16)
    normed = ext[HALO:, :]
    normed_ref[0] = normed
    turned_ref[0] = normed.T
    shift_matrices(docs_ref[0], lambda i, j, values: store_shift(shift, i, j, values))
    draw, delta, weight = step_terms(normed, dlow_ref[...], heads_ref, docs_ref[0])
    draw_ref[0] = draw
    delta_ref[0] = delta
    tiles = XBC // TILE
    blocks = length // 128

    def span_of(c):
        return slice(c * TILE, (c + 1) * TILE)

    def project(c):
        if c < tiles:
            raw_ref[0, c] = nn(ext[...], wraw_ref[c]).astype(BF16)

    def move(c):
        if c < tiles:
            for i in range(blocks):
                moved[c % 2 * blocks + i] = nn(
                    shift[i], raw_ref[0, c, i * 128 : i * 128 + SPAN, :]
                )

    project(0)
    project(1)
    move(0)
    for c in range(tiles):
        span = span_of(c)
        project(c + 2)
        move(c + 1)
        for b in range(0, length, 128):
            slot = c % 2 * blocks + b // 128
            for half in range(0, TILE, 128):
                hc = slice(c * TILE + half, c * TILE + half + 128)
                lanes = slice(half, half + 128)
                w = conv_ref[:, hc]
                for q in range(0, 128, 64):
                    z = w[4:5] + w[3:4] * raw_ref[0, c, HALO + b + q : HALO + b + q + 64, lanes].astype(F32)
                    for j in range(1, CONV):
                        at = (j - 1) * 128 + q
                        z = z + w[3 - j : 4 - j] * moved[slot, at : at + 64, lanes]
                    sig = sigmoid(z)
                    silu = z * sig
                    act[c % 2, b + q : b + q + 64, lanes] = silu
                    dsilu_ref[0, c, b + q : b + q + 64, lanes] = (sig + silu * (1.0 - sig)).astype(BF16)
        if c < INNER // TILE:
            val_ref[0, span, :] = act[c % 2].T.astype(BF16)
        else:
            wr_ref[0] = act[c % 2].astype(BF16)

    writers = wr_ref[0, :, :STATE]
    for h in range(HEADS):
        rows = slice(h * HEADDIM, (h + 1) * HEADDIM)
        scaled = val_ref[0, rows, :].astype(F32) * weight[h : h + 1, :]
        send_ref[0, rows, :] = nn(scaled.astype(BF16), writers).astype(BF16)


def enter(tokens, halo, gain, wraw, dlow, conv, heads, docs):
    n, length, _ = tokens.shape
    outs = [
        ((n, length, D), BF16),
        ((n, D, length), BF16),
        ((n, XBC // TILE, length + HALO, TILE), BF16),
        ((n, XBC // TILE, length, TILE), BF16),
        ((n, INNER, length), BF16),
        ((n, length, 2 * STATE), BF16),
        ((n, HP, length), F32),
        ((n, HP, length), F32),
        ((n, INNER, STATE), BF16),
    ]
    return pl.pallas_call(
        enter_kernel,
        grid=(n,),
        in_specs=[
            piece(length, D), piece(HALO, D), whole(gain.shape), whole(wraw.shape),
            whole(dlow.shape), whole(conv.shape), whole(heads.shape), piece(*docs.shape[1:]),
        ],
        out_specs=[piece(*s[1:]) for s, _ in outs],
        out_shape=[jax.ShapeDtypeStruct(s, t) for s, t in outs],
        scratch_shapes=[
            pltpu.VMEM((length + HALO, D), BF16),
            pltpu.VMEM((2 * (length // 128), (CONV - 1) * 128, TILE), F32),
            pltpu.VMEM((2, length, TILE), F32),
            pltpu.VMEM((length // 128, (CONV - 1) * 128, SPAN), BF16),
        ],
        compiler_params=params(("arbitrary",)),
        name="enter",
    )(tokens, halo, gain, wraw, dlow, conv, heads, docs)


class Copies:
    def __init__(self, *semaphores):
        self.semaphores, self.copies = semaphores, []

    def local(self, src, dst):
        copy = pltpu.make_async_copy(src, dst, self.semaphores[0].at[len(self.copies)])
        copy.start()
        self.copies.append(copy)
        return copy

    def remote(self, src, dst, device):
        k = len(self.copies)
        copy = pltpu.make_async_remote_copy(
            src, dst, self.semaphores[0].at[k], self.semaphores[1].at[k],
            device_id=device, device_id_type=MESH,
        )
        copy.start()
        self.copies.append(copy)
        return copy


def front_kernel(
    w_ref, tok_ref, small_ref, seg_ref, dlow_ref,
    wraw_ref, normed_ref, turned_ref, raw_ref, dsilu_ref, val_ref, wr_ref, draw_ref, delta_ref,
    send_ref, come_ref, conv_ref, gate_ref, heads_ref, docs_ref,
    mine, near, halo, wide, gain, ext, turned, raw, dsilu, val, moved, act, shift, weight,
    stored, send, recv,
):
    r, f, s = lax.axis_index("rep"), lax.axis_index("fsdp"), lax.axis_index("seq")
    fx, fy = f + 1 - 2 * lax.rem(f, 2), lax.rem(f + 2, 4)
    fd = lax.rem(fx + 2, 4)
    x_dev, y_dev, other = (r, fx, s), (r, fy, s), (r, f, 1 - s)
    pieces, length, _ = tok_ref.shape
    tiles, blocks = XBC // TILE, length // 128
    order = [tiles - 1, *range(tiles - 1)]
    barrier = pltpu.get_barrier_semaphore()
    for device in (x_dev, y_dev, other):
        pl.semaphore_signal(barrier, inc=1, device_id=device, device_id_type=MESH)
    for c in range(tiles):
        mine[c] = w_ref[:, INNER + c * TILE : INNER + (c + 1) * TILE].astype(BF16)
    near[...] = tok_ref[:, length - HALO :, :]
    pl.semaphore_wait(barrier, 3)
    outward, out = Copies(send, recv), Copies(stored)
    arriving = {}

    def block(c, owner):
        return wide.at[c, owner * 2 + s]

    def offer(at):
        if at < tiles:
            c = order[at]
            arriving[c] = [
                outward.remote(mine.at[c], block(c, f), device) for device in (x_dev, y_dev, other)
            ]
            wide[c, f * 2 + s] = mine[c]

    def relay(at):
        if at < tiles:
            c = order[at]
            from_x, from_y, _ = arriving[c]
            from_x.wait_recv()
            from_y.wait_recv()
            through = (fx, y_dev) if at % 2 == 0 else (fy, x_dev)
            across = block(c, through[0])
            arriving[c].append(outward.remote(across, across, through[1]))
            for owner in (fx, fy):
                arriving[c].append(outward.remote(block(c, owner), block(c, owner), other))

    def finish_tile(at):
        c = order[at]
        arriving[c][3].wait_recv()
        arriving[c].append(outward.remote(block(c, fd), block(c, fd), other))
        for k in (2, 4, 5, 6):
            arriving[c][k].wait_recv()
        out.local(wide.at[c], wraw_ref.at[c])

    bring_halo = outward.remote(near, halo, other)
    offer(0)
    offer(1)
    offer(2)
    unpack_small(small_ref, gain, conv_ref, gate_ref, heads_ref)
    unpack_documents(seg_ref, docs_ref, s == 1)
    bring_halo.wait_recv()
    for n in range(pieces):
        x = halo[n].astype(F32)
        scale = lax.rsqrt(jnp.mean(x * x, axis=-1, keepdims=True) + EPS)
        ext[n, :HALO, :] = (x * scale * gain[...]).astype(BF16)
    for n in range(pieces):
        if n == pieces - 1:
            relay(0)
        for b in range(0, length, 128):
            x = tok_ref[n, b : b + 128, :].astype(F32)
            scale = lax.rsqrt(jnp.mean(x * x, axis=-1, keepdims=True) + EPS)
            ext[n, HALO + b : HALO + b + 128, :] = (x * scale * gain[...]).astype(BF16)
        out.local(ext.at[n, pl.ds(HALO, length)], normed_ref.at[n])
        turned[n] = ext[n, HALO:, :].T
        out.local(turned.at[n], turned_ref.at[n])
        draw_ref[n], delta_ref[n], weight[n] = step_terms(
            ext[n, HALO:, :], dlow_ref[...], heads_ref, docs_ref[n]
        )
        shift_matrices(
            docs_ref[n], lambda i, j, values: store_shift(shift, n * blocks + i, j, values)
        )
    states = []
    for at, c in enumerate(order):
        relay(at + 1)
        offer(at + 3)
        finish_tile(at)
        columns = wide[c].reshape(D, TILE)
        for n in range(pieces):
            raw[n, c] = nn(ext[n], columns).astype(BF16)
            out.local(raw.at[n, c], raw_ref.at[n, c])
        for n in range(pieces):
            for i in range(blocks):
                moved[n * blocks + i] = nn(
                    shift[n * blocks + i], raw[n, c, i * 128 : i * 128 + SPAN, :]
                )
        for n in range(pieces):
            for b in range(0, length, 128):
                slot = n * blocks + b // 128
                for half in range(0, TILE, 128):
                    hc = slice(c * TILE + half, c * TILE + half + 128)
                    lanes = slice(half, half + 128)
                    w = conv_ref[:, hc]
                    for q in range(0, 128, 64):
                        here = raw[n, c, HALO + b + q : HALO + b + q + 64, lanes].astype(F32)
                        z = w[4:5] + w[3:4] * here
                        for j in range(1, CONV):
                            row = (j - 1) * 128 + q
                            z = z + w[3 - j : 4 - j] * moved[slot, row : row + 64, lanes]
                        sig = sigmoid(z)
                        silu = z * sig
                        act[n, b + q : b + q + 64, lanes] = silu
                        dsilu[n, c, b + q : b + q + 64, lanes] = (
                            sig + silu * (1.0 - sig)
                        ).astype(BF16)
            out.local(dsilu.at[n, c], dsilu_ref.at[n, c])
            if c == tiles - 1:
                wr_ref[n] = act[n].astype(BF16)
                continue
            rows = slice(c * TILE, (c + 1) * TILE)
            val[n, rows, :] = act[n].T.astype(BF16)
            out.local(val.at[n, rows], val_ref.at[n, rows])
            writers = wr_ref[n, :, :STATE]
            for h in range(c * 4, c * 4 + 4):
                head = slice(h * HEADDIM, (h + 1) * HEADDIM)
                scaled = val[n, head, :].astype(F32) * weight[n, h : h + 1, :]
                send_ref[n, head, :] = nn(scaled.astype(BF16), writers).astype(BF16)
            states.append(outward.remote(send_ref.at[n, rows], come_ref.at[n, rows], other))
    for copy in states:
        copy.wait_recv()
    for copy in outward.copies:
        copy.wait_send()
    for copy in out.copies:
        copy.wait()


def front(weight, tokens, small_rows, segments, dlow):
    rows = weight.shape[0]
    n, length, _ = tokens.shape
    tiles, blocks = XBC // TILE, length // 128
    vmem, hbm = pl.BlockSpec(memory_space=pltpu.VMEM), pl.BlockSpec(memory_space=pl.ANY)
    outs = [
        (hbm, (tiles, 8, rows, TILE), BF16),
        (hbm, (n, length, D), BF16),
        (hbm, (n, D, length), BF16),
        (hbm, (n, tiles, length + HALO, TILE), BF16),
        (hbm, (n, tiles, length, TILE), BF16),
        (hbm, (n, INNER, length), BF16),
        (vmem, (n, length, 2 * STATE), BF16),
        (vmem, (n, HP, length), F32),
        (vmem, (n, HP, length), F32),
        (vmem, (n, INNER, STATE), BF16),
        (vmem, (n, INNER, STATE), BF16),
        (vmem, (CONV + 1, XBC), F32),
        (vmem, (INNER // 128, 128), F32),
        (vmem, (8, 128), F32),
        (vmem, (n, 8, LEAD + length), F32),
    ]
    remote = 1 + 7 * tiles + n * (tiles - 1)
    local = tiles + 2 * n + 2 * n * tiles + n * (tiles - 1)
    return pl.pallas_call(
        front_kernel,
        in_specs=[vmem] * 5,
        out_specs=[spec for spec, _, _ in outs],
        out_shape=[jax.ShapeDtypeStruct(shape, kind) for _, shape, kind in outs],
        scratch_shapes=[
            pltpu.VMEM((tiles, rows, TILE), BF16),
            pltpu.VMEM((n, HALO, D), BF16),
            pltpu.VMEM((n, HALO, D), BF16),
            pltpu.VMEM((tiles, 8, rows, TILE), BF16),
            pltpu.VMEM((1, D), F32),
            pltpu.VMEM((n, length + HALO, D), BF16),
            pltpu.VMEM((n, D, length), BF16),
            pltpu.VMEM((n, tiles, length + HALO, TILE), BF16),
            pltpu.VMEM((n, tiles, length, TILE), BF16),
            pltpu.VMEM((n, INNER, length), BF16),
            pltpu.VMEM((n * blocks, (CONV - 1) * 128, TILE), F32),
            pltpu.VMEM((n, length, TILE), F32),
            pltpu.VMEM((n * blocks, (CONV - 1) * 128, SPAN), BF16),
            pltpu.VMEM((n, HP, length), F32),
            pltpu.SemaphoreType.DMA((local,)),
            pltpu.SemaphoreType.DMA((remote,)),
            pltpu.SemaphoreType.DMA((remote,)),
        ],
        compiler_params=pltpu.CompilerParams(
            collective_id=3, has_side_effects=True, vmem_limit_bytes=VMEM_LIMIT
        ),
        name="front",
    )(weight, tokens, small_rows, segments, dlow)


def chunk_terms(delta, rate, docs):
    own = docs[0:1, :]
    before = docs[BEFORE + 1 : BEFORE + 2, 0:1]
    last = docs[0:1, CH - 1 :]
    decay = -jnp.exp(rate) * delta
    totals = nn_high(decay, triangle(CH))
    end = totals[:, CH - 1 :]
    fade = jnp.exp(totals) * jnp.where(own == before, 1.0, 0.0)
    to_end = jnp.exp(end - totals) * jnp.where(own == last, 1.0, 0.0)
    passing = jnp.exp(end) * jnp.where(last == before, 1.0, 0.0)
    together = square_of(own) == own
    first = lax.broadcasted_iota(jnp.int32, (CH, CH), 0)
    second = lax.broadcasted_iota(jnp.int32, (CH, CH), 1)
    barred = jnp.where(together & (first <= second), 0.0, NEG)
    reach = jnp.where(together & (first >= second), 1.0, 0.0)
    return decay, totals, fade, to_end, passing, barred, reach


def forward_kernel(
    val_ref, w_ref, r_ref, delta_ref, heads_ref, docs_ref, in_ref,
    y_ref, start_ref,
    state, off, fresh,
):
    state[...] = jnp.where(lax.axis_index("seq") == 0, 0.0, in_ref[0].astype(F32))
    rate = column(heads_ref, RATE)
    for k in range(val_ref.shape[2] // CH):
        lanes = slice(k * CH, (k + 1) * CH)
        writers, readers = w_ref[0, lanes, :], r_ref[0, lanes, :]
        delta = delta_ref[0, :, lanes]
        _, totals, fade, to_end, passing, barred, _ = chunk_terms(
            delta, rate, docs_ref[0, :, LEAD + k * CH : LEAD + (k + 1) * CH]
        )
        columns = totals.T
        scores = nt(writers, readers)
        low_state = state[...].astype(BF16)
        start_ref[0, k] = low_state
        off[...] = nt(low_state, readers)
        for h in range(HEADS):
            rows = slice(h * HEADDIM, (h + 1) * HEADDIM)
            mixing = jnp.exp(totals[h : h + 1, :] - columns[:, h : h + 1] + barred) * scores
            scaled = val_ref[0, rows, lanes].astype(F32) * delta[h : h + 1, :]
            fresh[rows, :] = (scaled * to_end[h : h + 1, :]).astype(BF16)
            inside = nn(scaled.astype(BF16), mixing.astype(BF16))
            y_ref[0, rows, lanes] = inside + off[rows, :] * fade[h : h + 1, :]
        gained = nn(fresh[...], writers)
        for h in range(HEADS):
            rows = slice(h * HEADDIM, (h + 1) * HEADDIM)
            state[rows, :] = passing[h : h + 1, :] * state[rows, :] + gained[rows, :]


def forward_scan(values, wr, delta, heads, docs, incoming):
    n, _, length = values.shape
    chunks = length // CH
    return pl.pallas_call(
        forward_kernel,
        grid=(n,),
        in_specs=[
            piece(INNER, length),
            pl.BlockSpec((1, length, STATE), lambda i: (i, 0, 0)),
            pl.BlockSpec((1, length, STATE), lambda i: (i, 0, 1)),
            piece(HP, length),
            whole(heads.shape),
            piece(*docs.shape[1:]),
            piece(INNER, STATE),
        ],
        out_specs=[piece(INNER, length), piece(chunks, INNER, STATE)],
        scratch_shapes=[
            pltpu.VMEM((INNER, STATE), F32),
            pltpu.VMEM((INNER, CH), F32),
            pltpu.VMEM((INNER, CH), BF16),
        ],
        out_shape=[
            jax.ShapeDtypeStruct((n, INNER, length), F32),
            jax.ShapeDtypeStruct((n, chunks, INNER, STATE), BF16),
        ],
        compiler_params=params(("arbitrary",)),
        name="forward_scan",
    )(values, wr, wr, delta, heads, docs, incoming)


def backward_kernel(
    val_ref, w_ref, r_ref, delta_ref, draw_ref, heads_ref, docs_ref, gy_ref, first_ref,
    start_ref, in_ref, final_ref, dsilu_ref, conv_ref, near_ref,
    gval_ref, gwr_ref, gdraw_ref, gheads_ref, ghalo_ref,
    grad, link, off, fresh, faded, gdelta, paid, sums,
):
    n, step = pl.program_id(0), pl.program_id(1)
    rate = column(heads_ref, RATE)

    @pl.when(step == 0)
    def _():
        grad[...] = in_ref[0].astype(F32)
        product = in_ref[0].astype(F32) * final_ref[0].astype(F32)
        by_head = jnp.sum(product.reshape(HEADS, HEADDIM, STATE), axis=1)
        link[0:HEADS, :] = jnp.sum(by_head, axis=1, keepdims=True)
        link[HEADS:, :] = jnp.zeros((HP - HEADS, 1), F32)

    @pl.when((n == 0) & (step == 0))
    def _():
        sums[...] = jnp.zeros_like(sums)

    writers, readers = w_ref[0], r_ref[0]
    delta = delta_ref[0]
    decay, totals, fade, to_end, passing, barred, reach = chunk_terms(delta, rate, docs_ref[0])
    columns = totals.T
    scores = nt(writers, readers)
    low_grad = grad[...].astype(BF16)
    off[...] = nt(low_grad, writers)
    gscores = jnp.zeros((CH, CH), F32)
    gdelta[HEADS:, :] = jnp.zeros((HP - HEADS, CH), F32)
    paid[HEADS:, :] = jnp.zeros((HP - HEADS, CH), F32)
    for h in range(HEADS):
        rows = slice(h * HEADDIM, (h + 1) * HEADDIM)
        spread = jnp.exp(totals[h : h + 1, :] - columns[:, h : h + 1] + barred)
        values = val_ref[0, rows, :].astype(F32)
        gy = gy_ref[0, rows, :]
        gy32 = gy.astype(F32)
        scaled = values * delta[h : h + 1, :]
        fresh[rows, :] = (scaled * to_end[h : h + 1, :]).astype(BF16)
        faded[rows, :] = (gy32 * fade[h : h + 1, :]).astype(BF16)
        gscaled = nt(gy, (spread * scores).astype(BF16)) + off[rows, :] * to_end[h : h + 1, :]
        low = scaled.astype(BF16)
        gscores = gscores + tn(low, gy) * spread
        paid[h : h + 1, :] = jnp.sum(low.astype(F32) * gscaled, axis=0, keepdims=True)
        gdelta[h : h + 1, :] = jnp.sum(values * gscaled, axis=0, keepdims=True)
        gval_ref[0, rows, :] = (
            gscaled * delta[h : h + 1, :] + gy32 * heads_ref[SKIP : SKIP + 1, h : h + 1]
        ).astype(BF16)
    low_scores = gscores.astype(BF16)
    gwr_ref[0, :, :STATE] = nn(low_scores, readers) + tn(fresh[...], low_grad)
    gwr_ref[0, :, STATE:] = tn(low_scores, writers) + tn(faded[...], start_ref[0, 0])
    off[:, :STATE] = nn(faded[...], readers)
    for h in range(HEADS):
        rows = slice(h * HEADDIM, (h + 1) * HEADDIM)
        grad[rows, :] = passing[h : h + 1, :] * grad[rows, :] + off[rows, :STATE]
    following = jnp.where(docs_ref[0, 0:1, :] == docs_ref[0, 1:2, CH - 1 :], 1.0, 0.0)
    gdecay = nn_high(first_ref[0] - paid[...], reach) + following * link[...]
    link[...] = gdecay[:, :1]
    gtotal = gdelta[...] - jnp.exp(rate) * gdecay
    gdraw = gtotal * sigmoid(draw_ref[0])
    gdraw_ref[0] = gdraw
    sums[0] += gdraw
    sums[1] += gdecay * decay

    @pl.when(step == pl.num_programs(1) - 1)
    def _():
        taps = conv_ref[...]
        near = [
            square_of(
                jnp.where(near_ref[0, j : j + 1, :] == near_ref[0, 0:1, :], 1.0, 0.0)
            )[120:, :]
            for j in range(CONV)
        ]
        for c in range(XBC // 128):
            cols = slice(c * 128, (c + 1) * 128)
            if c < INNER // 128:
                here = gval_ref[0, cols, :].astype(F32).T[:8, :]
            else:
                here = gwr_ref[0, 0:8, c * 128 - INNER : c * 128 - INNER + 128]
            left = c * 128 % TILE
            pre = here * dsilu_ref[0, c * 128 // TILE, 0:8, left : left + 128].astype(F32)
            wide = jnp.concatenate([jnp.zeros((8, 128), F32), pre], axis=0)
            total = jnp.zeros((8, 128), F32)
            for j in range(1, CONV):
                total = total + taps[3 - j : 4 - j, cols] * wide[j : j + 8] * near[j]
            ghalo_ref[0, :, cols] = total

    @pl.when((n == pl.num_programs(0) - 1) & (step == pl.num_programs(1) - 1))
    def _():
        for i in range(2):
            both = jnp.concatenate([sums[i], jnp.zeros((128 - HP, CH), F32)], axis=0)
            gheads_ref[i : i + 1, :] = jnp.sum(both.T, axis=0, keepdims=True)
        gheads_ref[2:, :] = jnp.zeros((6, 128), F32)


def backward_scan(
    values, wr, delta, draw, heads, docs, gy, first, starts, incoming, final, dsilu, conv
):
    n, _, length = values.shape
    chunks = length // CH
    back = lambda k: chunks - 1 - k
    lanes = lambda rows: pl.BlockSpec((1, rows, CH), lambda i, k: (i, 0, back(k)))
    return pl.pallas_call(
        backward_kernel,
        grid=(n, chunks),
        in_specs=[
            lanes(INNER),
            pl.BlockSpec((1, CH, STATE), lambda i, k: (i, back(k), 0)),
            pl.BlockSpec((1, CH, STATE), lambda i, k: (i, back(k), 1)),
            lanes(HP),
            lanes(HP),
            whole(heads.shape, 2),
            pl.BlockSpec((1, 8, CH), lambda i, k: (i, 0, back(k) + LEAD // CH)),
            lanes(INNER),
            lanes(HP),
            pl.BlockSpec((1, 1, INNER, STATE), lambda i, k: (i, back(k), 0, 0)),
            pl.BlockSpec((1, INNER, STATE), lambda i, k: (i, 0, 0)),
            pl.BlockSpec((1, INNER, STATE), lambda i, k: (i, 0, 0)),
            pl.BlockSpec((1, XBC // TILE, 16, TILE), lambda i, k: (i, 0, 0, 0)),
            whole(conv.shape, 2),
            pl.BlockSpec((1, 8, 128), lambda i, k: (i, 0, 0)),
        ],
        out_specs=[
            lanes(INNER),
            pl.BlockSpec((1, CH, 2 * STATE), lambda i, k: (i, back(k), 0)),
            lanes(HP),
            pl.BlockSpec((8, 128), lambda i, k: (0, 0)),
            pl.BlockSpec((1, 8, XBC), lambda i, k: (i, 0, 0)),
        ],
        scratch_shapes=[
            pltpu.VMEM((INNER, STATE), F32),
            pltpu.VMEM((HP, 1), F32),
            pltpu.VMEM((INNER, CH), F32),
            pltpu.VMEM((INNER, CH), BF16),
            pltpu.VMEM((INNER, CH), BF16),
            pltpu.VMEM((HP, CH), F32),
            pltpu.VMEM((HP, CH), F32),
            pltpu.VMEM((2, HP, CH), F32),
        ],
        out_shape=[
            jax.ShapeDtypeStruct((n, INNER, length), BF16),
            jax.ShapeDtypeStruct((n, length, 2 * STATE), F32),
            jax.ShapeDtypeStruct((n, HP, length), F32),
            jax.ShapeDtypeStruct((8, 128), F32),
            jax.ShapeDtypeStruct((n, 8, XBC), F32),
        ],
        compiler_params=params(("arbitrary", "arbitrary")),
        name="backward_scan",
    )(
        values, wr, wr, delta, draw, heads, docs, gy, first, starts, incoming, final, dsilu,
        conv, docs,
    )


def leave_kernel(group, packed, *refs):
    if packed:
        weights_ref, *refs = refs
        *refs, wgate_ref, wout_ref, loaded = refs
    else:
        wgate_ref, wout_ref, *refs = refs
    (
        normed_ref, turned_ref, cot_ref, tok_ref, y_ref, val_ref, r_ref, gain_ref, delta_ref,
        heads_ref, docs_ref,
        out_ref, gy_ref, gnorm_ref, first_ref, gstate_ref, grads_ref, ggain_ref, gskip_ref,
        gate, gated, upward, lifted, faded, flat, total_out, total_gate, products, skips, gains,
        wide_gain, fade, total_state,
    ) = refs
    n, k = pl.program_id(0), pl.program_id(1)
    begin = (n == 0) & (k == 0)
    end = (n == pl.num_programs(0) - 1) & (k == pl.num_programs(1) - 1)
    length = delta_ref.shape[2]
    rows_out, rows_in = INNER // group, D // group
    tiles = INNER // TILE
    lanes = range(0, ROWS, 128)
    down = lambda s: jnp.sum(s, axis=0, keepdims=True)

    def fold(v):
        return jnp.sum(v.reshape(v.shape[0] // 8, 8, 128), axis=0)

    def loads():
        copies = []
        for p in range(group):
            for q, ref, at, left in (
                (2, wgate_ref, p * rows_in, 0), (3, wgate_ref, p * rows_in, D),
                (0, wout_ref, p * rows_out, 0), (1, wout_ref, p * rows_out + rows_in, 0),
            ):
                copies.append(
                    pltpu.make_async_copy(
                        weights_ref.at[p, q],
                        ref.at[pl.ds(at, rows_in), pl.ds(left, D)],
                        loaded.at[len(copies)],
                    )
                )
        return copies

    @pl.when(begin)
    def _():
        if packed:
            for copy in loads():
                copy.start()
        total_out[...] = jnp.zeros_like(total_out)
        total_gate[...] = jnp.zeros_like(total_gate)
        skips[...] = jnp.zeros_like(skips)
        gains[...] = jnp.zeros_like(gains)
        for q in range(INNER // 128):
            wide_gain[q * 128 : (q + 1) * 128, :] = square_of(gain_ref[q : q + 1, :])

    @pl.when(k == 0)
    def _():
        own = docs_ref[0, 0:1, LEAD:]
        before = docs_ref[0, BEFORE + 1 : BEFORE + 2, LEAD : LEAD + 1]
        totals = nn_high(-jnp.exp(column(heads_ref, RATE)) * delta_ref[0], triangle(length))
        fade[...] = jnp.exp(totals) * jnp.where(own == before, 1.0, 0.0)
        total_state[...] = jnp.zeros_like(total_state)

    if packed:

        @pl.when(begin)
        def _():
            for copy in loads():
                copy.wait()

    here = pl.ds(pl.multiple_of(k * ROWS, ROWS), ROWS)

    def span(c):
        return slice(c * TILE, (c + 1) * TILE)

    def head_rows(h):
        return slice(h * HEADDIM, (h + 1) * HEADDIM)

    def open_tile(c):
        if c < tiles:
            gate[span(c), :] = nn(normed_ref[0], wgate_ref[:, span(c)]).T.astype(BF16)
            upward[span(c), :] = nt(wout_ref[span(c), :], cot_ref[0])

    squares = [jnp.zeros((8, 128), F32) for _ in lanes]
    dots = [jnp.zeros((8, 128), F32) for _ in lanes]
    open_tile(0)
    for c in range(tiles):
        open_tile(c + 1)
        for h in range(c * 4, c * 4 + 4):
            rows = head_rows(h)
            skip = heads_ref[SKIP : SKIP + 1, h : h + 1]
            gain = wide_gain[rows, :]
            for i, b in enumerate(lanes):
                g = gate[rows, b : b + 128].astype(F32)
                values = val_ref[0, rows, b : b + 128].astype(F32)
                v = (y_ref[0, rows, b : b + 128] + skip * values) * (g * sigmoid(g))
                gated[rows, b : b + 128] = v
                squares[i] = squares[i] + fold(v * v)
                dots[i] = dots[i] + fold(upward[rows, b : b + 128] * gain * v)
    scale = [lax.rsqrt(down(s) * (1.0 / INNER) + EPS) for s in squares]
    pull = [s * s * s * down(d) * (1.0 / INNER) for s, d in zip(scale, dots)]

    def close_tile(c):
        low = lifted[span(c), :]
        flat[:, span(c)] = low.T
        total_out[span(c), :] += nn(low, cot_ref[0])
        total_gate[:, span(c)] += nt(turned_ref[0], gate[span(c), :])
        total_state[span(c), :] += nn(faded[c % 2], r_ref[0])

    for c in range(tiles):
        if c > 0:
            close_tile(c - 1)
        for h in range(c * 4, c * 4 + 4):
            eight = slice(h * 8, h * 8 + 8)
            skip = heads_ref[SKIP : SKIP + 1, h : h + 1]
            fading = fade[h : h + 1, here]
            sums = jnp.zeros((8, 128), F32)
            product = [jnp.zeros((8, 128), F32) for _ in lanes]
            for at in range(h * HEADDIM, (h + 1) * HEADDIM, SUB):
                rows = slice(at, at + SUB)
                inner = slice(at - c * TILE, at - c * TILE + SUB)
                gain = wide_gain[rows, :]
                gain_sums = gains[rows, :]
                for i, b in enumerate(lanes):
                    v = gated[rows, b : b + 128]
                    u = upward[rows, b : b + 128]
                    normal = v * scale[i]
                    lifted[rows, b : b + 128] = (normal * gain).astype(BF16)
                    gain_sums = gain_sums + u * normal
                    gv = scale[i] * (u * gain) - pull[i] * v
                    g = gate[rows, b : b + 128].astype(F32)
                    sig = sigmoid(g)
                    silu = g * sig
                    low = (gv * silu).astype(BF16)
                    gy_ref[0, rows, b : b + 128] = low
                    gm = low.astype(F32)
                    faded[c % 2, inner, b : b + 128] = (gm * fading[:, b : b + 128]).astype(BF16)
                    values = val_ref[0, rows, b : b + 128].astype(F32)
                    sums = sums + fold(gm * values)
                    y = y_ref[0, rows, b : b + 128]
                    product[i] = product[i] + fold(gm * y)
                    gate[rows, b : b + 128] = (
                        gv * (y + skip * values) * (sig + silu * (1.0 - sig))
                    ).astype(BF16)
                gains[rows, :] = gain_sums
            for i, b in enumerate(lanes):
                products[eight, b : b + 128] = product[i]
            skips[eight, :] += sums
    close_tile(tiles - 1)
    for b in range(0, D, TILE):
        branch = nn(flat[...], wout_ref[:, b : b + TILE])
        out_ref[0, :, b : b + TILE] = (tok_ref[0, :, b : b + TILE].astype(F32) + branch).astype(BF16)
    for b in range(0, D, TILE):
        gnorm_ref[0, b : b + TILE, :] = nn(wgate_ref[b : b + TILE, :], gate[...]).astype(BF16)
    first_ref[0, 0:HEADS, :] = jnp.sum(products[...].reshape(HEADS, 8, ROWS), axis=1)
    first_ref[0, HEADS:, :] = jnp.zeros((HP - HEADS, ROWS), F32)

    @pl.when(k == pl.num_programs(1) - 1)
    def _():
        gstate_ref[0] = total_state[...].astype(BF16)

    @pl.when(end)
    def _():
        for p in range(group):
            grads_ref[p, :rows_out, :] = total_out[p * rows_out : (p + 1) * rows_out, :].astype(BF16)
            for half in range(2):
                at = rows_out + half * rows_in
                grads_ref[p, at : at + rows_in, :] = total_gate[
                    p * rows_in : (p + 1) * rows_in, half * D : (half + 1) * D
                ].astype(BF16)
        for q in range(INNER // 128):
            ggain_ref[q : q + 1, :] = down(gains[q * 128 : (q + 1) * 128, :].T)
        ggain_ref[INNER // 128 :, :] = jnp.zeros((16 - INNER // 128, 128), F32)
        by_head = jnp.sum(skips[...].reshape(HEADS, 8, 128), axis=1)
        by_head = jnp.concatenate([by_head, jnp.zeros((128 - HEADS, 128), F32)], axis=0)
        gskip_ref[0:1, :] = down(by_head.T)
        gskip_ref[1:, :] = jnp.zeros((7, 128), F32)


def leave(weights, normed, turned, cot, tokens, y, values, wr, gain, delta, heads, docs):
    n, length, _ = normed.shape
    group, _, rows_in, _ = weights.shape
    packed = rows_in % 16 == 0
    if packed:
        weights, loaded = [weights], [pl.BlockSpec(memory_space=pl.ANY)]
        scratch = [
            pltpu.VMEM((D, INNER), BF16),
            pltpu.VMEM((INNER, D), BF16),
            pltpu.SemaphoreType.DMA((4 * group,)),
        ]
    else:
        gate = jnp.concatenate([weights[:, 2], weights[:, 3]], axis=-1).reshape(D, INNER)
        weights = [gate, weights[:, :2].reshape(INNER, D)]
        loaded, scratch = [whole(a.shape, 2) for a in weights], []
    grads = (group, 4 * rows_in, D)
    rows = lambda width: pl.BlockSpec((1, ROWS, width), lambda i, k: (i, k, 0))
    lanes = lambda height: pl.BlockSpec((1, height, ROWS), lambda i, k: (i, 0, k))
    each = lambda *shape: pl.BlockSpec((1,) + shape, lambda i, k: (i, 0, 0))
    return pl.pallas_call(
        partial(leave_kernel, group, packed),
        grid=(n, length // ROWS),
        in_specs=loaded + [
            rows(D), lanes(D), rows(D), rows(D), lanes(INNER), lanes(INNER),
            pl.BlockSpec((1, ROWS, STATE), lambda i, k: (i, k, 1)),
            whole(gain.shape, 2), each(HP, length), whole(heads.shape, 2), each(*docs.shape[1:]),
        ],
        out_specs=[
            rows(D), lanes(INNER), lanes(D), lanes(HP), each(INNER, STATE), whole(grads, 2),
            whole((16, 128), 2), whole((8, 128), 2),
        ],
        scratch_shapes=[
            pltpu.VMEM((INNER, ROWS), BF16),
            pltpu.VMEM((INNER, ROWS), F32),
            pltpu.VMEM((INNER, ROWS), F32),
            pltpu.VMEM((INNER, ROWS), BF16),
            pltpu.VMEM((2, TILE, ROWS), BF16),
            pltpu.VMEM((ROWS, INNER), BF16),
            pltpu.VMEM((INNER, D), F32),
            pltpu.VMEM((D, INNER), F32),
            pltpu.VMEM((HEADS * 8, ROWS), F32),
            pltpu.VMEM((HEADS * 8, 128), F32),
            pltpu.VMEM((INNER, 128), F32),
            pltpu.VMEM((INNER, 128), F32),
            pltpu.VMEM((HP, length), F32),
            pltpu.VMEM((INNER, STATE), F32),
        ] + scratch,
        out_shape=[
            jax.ShapeDtypeStruct((n, length, D), BF16),
            jax.ShapeDtypeStruct((n, INNER, length), BF16),
            jax.ShapeDtypeStruct((n, D, length), BF16),
            jax.ShapeDtypeStruct((n, HP, length), F32),
            jax.ShapeDtypeStruct((n, INNER, STATE), BF16),
            jax.ShapeDtypeStruct(grads, BF16),
            jax.ShapeDtypeStruct((16, 128), F32),
            jax.ShapeDtypeStruct((8, 128), F32),
        ],
        compiler_params=params(("arbitrary", "arbitrary")),
        name="leave",
    )(*weights, normed, turned, cot, tokens, y, values, wr, gain, delta, heads, docs)


def exit_kernel(
    gval_ref, gwr_ref, dsilu_ref, raw_ref, docs_ref, conv_ref, back_ref, normed_ref, turned_ref,
    wraw_ref, gdraw_ref, dlow_ref, gnorm_ref, tok_ref, cot_ref, gain_ref,
    grad_ref, graw_ref, gdelta_ref, ggain_ref, gconv_ref,
    pre, low_pre, moved, halo_terms, shift, low, lifted, total, sums,
):
    n = pl.program_id(0)
    length = dsilu_ref.shape[2]
    last = n == pl.num_programs(0) - 1

    @pl.when(n == 0)
    def _():
        total[...] = jnp.zeros_like(total)
        sums[...] = jnp.zeros_like(sums)
        gdelta_ref[...] = jnp.zeros_like(gdelta_ref)
        ggain_ref[...] = jnp.zeros_like(ggain_ref)

    def shifts(rows, extent, near):
        first = lax.broadcasted_iota(jnp.int32, (rows, extent), 0)
        second = lax.broadcasted_iota(jnp.int32, (rows, extent), 1)
        return [
            jnp.where(second == first + j, near[j - 1], 0.0).astype(BF16) for j in range(1, CONV)
        ]

    near = [
        jnp.where(docs_ref[0, j : j + 1, :] == docs_ref[0, 0:1, :], 1.0, 0.0)
        for j in range(1, CONV)
    ]
    for i in range(length // 128):
        square = [square_of(v[:, LEAD + i * 128 : LEAD + i * 128 + 128]) for v in near]
        square = [jnp.concatenate([v, v[:, : SPAN - 128]], axis=1) for v in square]
        shift[i] = jnp.concatenate(shifts(128, SPAN, square), axis=0)
    square = [square_of(v[:, LEAD - 128 : LEAD])[128 - HALO :, : 2 * HALO] for v in near]
    ahead = jnp.concatenate(shifts(HALO, 2 * HALO, square), axis=0)
    for slot in range(2):
        low_pre[slot, :HALO, :] = jnp.zeros((HALO, TILE), BF16)
        low_pre[slot, HALO + length :, :] = jnp.zeros((HALO, TILE), BF16)
    tiles = XBC // TILE
    blocks = length // 128

    def span_of(c):
        return slice(c * TILE, (c + 1) * TILE)

    def open_tile(c):
        if c == tiles:
            return
        if c < INNER // TILE:
            here = gval_ref[0, span_of(c), :].astype(F32).T
        else:
            here = gwr_ref[0]
        here = here * dsilu_ref[0, c].astype(F32)
        pre[c % 2] = here
        low_pre[c % 2, HALO : HALO + length, :] = here.astype(BF16)
        halo_terms[c % 2] = nn(ahead, low_pre[c % 2, : 2 * HALO, :])
        for i in range(blocks):
            moved[c % 2 * blocks + i] = nn(
                shift[i], low_pre[c % 2, HALO + i * 128 : HALO + i * 128 + SPAN, :]
            )

    def close_tile(c):
        total[:, span_of(c)] += nn(turned_ref[0], low[c % 2])
        through = nt(low[c % 2], wraw_ref[c])
        if c == 0:
            lifted[...] = through
        else:
            lifted[...] += through

    def fold(v):
        return jnp.sum(v.reshape(v.shape[0] // 8, 8, 128), axis=0)

    open_tile(0)
    for c in range(tiles):
        slot = c % 2
        open_tile(c + 1)
        if c > 0:
            close_tile(c - 1)
        for half in range(0, TILE, 128):
            cols = slice(half, half + 128)
            wide = slice(c * TILE + half, c * TILE + half + 128)
            w = conv_ref[:, wide]
            folded = [sums[k, :, wide] for k in range(CONV + 1)]
            raw = raw_ref[0, c, :HALO, cols].astype(F32)
            for j in range(1, CONV):
                term = halo_terms[slot, (j - 1) * HALO : j * HALO, cols]
                folded[3 - j] = folded[3 - j] + fold(raw * term)
            for b in range(0, length, 64):
                raw = raw_ref[0, c, HALO + b : HALO + b + 64, cols].astype(F32)
                now = pre[slot, b : b + 64, cols]
                grad = w[3:4] * now
                folded[3] = folded[3] + fold(raw * now)
                folded[4] = folded[4] + fold(now)
                for j in range(1, CONV):
                    at = (j - 1) * 128 + b % 128
                    term = moved[slot * blocks + b // 128, at : at + 64, cols]
                    grad = grad + w[3 - j : 4 - j] * term
                    folded[3 - j] = folded[3 - j] + fold(raw * term)
                if b == length - 64:
                    grad = jnp.concatenate([grad[:56], grad[56:] + back_ref[0, :, wide]], axis=0)
                low[slot, b : b + 64, cols] = grad.astype(BF16)
            for k in range(CONV + 1):
                sums[k, :, wide] = folded[k]
    close_tile(tiles - 1)

    gdraw = gdraw_ref[0].astype(BF16)
    gdelta_ref[...] += nn(gdraw, normed_ref[0])
    gain = gain_ref[...]
    gains = jnp.zeros((8, D), F32)
    for b in range(0, length, 128):
        rows = slice(b, b + 128)
        up = lifted[rows, :] + gnorm_ref[0, :, rows].astype(F32).T + tn(gdraw[:, rows], dlow_ref[...])
        x = tok_ref[0, rows, :].astype(F32)
        scale = lax.rsqrt(jnp.mean(x * x, axis=-1, keepdims=True) + EPS)
        normal = x * scale
        gains = gains + jnp.sum((up * normal).reshape(16, 8, D), axis=0)
        up = up * gain
        inner = jnp.mean(up * normal, axis=-1, keepdims=True)
        grad = cot_ref[0, rows, :].astype(F32) + scale * (up - normal * inner)
        grad_ref[0, rows, :] = grad.astype(BF16)
    ggain_ref[0:1, :] += jnp.sum(gains, axis=0, keepdims=True)

    @pl.when(last)
    def _():
        graw_ref[...] = total[...].astype(BF16)
        gconv_ref[0 : CONV + 1, :] = jnp.sum(sums[...], axis=1)


def leave_back(
    gval, gwr, dsilu, raw, docs, conv, back, normed, turned, wraw, gdraw, dlow, gnorm, tokens,
    cotangent, gain,
):
    n, length, _ = tokens.shape
    return pl.pallas_call(
        exit_kernel,
        grid=(n,),
        in_specs=[
            piece(INNER, length), piece(length, 2 * STATE), piece(XBC // TILE, length, TILE),
            piece(XBC // TILE, length + HALO, TILE), piece(*docs.shape[1:]), whole(conv.shape), piece(8, XBC),
            piece(length, D), piece(D, length), whole(wraw.shape), piece(HP, length),
            whole(dlow.shape), piece(D, length), piece(length, D), piece(length, D),
            whole(gain.shape),
        ],
        out_specs=[
            piece(length, D), whole((D, XBC)), whole((HP, D)), whole((8, D)), whole((8, XBC)),
        ],
        out_shape=[
            jax.ShapeDtypeStruct((n, length, D), BF16),
            jax.ShapeDtypeStruct((D, XBC), BF16),
            jax.ShapeDtypeStruct((HP, D), F32),
            jax.ShapeDtypeStruct((8, D), F32),
            jax.ShapeDtypeStruct((8, XBC), F32),
        ],
        scratch_shapes=[
            pltpu.VMEM((2, length, TILE), F32),
            pltpu.VMEM((2, length + 2 * HALO, TILE), BF16),
            pltpu.VMEM((2 * (length // 128), (CONV - 1) * 128, TILE), F32),
            pltpu.VMEM((2, (CONV - 1) * HALO, TILE), F32),
            pltpu.VMEM((length // 128, (CONV - 1) * 128, SPAN), BF16),
            pltpu.VMEM((2, length, TILE), BF16),
            pltpu.VMEM((length, D), F32),
            pltpu.VMEM((D, XBC), F32),
            pltpu.VMEM((CONV + 1, 8, XBC), F32),
        ],
        compiler_params=params(("arbitrary",)),
        name="leave_back",
    )(
        gval, gwr, dsilu, raw, docs, conv, back, normed, turned, wraw, gdraw, dlow, gnorm, tokens,
        cotangent, gain,
    )


def tiles_of(extent):
    return -(-extent // 128)


def pieces_of(rows):
    return [(i, i * 128, min(128, rows - i * 128)) for i in range(tiles_of(rows))]


def split_three(v):
    high = v.astype(BF16)
    rest = v - high.astype(F32)
    middle = rest.astype(BF16)
    low = (rest - middle.astype(F32)).astype(BF16)
    return jnp.concatenate([high, middle, low], axis=0)


def join_three(v):
    return v[0:8] + v[8:16] + v[16:24]


def inverse_factor(gram):
    rows = lax.broadcasted_iota(jnp.int32, (8, 8), 0)
    cols = lax.broadcasted_iota(jnp.int32, (8, 8), 1)
    left, right = gram, jnp.where(rows == cols, 1.0, 0.0)
    for j in range(7):
        factor = jnp.where(rows[:, :1] > j, left[:, j : j + 1] / left[j : j + 1, j : j + 1], 0.0)
        left, right = left - factor * left[j : j + 1, :], right - factor * right[j : j + 1, :]
    pivots = jnp.sum(jnp.where(rows == cols, left, 0.0), axis=1, keepdims=True)
    return right * lax.rsqrt(pivots)


RIGHT_OUT = PROJ // 128
DELTA = RIGHT_OUT + D // 128
REST = DELTA + HEADS // 8 * (D // 128)
REST_ROWS = D // 128 + (CONV + 1) * (XBC // 128) + INNER // 128 + 3
SUMMED = REST + -(-REST_ROWS // 8)


class Scatter:
    def __init__(self, group, x_ref, from_core, pairs, from_far, joint, send, recv):
        self.nf = group // 2
        self.x_ref, self.from_core, self.pairs, self.from_far = x_ref, from_core, pairs, from_far
        self.joint, self.send, self.recv = joint, send, recv
        self.r, self.f, self.s = (lax.axis_index(name) for name in ("rep", "fsdp", "seq"))
        self.copies = []
        half = x_ref.shape[1] // 2
        self.parts = [slice(0, half), slice(half, 2 * half)]
        f = self.f
        if self.nf == 4:
            x, y = f + 1 - 2 * lax.rem(f, 2), lax.rem(f + 2, 4)
            self.order = [lax.rem(x + 2, 4), x, y, f]
        else:
            self.order = [lax.rem(f + 1 + j, self.nf) for j in range(self.nf)]

    def start(self, src, dst, device):
        k = len(self.copies)
        copy = pltpu.make_async_remote_copy(
            src, dst, self.send.at[k], self.recv.at[k], device_id=device, device_id_type=MESH
        )
        copy.start()
        self.copies.append(copy)
        return copy

    def begin(self):
        other = (self.r, self.f, 1 - self.s)
        self.near = [
            self.start(self.x_ref.at[f * 2 + 1 - self.s], self.from_core.at[j], other)
            for j, f in enumerate(self.order)
        ]

    def device(self, j):
        return (self.r, self.order[j], self.s)

    def cross(self):
        self.far = []
        for j, f in enumerate(self.order):
            self.near[j].wait_recv()
            total = self.x_ref[f * 2 + self.s].astype(F32) + self.from_core[j].astype(F32)
            self.pairs[j] = total.astype(BF16)
            if self.nf != 4 and j < self.nf - 1:
                self.far.append(self.start(self.pairs.at[j], self.from_far.at[j], self.device(j)))
            if self.nf == 4 and j < 3:
                for half, part in enumerate(self.parts):
                    if j == 0 or half == j - 1:
                        to = half + 1 if j == 0 else j
                        self.far.append(
                            self.start(
                                self.pairs.at[j, part], self.from_far.at[j, part], self.device(to)
                            )
                        )

    def turn(self):
        if self.nf != 4:
            return
        for half, part in enumerate(self.parts):
            self.far[half].wait_recv()
            to = 2 - half
            total = self.pairs[to, part].astype(F32) + self.from_far[0, part].astype(F32)
            self.joint[half] = total.astype(BF16)
            self.far.append(
                self.start(self.joint.at[half], self.from_far.at[to, part], self.device(to))
            )

    def end(self, o_ref):
        if self.nf == 4:
            for copy in self.far[2:]:
                copy.wait_recv()
            total = self.pairs[3].astype(F32)
            for j in (1, 2):
                total = total + self.from_far[j].astype(F32)
        else:
            total = self.pairs[self.nf - 1].astype(F32)
            for j, copy in enumerate(self.far):
                copy.wait_recv()
                total = total + self.from_far[j].astype(F32)
        o_ref[...] = total
        for copy in self.copies:
            copy.wait_send()


class Exchange:
    def __init__(self, group, replicas):
        self.group, self.replicas = group, replicas
        r, f, s = lax.axis_index("rep"), lax.axis_index("fsdp"), lax.axis_index("seq")
        self.r, self.me = r, f * 2 + s
        self.peers = []
        for j in range(1, group):
            p = lax.rem(self.me + j, group)
            self.peers.append((p, (r, lax.div(p, 2), lax.rem(p, 2))))
        self.others = [(lax.rem(r + j, replicas), f, s) for j in range(1, replicas)]

    def greet(self):
        barrier = pltpu.get_barrier_semaphore()
        for device in [d for _, d in self.peers] + self.others:
            pl.semaphore_signal(barrier, inc=1, device_id=device, device_id_type=MESH)

    def met(self):
        pl.semaphore_wait(pltpu.get_barrier_semaphore(), self.group + self.replicas - 2)

    def sum(self, x_ref, o_ref, own, from_group, from_reps, send, recv, second=None, third=None):
        group, replicas, me = self.group, self.replicas, self.me
        width = own.shape[0]
        copies = []

        def start(src, dst, device):
            k = len(copies)
            copy = pltpu.make_async_remote_copy(
                src, dst, send.at[k], recv.at[k], device_id=device, device_id_type=MESH
            )
            copy.start()
            copies.append(copy)
            return copy

        arriving = [
            start(x_ref.at[pl.ds(p * width, width)], from_group.at[j], device)
            for j, (p, device) in enumerate(self.peers)
        ]
        total = x_ref[pl.ds(me * width, width)]
        for j, copy in enumerate(arriving):
            copy.wait_recv()
            total = total + from_group[j]
        own[...] = total
        from_reps[pl.ds(self.r, 1)] = total[None]
        arriving = [start(own, from_reps.at[self.r], device) for device in self.others]
        if second is not None:
            second()
        for copy in arriving:
            copy.wait_recv()
        total = from_reps[0]
        for j in range(1, replicas):
            total = total + from_reps[j]
        mine = pl.ds(me * width, width)
        o_ref[mine] = total
        arriving = [start(o_ref.at[mine], o_ref.at[mine], device) for _, device in self.peers]
        if third is not None:
            third()
        for copy in arriving:
            copy.wait_recv()
        for copy in copies:
            copy.wait_send()


def compress_kernel(
    group, replicas,
    sin_ref, sout_ref, grads_ref, raw_ref, ein_ref, eout_ref, gdelta_ref, ggain_ref,
    gconv_ref, ggate_ref, gheads_ref, gskip_ref,
    sum_ref, left_in_ref, left_out_ref, turned_in_ref, turned_out_ref, raw_total_ref,
    lefts, left_sums, hat, rights,
    own_a, group_a, reps_a, own_b, group_b, reps_b, send_a, recv_a, send_b, recv_b,
    from_core, pairs, from_far, joint, send_c, recv_c, held_raw, held_grads, held_in, held_out,
    split_in, split_out, load,
):
    rows_in, rows_out = ein_ref.shape[0], eout_ref.shape[0]
    out_part = slice(0, rows_out)
    gate_parts = [slice(rows_out + i * rows_in, rows_out + (i + 1) * rows_in) for i in range(2)]
    ahead = tiles_of(rows_in)
    width = ahead + tiles_of(rows_out)
    exchange = Exchange(group, replicas)
    exchange.greet()
    loads = [
        pltpu.make_async_copy(src, dst, load.at[k])
        for k, (src, dst) in enumerate(
            ((ein_ref, held_in), (eout_ref, held_out), (grads_ref, held_grads), (raw_ref, held_raw))
        )
    ]
    for copy in loads:
        copy.start()
    raw_ref, grads_ref = held_raw, held_grads

    lefts[...] = jnp.zeros_like(lefts)
    mine = pl.ds(exchange.me * width, width)

    def place(index, values, rows, first):
        for i, at, n in pieces_of(rows):
            lefts[index + first + i, :, :n] += values[:, at : at + n]

    def place_own(values, rows, first):
        for i, at, n in pieces_of(rows):
            part = values[:, at : at + n]
            if n < 128:
                part = jnp.concatenate([part, jnp.zeros((8, 128 - n), F32)], axis=1)
            where = pl.ds(exchange.me * width + first + i, 1)
            lefts[where] = lefts[where] + part[None]

    s_in, s_out = split_three(sin_ref[...]), split_three(sout_ref[...])
    for k, (held, split, start, rows, first) in enumerate(
        ((held_in, split_in, s_in, rows_in, 0), (held_out, split_out, s_out, rows_out, ahead))
    ):
        loads[k].wait()
        high = held[...].astype(BF16)
        split[0] = high
        split[1] = (held[...] - high.astype(F32)).astype(BF16)
        place_own(join_three(nt(start, split[0]) + nt(start, split[1])), rows, first)
    loads[2].wait()
    for p in range(group):
        product = nt(s_in[:, :D], grads_ref[p, gate_parts[0]])
        product = product + nt(s_in[:, D:INNER], grads_ref[p, gate_parts[1]])
        place(p * width, join_three(product), rows_in, 0)
        place(p * width, join_three(nt(s_out, grads_ref[p, out_part])), rows_out, ahead)
    loads[3].wait()
    exchange.met()
    scatter = Scatter(group, raw_ref, from_core, pairs, from_far, joint, send_c, recv_c)
    scatter.begin()
    for p in range(group):
        place(p * width, join_three(nt(s_in[:, INNER:], raw_ref[p])), rows_in, 0)
    exchange.sum(
        lefts, left_sums, own_a, group_a, reps_a, send_a, recv_a, scatter.cross, scatter.turn
    )

    for first, last in ((0, ahead), (ahead, width)):
        gram = jnp.zeros((8, 8), F32)
        for p in range(group):
            for i in range(first, last):
                tile = left_sums[p * width + i] * (1.0 / replicas)
                gram = gram + nt_high(tile, tile)
        inverse = inverse_factor(gram)
        for p in range(group):
            for i in range(first, last):
                hat[p * width + i] = nn_high(inverse, left_sums[p * width + i] * (1.0 / replicas))
    own = hat[mine]
    for first, rows, left_ref, turned_ref in (
        (0, rows_in, left_in_ref, turned_in_ref), (ahead, rows_out, left_out_ref, turned_out_ref)
    ):
        for i, at, n in pieces_of(rows):
            turned_ref[:, at : at + n] = own[first + i][:, :n]
            left_ref[at : at + n, :] = own[first + i].T[:n, :]

    def joined(tiles, start, rows):
        return jnp.concatenate([tiles[start + i][:, :n] for i, _, n in pieces_of(rows)], axis=1)

    def product(matrices, rows, skipped, error, at):
        spread = [split_three(joined(hat, p * width + skipped, rows)) for p in range(group)]
        mixed = split_three(joined(own, skipped, rows))
        columns = 0
        for ref, part, extent in matrices:
            for b in range(0, extent, TILE):
                total = nn(spread[0], ref[0, part, b : b + TILE])
                for p in range(1, group):
                    total = total + nn(spread[p], ref[p, part, b : b + TILE])
                here = columns + b
                total = total + nn(mixed, error[0, :, here : here + TILE])
                total = total + nn(mixed, error[1, :, here : here + TILE])
                right = join_three(total)
                for half in range(0, TILE, 128):
                    rights[at + (here + half) // 128] = right[:, half : half + 128]
            columns += extent

    every = slice(0, rows_in)
    product(
        [(grads_ref, part, D) for part in gate_parts] + [(raw_ref, every, XBC)],
        rows_in, 0, split_in, 0,
    )
    product([(grads_ref, out_part, D)], rows_out, ahead, split_out, RIGHT_OUT)
    for g in range(HEADS // 8):
        for q in range(D // 128):
            rights[DELTA + g * (D // 128) + q] = gdelta_ref[
                g * 8 : g * 8 + 8, q * 128 : q * 128 + 128
            ]
    rights[REST:] = jnp.zeros((rights.shape[0] - REST, 8, 128), F32)
    rest = [ggain_ref[0:1, q * 128 : q * 128 + 128] for q in range(D // 128)]
    for k in range(CONV + 1):
        rest += [gconv_ref[k : k + 1, q * 128 : q * 128 + 128] for q in range(XBC // 128)]
    rest += [ggate_ref[q : q + 1, :] for q in range(INNER // 128)]
    rest += [gheads_ref[0:1, :], gheads_ref[1:2, :], gskip_ref[0:1, :]]
    for i in range(0, REST_ROWS, 8):
        eight = rest[i : i + 8]
        rights[REST + i // 8, : len(eight), :] = jnp.concatenate(eight, axis=0)
    exchange.sum(rights, sum_ref, own_b, group_b, reps_b, send_b, recv_b)
    scatter.end(raw_total_ref)


def compress(starts, grads, raw, errors, smalls):
    group = grads.shape[0]
    replicas = lax.axis_size("rep")
    raw = raw.reshape(group, D // group, XBC)
    rows_in, rows_out = errors[0].shape[0], errors[1].shape[0]
    width = tiles_of(rows_in) + tiles_of(rows_out)
    block = (rows_in, XBC)
    share = -(-SUMMED // group)
    dma = pltpu.SemaphoreType.DMA((2 * (group - 1) + replicas - 1,))
    tiles = lambda *n: pltpu.VMEM(n + (8, 128), F32)
    vmem = pl.BlockSpec(memory_space=pltpu.VMEM)
    arrays = [*starts, grads, raw, *errors, *smalls]
    return pl.pallas_call(
        partial(compress_kernel, group, replicas),
        out_shape=[
            jax.ShapeDtypeStruct((group * share, 8, 128), F32),
            jax.ShapeDtypeStruct((rows_in, 8), F32),
            jax.ShapeDtypeStruct((rows_out, 8), F32),
            jax.ShapeDtypeStruct((8, rows_in), F32),
            jax.ShapeDtypeStruct((8, rows_out), F32),
            jax.ShapeDtypeStruct((rows_in, XBC), F32),
        ],
        in_specs=[vmem] * 2 + [pl.BlockSpec(memory_space=pl.ANY)] * 4 + [vmem] * len(smalls),
        out_specs=[vmem] * 6,
        scratch_shapes=[
            tiles(group * width), tiles(group * width), tiles(group * width),
            tiles(group * share),
            tiles(width), tiles(group - 1, width), tiles(replicas, width),
            tiles(share), tiles(group - 1, share), tiles(replicas, share),
            dma, dma, dma, dma,
            pltpu.VMEM((group // 2,) + block, BF16),
            pltpu.VMEM((group // 2,) + block, BF16),
            pltpu.VMEM((group // 2 - 1,) + block, BF16),
            pltpu.VMEM((2, rows_in // 2, XBC), BF16),
            pltpu.SemaphoreType.DMA((group + 2,)),
            pltpu.SemaphoreType.DMA((group + 2,)),
            pltpu.VMEM(raw.shape, BF16),
            pltpu.VMEM(grads.shape, BF16),
            pltpu.VMEM(errors[0].shape, F32),
            pltpu.VMEM(errors[1].shape, F32),
            pltpu.VMEM((2,) + errors[0].shape, BF16),
            pltpu.VMEM((2,) + errors[1].shape, BF16),
            pltpu.SemaphoreType.DMA((4,)),
        ],
        compiler_params=pltpu.CompilerParams(
            collective_id=2, has_side_effects=True, vmem_limit_bytes=VMEM_LIMIT
        ),
        name="compress",
    )(*arrays)


def finish_kernel(
    rates, replicas, rights_ref, tin_ref, tout_ref, lin_ref, lout_ref,
    win_ref, min_ref, ein_ref, raw_ref, wout_ref, mout_ref, eout_ref, out_ref, low_ref, high_ref,
    nwin_ref, nmin_ref, nein_ref, nwout_ref, nmout_ref, neout_ref,
    rin_ref, rout_ref, ntin_ref, ntout_ref,
):
    @pl.when(pl.program_id(0) == 0)
    def _():
        for ref, at, extent in ((rin_ref, 0, PROJ), (rout_ref, RIGHT_OUT, D)):
            for q in range(extent // 128):
                ref[:, q * 128 : q * 128 + 128] = rights_ref[at + q] * (1.0 / replicas)
        ntin_ref[...] = tin_ref[...]
        ntout_ref[...] = tout_ref[...]

    def update(w, m, e, nw, nm, ne, left_ref, grads, at, rate):
        rows = w.shape[0]
        left = [jnp.broadcast_to(left_ref[:, k : k + 1], (rows, 128)) for k in range(8)]
        begin = 0
        for grad in grads:
            for b in range(0, grad.shape[1], 128):
                cols = slice(begin + b, begin + b + 128)
                right = rights_ref[at + (begin + b) // 128] * (1.0 / replicas)
                approx = left[0] * right[0:1]
                for k in range(1, 8):
                    approx = approx + left[k] * right[k : k + 1]
                momentum = MOMENTUM * m[:, cols] + approx
                nm[:, cols] = momentum
                nw[:, cols] = w[:, cols] - rate * momentum
                ne[:, cols] = (grad[:, b : b + 128].astype(F32) + e[:, cols]) - approx
            begin += grad.shape[1]

    update(
        win_ref, min_ref, ein_ref, nwin_ref, nmin_ref, nein_ref, lin_ref, (low_ref, high_ref, raw_ref), 0,
        rates[0],
    )
    update(
        wout_ref, mout_ref, eout_ref, nwout_ref, nmout_ref, neout_ref, lout_ref, (out_ref,),
        RIGHT_OUT, rates[1],
    )


def finish(rates, replicas, rights, turned_in, turned_out, left_in, left_out, wide, narrow, grads):
    rows_in, rows_out = left_in.shape[0], left_out.shape[0]
    steps = 3 if rows_in % 48 == 0 else 1
    block = lambda a: pl.BlockSpec((a.shape[0] // steps, a.shape[1]), lambda i: (i, 0))
    like = lambda a: jax.ShapeDtypeStruct(a.shape, F32)
    step_in, step_out = rows_in // steps, rows_out // steps
    parts = [pl.BlockSpec((step_out, D), lambda i: (i, 0))] + [
        pl.BlockSpec((step_in, D), lambda i, k=k: ((rows_out + k * rows_in) // step_in + i, 0))
        for k in range(2)
    ]
    arrays = [*wide, *narrow]
    outs = [*wide[:3], *narrow[:3]]
    extra = [(8, PROJ), (8, D), turned_in.shape, turned_out.shape]
    return pl.pallas_call(
        partial(finish_kernel, rates, replicas),
        grid=(steps,),
        in_specs=[
            whole(rights.shape), whole(turned_in.shape), whole(turned_out.shape),
            block(left_in), block(left_out), *map(block, arrays), *parts,
        ],
        out_specs=[*map(block, outs), *map(whole, extra)],
        out_shape=[*map(like, outs), *(jax.ShapeDtypeStruct(e, F32) for e in extra)],
        compiler_params=params(("arbitrary",)),
        name="finish",
    )(rights, turned_in, turned_out, left_in, left_out, *arrays, grads, grads, grads)


def step_rates(tokens_replica):
    grad_scale = 0.3 * math.sqrt(tokens_replica)
    return (
        0.5 / (math.sqrt(D) * grad_scale),
        0.5 / (math.sqrt(INNER) * grad_scale),
        0.1 / grad_scale,
    )


def to_later(block):
    return lax.ppermute(block, "seq", [(i, i + 1) for i in range(lax.axis_size("seq") - 1)])


def to_earlier(block):
    return lax.ppermute(block, "seq", [(i + 1, i) for i in range(lax.axis_size("seq") - 1)])


def gather_rows(shard):
    return lax.all_gather(shard, ("fsdp", "seq"), axis=0, tiled=True)


def scatter_rows(total):
    return lax.psum_scatter(total, ("fsdp", "seq"), scatter_dimension=0, tiled=True)


def body(
    tokens,
    cotangent,
    segments,
    input_weight,
    output_weight,
    small_values,
    input_momentum,
    output_momentum,
    small_momentum,
    input_error,
    output_error,
    input_start,
    output_start,
):
    shape = tokens.shape
    pieces = shape[0] * shape[1]
    length = shape[2]
    replicas = lax.axis_size("rep")
    tokens_replica = pieces * length * lax.axis_size("fsdp") * lax.axis_size("seq")
    rate_in, rate_out, rate_small = step_rates(tokens_replica)

    tokens = tokens.reshape(pieces, length, D)
    cotangent = cotangent.reshape(pieces, length, D)
    small_rows = jnp.pad(small_values, (0, -small_values.shape[0] % 1024)).reshape(-1, 128)
    group = lax.axis_size("fsdp") * lax.axis_size("seq")
    weights = jnp.concatenate(
        [output_weight, input_weight[:, :D], input_weight[:, D:INNER]], axis=0
    ).astype(BF16)
    weights = gather_rows(weights).reshape(group, 4, -1, D)
    delta_rows = small_values[D:AT_CONV].reshape(D, HEADS).astype(BF16).T
    delta_rows = jnp.pad(delta_rows, ((0, HP - HEADS), (0, 0)))
    segments = segments.reshape(pieces, 1, segments.shape[2])
    norm_gain = small_values[:D].reshape(1, D)
    if lax.axis_size("fsdp") == 4 and input_weight.shape[0] % 16 == 0:
        (
            raw_full, normed, turned, raw, dsilu, values, wr, draw, delta, send, come,
            conv, gate_gain, heads, docs,
        ) = front(input_weight, tokens, small_rows, segments, delta_rows)
        raw_full = raw_full.reshape(XBC // TILE, D, TILE)
    else:
        raw_full, halo, _, conv, gate_gain, heads, docs = gather_raw(
            input_weight, tokens, small_rows, segments
        )
        raw_full = raw_full.reshape(D, XBC // TILE, TILE).transpose(1, 0, 2)
        normed, turned, raw, dsilu, values, wr, draw, delta, send = enter(
            tokens, halo, norm_gain, raw_full, delta_rows, conv, heads, docs
        )
        come = to_later(send)
    y, starts = forward_scan(values, wr, delta, heads, docs, come)
    output, gy, gnorm, first, gstate, grads, ggate, gskip = leave(
        weights, normed, turned, cotangent, tokens, y, values, wr, gate_gain, delta, heads, docs
    )
    total = scatter_rows(grads.reshape(-1, D))
    gval, gwr, gdraw, gheads, ghalo = backward_scan(
        values, wr, delta, draw, heads, docs, gy, first, starts, to_earlier(gstate), send, dsilu,
        conv,
    )
    input_grad, grad_raw, gdelta, ggain, gconv = leave_back(
        gval, gwr, dsilu, raw, docs, conv, to_earlier(ghalo), normed, turned, raw_full, gdraw,
        delta_rows, gnorm, tokens, cotangent, norm_gain,
    )
    rights, left_in, left_out, turned_in, turned_out, raw_total = compress(
        (input_start.T, output_start.T),
        grads,
        grad_raw,
        (input_error[0], output_error[0]),
        (gdelta, ggain, gconv, ggate, gheads, gskip),
    )
    (
        new_input_weight, new_input_momentum, new_input_error,
        new_output_weight, new_output_momentum, new_output_error,
        input_right, output_right, input_left, output_left,
    ) = finish(
        (rate_in, rate_out), replicas, rights, turned_in, turned_out, left_in, left_out,
        (input_weight, input_momentum, input_error[0], raw_total),
        (output_weight, output_momentum, output_error[0]),
        total,
    )
    rest = rights[REST:SUMMED].reshape(-1, 128)[:REST_ROWS]
    turned_delta = rights[DELTA:REST].reshape(HEADS // 8, D // 128, 8, 128)
    small_sum = jnp.concatenate(
        [
            rest[: D // 128].reshape(-1),
            turned_delta.transpose(1, 3, 0, 2).reshape(-1),
            rest[D // 128 : -3].reshape(-1),
            rest[-3:, :HEADS].reshape(-1),
        ]
    )
    new_small_momentum = MOMENTUM * small_momentum + small_sum / replicas
    new_small_values = small_values - rate_small * new_small_momentum
    return (
        output.reshape(shape),
        input_grad.reshape(shape),
        new_input_weight,
        new_output_weight,
        new_input_momentum,
        new_output_momentum,
        new_small_values,
        new_small_momentum,
        input_left.T,
        input_right.T,
        output_left.T,
        output_right.T,
        new_input_error[None],
        new_output_error[None],
    )


def solution(mesh):
    return jax.shard_map(
        body,
        mesh=mesh,
        in_specs=(
            P(None, ("rep", "fsdp"), "seq", None),
            P(None, ("rep", "fsdp"), "seq", None),
            P(None, ("rep", "fsdp"), None),
            P(("fsdp", "seq"), None),
            P(("fsdp", "seq"), None),
            P(),
            P(("fsdp", "seq"), None),
            P(("fsdp", "seq"), None),
            P(),
            P("rep", ("fsdp", "seq"), None),
            P("rep", ("fsdp", "seq"), None),
            P(),
            P(),
        ),
        out_specs=(
            P(None, ("rep", "fsdp"), "seq", None),
            P(None, ("rep", "fsdp"), "seq", None),
            P(("fsdp", "seq"), None),
            P(("fsdp", "seq"), None),
            P(("fsdp", "seq"), None),
            P(("fsdp", "seq"), None),
            P(),
            P(),
            P(("fsdp", "seq"), None),
            P(),
            P(("fsdp", "seq"), None),
            P(),
            P("rep", ("fsdp", "seq"), None),
            P("rep", ("fsdp", "seq"), None),
        ),
        check_vma=False,
    )
```

```python
from functools import partial
import math

import jax
import jax.numpy as jnp
from jax import lax
from jax.experimental import pallas as pl
from jax.experimental.pallas import tpu as pltpu
from jax.sharding import PartitionSpec as P

D = 768
INNER = 1536
HEADS = 24
HEADDIM = 64
STATE = 128
CONV = 4
PROJ = 3328
XBC = 1792

EPS = 1e-05
MOMENTUM = 0.9
HIGH = lax.Precision.HIGHEST
F32 = jnp.float32
BF16 = jnp.bfloat16
HP = 32
CH = 128
HALO = 16
TILE = 256
SUB = 16
ROWS = 256
SPAN = 128 + HALO
NEG = -1e30
VMEM_LIMIT = 63 * 2**20
MESH = pl.DeviceIdType.MESH

BEFORE = 3
LEAD = 128
BIAS, RATE, SKIP = 0, 1, 2
AT_CONV = D + D * HEADS
AT_GATE = AT_CONV + (CONV + 1) * XBC
AT_HEADS = AT_GATE + INNER


def nn(a, b):
    return lax.dot_general(a, b, (((1,), (0,)), ((), ())), preferred_element_type=F32)


def nt(a, b):
    return lax.dot_general(a, b, (((1,), (1,)), ((), ())), preferred_element_type=F32)


def tn(a, b):
    return lax.dot_general(a, b, (((0,), (0,)), ((), ())), preferred_element_type=F32)


def nn_high(a, b):
    return lax.dot_general(
        a, b, (((1,), (0,)), ((), ())), precision=HIGH, preferred_element_type=F32
    )


def nt_high(a, b):
    return lax.dot_general(
        a, b, (((1,), (1,)), ((), ())), precision=HIGH, preferred_element_type=F32
    )


def tn_high(a, b):
    return lax.dot_general(
        a, b, (((0,), (0,)), ((), ())), precision=HIGH, preferred_element_type=F32
    )


def softplus(v):
    return jnp.maximum(v, 0.0) + jnp.log1p(jnp.exp(-jnp.abs(v)))


def sigmoid(v):
    return 0.5 + 0.5 * jnp.tanh(0.5 * v)


def triangle(extent):
    return jnp.where(
        lax.broadcasted_iota(jnp.int32, (extent, extent), 0)
        <= lax.broadcasted_iota(jnp.int32, (extent, extent), 1),
        1.0,
        0.0,
    )


def times_mask(v, mask):
    rows = v.shape[0]
    product = nn(split_three(v), mask.astype(BF16))
    return product[:rows] + product[rows : 2 * rows] + product[2 * rows :]


def column(heads_ref, row):
    return heads_ref[...].T[:HP, row : row + 1]


def square_of(row):
    return jnp.broadcast_to(row, (128, 128)).T


def params(semantics, **more):
    return pltpu.CompilerParams(
        dimension_semantics=semantics, vmem_limit_bytes=VMEM_LIMIT, **more
    )


def piece(*shape):
    return pl.BlockSpec((1,) + shape, lambda i: (i,) + (0,) * len(shape))


def whole(shape, ranks=1):
    index = (lambda i: (0,) * len(shape)) if ranks == 1 else (lambda i, k: (0,) * len(shape))
    return pl.BlockSpec(shape, index, pipeline_mode=pl.Buffered(1))


def unpack_small(rows_ref, gain_ref, conv_ref, gate_ref, heads_ref):
    for q in range(D // 128):
        gain_ref[:, q * 128 : q * 128 + 128] = rows_ref[q : q + 1, :]
    at = AT_CONV // 128
    for k in range(CONV + 1):
        for q in range(XBC // 128):
            conv_ref[k : k + 1, q * 128 : q * 128 + 128] = rows_ref[at : at + 1, :]
            at += 1
    gate_ref[...] = rows_ref[at : at + INNER // 128, :]
    row = jnp.broadcast_to(rows_ref[at + INNER // 128 : at + INNER // 128 + 1, :], (8, 128))
    place = lax.broadcasted_iota(jnp.int32, (8, 128), 0)
    heads = jnp.zeros((8, 128), F32)
    for k in range(3):
        moved = row if k == 0 else pltpu.roll(row, 128 - k * HEADS, 1)
        heads = jnp.where(place == k, moved, heads)
    lane = lax.broadcasted_iota(jnp.int32, (8, 128), 1)
    heads_ref[...] = jnp.where(lane < HEADS, heads, 0.0)


def unpack_documents(seg_ref, docs_ref, later):
    n, _, extent = docs_ref.shape
    length = extent - LEAD
    place = lax.broadcasted_iota(jnp.int32, (8, extent), 0)
    for i in range(n):
        ids = jnp.broadcast_to(seg_ref[i].astype(F32), (8, seg_ref.shape[2]))
        ahead, behind = jnp.full((8, LEAD), -1.0, F32), jnp.full((8, LEAD), -3.0, F32)
        ids = jnp.concatenate([ahead, ids, behind], axis=1)
        total = ids.shape[1]
        docs = jnp.zeros((8, extent), F32)
        for row, offset in enumerate((0, 1, 2, 3, -1, -2, -3)):
            moved = ids if offset == 0 else pltpu.roll(ids, (-offset) % total, 1)
            here = jnp.where(later, moved[:, length : length + extent], moved[:, :extent])
            docs = jnp.where(place == row, here, docs)
        docs_ref[i] = docs


def gather_kernel(
    nf, w_ref, tok_ref, small_ref, seg_ref,
    o_ref, halo_ref, gain_ref, conv_ref, gate_ref, heads_ref, docs_ref,
    mine, near, local, send, recv,
):
    r, f, s = lax.axis_index("rep"), lax.axis_index("fsdp"), lax.axis_index("seq")
    other = (r, f, 1 - s)
    if nf == 4:
        fx, fy = f + 1 - 2 * lax.rem(f, 2), lax.rem(f + 2, 4)
        fd = lax.rem(fx + 2, 4)
        far = [(r, fx, s), (r, fy, s)]
    else:
        far = [(r, lax.rem(f + j, nf), s) for j in range(1, nf)]
    barrier = pltpu.get_barrier_semaphore()
    for device in far + [other]:
        pl.semaphore_signal(barrier, inc=1, device_id=device, device_id_type=MESH)
    mine[...] = w_ref[:, INNER:].astype(BF16)
    near[...] = tok_ref[:, tok_ref.shape[1] - HALO :, :]
    pl.semaphore_wait(barrier, len(far) + 1)
    copies = []

    def start(src, dst, device):
        k = len(copies)
        copy = pltpu.make_async_remote_copy(
            src, dst, send.at[k], recv.at[k], device_id=device, device_id_type=MESH
        )
        copy.start()
        copies.append(copy)
        return copy

    def block(owner):
        return o_ref.at[owner * 2 + s]

    own = pltpu.make_async_copy(mine, block(f), local)
    own.start()
    if nf == 4:
        x_dev, y_dev = far
        half = mine.shape[0] // 2
        low, high = pl.ds(0, half), pl.ds(half, half)
        from_x, from_y, from_d = block(fx), block(fy), block(fd)
        x_low = start(mine.at[low], block(f).at[low], x_dev)
        y_high = start(mine.at[high], block(f).at[high], y_dev)
        x_high = start(mine.at[high], block(f).at[high], x_dev)
        y_low = start(mine.at[low], block(f).at[low], y_dev)
        late = [start(mine, block(f), other), start(near, halo_ref, other)]
        unpack_small(small_ref, gain_ref, conv_ref, gate_ref, heads_ref)
        unpack_documents(seg_ref, docs_ref, s == 1)
        x_low.wait_recv()
        d_low = start(from_x.at[low], from_x.at[low], y_dev)
        y_high.wait_recv()
        d_high = start(from_y.at[high], from_y.at[high], x_dev)
        x_high.wait_recv()
        late.append(start(from_x, from_x, other))
        y_low.wait_recv()
        late.append(start(from_y, from_y, other))
        d_low.wait_recv()
        late.append(start(from_d.at[low], from_d.at[low], other))
        d_high.wait_recv()
        late.append(start(from_d.at[high], from_d.at[high], other))
    else:
        first = [start(mine, block(f), device) for device in far]
        late = [start(mine, block(f), other), start(near, halo_ref, other)]
        unpack_small(small_ref, gain_ref, conv_ref, gate_ref, heads_ref)
        unpack_documents(seg_ref, docs_ref, s == 1)
        for j, copy in enumerate(first):
            copy.wait_recv()
            source = block(lax.rem(f - 1 - j + nf, nf))
            late.append(start(source, source, other))
    for copy in late:
        copy.wait_recv()
    for copy in copies:
        copy.wait_send()
    own.wait()


def gather_raw(weight, tokens, small_rows, segments):
    nf = lax.axis_size("fsdp")
    rows = weight.shape[0]
    n, length, _ = tokens.shape
    vmem = pl.BlockSpec(memory_space=pltpu.VMEM)
    dma = pltpu.SemaphoreType.DMA
    count = 12 if nf == 4 else 2 * nf
    full, *rest = pl.pallas_call(
        partial(gather_kernel, nf),
        out_shape=[
            jax.ShapeDtypeStruct((2 * nf, rows, XBC), BF16),
            jax.ShapeDtypeStruct((n, HALO, D), BF16),
            jax.ShapeDtypeStruct((1, D), F32),
            jax.ShapeDtypeStruct((CONV + 1, XBC), F32),
            jax.ShapeDtypeStruct((INNER // 128, 128), F32),
            jax.ShapeDtypeStruct((8, 128), F32),
            jax.ShapeDtypeStruct((n, 8, LEAD + length), F32),
        ],
        in_specs=[vmem] * 4,
        out_specs=[pl.BlockSpec(memory_space=pl.ANY)] + [vmem] * 6,
        scratch_shapes=[
            pltpu.VMEM((rows, XBC), BF16),
            pltpu.VMEM((n, HALO, D), BF16),
            dma,
            dma((count,)),
            dma((count,)),
        ],
        compiler_params=pltpu.CompilerParams(
            collective_id=1, has_side_effects=True, vmem_limit_bytes=VMEM_LIMIT
        ),
        name="gather_raw",
    )(weight, tokens, small_rows, segments)
    return full.reshape(2 * nf * rows, XBC), *rest


def store_shift(shift, i, j, values):
    shift[i, (j - 1) * 128 : j * 128, :] = values


def shift_matrices(docs, store):
    own = docs[0:1, LEAD:]
    rows = lax.broadcasted_iota(jnp.int32, (128, SPAN), 0)
    cols = lax.broadcasted_iota(jnp.int32, (128, SPAN), 1)
    for j in range(1, CONV):
        same = jnp.where(docs[BEFORE + j : BEFORE + j + 1, LEAD:] == own, 1.0, 0.0)
        for i in range(own.shape[1] // 128):
            here = square_of(same[:, i * 128 : i * 128 + 128])
            here = jnp.concatenate([here, here[:, : SPAN - 128]], axis=1)
            store(i, j, jnp.where(cols == rows + (HALO - j), here, 0.0).astype(BF16))


def step_terms(normed, dlow, heads_ref, docs):
    length = normed.shape[0]
    own = docs[0:1, LEAD:]
    draw = nt(dlow, normed) + column(heads_ref, BIAS)
    delta = softplus(draw)
    totals = times_mask(-jnp.exp(column(heads_ref, RATE)) * delta, triangle(length))
    keep = jnp.where(own == own[:, length - 1 :], 1.0, 0.0)
    return draw, delta, jnp.exp(totals[:, length - 1 :] - totals) * keep * delta


def enter_kernel(
    tok_ref, halo_ref, gain_ref, wraw_ref, dlow_ref, conv_ref, heads_ref, docs_ref,
    normed_ref, turned_ref, raw_ref, dsilu_ref, val_ref, wr_ref, draw_ref, delta_ref, send_ref,
    ext, moved, act, shift,
):
    length = tok_ref.shape[1]
    gain = gain_ref[...]
    for start, rows, src in ((0, HALO, halo_ref), (HALO, length, tok_ref)):
        for b in range(0, rows, 128):
            n = min(128, rows - b)
            x = src[0, b : b + n, :].astype(F32)
            scale = lax.rsqrt(jnp.mean(x * x, axis=-1, keepdims=True) + EPS)
            ext[start + b : start + b + n, :] = (x * scale * gain).astype(BF16)
    normed = ext[HALO:, :]
    normed_ref[0] = normed
    turned_ref[0] = normed.T
    shift_matrices(docs_ref[0], lambda i, j, values: store_shift(shift, i, j, values))
    draw, delta, weight = step_terms(normed, dlow_ref[...], heads_ref, docs_ref[0])
    draw_ref[0] = draw
    delta_ref[0] = delta
    tiles = XBC // TILE
    blocks = length // 128

    def span_of(c):
        return slice(c * TILE, (c + 1) * TILE)

    def project(c):
        if c < tiles:
            raw_ref[0, c] = nn(ext[...], wraw_ref[c]).astype(BF16)

    def move(c):
        if c < tiles:
            for i in range(blocks):
                moved[c % 2 * blocks + i] = nn(
                    shift[i], raw_ref[0, c, i * 128 : i * 128 + SPAN, :]
                )

    project(0)
    project(1)
    move(0)
    for c in range(tiles):
        span = span_of(c)
        project(c + 2)
        move(c + 1)
        for b in range(0, length, 128):
            slot = c % 2 * blocks + b // 128
            for half in range(0, TILE, 128):
                hc = slice(c * TILE + half, c * TILE + half + 128)
                lanes = slice(half, half + 128)
                w = conv_ref[:, hc]
                for q in range(0, 128, 64):
                    z = w[4:5] + w[3:4] * raw_ref[0, c, HALO + b + q : HALO + b + q + 64, lanes].astype(F32)
                    for j in range(1, CONV):
                        at = (j - 1) * 128 + q
                        z = z + w[3 - j : 4 - j] * moved[slot, at : at + 64, lanes]
                    sig = sigmoid(z)
                    silu = z * sig
                    act[c % 2, b + q : b + q + 64, lanes] = silu
                    dsilu_ref[0, c, b + q : b + q + 64, lanes] = (sig + silu * (1.0 - sig)).astype(BF16)
        if c < INNER // TILE:
            val_ref[0, span, :] = act[c % 2].T.astype(BF16)
        else:
            wr_ref[0] = act[c % 2].astype(BF16)

    writers = wr_ref[0, :, :STATE]
    for h in range(HEADS):
        rows = slice(h * HEADDIM, (h + 1) * HEADDIM)
        scaled = val_ref[0, rows, :].astype(F32) * weight[h : h + 1, :]
        send_ref[0, rows, :] = nn(scaled.astype(BF16), writers).astype(BF16)


def enter(tokens, halo, gain, wraw, dlow, conv, heads, docs):
    n, length, _ = tokens.shape
    outs = [
        ((n, length, D), BF16),
        ((n, D, length), BF16),
        ((n, XBC // TILE, length + HALO, TILE), BF16),
        ((n, XBC // TILE, length, TILE), BF16),
        ((n, INNER, length), BF16),
        ((n, length, 2 * STATE), BF16),
        ((n, HP, length), F32),
        ((n, HP, length), F32),
        ((n, INNER, STATE), BF16),
    ]
    return pl.pallas_call(
        enter_kernel,
        grid=(n,),
        in_specs=[
            piece(length, D), piece(HALO, D), whole(gain.shape), whole(wraw.shape),
            whole(dlow.shape), whole(conv.shape), whole(heads.shape), piece(*docs.shape[1:]),
        ],
        out_specs=[piece(*s[1:]) for s, _ in outs],
        out_shape=[jax.ShapeDtypeStruct(s, t) for s, t in outs],
        scratch_shapes=[
            pltpu.VMEM((length + HALO, D), BF16),
            pltpu.VMEM((2 * (length // 128), (CONV - 1) * 128, TILE), F32),
            pltpu.VMEM((2, length, TILE), F32),
            pltpu.VMEM((length // 128, (CONV - 1) * 128, SPAN), BF16),
        ],
        compiler_params=params(("arbitrary",)),
        name="enter",
    )(tokens, halo, gain, wraw, dlow, conv, heads, docs)


class Copies:
    def __init__(self, *semaphores):
        self.semaphores, self.copies = semaphores, []

    def local(self, src, dst):
        copy = pltpu.make_async_copy(src, dst, self.semaphores[0].at[len(self.copies)])
        copy.start()
        self.copies.append(copy)
        return copy

    def remote(self, src, dst, device):
        k = len(self.copies)
        copy = pltpu.make_async_remote_copy(
            src, dst, self.semaphores[0].at[k], self.semaphores[1].at[k],
            device_id=device, device_id_type=MESH,
        )
        copy.start()
        self.copies.append(copy)
        return copy

    def plan(self, amount, ends, device=None):
        first = len(self.copies)

        def copy(n):
            semaphores = [group.at[first + n] for group in self.semaphores]
            if device is None:
                return pltpu.make_async_copy(*ends(n), *semaphores)
            return pltpu.make_async_remote_copy(
                *ends(n), *semaphores, device_id=device, device_id_type=MESH
            )

        self.copies.extend(copy(n) for n in range(amount))
        return lambda n: copy(n).start()


def front_kernel(
    w_ref, tok_ref, small_ref, seg_ref, dlow_ref,
    wraw_ref, normed_ref, turned_ref, raw_ref, dsilu_ref, val_ref, wr_ref, draw_ref, delta_ref,
    send_ref, come_ref, conv_ref, gate_ref, heads_ref, docs_ref,
    mine, near, halo, wide, gain, ext, turned, raw, dsilu, val, moved, act, shift, weight,
    stored, send, recv,
):
    r, f, s = lax.axis_index("rep"), lax.axis_index("fsdp"), lax.axis_index("seq")
    fx, fy = f + 1 - 2 * lax.rem(f, 2), lax.rem(f + 2, 4)
    fd = lax.rem(fx + 2, 4)
    x_dev, y_dev, other = (r, fx, s), (r, fy, s), (r, f, 1 - s)
    pieces, length, _ = tok_ref.shape
    tiles, blocks = XBC // TILE, length // 128
    order = [tiles - 1, *range(tiles - 1)]
    barrier = pltpu.get_barrier_semaphore()
    for device in (x_dev, y_dev, other):
        pl.semaphore_signal(barrier, inc=1, device_id=device, device_id_type=MESH)
    for c in range(tiles):
        mine[c] = w_ref[:, INNER + c * TILE : INNER + (c + 1) * TILE].astype(BF16)
    near[...] = tok_ref[:, length - HALO :, :]
    pl.semaphore_wait(barrier, 3)
    outward, out = Copies(send, recv), Copies(stored)
    arriving = {}

    def block(c, owner):
        return wide.at[c, owner * 2 + s]

    def offer(at):
        if at < tiles:
            c = order[at]
            arriving[c] = [
                outward.remote(mine.at[c], block(c, f), device) for device in (x_dev, y_dev, other)
            ]
            wide[c, f * 2 + s] = mine[c]

    def relay(at):
        if at < tiles:
            c = order[at]
            from_x, from_y, _ = arriving[c]
            from_x.wait_recv()
            from_y.wait_recv()
            through = (fx, y_dev) if at % 2 == 0 else (fy, x_dev)
            across = block(c, through[0])
            arriving[c].append(outward.remote(across, across, through[1]))
            for owner in (fx, fy):
                arriving[c].append(outward.remote(block(c, owner), block(c, owner), other))

    def finish_tile(at):
        c = order[at]
        arriving[c][3].wait_recv()
        arriving[c].append(outward.remote(block(c, fd), block(c, fd), other))
        for k in (2, 4, 5, 6):
            arriving[c][k].wait_recv()
        out.local(wide.at[c], wraw_ref.at[c])

    bring_halo = outward.remote(near, halo, other)
    offer(0)
    offer(1)
    offer(2)
    unpack_small(small_ref, gain, conv_ref, gate_ref, heads_ref)
    unpack_documents(seg_ref, docs_ref, s == 1)
    bring_halo.wait_recv()
    for n in range(pieces):
        x = halo[n].astype(F32)
        scale = lax.rsqrt(jnp.mean(x * x, axis=-1, keepdims=True) + EPS)
        ext[n, :HALO, :] = (x * scale * gain[...]).astype(BF16)
    normed_out = out.plan(pieces, lambda n: (ext.at[n, pl.ds(HALO, length)], normed_ref.at[n]))
    turned_out = out.plan(pieces, lambda n: (turned.at[n], turned_ref.at[n]))

    def normalise(n, carry):
        for b in range(0, length, 128):
            x = tok_ref[n, b : b + 128, :].astype(F32)
            scale = lax.rsqrt(jnp.mean(x * x, axis=-1, keepdims=True) + EPS)
            ext[n, HALO + b : HALO + b + 128, :] = (x * scale * gain[...]).astype(BF16)
        normed_out(n)
        turned[n] = ext[n, HALO:, :].T
        turned_out(n)
        return carry

    def prepare(n, carry):
        draw_ref[n], delta_ref[n], weight[n] = step_terms(
            ext[n, HALO:, :], dlow_ref[...], heads_ref, docs_ref[n]
        )
        shift_matrices(
            docs_ref[n], lambda i, j, values: store_shift(shift, n * blocks + i, j, values)
        )
        return carry

    lax.fori_loop(0, pieces, normalise, 0)
    relay(0)
    lax.fori_loop(0, pieces, prepare, 0)

    states = []
    for at, c in enumerate(order):
        relay(at + 1)
        offer(at + 3)
        finish_tile(at)
        columns = wide[c].reshape(D, TILE)
        for n in range(pieces):
            raw[n, c] = nn(ext[n], columns).astype(BF16)
            out.local(raw.at[n, c], raw_ref.at[n, c])
        for n in range(pieces):
            for i in range(blocks):
                moved[n * blocks + i] = nn(
                    shift[n * blocks + i], raw[n, c, i * 128 : i * 128 + SPAN, :]
                )
        for n in range(pieces):
            for b in range(0, length, 128):
                slot = n * blocks + b // 128
                for half in range(0, TILE, 128):
                    hc = slice(c * TILE + half, c * TILE + half + 128)
                    lanes = slice(half, half + 128)
                    w = conv_ref[:, hc]
                    for q in range(0, 128, 64):
                        here = raw[n, c, HALO + b + q : HALO + b + q + 64, lanes].astype(F32)
                        z = w[4:5] + w[3:4] * here
                        for j in range(1, CONV):
                            row = (j - 1) * 128 + q
                            z = z + w[3 - j : 4 - j] * moved[slot, row : row + 64, lanes]
                        sig = sigmoid(z)
                        silu = z * sig
                        act[n, b + q : b + q + 64, lanes] = silu
                        dsilu[n, c, b + q : b + q + 64, lanes] = (
                            sig + silu * (1.0 - sig)
                        ).astype(BF16)
            out.local(dsilu.at[n, c], dsilu_ref.at[n, c])
            if c == tiles - 1:
                wr_ref[n] = act[n].astype(BF16)
                continue
            rows = slice(c * TILE, (c + 1) * TILE)
            val[n, rows, :] = act[n].T.astype(BF16)
            out.local(val.at[n, rows], val_ref.at[n, rows])
            writers = wr_ref[n, :, :STATE]
            for h in range(c * 4, c * 4 + 4):
                head = slice(h * HEADDIM, (h + 1) * HEADDIM)
                scaled = val[n, head, :].astype(F32) * weight[n, h : h + 1, :]
                send_ref[n, head, :] = nn(scaled.astype(BF16), writers).astype(BF16)
            states.append(outward.remote(send_ref.at[n, rows], come_ref.at[n, rows], other))
    for copy in states:
        copy.wait_recv()
    for copy in outward.copies:
        copy.wait_send()
    for copy in out.copies:
        copy.wait()


def front(weight, tokens, small_rows, segments, dlow):
    rows = weight.shape[0]
    n, length, _ = tokens.shape
    tiles, blocks = XBC // TILE, length // 128
    vmem, hbm = pl.BlockSpec(memory_space=pltpu.VMEM), pl.BlockSpec(memory_space=pl.ANY)
    outs = [
        (hbm, (tiles, 8, rows, TILE), BF16),
        (hbm, (n, length, D), BF16),
        (hbm, (n, D, length), BF16),
        (hbm, (n, tiles, length + HALO, TILE), BF16),
        (hbm, (n, tiles, length, TILE), BF16),
        (hbm, (n, INNER, length), BF16),
        (vmem, (n, length, 2 * STATE), BF16),
        (vmem, (n, HP, length), F32),
        (vmem, (n, HP, length), F32),
        (vmem, (n, INNER, STATE), BF16),
        (vmem, (n, INNER, STATE), BF16),
        (vmem, (CONV + 1, XBC), F32),
        (vmem, (INNER // 128, 128), F32),
        (vmem, (8, 128), F32),
        (vmem, (n, 8, LEAD + length), F32),
    ]
    remote = 1 + 7 * tiles + n * (tiles - 1)
    local = tiles + 2 * n + 2 * n * tiles + n * (tiles - 1)
    return pl.pallas_call(
        front_kernel,
        in_specs=[vmem] * 5,
        out_specs=[spec for spec, _, _ in outs],
        out_shape=[jax.ShapeDtypeStruct(shape, kind) for _, shape, kind in outs],
        scratch_shapes=[
            pltpu.VMEM((tiles, rows, TILE), BF16),
            pltpu.VMEM((n, HALO, D), BF16),
            pltpu.VMEM((n, HALO, D), BF16),
            pltpu.VMEM((tiles, 8, rows, TILE), BF16),
            pltpu.VMEM((1, D), F32),
            pltpu.VMEM((n, length + HALO, D), BF16),
            pltpu.VMEM((n, D, length), BF16),
            pltpu.VMEM((n, tiles, length + HALO, TILE), BF16),
            pltpu.VMEM((n, tiles, length, TILE), BF16),
            pltpu.VMEM((n, INNER, length), BF16),
            pltpu.VMEM((n * blocks, (CONV - 1) * 128, TILE), F32),
            pltpu.VMEM((n, length, TILE), F32),
            pltpu.VMEM((n * blocks, (CONV - 1) * 128, SPAN), BF16),
            pltpu.VMEM((n, HP, length), F32),
            pltpu.SemaphoreType.DMA((local,)),
            pltpu.SemaphoreType.DMA((remote,)),
            pltpu.SemaphoreType.DMA((remote,)),
        ],
        compiler_params=pltpu.CompilerParams(
            collective_id=3, has_side_effects=True, vmem_limit_bytes=VMEM_LIMIT
        ),
        name="front",
    )(weight, tokens, small_rows, segments, dlow)


def chunk_terms(delta, rate, docs):
    own = docs[0:1, :]
    before = docs[BEFORE + 1 : BEFORE + 2, 0:1]
    last = docs[0:1, CH - 1 :]
    decay = -jnp.exp(rate) * delta
    totals = times_mask(decay, triangle(CH))
    end = totals[:, CH - 1 :]
    fade = jnp.exp(totals) * jnp.where(own == before, 1.0, 0.0)
    to_end = jnp.exp(end - totals) * jnp.where(own == last, 1.0, 0.0)
    passing = jnp.exp(end) * jnp.where(last == before, 1.0, 0.0)
    together = square_of(own) == own
    first = lax.broadcasted_iota(jnp.int32, (CH, CH), 0)
    second = lax.broadcasted_iota(jnp.int32, (CH, CH), 1)
    barred = jnp.where(together & (first <= second), 0.0, NEG)
    reach = jnp.where(together & (first >= second), 1.0, 0.0)
    return decay, totals, fade, to_end, passing, barred, reach


def forward_kernel(
    val_ref, w_ref, r_ref, delta_ref, heads_ref, docs_ref, in_ref,
    y_ref, start_ref,
    state, off, fresh,
):
    state[...] = jnp.where(lax.axis_index("seq") == 0, 0.0, in_ref[0].astype(F32))
    rate = column(heads_ref, RATE)
    for k in range(val_ref.shape[2] // CH):
        lanes = slice(k * CH, (k + 1) * CH)
        writers, readers = w_ref[0, lanes, :], r_ref[0, lanes, :]
        delta = delta_ref[0, :, lanes]
        _, totals, fade, to_end, passing, barred, _ = chunk_terms(
            delta, rate, docs_ref[0, :, LEAD + k * CH : LEAD + (k + 1) * CH]
        )
        columns = totals.T
        scores = nt(writers, readers)
        low_state = state[...].astype(BF16)
        start_ref[0, k] = low_state
        off[...] = nt(low_state, readers)
        for h in range(HEADS):
            rows = slice(h * HEADDIM, (h + 1) * HEADDIM)
            mixing = jnp.exp(totals[h : h + 1, :] - columns[:, h : h + 1] + barred) * scores
            scaled = val_ref[0, rows, lanes].astype(F32) * delta[h : h + 1, :]
            fresh[rows, :] = (scaled * to_end[h : h + 1, :]).astype(BF16)
            inside = nn(scaled.astype(BF16), mixing.astype(BF16))
            y_ref[0, rows, lanes] = inside + off[rows, :] * fade[h : h + 1, :]
        gained = nn(fresh[...], writers)
        for h in range(HEADS):
            rows = slice(h * HEADDIM, (h + 1) * HEADDIM)
            state[rows, :] = passing[h : h + 1, :] * state[rows, :] + gained[rows, :]


def forward_scan(values, wr, delta, heads, docs, incoming):
    n, _, length = values.shape
    chunks = length // CH
    return pl.pallas_call(
        forward_kernel,
        grid=(n,),
        in_specs=[
            piece(INNER, length),
            pl.BlockSpec((1, length, STATE), lambda i: (i, 0, 0)),
            pl.BlockSpec((1, length, STATE), lambda i: (i, 0, 1)),
            piece(HP, length),
            whole(heads.shape),
            piece(*docs.shape[1:]),
            piece(INNER, STATE),
        ],
        out_specs=[piece(INNER, length), piece(chunks, INNER, STATE)],
        scratch_shapes=[
            pltpu.VMEM((INNER, STATE), F32),
            pltpu.VMEM((INNER, CH), F32),
            pltpu.VMEM((INNER, CH), BF16),
        ],
        out_shape=[
            jax.ShapeDtypeStruct((n, INNER, length), F32),
            jax.ShapeDtypeStruct((n, chunks, INNER, STATE), BF16),
        ],
        compiler_params=params(("arbitrary",)),
        name="forward_scan",
    )(values, wr, wr, delta, heads, docs, incoming)


def backward_kernel(
    val_ref, w_ref, r_ref, delta_ref, draw_ref, heads_ref, docs_ref, gy_ref, first_ref,
    start_ref, in_ref, final_ref, dsilu_ref, conv_ref, near_ref,
    gval_ref, gwr_ref, gdraw_ref, gheads_ref, ghalo_ref,
    grad, link, off, fresh, faded, gdelta, paid, sums,
):
    n, step = pl.program_id(0), pl.program_id(1)
    rate = column(heads_ref, RATE)

    @pl.when(step == 0)
    def _():
        grad[...] = in_ref[0].astype(F32)
        product = in_ref[0].astype(F32) * final_ref[0].astype(F32)
        by_head = jnp.sum(product.reshape(HEADS, HEADDIM, STATE), axis=1)
        link[0:HEADS, :] = jnp.sum(by_head, axis=1, keepdims=True)
        link[HEADS:, :] = jnp.zeros((HP - HEADS, 1), F32)

    @pl.when((n == 0) & (step == 0))
    def _():
        sums[...] = jnp.zeros_like(sums)

    writers, readers = w_ref[0], r_ref[0]
    delta = delta_ref[0]
    decay, totals, fade, to_end, passing, barred, reach = chunk_terms(delta, rate, docs_ref[0])
    columns = totals.T
    scores = nt(writers, readers)
    low_grad = grad[...].astype(BF16)
    off[...] = nt(low_grad, writers)
    gscores = jnp.zeros((CH, CH), F32)
    gdelta[HEADS:, :] = jnp.zeros((HP - HEADS, CH), F32)
    paid[HEADS:, :] = jnp.zeros((HP - HEADS, CH), F32)
    for h in range(HEADS):
        rows = slice(h * HEADDIM, (h + 1) * HEADDIM)
        spread = jnp.exp(totals[h : h + 1, :] - columns[:, h : h + 1] + barred)
        values = val_ref[0, rows, :].astype(F32)
        gy = gy_ref[0, rows, :]
        gy32 = gy.astype(F32)
        scaled = values * delta[h : h + 1, :]
        fresh[rows, :] = (scaled * to_end[h : h + 1, :]).astype(BF16)
        faded[rows, :] = (gy32 * fade[h : h + 1, :]).astype(BF16)
        gscaled = nt(gy, (spread * scores).astype(BF16)) + off[rows, :] * to_end[h : h + 1, :]
        low = scaled.astype(BF16)
        gscores = gscores + tn(low, gy) * spread
        paid[h : h + 1, :] = jnp.sum(low.astype(F32) * gscaled, axis=0, keepdims=True)
        gdelta[h : h + 1, :] = jnp.sum(values * gscaled, axis=0, keepdims=True)
        gval_ref[0, rows, :] = (
            gscaled * delta[h : h + 1, :] + gy32 * heads_ref[SKIP : SKIP + 1, h : h + 1]
        ).astype(BF16)
    low_scores = gscores.astype(BF16)
    gwr_ref[0, :, :STATE] = nn(low_scores, readers) + tn(fresh[...], low_grad)
    gwr_ref[0, :, STATE:] = tn(low_scores, writers) + tn(faded[...], start_ref[0, 0])
    off[:, :STATE] = nn(faded[...], readers)
    for h in range(HEADS):
        rows = slice(h * HEADDIM, (h + 1) * HEADDIM)
        grad[rows, :] = passing[h : h + 1, :] * grad[rows, :] + off[rows, :STATE]
    following = jnp.where(docs_ref[0, 0:1, :] == docs_ref[0, 1:2, CH - 1 :], 1.0, 0.0)
    gdecay = times_mask(first_ref[0] - paid[...], reach) + following * link[...]
    link[...] = gdecay[:, :1]
    gtotal = gdelta[...] - jnp.exp(rate) * gdecay
    gdraw = gtotal * sigmoid(draw_ref[0])
    gdraw_ref[0] = gdraw
    sums[0] += gdraw
    sums[1] += gdecay * decay

    @pl.when(step == pl.num_programs(1) - 1)
    def _():
        taps = conv_ref[...]
        near = [
            square_of(
                jnp.where(near_ref[0, j : j + 1, :] == near_ref[0, 0:1, :], 1.0, 0.0)
            )[120:, :]
            for j in range(CONV)
        ]
        for c in range(XBC // 128):
            cols = slice(c * 128, (c + 1) * 128)
            if c < INNER // 128:
                here = gval_ref[0, cols, :].astype(F32).T[:8, :]
            else:
                here = gwr_ref[0, 0:8, c * 128 - INNER : c * 128 - INNER + 128]
            left = c * 128 % TILE
            pre = here * dsilu_ref[0, c * 128 // TILE, 0:8, left : left + 128].astype(F32)
            wide = jnp.concatenate([jnp.zeros((8, 128), F32), pre], axis=0)
            total = jnp.zeros((8, 128), F32)
            for j in range(1, CONV):
                total = total + taps[3 - j : 4 - j, cols] * wide[j : j + 8] * near[j]
            ghalo_ref[0, :, cols] = total

    @pl.when((n == pl.num_programs(0) - 1) & (step == pl.num_programs(1) - 1))
    def _():
        for i in range(2):
            both = jnp.concatenate([sums[i], jnp.zeros((128 - HP, CH), F32)], axis=0)
            gheads_ref[i : i + 1, :] = jnp.sum(both.T, axis=0, keepdims=True)
        gheads_ref[2:, :] = jnp.zeros((6, 128), F32)


def backward_scan(
    values, wr, delta, draw, heads, docs, gy, first, starts, incoming, final, dsilu, conv
):
    n, _, length = values.shape
    chunks = length // CH
    back = lambda k: chunks - 1 - k
    lanes = lambda rows: pl.BlockSpec((1, rows, CH), lambda i, k: (i, 0, back(k)))
    return pl.pallas_call(
        backward_kernel,
        grid=(n, chunks),
        in_specs=[
            lanes(INNER),
            pl.BlockSpec((1, CH, STATE), lambda i, k: (i, back(k), 0)),
            pl.BlockSpec((1, CH, STATE), lambda i, k: (i, back(k), 1)),
            lanes(HP),
            lanes(HP),
            whole(heads.shape, 2),
            pl.BlockSpec((1, 8, CH), lambda i, k: (i, 0, back(k) + LEAD // CH)),
            lanes(INNER),
            lanes(HP),
            pl.BlockSpec((1, 1, INNER, STATE), lambda i, k: (i, back(k), 0, 0)),
            pl.BlockSpec((1, INNER, STATE), lambda i, k: (i, 0, 0)),
            pl.BlockSpec((1, INNER, STATE), lambda i, k: (i, 0, 0)),
            pl.BlockSpec((1, XBC // TILE, 16, TILE), lambda i, k: (i, 0, 0, 0)),
            whole(conv.shape, 2),
            pl.BlockSpec((1, 8, 128), lambda i, k: (i, 0, 0)),
        ],
        out_specs=[
            lanes(INNER),
            pl.BlockSpec((1, CH, 2 * STATE), lambda i, k: (i, back(k), 0)),
            lanes(HP),
            pl.BlockSpec((8, 128), lambda i, k: (0, 0)),
            pl.BlockSpec((1, 8, XBC), lambda i, k: (i, 0, 0)),
        ],
        scratch_shapes=[
            pltpu.VMEM((INNER, STATE), F32),
            pltpu.VMEM((HP, 1), F32),
            pltpu.VMEM((INNER, CH), F32),
            pltpu.VMEM((INNER, CH), BF16),
            pltpu.VMEM((INNER, CH), BF16),
            pltpu.VMEM((HP, CH), F32),
            pltpu.VMEM((HP, CH), F32),
            pltpu.VMEM((2, HP, CH), F32),
        ],
        out_shape=[
            jax.ShapeDtypeStruct((n, INNER, length), BF16),
            jax.ShapeDtypeStruct((n, length, 2 * STATE), F32),
            jax.ShapeDtypeStruct((n, HP, length), F32),
            jax.ShapeDtypeStruct((8, 128), F32),
            jax.ShapeDtypeStruct((n, 8, XBC), F32),
        ],
        compiler_params=params(("arbitrary", "arbitrary")),
        name="backward_scan",
    )(
        values, wr, wr, delta, draw, heads, docs, gy, first, starts, incoming, final, dsilu,
        conv, docs,
    )


def leave_kernel(group, packed, *refs):
    if packed:
        weights_ref, *refs = refs
        *refs, wgate_ref, wout_ref, loaded = refs
    else:
        wgate_ref, wout_ref, *refs = refs
    (
        normed_ref, turned_ref, cot_ref, tok_ref, y_ref, val_ref, r_ref, gain_ref, delta_ref,
        heads_ref, docs_ref,
        out_ref, gy_ref, gnorm_ref, first_ref, gstate_ref, grads_ref, ggain_ref, gskip_ref,
        gate, gated, upward, lifted, faded, flat, total_out, total_gate, products, skips, gains,
        wide_gain, fade, total_state,
    ) = refs
    n, k = pl.program_id(0), pl.program_id(1)
    begin = (n == 0) & (k == 0)
    end = (n == pl.num_programs(0) - 1) & (k == pl.num_programs(1) - 1)
    length = delta_ref.shape[2]
    rows_out, rows_in = INNER // group, D // group
    tiles = INNER // TILE
    lanes = range(0, ROWS, 128)
    down = lambda s: jnp.sum(s, axis=0, keepdims=True)

    def fold(v):
        return jnp.sum(v.reshape(v.shape[0] // 8, 8, 128), axis=0)

    def loads():
        copies = []
        for p in range(group):
            for q, ref, at, left in (
                (2, wgate_ref, p * rows_in, 0), (3, wgate_ref, p * rows_in, D),
                (0, wout_ref, p * rows_out, 0), (1, wout_ref, p * rows_out + rows_in, 0),
            ):
                copies.append(
                    pltpu.make_async_copy(
                        weights_ref.at[p, q],
                        ref.at[pl.ds(at, rows_in), pl.ds(left, D)],
                        loaded.at[len(copies)],
                    )
                )
        return copies

    @pl.when(begin)
    def _():
        if packed:
            for copy in loads():
                copy.start()
        total_out[...] = jnp.zeros_like(total_out)
        total_gate[...] = jnp.zeros_like(total_gate)
        skips[...] = jnp.zeros_like(skips)
        gains[...] = jnp.zeros_like(gains)
        for q in range(INNER // 128):
            wide_gain[q * 128 : (q + 1) * 128, :] = square_of(gain_ref[q : q + 1, :])

    @pl.when(k == 0)
    def _():
        own = docs_ref[0, 0:1, LEAD:]
        before = docs_ref[0, BEFORE + 1 : BEFORE + 2, LEAD : LEAD + 1]
        totals = times_mask(-jnp.exp(column(heads_ref, RATE)) * delta_ref[0], triangle(length))
        fade[...] = jnp.exp(totals) * jnp.where(own == before, 1.0, 0.0)
        total_state[...] = jnp.zeros_like(total_state)

    if packed:

        @pl.when(begin)
        def _():
            for copy in loads():
                copy.wait()

    here = pl.ds(pl.multiple_of(k * ROWS, ROWS), ROWS)

    def span(c):
        return slice(c * TILE, (c + 1) * TILE)

    def head_rows(h):
        return slice(h * HEADDIM, (h + 1) * HEADDIM)

    def open_tile(c):
        if c < tiles:
            gate[span(c), :] = nn(normed_ref[0], wgate_ref[:, span(c)]).T.astype(BF16)
            upward[span(c), :] = nt(wout_ref[span(c), :], cot_ref[0])

    squares = [jnp.zeros((8, 128), F32) for _ in lanes]
    dots = [jnp.zeros((8, 128), F32) for _ in lanes]
    open_tile(0)
    for c in range(tiles):
        open_tile(c + 1)
        for h in range(c * 4, c * 4 + 4):
            rows = head_rows(h)
            skip = heads_ref[SKIP : SKIP + 1, h : h + 1]
            gain = wide_gain[rows, :]
            for i, b in enumerate(lanes):
                g = gate[rows, b : b + 128].astype(F32)
                values = val_ref[0, rows, b : b + 128].astype(F32)
                v = (y_ref[0, rows, b : b + 128] + skip * values) * (g * sigmoid(g))
                gated[rows, b : b + 128] = v
                squares[i] = squares[i] + fold(v * v)
                dots[i] = dots[i] + fold(upward[rows, b : b + 128] * gain * v)
    scale = [lax.rsqrt(down(s) * (1.0 / INNER) + EPS) for s in squares]
    pull = [s * s * s * down(d) * (1.0 / INNER) for s, d in zip(scale, dots)]

    def close_tile(c):
        low = lifted[span(c), :]
        flat[:, span(c)] = low.T
        total_out[span(c), :] += nn(low, cot_ref[0])
        total_gate[:, span(c)] += nt(turned_ref[0], gate[span(c), :])
        total_state[span(c), :] += nn(faded[c % 2], r_ref[0])

    for c in range(tiles):
        if c > 0:
            close_tile(c - 1)
        for h in range(c * 4, c * 4 + 4):
            eight = slice(h * 8, h * 8 + 8)
            skip = heads_ref[SKIP : SKIP + 1, h : h + 1]
            fading = fade[h : h + 1, here]
            sums = jnp.zeros((8, 128), F32)
            product = [jnp.zeros((8, 128), F32) for _ in lanes]
            for at in range(h * HEADDIM, (h + 1) * HEADDIM, SUB):
                rows = slice(at, at + SUB)
                inner = slice(at - c * TILE, at - c * TILE + SUB)
                gain = wide_gain[rows, :]
                gain_sums = gains[rows, :]
                for i, b in enumerate(lanes):
                    v = gated[rows, b : b + 128]
                    u = upward[rows, b : b + 128]
                    normal = v * scale[i]
                    lifted[rows, b : b + 128] = (normal * gain).astype(BF16)
                    gain_sums = gain_sums + u * normal
                    gv = scale[i] * (u * gain) - pull[i] * v
                    g = gate[rows, b : b + 128].astype(F32)
                    sig = sigmoid(g)
                    silu = g * sig
                    low = (gv * silu).astype(BF16)
                    gy_ref[0, rows, b : b + 128] = low
                    gm = low.astype(F32)
                    faded[c % 2, inner, b : b + 128] = (gm * fading[:, b : b + 128]).astype(BF16)
                    values = val_ref[0, rows, b : b + 128].astype(F32)
                    sums = sums + fold(gm * values)
                    y = y_ref[0, rows, b : b + 128]
                    product[i] = product[i] + fold(gm * y)
                    gate[rows, b : b + 128] = (
                        gv * (y + skip * values) * (sig + silu * (1.0 - sig))
                    ).astype(BF16)
                gains[rows, :] = gain_sums
            for i, b in enumerate(lanes):
                products[eight, b : b + 128] = product[i]
            skips[eight, :] += sums
    close_tile(tiles - 1)
    for b in range(0, D, TILE):
        branch = nn(flat[...], wout_ref[:, b : b + TILE])
        out_ref[0, :, b : b + TILE] = (tok_ref[0, :, b : b + TILE].astype(F32) + branch).astype(BF16)
    for b in range(0, D, TILE):
        gnorm_ref[0, b : b + TILE, :] = nn(wgate_ref[b : b + TILE, :], gate[...]).astype(BF16)
    first_ref[0, 0:HEADS, :] = jnp.sum(products[...].reshape(HEADS, 8, ROWS), axis=1)
    first_ref[0, HEADS:, :] = jnp.zeros((HP - HEADS, ROWS), F32)

    @pl.when(k == pl.num_programs(1) - 1)
    def _():
        gstate_ref[0] = total_state[...].astype(BF16)

    @pl.when(end)
    def _():
        for p in range(group):
            grads_ref[p, :rows_out, :] = total_out[p * rows_out : (p + 1) * rows_out, :].astype(BF16)
            for half in range(2):
                at = rows_out + half * rows_in
                grads_ref[p, at : at + rows_in, :] = total_gate[
                    p * rows_in : (p + 1) * rows_in, half * D : (half + 1) * D
                ].astype(BF16)
        for q in range(INNER // 128):
            ggain_ref[q : q + 1, :] = down(gains[q * 128 : (q + 1) * 128, :].T)
        ggain_ref[INNER // 128 :, :] = jnp.zeros((16 - INNER // 128, 128), F32)
        by_head = jnp.sum(skips[...].reshape(HEADS, 8, 128), axis=1)
        by_head = jnp.concatenate([by_head, jnp.zeros((128 - HEADS, 128), F32)], axis=0)
        gskip_ref[0:1, :] = down(by_head.T)
        gskip_ref[1:, :] = jnp.zeros((7, 128), F32)


def leave(weights, normed, turned, cot, tokens, y, values, wr, gain, delta, heads, docs):
    n, length, _ = normed.shape
    group, _, rows_in, _ = weights.shape
    packed = rows_in % 16 == 0
    if packed:
        weights, loaded = [weights], [pl.BlockSpec(memory_space=pl.ANY)]
        scratch = [
            pltpu.VMEM((D, INNER), BF16),
            pltpu.VMEM((INNER, D), BF16),
            pltpu.SemaphoreType.DMA((4 * group,)),
        ]
    else:
        gate = jnp.concatenate([weights[:, 2], weights[:, 3]], axis=-1).reshape(D, INNER)
        weights = [gate, weights[:, :2].reshape(INNER, D)]
        loaded, scratch = [whole(a.shape, 2) for a in weights], []
    grads = (group, 4 * rows_in, D)
    rows = lambda width: pl.BlockSpec((1, ROWS, width), lambda i, k: (i, k, 0))
    lanes = lambda height: pl.BlockSpec((1, height, ROWS), lambda i, k: (i, 0, k))
    each = lambda *shape: pl.BlockSpec((1,) + shape, lambda i, k: (i, 0, 0))
    return pl.pallas_call(
        partial(leave_kernel, group, packed),
        grid=(n, length // ROWS),
        in_specs=loaded + [
            rows(D), lanes(D), rows(D), rows(D), lanes(INNER), lanes(INNER),
            pl.BlockSpec((1, ROWS, STATE), lambda i, k: (i, k, 1)),
            whole(gain.shape, 2), each(HP, length), whole(heads.shape, 2), each(*docs.shape[1:]),
        ],
        out_specs=[
            rows(D), lanes(INNER), lanes(D), lanes(HP), each(INNER, STATE), whole(grads, 2),
            whole((16, 128), 2), whole((8, 128), 2),
        ],
        scratch_shapes=[
            pltpu.VMEM((INNER, ROWS), BF16),
            pltpu.VMEM((INNER, ROWS), F32),
            pltpu.VMEM((INNER, ROWS), F32),
            pltpu.VMEM((INNER, ROWS), BF16),
            pltpu.VMEM((2, TILE, ROWS), BF16),
            pltpu.VMEM((ROWS, INNER), BF16),
            pltpu.VMEM((INNER, D), F32),
            pltpu.VMEM((D, INNER), F32),
            pltpu.VMEM((HEADS * 8, ROWS), F32),
            pltpu.VMEM((HEADS * 8, 128), F32),
            pltpu.VMEM((INNER, 128), F32),
            pltpu.VMEM((INNER, 128), F32),
            pltpu.VMEM((HP, length), F32),
            pltpu.VMEM((INNER, STATE), F32),
        ] + scratch,
        out_shape=[
            jax.ShapeDtypeStruct((n, length, D), BF16),
            jax.ShapeDtypeStruct((n, INNER, length), BF16),
            jax.ShapeDtypeStruct((n, D, length), BF16),
            jax.ShapeDtypeStruct((n, HP, length), F32),
            jax.ShapeDtypeStruct((n, INNER, STATE), BF16),
            jax.ShapeDtypeStruct(grads, BF16),
            jax.ShapeDtypeStruct((16, 128), F32),
            jax.ShapeDtypeStruct((8, 128), F32),
        ],
        compiler_params=params(("arbitrary", "arbitrary")),
        name="leave",
    )(*weights, normed, turned, cot, tokens, y, values, wr, gain, delta, heads, docs)


def exit_kernel(
    gval_ref, gwr_ref, dsilu_ref, raw_ref, docs_ref, conv_ref, back_ref, normed_ref, turned_ref,
    wraw_ref, gdraw_ref, dlow_ref, gnorm_ref, tok_ref, cot_ref, gain_ref,
    grad_ref, graw_ref, gdelta_ref, ggain_ref, gconv_ref,
    pre, low_pre, moved, halo_terms, shift, low, lifted, total, sums,
):
    n = pl.program_id(0)
    length = dsilu_ref.shape[2]
    last = n == pl.num_programs(0) - 1

    @pl.when(n == 0)
    def _():
        total[...] = jnp.zeros_like(total)
        sums[...] = jnp.zeros_like(sums)
        gdelta_ref[...] = jnp.zeros_like(gdelta_ref)
        ggain_ref[...] = jnp.zeros_like(ggain_ref)

    def shifts(rows, extent, near):
        first = lax.broadcasted_iota(jnp.int32, (rows, extent), 0)
        second = lax.broadcasted_iota(jnp.int32, (rows, extent), 1)
        return [
            jnp.where(second == first + j, near[j - 1], 0.0).astype(BF16) for j in range(1, CONV)
        ]

    near = [
        jnp.where(docs_ref[0, j : j + 1, :] == docs_ref[0, 0:1, :], 1.0, 0.0)
        for j in range(1, CONV)
    ]
    for i in range(length // 128):
        square = [square_of(v[:, LEAD + i * 128 : LEAD + i * 128 + 128]) for v in near]
        square = [jnp.concatenate([v, v[:, : SPAN - 128]], axis=1) for v in square]
        shift[i] = jnp.concatenate(shifts(128, SPAN, square), axis=0)
    square = [square_of(v[:, LEAD - 128 : LEAD])[128 - HALO :, : 2 * HALO] for v in near]
    ahead = jnp.concatenate(shifts(HALO, 2 * HALO, square), axis=0)
    for slot in range(2):
        low_pre[slot, :HALO, :] = jnp.zeros((HALO, TILE), BF16)
        low_pre[slot, HALO + length :, :] = jnp.zeros((HALO, TILE), BF16)
    tiles = XBC // TILE
    blocks = length // 128

    def span_of(c):
        return slice(c * TILE, (c + 1) * TILE)

    def open_tile(c):
        if c == tiles:
            return
        if c < INNER // TILE:
            here = gval_ref[0, span_of(c), :].astype(F32).T
        else:
            here = gwr_ref[0]
        here = here * dsilu_ref[0, c].astype(F32)
        pre[c % 2] = here
        low_pre[c % 2, HALO : HALO + length, :] = here.astype(BF16)
        halo_terms[c % 2] = nn(ahead, low_pre[c % 2, : 2 * HALO, :])
        for i in range(blocks):
            moved[c % 2 * blocks + i] = nn(
                shift[i], low_pre[c % 2, HALO + i * 128 : HALO + i * 128 + SPAN, :]
            )

    def close_tile(c):
        total[:, span_of(c)] += nn(turned_ref[0], low[c % 2])
        through = nt(low[c % 2], wraw_ref[c])
        if c == 0:
            lifted[...] = through
        else:
            lifted[...] += through

    def fold(v):
        return jnp.sum(v.reshape(v.shape[0] // 8, 8, 128), axis=0)

    open_tile(0)
    for c in range(tiles):
        slot = c % 2
        open_tile(c + 1)
        if c > 0:
            close_tile(c - 1)
        for half in range(0, TILE, 128):
            cols = slice(half, half + 128)
            wide = slice(c * TILE + half, c * TILE + half + 128)
            w = conv_ref[:, wide]
            folded = [sums[k, :, wide] for k in range(CONV + 1)]
            raw = raw_ref[0, c, :HALO, cols].astype(F32)
            for j in range(1, CONV):
                term = halo_terms[slot, (j - 1) * HALO : j * HALO, cols]
                folded[3 - j] = folded[3 - j] + fold(raw * term)
            for b in range(0, length, 64):
                raw = raw_ref[0, c, HALO + b : HALO + b + 64, cols].astype(F32)
                now = pre[slot, b : b + 64, cols]
                grad = w[3:4] * now
                folded[3] = folded[3] + fold(raw * now)
                folded[4] = folded[4] + fold(now)
                for j in range(1, CONV):
                    at = (j - 1) * 128 + b % 128
                    term = moved[slot * blocks + b // 128, at : at + 64, cols]
                    grad = grad + w[3 - j : 4 - j] * term
                    folded[3 - j] = folded[3 - j] + fold(raw * term)
                if b == length - 64:
                    grad = jnp.concatenate([grad[:56], grad[56:] + back_ref[0, :, wide]], axis=0)
                low[slot, b : b + 64, cols] = grad.astype(BF16)
            for k in range(CONV + 1):
                sums[k, :, wide] = folded[k]
    close_tile(tiles - 1)

    gdraw = gdraw_ref[0].astype(BF16)
    gdelta_ref[...] += nn(gdraw, normed_ref[0])
    gain = gain_ref[...]
    gains = jnp.zeros((8, D), F32)
    for b in range(0, length, 128):
        rows = slice(b, b + 128)
        up = lifted[rows, :] + gnorm_ref[0, :, rows].astype(F32).T + tn(gdraw[:, rows], dlow_ref[...])
        x = tok_ref[0, rows, :].astype(F32)
        scale = lax.rsqrt(jnp.mean(x * x, axis=-1, keepdims=True) + EPS)
        normal = x * scale
        gains = gains + jnp.sum((up * normal).reshape(16, 8, D), axis=0)
        up = up * gain
        inner = jnp.mean(up * normal, axis=-1, keepdims=True)
        grad = cot_ref[0, rows, :].astype(F32) + scale * (up - normal * inner)
        grad_ref[0, rows, :] = grad.astype(BF16)
    ggain_ref[0:1, :] += jnp.sum(gains, axis=0, keepdims=True)

    @pl.when(last)
    def _():
        graw_ref[...] = total[...].astype(BF16)
        gconv_ref[0 : CONV + 1, :] = jnp.sum(sums[...], axis=1)


def leave_back(
    gval, gwr, dsilu, raw, docs, conv, back, normed, turned, wraw, gdraw, dlow, gnorm, tokens,
    cotangent, gain,
):
    n, length, _ = tokens.shape
    return pl.pallas_call(
        exit_kernel,
        grid=(n,),
        in_specs=[
            piece(INNER, length), piece(length, 2 * STATE), piece(XBC // TILE, length, TILE),
            piece(XBC // TILE, length + HALO, TILE), piece(*docs.shape[1:]), whole(conv.shape), piece(8, XBC),
            piece(length, D), piece(D, length), whole(wraw.shape), piece(HP, length),
            whole(dlow.shape), piece(D, length), piece(length, D), piece(length, D),
            whole(gain.shape),
        ],
        out_specs=[
            piece(length, D), whole((D, XBC)), whole((HP, D)), whole((8, D)), whole((8, XBC)),
        ],
        out_shape=[
            jax.ShapeDtypeStruct((n, length, D), BF16),
            jax.ShapeDtypeStruct((D, XBC), BF16),
            jax.ShapeDtypeStruct((HP, D), F32),
            jax.ShapeDtypeStruct((8, D), F32),
            jax.ShapeDtypeStruct((8, XBC), F32),
        ],
        scratch_shapes=[
            pltpu.VMEM((2, length, TILE), F32),
            pltpu.VMEM((2, length + 2 * HALO, TILE), BF16),
            pltpu.VMEM((2 * (length // 128), (CONV - 1) * 128, TILE), F32),
            pltpu.VMEM((2, (CONV - 1) * HALO, TILE), F32),
            pltpu.VMEM((length // 128, (CONV - 1) * 128, SPAN), BF16),
            pltpu.VMEM((2, length, TILE), BF16),
            pltpu.VMEM((length, D), F32),
            pltpu.VMEM((D, XBC), F32),
            pltpu.VMEM((CONV + 1, 8, XBC), F32),
        ],
        compiler_params=params(("arbitrary",)),
        name="leave_back",
    )(
        gval, gwr, dsilu, raw, docs, conv, back, normed, turned, wraw, gdraw, dlow, gnorm, tokens,
        cotangent, gain,
    )


def tiles_of(extent):
    return -(-extent // 128)


def pieces_of(rows):
    return [(i, i * 128, min(128, rows - i * 128)) for i in range(tiles_of(rows))]


def split_three(v):
    high = v.astype(BF16)
    rest = v - high.astype(F32)
    middle = rest.astype(BF16)
    low = (rest - middle.astype(F32)).astype(BF16)
    return jnp.concatenate([high, middle, low], axis=0)


def join_three(v):
    return v[0:8] + v[8:16] + v[16:24]


def inverse_factor(gram):
    rows = lax.broadcasted_iota(jnp.int32, (8, 8), 0)
    cols = lax.broadcasted_iota(jnp.int32, (8, 8), 1)
    left, right = gram, jnp.where(rows == cols, 1.0, 0.0)
    for j in range(7):
        factor = jnp.where(rows[:, :1] > j, left[:, j : j + 1] / left[j : j + 1, j : j + 1], 0.0)
        left, right = left - factor * left[j : j + 1, :], right - factor * right[j : j + 1, :]
    pivots = jnp.sum(jnp.where(rows == cols, left, 0.0), axis=1, keepdims=True)
    return right * lax.rsqrt(pivots)


RIGHT_OUT = PROJ // 128
DELTA = RIGHT_OUT + D // 128
REST = DELTA + HEADS // 8 * (D // 128)
REST_ROWS = D // 128 + (CONV + 1) * (XBC // 128) + INNER // 128 + 3
SUMMED = REST + -(-REST_ROWS // 8)


class Scatter:
    def __init__(self, group, x_ref, from_core, pairs, from_far, joint, send, recv):
        self.nf = group // 2
        self.x_ref, self.from_core, self.pairs, self.from_far = x_ref, from_core, pairs, from_far
        self.joint, self.send, self.recv = joint, send, recv
        self.r, self.f, self.s = (lax.axis_index(name) for name in ("rep", "fsdp", "seq"))
        self.copies = []
        half = x_ref.shape[1] // 2
        self.parts = [slice(0, half), slice(half, 2 * half)]
        f = self.f
        if self.nf == 4:
            x, y = f + 1 - 2 * lax.rem(f, 2), lax.rem(f + 2, 4)
            self.order = [lax.rem(x + 2, 4), x, y, f]
        else:
            self.order = [lax.rem(f + 1 + j, self.nf) for j in range(self.nf)]

    def start(self, src, dst, device):
        k = len(self.copies)
        copy = pltpu.make_async_remote_copy(
            src, dst, self.send.at[k], self.recv.at[k], device_id=device, device_id_type=MESH
        )
        copy.start()
        self.copies.append(copy)
        return copy

    def begin(self):
        other = (self.r, self.f, 1 - self.s)
        self.near = [
            self.start(self.x_ref.at[f * 2 + 1 - self.s], self.from_core.at[j], other)
            for j, f in enumerate(self.order)
        ]

    def device(self, j):
        return (self.r, self.order[j], self.s)

    def cross(self):
        self.far = []
        for j, f in enumerate(self.order):
            self.near[j].wait_recv()
            total = self.x_ref[f * 2 + self.s].astype(F32) + self.from_core[j].astype(F32)
            self.pairs[j] = total.astype(BF16)
            if self.nf != 4 and j < self.nf - 1:
                self.far.append(self.start(self.pairs.at[j], self.from_far.at[j], self.device(j)))
            if self.nf == 4 and j < 3:
                for half, part in enumerate(self.parts):
                    if j == 0 or half == j - 1:
                        to = half + 1 if j == 0 else j
                        self.far.append(
                            self.start(
                                self.pairs.at[j, part], self.from_far.at[j, part], self.device(to)
                            )
                        )

    def turn(self):
        if self.nf != 4:
            return
        for half, part in enumerate(self.parts):
            self.far[half].wait_recv()
            to = 2 - half
            total = self.pairs[to, part].astype(F32) + self.from_far[0, part].astype(F32)
            self.joint[half] = total.astype(BF16)
            self.far.append(
                self.start(self.joint.at[half], self.from_far.at[to, part], self.device(to))
            )

    def end(self, o_ref):
        if self.nf == 4:
            for copy in self.far[2:]:
                copy.wait_recv()
            total = self.pairs[3].astype(F32)
            for j in (1, 2):
                total = total + self.from_far[j].astype(F32)
        else:
            total = self.pairs[self.nf - 1].astype(F32)
            for j, copy in enumerate(self.far):
                copy.wait_recv()
                total = total + self.from_far[j].astype(F32)
        o_ref[...] = total
        for copy in self.copies:
            copy.wait_send()


class Exchange:
    def __init__(self, group, replicas):
        self.group, self.replicas = group, replicas
        r, f, s = lax.axis_index("rep"), lax.axis_index("fsdp"), lax.axis_index("seq")
        self.r, self.me = r, f * 2 + s
        self.peers = []
        for j in range(1, group):
            p = lax.rem(self.me + j, group)
            self.peers.append((p, (r, lax.div(p, 2), lax.rem(p, 2))))
        self.others = [(lax.rem(r + j, replicas), f, s) for j in range(1, replicas)]

    def greet(self):
        barrier = pltpu.get_barrier_semaphore()
        for device in [d for _, d in self.peers] + self.others:
            pl.semaphore_signal(barrier, inc=1, device_id=device, device_id_type=MESH)

    def met(self):
        pl.semaphore_wait(pltpu.get_barrier_semaphore(), self.group + self.replicas - 2)

    def sum(self, x_ref, o_ref, own, from_group, from_reps, send, recv, second=None, third=None):
        group, replicas, me = self.group, self.replicas, self.me
        width = own.shape[0]
        copies = []

        def start(src, dst, device):
            k = len(copies)
            copy = pltpu.make_async_remote_copy(
                src, dst, send.at[k], recv.at[k], device_id=device, device_id_type=MESH
            )
            copy.start()
            copies.append(copy)
            return copy

        arriving = [
            start(x_ref.at[pl.ds(p * width, width)], from_group.at[j], device)
            for j, (p, device) in enumerate(self.peers)
        ]
        total = x_ref[pl.ds(me * width, width)]
        for j, copy in enumerate(arriving):
            copy.wait_recv()
            total = total + from_group[j]
        own[...] = total
        from_reps[pl.ds(self.r, 1)] = total[None]
        arriving = [start(own, from_reps.at[self.r], device) for device in self.others]
        if second is not None:
            second()
        for copy in arriving:
            copy.wait_recv()
        total = from_reps[0]
        for j in range(1, replicas):
            total = total + from_reps[j]
        mine = pl.ds(me * width, width)
        o_ref[mine] = total
        arriving = [start(o_ref.at[mine], o_ref.at[mine], device) for _, device in self.peers]
        if third is not None:
            third()
        for copy in arriving:
            copy.wait_recv()
        for copy in copies:
            copy.wait_send()


def compress_kernel(
    group, replicas,
    sin_ref, sout_ref, grads_ref, raw_ref, ein_ref, eout_ref, gdelta_ref, ggain_ref,
    gconv_ref, ggate_ref, gheads_ref, gskip_ref,
    sum_ref, left_in_ref, left_out_ref, turned_in_ref, turned_out_ref, raw_total_ref,
    lefts, left_sums, hat, rights,
    own_a, group_a, reps_a, own_b, group_b, reps_b, send_a, recv_a, send_b, recv_b,
    from_core, pairs, from_far, joint, send_c, recv_c, held_raw, held_grads, held_in, held_out,
    split_in, split_out, load,
):
    rows_in, rows_out = ein_ref.shape[0], eout_ref.shape[0]
    out_part = slice(0, rows_out)
    gate_parts = [slice(rows_out + i * rows_in, rows_out + (i + 1) * rows_in) for i in range(2)]
    ahead = tiles_of(rows_in)
    width = ahead + tiles_of(rows_out)
    exchange = Exchange(group, replicas)
    exchange.greet()
    loads = [
        pltpu.make_async_copy(src, dst, load.at[k])
        for k, (src, dst) in enumerate(
            ((ein_ref, held_in), (eout_ref, held_out), (grads_ref, held_grads), (raw_ref, held_raw))
        )
    ]
    for copy in loads:
        copy.start()
    raw_ref, grads_ref = held_raw, held_grads

    lefts[...] = jnp.zeros_like(lefts)
    mine = pl.ds(exchange.me * width, width)

    def place(index, values, rows, first):
        for i, at, n in pieces_of(rows):
            lefts[index + first + i, :, :n] += values[:, at : at + n]

    def place_own(values, rows, first):
        for i, at, n in pieces_of(rows):
            part = values[:, at : at + n]
            if n < 128:
                part = jnp.concatenate([part, jnp.zeros((8, 128 - n), F32)], axis=1)
            where = pl.ds(exchange.me * width + first + i, 1)
            lefts[where] = lefts[where] + part[None]

    s_in, s_out = split_three(sin_ref[...]), split_three(sout_ref[...])
    for k, (held, split, start, rows, first) in enumerate(
        ((held_in, split_in, s_in, rows_in, 0), (held_out, split_out, s_out, rows_out, ahead))
    ):
        loads[k].wait()
        high = held[...].astype(BF16)
        split[0] = high
        split[1] = (held[...] - high.astype(F32)).astype(BF16)
        place_own(join_three(nt(start, split[0]) + nt(start, split[1])), rows, first)
    loads[2].wait()
    for p in range(group):
        product = nt(s_in[:, :D], grads_ref[p, gate_parts[0]])
        product = product + nt(s_in[:, D:INNER], grads_ref[p, gate_parts[1]])
        place(p * width, join_three(product), rows_in, 0)
        place(p * width, join_three(nt(s_out, grads_ref[p, out_part])), rows_out, ahead)
    loads[3].wait()
    exchange.met()
    scatter = Scatter(group, raw_ref, from_core, pairs, from_far, joint, send_c, recv_c)
    scatter.begin()
    for p in range(group):
        place(p * width, join_three(nt(s_in[:, INNER:], raw_ref[p])), rows_in, 0)
    exchange.sum(
        lefts, left_sums, own_a, group_a, reps_a, send_a, recv_a, scatter.cross, scatter.turn
    )

    for first, last in ((0, ahead), (ahead, width)):
        gram = jnp.zeros((8, 8), F32)
        for p in range(group):
            for i in range(first, last):
                tile = left_sums[p * width + i] * (1.0 / replicas)
                gram = gram + nt_high(tile, tile)
        inverse = inverse_factor(gram)
        for p in range(group):
            for i in range(first, last):
                hat[p * width + i] = nn_high(inverse, left_sums[p * width + i] * (1.0 / replicas))
    own = hat[mine]
    for first, rows, left_ref, turned_ref in (
        (0, rows_in, left_in_ref, turned_in_ref), (ahead, rows_out, left_out_ref, turned_out_ref)
    ):
        for i, at, n in pieces_of(rows):
            turned_ref[:, at : at + n] = own[first + i][:, :n]
            left_ref[at : at + n, :] = own[first + i].T[:n, :]

    def joined(tiles, start, rows):
        return jnp.concatenate([tiles[start + i][:, :n] for i, _, n in pieces_of(rows)], axis=1)

    def product(matrices, rows, skipped, error, at):
        spread = [split_three(joined(hat, p * width + skipped, rows)) for p in range(group)]
        mixed = split_three(joined(own, skipped, rows))
        columns = 0
        for ref, part, extent in matrices:
            for b in range(0, extent, TILE):
                total = nn(spread[0], ref[0, part, b : b + TILE])
                for p in range(1, group):
                    total = total + nn(spread[p], ref[p, part, b : b + TILE])
                here = columns + b
                total = total + nn(mixed, error[0, :, here : here + TILE])
                total = total + nn(mixed, error[1, :, here : here + TILE])
                right = join_three(total)
                for half in range(0, TILE, 128):
                    rights[at + (here + half) // 128] = right[:, half : half + 128]
            columns += extent

    every = slice(0, rows_in)
    product(
        [(grads_ref, part, D) for part in gate_parts] + [(raw_ref, every, XBC)],
        rows_in, 0, split_in, 0,
    )
    product([(grads_ref, out_part, D)], rows_out, ahead, split_out, RIGHT_OUT)
    for g in range(HEADS // 8):
        for q in range(D // 128):
            rights[DELTA + g * (D // 128) + q] = gdelta_ref[
                g * 8 : g * 8 + 8, q * 128 : q * 128 + 128
            ]
    rights[REST:] = jnp.zeros((rights.shape[0] - REST, 8, 128), F32)
    rest = [ggain_ref[0:1, q * 128 : q * 128 + 128] for q in range(D // 128)]
    for k in range(CONV + 1):
        rest += [gconv_ref[k : k + 1, q * 128 : q * 128 + 128] for q in range(XBC // 128)]
    rest += [ggate_ref[q : q + 1, :] for q in range(INNER // 128)]
    rest += [gheads_ref[0:1, :], gheads_ref[1:2, :], gskip_ref[0:1, :]]
    for i in range(0, REST_ROWS, 8):
        eight = rest[i : i + 8]
        rights[REST + i // 8, : len(eight), :] = jnp.concatenate(eight, axis=0)
    exchange.sum(rights, sum_ref, own_b, group_b, reps_b, send_b, recv_b)
    scatter.end(raw_total_ref)


def compress(starts, grads, raw, errors, smalls):
    group = grads.shape[0]
    replicas = lax.axis_size("rep")
    raw = raw.reshape(group, D // group, XBC)
    rows_in, rows_out = errors[0].shape[0], errors[1].shape[0]
    width = tiles_of(rows_in) + tiles_of(rows_out)
    block = (rows_in, XBC)
    share = -(-SUMMED // group)
    dma = pltpu.SemaphoreType.DMA((2 * (group - 1) + replicas - 1,))
    tiles = lambda *n: pltpu.VMEM(n + (8, 128), F32)
    vmem = pl.BlockSpec(memory_space=pltpu.VMEM)
    arrays = [*starts, grads, raw, *errors, *smalls]
    return pl.pallas_call(
        partial(compress_kernel, group, replicas),
        out_shape=[
            jax.ShapeDtypeStruct((group * share, 8, 128), F32),
            jax.ShapeDtypeStruct((rows_in, 8), F32),
            jax.ShapeDtypeStruct((rows_out, 8), F32),
            jax.ShapeDtypeStruct((8, rows_in), F32),
            jax.ShapeDtypeStruct((8, rows_out), F32),
            jax.ShapeDtypeStruct((rows_in, XBC), F32),
        ],
        in_specs=[vmem] * 2 + [pl.BlockSpec(memory_space=pl.ANY)] * 4 + [vmem] * len(smalls),
        out_specs=[vmem] * 6,
        scratch_shapes=[
            tiles(group * width), tiles(group * width), tiles(group * width),
            tiles(group * share),
            tiles(width), tiles(group - 1, width), tiles(replicas, width),
            tiles(share), tiles(group - 1, share), tiles(replicas, share),
            dma, dma, dma, dma,
            pltpu.VMEM((group // 2,) + block, BF16),
            pltpu.VMEM((group // 2,) + block, BF16),
            pltpu.VMEM((group // 2 - 1,) + block, BF16),
            pltpu.VMEM((2, rows_in // 2, XBC), BF16),
            pltpu.SemaphoreType.DMA((group + 2,)),
            pltpu.SemaphoreType.DMA((group + 2,)),
            pltpu.VMEM(raw.shape, BF16),
            pltpu.VMEM(grads.shape, BF16),
            pltpu.VMEM(errors[0].shape, F32),
            pltpu.VMEM(errors[1].shape, F32),
            pltpu.VMEM((2,) + errors[0].shape, BF16),
            pltpu.VMEM((2,) + errors[1].shape, BF16),
            pltpu.SemaphoreType.DMA((4,)),
        ],
        compiler_params=pltpu.CompilerParams(
            collective_id=2, has_side_effects=True, vmem_limit_bytes=VMEM_LIMIT
        ),
        name="compress",
    )(*arrays)


def finish_kernel(
    rates, replicas, rights_ref, tin_ref, tout_ref, lin_ref, lout_ref,
    win_ref, min_ref, ein_ref, raw_ref, wout_ref, mout_ref, eout_ref, out_ref, low_ref, high_ref,
    nwin_ref, nmin_ref, nein_ref, nwout_ref, nmout_ref, neout_ref,
    rin_ref, rout_ref, ntin_ref, ntout_ref,
):
    @pl.when(pl.program_id(0) == 0)
    def _():
        for ref, at, extent in ((rin_ref, 0, PROJ), (rout_ref, RIGHT_OUT, D)):
            for q in range(extent // 128):
                ref[:, q * 128 : q * 128 + 128] = rights_ref[at + q] * (1.0 / replicas)
        ntin_ref[...] = tin_ref[...]
        ntout_ref[...] = tout_ref[...]

    def update(w, m, e, nw, nm, ne, left_ref, grads, at, rate):
        rows = w.shape[0]
        left = [jnp.broadcast_to(left_ref[:, k : k + 1], (rows, 128)) for k in range(8)]
        begin = 0
        for grad in grads:
            for b in range(0, grad.shape[1], 128):
                cols = slice(begin + b, begin + b + 128)
                right = rights_ref[at + (begin + b) // 128] * (1.0 / replicas)
                approx = left[0] * right[0:1]
                for k in range(1, 8):
                    approx = approx + left[k] * right[k : k + 1]
                momentum = MOMENTUM * m[:, cols] + approx
                nm[:, cols] = momentum
                nw[:, cols] = w[:, cols] - rate * momentum
                ne[:, cols] = (grad[:, b : b + 128].astype(F32) + e[:, cols]) - approx
            begin += grad.shape[1]

    update(
        win_ref, min_ref, ein_ref, nwin_ref, nmin_ref, nein_ref, lin_ref, (low_ref, high_ref, raw_ref), 0,
        rates[0],
    )
    update(
        wout_ref, mout_ref, eout_ref, nwout_ref, nmout_ref, neout_ref, lout_ref, (out_ref,),
        RIGHT_OUT, rates[1],
    )


def finish(rates, replicas, rights, turned_in, turned_out, left_in, left_out, wide, narrow, grads):
    rows_in, rows_out = left_in.shape[0], left_out.shape[0]
    steps = 3 if rows_in % 48 == 0 else 1
    block = lambda a: pl.BlockSpec((a.shape[0] // steps, a.shape[1]), lambda i: (i, 0))
    like = lambda a: jax.ShapeDtypeStruct(a.shape, F32)
    step_in, step_out = rows_in // steps, rows_out // steps
    parts = [pl.BlockSpec((step_out, D), lambda i: (i, 0))] + [
        pl.BlockSpec((step_in, D), lambda i, k=k: ((rows_out + k * rows_in) // step_in + i, 0))
        for k in range(2)
    ]
    arrays = [*wide, *narrow]
    outs = [*wide[:3], *narrow[:3]]
    extra = [(8, PROJ), (8, D), turned_in.shape, turned_out.shape]
    return pl.pallas_call(
        partial(finish_kernel, rates, replicas),
        grid=(steps,),
        in_specs=[
            whole(rights.shape), whole(turned_in.shape), whole(turned_out.shape),
            block(left_in), block(left_out), *map(block, arrays), *parts,
        ],
        out_specs=[*map(block, outs), *map(whole, extra)],
        out_shape=[*map(like, outs), *(jax.ShapeDtypeStruct(e, F32) for e in extra)],
        compiler_params=params(("arbitrary",)),
        name="finish",
    )(rights, turned_in, turned_out, left_in, left_out, *arrays, grads, grads, grads)


def step_rates(tokens_replica):
    grad_scale = 0.3 * math.sqrt(tokens_replica)
    return (
        0.5 / (math.sqrt(D) * grad_scale),
        0.5 / (math.sqrt(INNER) * grad_scale),
        0.1 / grad_scale,
    )


def to_later(block):
    return lax.ppermute(block, "seq", [(i, i + 1) for i in range(lax.axis_size("seq") - 1)])


def to_earlier(block):
    return lax.ppermute(block, "seq", [(i + 1, i) for i in range(lax.axis_size("seq") - 1)])


def gather_rows(shard):
    return lax.all_gather(shard, ("fsdp", "seq"), axis=0, tiled=True)


def scatter_rows(total):
    return lax.psum_scatter(total, ("fsdp", "seq"), scatter_dimension=0, tiled=True)


def body(
    tokens,
    cotangent,
    segments,
    input_weight,
    output_weight,
    small_values,
    input_momentum,
    output_momentum,
    small_momentum,
    input_error,
    output_error,
    input_start,
    output_start,
):
    shape = tokens.shape
    pieces = shape[0] * shape[1]
    length = shape[2]
    replicas = lax.axis_size("rep")
    tokens_replica = pieces * length * lax.axis_size("fsdp") * lax.axis_size("seq")
    rate_in, rate_out, rate_small = step_rates(tokens_replica)

    tokens = tokens.reshape(pieces, length, D)
    cotangent = cotangent.reshape(pieces, length, D)
    small_rows = jnp.pad(small_values, (0, -small_values.shape[0] % 1024)).reshape(-1, 128)
    group = lax.axis_size("fsdp") * lax.axis_size("seq")
    weights = jnp.concatenate(
        [output_weight, input_weight[:, :D], input_weight[:, D:INNER]], axis=0
    ).astype(BF16)
    weights = gather_rows(weights).reshape(group, 4, -1, D)
    delta_rows = small_values[D:AT_CONV].reshape(D, HEADS).astype(BF16).T
    delta_rows = jnp.pad(delta_rows, ((0, HP - HEADS), (0, 0)))
    segments = segments.reshape(pieces, 1, segments.shape[2])
    norm_gain = small_values[:D].reshape(1, D)
    if lax.axis_size("fsdp") == 4 and input_weight.shape[0] % 16 == 0:
        (
            raw_full, normed, turned, raw, dsilu, values, wr, draw, delta, send, come,
            conv, gate_gain, heads, docs,
        ) = front(input_weight, tokens, small_rows, segments, delta_rows)
        raw_full = raw_full.reshape(XBC // TILE, D, TILE)
    else:
        raw_full, halo, _, conv, gate_gain, heads, docs = gather_raw(
            input_weight, tokens, small_rows, segments
        )
        raw_full = raw_full.reshape(D, XBC // TILE, TILE).transpose(1, 0, 2)
        normed, turned, raw, dsilu, values, wr, draw, delta, send = enter(
            tokens, halo, norm_gain, raw_full, delta_rows, conv, heads, docs
        )
        come = to_later(send)
    y, starts = forward_scan(values, wr, delta, heads, docs, come)
    output, gy, gnorm, first, gstate, grads, ggate, gskip = leave(
        weights, normed, turned, cotangent, tokens, y, values, wr, gate_gain, delta, heads, docs
    )
    total = scatter_rows(grads.reshape(-1, D))
    gval, gwr, gdraw, gheads, ghalo = backward_scan(
        values, wr, delta, draw, heads, docs, gy, first, starts, to_earlier(gstate), send, dsilu,
        conv,
    )
    input_grad, grad_raw, gdelta, ggain, gconv = leave_back(
        gval, gwr, dsilu, raw, docs, conv, to_earlier(ghalo), normed, turned, raw_full, gdraw,
        delta_rows, gnorm, tokens, cotangent, norm_gain,
    )
    rights, left_in, left_out, turned_in, turned_out, raw_total = compress(
        (input_start.T, output_start.T),
        grads,
        grad_raw,
        (input_error[0], output_error[0]),
        (gdelta, ggain, gconv, ggate, gheads, gskip),
    )
    (
        new_input_weight, new_input_momentum, new_input_error,
        new_output_weight, new_output_momentum, new_output_error,
        input_right, output_right, input_left, output_left,
    ) = finish(
        (rate_in, rate_out), replicas, rights, turned_in, turned_out, left_in, left_out,
        (input_weight, input_momentum, input_error[0], raw_total),
        (output_weight, output_momentum, output_error[0]),
        total,
    )
    rest = rights[REST:SUMMED].reshape(-1, 128)[:REST_ROWS]
    turned_delta = rights[DELTA:REST].reshape(HEADS // 8, D // 128, 8, 128)
    small_sum = jnp.concatenate(
        [
            rest[: D // 128].reshape(-1),
            turned_delta.transpose(1, 3, 0, 2).reshape(-1),
            rest[D // 128 : -3].reshape(-1),
            rest[-3:, :HEADS].reshape(-1),
        ]
    )
    new_small_momentum = MOMENTUM * small_momentum + small_sum / replicas
    new_small_values = small_values - rate_small * new_small_momentum
    return (
        output.reshape(shape),
        input_grad.reshape(shape),
        new_input_weight,
        new_output_weight,
        new_input_momentum,
        new_output_momentum,
        new_small_values,
        new_small_momentum,
        input_left.T,
        input_right.T,
        output_left.T,
        output_right.T,
        new_input_error[None],
        new_output_error[None],
    )


def solution(mesh):
    return jax.shard_map(
        body,
        mesh=mesh,
        in_specs=(
            P(None, ("rep", "fsdp"), "seq", None),
            P(None, ("rep", "fsdp"), "seq", None),
            P(None, ("rep", "fsdp"), None),
            P(("fsdp", "seq"), None),
            P(("fsdp", "seq"), None),
            P(),
            P(("fsdp", "seq"), None),
            P(("fsdp", "seq"), None),
            P(),
            P("rep", ("fsdp", "seq"), None),
            P("rep", ("fsdp", "seq"), None),
            P(),
            P(),
        ),
        out_specs=(
            P(None, ("rep", "fsdp"), "seq", None),
            P(None, ("rep", "fsdp"), "seq", None),
            P(("fsdp", "seq"), None),
            P(("fsdp", "seq"), None),
            P(("fsdp", "seq"), None),
            P(("fsdp", "seq"), None),
            P(),
            P(),
            P(("fsdp", "seq"), None),
            P(),
            P(("fsdp", "seq"), None),
            P(),
            P("rep", ("fsdp", "seq"), None),
            P("rep", ("fsdp", "seq"), None),
        ),
        check_vma=False,
    )
```

```python
from functools import partial
import math

import jax
import jax.numpy as jnp
from jax import lax
from jax.experimental import pallas as pl
from jax.experimental.pallas import tpu as pltpu
from jax.sharding import PartitionSpec as P

D = 768
INNER = 1536
HEADS = 24
HEADDIM = 64
STATE = 128
CONV = 4
PROJ = 3328
XBC = 1792

EPS = 1e-05
MOMENTUM = 0.9
HIGH = lax.Precision.HIGHEST
F32 = jnp.float32
BF16 = jnp.bfloat16
HP = 32
CH = 128
HALO = 16
TILE = 256
SUB = 16
ROWS = 256
SPAN = 128 + HALO
NEG = -1e30
VMEM_LIMIT = 63 * 2**20
MESH = pl.DeviceIdType.MESH

BEFORE = 3
LEAD = 128
BIAS, RATE, SKIP = 0, 1, 2
AT_CONV = D + D * HEADS
AT_GATE = AT_CONV + (CONV + 1) * XBC
AT_HEADS = AT_GATE + INNER


def nn(a, b):
    return lax.dot_general(a, b, (((1,), (0,)), ((), ())), preferred_element_type=F32)


def nt(a, b):
    return lax.dot_general(a, b, (((1,), (1,)), ((), ())), preferred_element_type=F32)


def tn(a, b):
    return lax.dot_general(a, b, (((0,), (0,)), ((), ())), preferred_element_type=F32)


def nn_high(a, b):
    return lax.dot_general(
        a, b, (((1,), (0,)), ((), ())), precision=HIGH, preferred_element_type=F32
    )


def nt_high(a, b):
    return lax.dot_general(
        a, b, (((1,), (1,)), ((), ())), precision=HIGH, preferred_element_type=F32
    )


def tn_high(a, b):
    return lax.dot_general(
        a, b, (((0,), (0,)), ((), ())), precision=HIGH, preferred_element_type=F32
    )


def softplus(v):
    return jnp.maximum(v, 0.0) + jnp.log1p(jnp.exp(-jnp.abs(v)))


def sigmoid(v):
    return 0.5 + 0.5 * jnp.tanh(0.5 * v)


def triangle(extent):
    return jnp.where(
        lax.broadcasted_iota(jnp.int32, (extent, extent), 0)
        <= lax.broadcasted_iota(jnp.int32, (extent, extent), 1),
        1.0,
        0.0,
    )


def times_mask(v, mask):
    rows = v.shape[0]
    product = nn(split_three(v), mask.astype(BF16))
    return product[:rows] + product[rows : 2 * rows] + product[2 * rows :]


def column(heads_ref, row):
    return heads_ref[...].T[:HP, row : row + 1]


def square_of(row):
    return jnp.broadcast_to(row, (128, 128)).T


def params(semantics, **more):
    return pltpu.CompilerParams(
        dimension_semantics=semantics, vmem_limit_bytes=VMEM_LIMIT, **more
    )


def piece(*shape):
    return pl.BlockSpec((1,) + shape, lambda i: (i,) + (0,) * len(shape))


def whole(shape, ranks=1):
    index = (lambda i: (0,) * len(shape)) if ranks == 1 else (lambda i, k: (0,) * len(shape))
    return pl.BlockSpec(shape, index, pipeline_mode=pl.Buffered(1))


def unpack_small(rows_ref, gain_ref, conv_ref, gate_ref, heads_ref):
    for q in range(D // 128):
        gain_ref[:, q * 128 : q * 128 + 128] = rows_ref[q : q + 1, :]
    at = AT_CONV // 128
    for k in range(CONV + 1):
        for q in range(XBC // 128):
            conv_ref[k : k + 1, q * 128 : q * 128 + 128] = rows_ref[at : at + 1, :]
            at += 1
    gate_ref[...] = rows_ref[at : at + INNER // 128, :]
    row = jnp.broadcast_to(rows_ref[at + INNER // 128 : at + INNER // 128 + 1, :], (8, 128))
    place = lax.broadcasted_iota(jnp.int32, (8, 128), 0)
    heads = jnp.zeros((8, 128), F32)
    for k in range(3):
        moved = row if k == 0 else pltpu.roll(row, 128 - k * HEADS, 1)
        heads = jnp.where(place == k, moved, heads)
    lane = lax.broadcasted_iota(jnp.int32, (8, 128), 1)
    heads_ref[...] = jnp.where(lane < HEADS, heads, 0.0)


def unpack_documents(seg_ref, docs_ref, later):
    n, _, extent = docs_ref.shape
    length = extent - LEAD
    place = lax.broadcasted_iota(jnp.int32, (8, extent), 0)
    for i in range(n):
        ids = jnp.broadcast_to(seg_ref[i].astype(F32), (8, seg_ref.shape[2]))
        ahead, behind = jnp.full((8, LEAD), -1.0, F32), jnp.full((8, LEAD), -3.0, F32)
        ids = jnp.concatenate([ahead, ids, behind], axis=1)
        total = ids.shape[1]
        docs = jnp.zeros((8, extent), F32)
        for row, offset in enumerate((0, 1, 2, 3, -1, -2, -3)):
            moved = ids if offset == 0 else pltpu.roll(ids, (-offset) % total, 1)
            here = jnp.where(later, moved[:, length : length + extent], moved[:, :extent])
            docs = jnp.where(place == row, here, docs)
        docs_ref[i] = docs


def gather_kernel(
    nf, w_ref, tok_ref, small_ref, seg_ref,
    o_ref, halo_ref, gain_ref, conv_ref, gate_ref, heads_ref, docs_ref,
    mine, near, local, send, recv,
):
    r, f, s = lax.axis_index("rep"), lax.axis_index("fsdp"), lax.axis_index("seq")
    other = (r, f, 1 - s)
    if nf == 4:
        fx, fy = f + 1 - 2 * lax.rem(f, 2), lax.rem(f + 2, 4)
        fd = lax.rem(fx + 2, 4)
        far = [(r, fx, s), (r, fy, s)]
    else:
        far = [(r, lax.rem(f + j, nf), s) for j in range(1, nf)]
    barrier = pltpu.get_barrier_semaphore()
    for device in far + [other]:
        pl.semaphore_signal(barrier, inc=1, device_id=device, device_id_type=MESH)
    mine[...] = w_ref[:, INNER:].astype(BF16)
    near[...] = tok_ref[:, tok_ref.shape[1] - HALO :, :]
    pl.semaphore_wait(barrier, len(far) + 1)
    copies = []

    def start(src, dst, device):
        k = len(copies)
        copy = pltpu.make_async_remote_copy(
            src, dst, send.at[k], recv.at[k], device_id=device, device_id_type=MESH
        )
        copy.start()
        copies.append(copy)
        return copy

    def block(owner):
        return o_ref.at[owner * 2 + s]

    own = pltpu.make_async_copy(mine, block(f), local)
    own.start()
    if nf == 4:
        x_dev, y_dev = far
        half = mine.shape[0] // 2
        low, high = pl.ds(0, half), pl.ds(half, half)
        from_x, from_y, from_d = block(fx), block(fy), block(fd)
        x_low = start(mine.at[low], block(f).at[low], x_dev)
        y_high = start(mine.at[high], block(f).at[high], y_dev)
        x_high = start(mine.at[high], block(f).at[high], x_dev)
        y_low = start(mine.at[low], block(f).at[low], y_dev)
        late = [start(mine, block(f), other), start(near, halo_ref, other)]
        unpack_small(small_ref, gain_ref, conv_ref, gate_ref, heads_ref)
        unpack_documents(seg_ref, docs_ref, s == 1)
        x_low.wait_recv()
        d_low = start(from_x.at[low], from_x.at[low], y_dev)
        y_high.wait_recv()
        d_high = start(from_y.at[high], from_y.at[high], x_dev)
        x_high.wait_recv()
        late.append(start(from_x, from_x, other))
        y_low.wait_recv()
        late.append(start(from_y, from_y, other))
        d_low.wait_recv()
        late.append(start(from_d.at[low], from_d.at[low], other))
        d_high.wait_recv()
        late.append(start(from_d.at[high], from_d.at[high], other))
    else:
        first = [start(mine, block(f), device) for device in far]
        late = [start(mine, block(f), other), start(near, halo_ref, other)]
        unpack_small(small_ref, gain_ref, conv_ref, gate_ref, heads_ref)
        unpack_documents(seg_ref, docs_ref, s == 1)
        for j, copy in enumerate(first):
            copy.wait_recv()
            source = block(lax.rem(f - 1 - j + nf, nf))
            late.append(start(source, source, other))
    for copy in late:
        copy.wait_recv()
    for copy in copies:
        copy.wait_send()
    own.wait()


def gather_raw(weight, tokens, small_rows, segments):
    nf = lax.axis_size("fsdp")
    rows = weight.shape[0]
    n, length, _ = tokens.shape
    vmem = pl.BlockSpec(memory_space=pltpu.VMEM)
    dma = pltpu.SemaphoreType.DMA
    count = 12 if nf == 4 else 2 * nf
    full, *rest = pl.pallas_call(
        partial(gather_kernel, nf),
        out_shape=[
            jax.ShapeDtypeStruct((2 * nf, rows, XBC), BF16),
            jax.ShapeDtypeStruct((n, HALO, D), BF16),
            jax.ShapeDtypeStruct((1, D), F32),
            jax.ShapeDtypeStruct((CONV + 1, XBC), F32),
            jax.ShapeDtypeStruct((INNER // 128, 128), F32),
            jax.ShapeDtypeStruct((8, 128), F32),
            jax.ShapeDtypeStruct((n, 8, LEAD + length), F32),
        ],
        in_specs=[vmem] * 4,
        out_specs=[pl.BlockSpec(memory_space=pl.ANY)] + [vmem] * 6,
        scratch_shapes=[
            pltpu.VMEM((rows, XBC), BF16),
            pltpu.VMEM((n, HALO, D), BF16),
            dma,
            dma((count,)),
            dma((count,)),
        ],
        compiler_params=pltpu.CompilerParams(
            collective_id=1, has_side_effects=True, vmem_limit_bytes=VMEM_LIMIT
        ),
        name="gather_raw",
    )(weight, tokens, small_rows, segments)
    return full.reshape(2 * nf * rows, XBC), *rest


def store_shift(shift, i, j, values):
    shift[i, (j - 1) * 128 : j * 128, :] = values


def shift_matrices(docs, store):
    own = docs[0:1, LEAD:]
    rows = lax.broadcasted_iota(jnp.int32, (128, SPAN), 0)
    cols = lax.broadcasted_iota(jnp.int32, (128, SPAN), 1)
    for j in range(1, CONV):
        same = jnp.where(docs[BEFORE + j : BEFORE + j + 1, LEAD:] == own, 1.0, 0.0)
        for i in range(own.shape[1] // 128):
            here = square_of(same[:, i * 128 : i * 128 + 128])
            here = jnp.concatenate([here, here[:, : SPAN - 128]], axis=1)
            store(i, j, jnp.where(cols == rows + (HALO - j), here, 0.0).astype(BF16))


def step_terms(normed, dlow, heads_ref, docs):
    length = normed.shape[0]
    own = docs[0:1, LEAD:]
    draw = nt(dlow, normed) + column(heads_ref, BIAS)
    delta = softplus(draw)
    totals = times_mask(-jnp.exp(column(heads_ref, RATE)) * delta, triangle(length))
    keep = jnp.where(own == own[:, length - 1 :], 1.0, 0.0)
    return draw, delta, jnp.exp(totals[:, length - 1 :] - totals) * keep * delta


def enter_kernel(
    tok_ref, halo_ref, gain_ref, wraw_ref, dlow_ref, conv_ref, heads_ref, docs_ref,
    normed_ref, turned_ref, raw_ref, dsilu_ref, val_ref, wr_ref, draw_ref, delta_ref, send_ref,
    ext, moved, act, shift,
):
    length = tok_ref.shape[1]
    gain = gain_ref[...]
    for start, rows, src in ((0, HALO, halo_ref), (HALO, length, tok_ref)):
        for b in range(0, rows, 128):
            n = min(128, rows - b)
            x = src[0, b : b + n, :].astype(F32)
            scale = lax.rsqrt(jnp.mean(x * x, axis=-1, keepdims=True) + EPS)
            ext[start + b : start + b + n, :] = (x * scale * gain).astype(BF16)
    normed = ext[HALO:, :]
    normed_ref[0] = normed
    turned_ref[0] = normed.T
    shift_matrices(docs_ref[0], lambda i, j, values: store_shift(shift, i, j, values))
    draw, delta, weight = step_terms(normed, dlow_ref[...], heads_ref, docs_ref[0])
    draw_ref[0] = draw
    delta_ref[0] = delta
    tiles = XBC // TILE
    blocks = length // 128

    def span_of(c):
        return slice(c * TILE, (c + 1) * TILE)

    def project(c):
        if c < tiles:
            raw_ref[0, c] = nn(ext[...], wraw_ref[c]).astype(BF16)

    def move(c):
        if c < tiles:
            for i in range(blocks):
                moved[c % 2 * blocks + i] = nn(
                    shift[i], raw_ref[0, c, i * 128 : i * 128 + SPAN, :]
                )

    project(0)
    project(1)
    move(0)
    for c in range(tiles):
        span = span_of(c)
        project(c + 2)
        move(c + 1)
        for b in range(0, length, 128):
            slot = c % 2 * blocks + b // 128
            for half in range(0, TILE, 128):
                hc = slice(c * TILE + half, c * TILE + half + 128)
                lanes = slice(half, half + 128)
                w = conv_ref[:, hc]
                for q in range(0, 128, 64):
                    z = w[4:5] + w[3:4] * raw_ref[0, c, HALO + b + q : HALO + b + q + 64, lanes].astype(F32)
                    for j in range(1, CONV):
                        at = (j - 1) * 128 + q
                        z = z + w[3 - j : 4 - j] * moved[slot, at : at + 64, lanes]
                    sig = sigmoid(z)
                    silu = z * sig
                    act[c % 2, b + q : b + q + 64, lanes] = silu
                    dsilu_ref[0, c, b + q : b + q + 64, lanes] = (sig + silu * (1.0 - sig)).astype(BF16)
        if c < INNER // TILE:
            val_ref[0, span, :] = act[c % 2].T.astype(BF16)
        else:
            wr_ref[0] = act[c % 2].astype(BF16)

    writers = wr_ref[0, :, :STATE]
    for h in range(HEADS):
        rows = slice(h * HEADDIM, (h + 1) * HEADDIM)
        scaled = val_ref[0, rows, :].astype(F32) * weight[h : h + 1, :]
        send_ref[0, rows, :] = nn(scaled.astype(BF16), writers).astype(BF16)


def enter(tokens, halo, gain, wraw, dlow, conv, heads, docs):
    n, length, _ = tokens.shape
    outs = [
        ((n, length, D), BF16),
        ((n, D, length), BF16),
        ((n, XBC // TILE, length + HALO, TILE), BF16),
        ((n, XBC // TILE, length, TILE), BF16),
        ((n, INNER, length), BF16),
        ((n, length, 2 * STATE), BF16),
        ((n, HP, length), F32),
        ((n, HP, length), F32),
        ((n, INNER, STATE), BF16),
    ]
    return pl.pallas_call(
        enter_kernel,
        grid=(n,),
        in_specs=[
            piece(length, D), piece(HALO, D), whole(gain.shape), whole(wraw.shape),
            whole(dlow.shape), whole(conv.shape), whole(heads.shape), piece(*docs.shape[1:]),
        ],
        out_specs=[piece(*s[1:]) for s, _ in outs],
        out_shape=[jax.ShapeDtypeStruct(s, t) for s, t in outs],
        scratch_shapes=[
            pltpu.VMEM((length + HALO, D), BF16),
            pltpu.VMEM((2 * (length // 128), (CONV - 1) * 128, TILE), F32),
            pltpu.VMEM((2, length, TILE), F32),
            pltpu.VMEM((length // 128, (CONV - 1) * 128, SPAN), BF16),
        ],
        compiler_params=params(("arbitrary",)),
        name="enter",
    )(tokens, halo, gain, wraw, dlow, conv, heads, docs)


class Copies:
    def __init__(self, *semaphores):
        self.semaphores, self.copies = semaphores, []

    def local(self, src, dst):
        copy = pltpu.make_async_copy(src, dst, self.semaphores[0].at[len(self.copies)])
        copy.start()
        self.copies.append(copy)
        return copy

    def remote(self, src, dst, device):
        k = len(self.copies)
        copy = pltpu.make_async_remote_copy(
            src, dst, self.semaphores[0].at[k], self.semaphores[1].at[k],
            device_id=device, device_id_type=MESH,
        )
        copy.start()
        self.copies.append(copy)
        return copy

    def plan(self, amount, ends, device=None):
        first = len(self.copies)

        def copy(n):
            semaphores = [group.at[first + n] for group in self.semaphores]
            if device is None:
                return pltpu.make_async_copy(*ends(n), *semaphores)
            return pltpu.make_async_remote_copy(
                *ends(n), *semaphores, device_id=device, device_id_type=MESH
            )

        self.copies.extend(copy(n) for n in range(amount))
        return lambda n: copy(n).start()


def front_kernel(
    w_ref, tok_ref, small_ref, seg_ref, dlow_ref,
    wraw_ref, normed_ref, turned_ref, raw_ref, dsilu_ref, val_ref, wr_ref, draw_ref, delta_ref,
    send_ref, come_ref, conv_ref, gate_ref, heads_ref, docs_ref,
    mine, near, halo, wide, gain, ext, turned, raw, dsilu, val, moved, act, shift, weight,
    stored, send, recv,
):
    r, f, s = lax.axis_index("rep"), lax.axis_index("fsdp"), lax.axis_index("seq")
    fx, fy = f + 1 - 2 * lax.rem(f, 2), lax.rem(f + 2, 4)
    fd = lax.rem(fx + 2, 4)
    x_dev, y_dev, other = (r, fx, s), (r, fy, s), (r, f, 1 - s)
    pieces, length, _ = tok_ref.shape
    tiles, blocks = XBC // TILE, length // 128
    order = [tiles - 1, *range(tiles - 1)]
    barrier = pltpu.get_barrier_semaphore()
    for device in (x_dev, y_dev, other):
        pl.semaphore_signal(barrier, inc=1, device_id=device, device_id_type=MESH)
    for c in range(tiles):
        mine[c] = w_ref[:, INNER + c * TILE : INNER + (c + 1) * TILE].astype(BF16)
    near[...] = tok_ref[:, length - HALO :, :]
    pl.semaphore_wait(barrier, 3)
    outward, out = Copies(send, recv), Copies(stored)
    arriving = {}

    def block(c, owner):
        return wide.at[c, owner * 2 + s]

    def offer(at):
        if at < tiles:
            c = order[at]
            arriving[c] = [
                outward.remote(mine.at[c], block(c, f), device) for device in (x_dev, y_dev, other)
            ]
            wide[c, f * 2 + s] = mine[c]

    def relay(at):
        if at < tiles:
            c = order[at]
            from_x, from_y, _ = arriving[c]
            from_x.wait_recv()
            from_y.wait_recv()
            through = (fx, y_dev) if at % 2 == 0 else (fy, x_dev)
            across = block(c, through[0])
            arriving[c].append(outward.remote(across, across, through[1]))
            for owner in (fx, fy):
                arriving[c].append(outward.remote(block(c, owner), block(c, owner), other))

    def finish_tile(at):
        c = order[at]
        arriving[c][3].wait_recv()
        arriving[c].append(outward.remote(block(c, fd), block(c, fd), other))
        for k in (2, 4, 5, 6):
            arriving[c][k].wait_recv()
        out.local(wide.at[c], wraw_ref.at[c])

    bring_halo = outward.remote(near, halo, other)
    offer(0)
    offer(1)
    offer(2)
    unpack_small(small_ref, gain, conv_ref, gate_ref, heads_ref)
    unpack_documents(seg_ref, docs_ref, s == 1)
    bring_halo.wait_recv()
    for n in range(pieces):
        x = halo[n].astype(F32)
        scale = lax.rsqrt(jnp.mean(x * x, axis=-1, keepdims=True) + EPS)
        ext[n, :HALO, :] = (x * scale * gain[...]).astype(BF16)
    normed_out = out.plan(pieces, lambda n: (ext.at[n, pl.ds(HALO, length)], normed_ref.at[n]))
    turned_out = out.plan(pieces, lambda n: (turned.at[n], turned_ref.at[n]))

    def normalise(n, carry):
        for b in range(0, length, 128):
            x = tok_ref[n, b : b + 128, :].astype(F32)
            scale = lax.rsqrt(jnp.mean(x * x, axis=-1, keepdims=True) + EPS)
            ext[n, HALO + b : HALO + b + 128, :] = (x * scale * gain[...]).astype(BF16)
        normed_out(n)
        turned[n] = ext[n, HALO:, :].T
        turned_out(n)
        return carry

    def prepare(n, carry):
        draw_ref[n], delta_ref[n], weight[n] = step_terms(
            ext[n, HALO:, :], dlow_ref[...], heads_ref, docs_ref[n]
        )
        shift_matrices(
            docs_ref[n], lambda i, j, values: store_shift(shift, n * blocks + i, j, values)
        )
        return carry

    lax.fori_loop(0, pieces, normalise, 0)
    relay(0)
    lax.fori_loop(0, pieces, prepare, 0)

    states = []
    for at, c in enumerate(order):
        relay(at + 1)
        offer(at + 3)
        finish_tile(at)
        columns = wide[c].reshape(D, TILE)
        for n in range(pieces):
            raw[n, c] = nn(ext[n], columns).astype(BF16)
            out.local(raw.at[n, c], raw_ref.at[n, c])
        for n in range(pieces):
            for i in range(blocks):
                moved[n * blocks + i] = nn(
                    shift[n * blocks + i], raw[n, c, i * 128 : i * 128 + SPAN, :]
                )
        for n in range(pieces):
            for b in range(0, length, 128):
                slot = n * blocks + b // 128
                for half in range(0, TILE, 128):
                    hc = slice(c * TILE + half, c * TILE + half + 128)
                    lanes = slice(half, half + 128)
                    w = conv_ref[:, hc]
                    for q in range(0, 128, 64):
                        here = raw[n, c, HALO + b + q : HALO + b + q + 64, lanes].astype(F32)
                        z = w[4:5] + w[3:4] * here
                        for j in range(1, CONV):
                            row = (j - 1) * 128 + q
                            z = z + w[3 - j : 4 - j] * moved[slot, row : row + 64, lanes]
                        sig = sigmoid(z)
                        silu = z * sig
                        act[n, b + q : b + q + 64, lanes] = silu
                        dsilu[n, c, b + q : b + q + 64, lanes] = (
                            sig + silu * (1.0 - sig)
                        ).astype(BF16)
            out.local(dsilu.at[n, c], dsilu_ref.at[n, c])
            if c == tiles - 1:
                wr_ref[n] = act[n].astype(BF16)
                continue
            rows = slice(c * TILE, (c + 1) * TILE)
            val[n, rows, :] = act[n].T.astype(BF16)
            out.local(val.at[n, rows], val_ref.at[n, rows])
            writers = wr_ref[n, :, :STATE]
            for h in range(c * 4, c * 4 + 4):
                head = slice(h * HEADDIM, (h + 1) * HEADDIM)
                scaled = val[n, head, :].astype(F32) * weight[n, h : h + 1, :]
                send_ref[n, head, :] = nn(scaled.astype(BF16), writers).astype(BF16)
            states.append(outward.remote(send_ref.at[n, rows], come_ref.at[n, rows], other))
    for copy in states:
        copy.wait_recv()
    for copy in outward.copies:
        copy.wait_send()
    for copy in out.copies:
        copy.wait()


def front(weight, tokens, small_rows, segments, dlow):
    rows = weight.shape[0]
    n, length, _ = tokens.shape
    tiles, blocks = XBC // TILE, length // 128
    vmem, hbm = pl.BlockSpec(memory_space=pltpu.VMEM), pl.BlockSpec(memory_space=pl.ANY)
    outs = [
        (hbm, (tiles, 8, rows, TILE), BF16),
        (hbm, (n, length, D), BF16),
        (hbm, (n, D, length), BF16),
        (hbm, (n, tiles, length + HALO, TILE), BF16),
        (hbm, (n, tiles, length, TILE), BF16),
        (hbm, (n, INNER, length), BF16),
        (vmem, (n, length, 2 * STATE), BF16),
        (vmem, (n, HP, length), F32),
        (vmem, (n, HP, length), F32),
        (vmem, (n, INNER, STATE), BF16),
        (vmem, (n, INNER, STATE), BF16),
        (vmem, (CONV + 1, XBC), F32),
        (vmem, (INNER // 128, 128), F32),
        (vmem, (8, 128), F32),
        (vmem, (n, 8, LEAD + length), F32),
    ]
    remote = 1 + 7 * tiles + n * (tiles - 1)
    local = tiles + 2 * n + 2 * n * tiles + n * (tiles - 1)
    return pl.pallas_call(
        front_kernel,
        in_specs=[vmem] * 5,
        out_specs=[spec for spec, _, _ in outs],
        out_shape=[jax.ShapeDtypeStruct(shape, kind) for _, shape, kind in outs],
        scratch_shapes=[
            pltpu.VMEM((tiles, rows, TILE), BF16),
            pltpu.VMEM((n, HALO, D), BF16),
            pltpu.VMEM((n, HALO, D), BF16),
            pltpu.VMEM((tiles, 8, rows, TILE), BF16),
            pltpu.VMEM((1, D), F32),
            pltpu.VMEM((n, length + HALO, D), BF16),
            pltpu.VMEM((n, D, length), BF16),
            pltpu.VMEM((n, tiles, length + HALO, TILE), BF16),
            pltpu.VMEM((n, tiles, length, TILE), BF16),
            pltpu.VMEM((n, INNER, length), BF16),
            pltpu.VMEM((n * blocks, (CONV - 1) * 128, TILE), F32),
            pltpu.VMEM((n, length, TILE), F32),
            pltpu.VMEM((n * blocks, (CONV - 1) * 128, SPAN), BF16),
            pltpu.VMEM((n, HP, length), F32),
            pltpu.SemaphoreType.DMA((local,)),
            pltpu.SemaphoreType.DMA((remote,)),
            pltpu.SemaphoreType.DMA((remote,)),
        ],
        compiler_params=pltpu.CompilerParams(
            collective_id=3, has_side_effects=True, vmem_limit_bytes=VMEM_LIMIT
        ),
        name="front",
    )(weight, tokens, small_rows, segments, dlow)


def chunk_terms(delta, rate, docs):
    own = docs[0:1, :]
    before = docs[BEFORE + 1 : BEFORE + 2, 0:1]
    last = docs[0:1, CH - 1 :]
    decay = -jnp.exp(rate) * delta
    totals = times_mask(decay, triangle(CH))
    end = totals[:, CH - 1 :]
    fade = jnp.exp(totals) * jnp.where(own == before, 1.0, 0.0)
    to_end = jnp.exp(end - totals) * jnp.where(own == last, 1.0, 0.0)
    passing = jnp.exp(end) * jnp.where(last == before, 1.0, 0.0)
    together = square_of(own) == own
    first = lax.broadcasted_iota(jnp.int32, (CH, CH), 0)
    second = lax.broadcasted_iota(jnp.int32, (CH, CH), 1)
    barred = jnp.where(together & (first <= second), 0.0, NEG)
    reach = jnp.where(together & (first >= second), 1.0, 0.0)
    return decay, totals, fade, to_end, passing, barred, reach


def forward_kernel(
    val_ref, w_ref, r_ref, delta_ref, heads_ref, docs_ref, in_ref,
    y_ref, start_ref,
    state, off, fresh,
):
    state[...] = jnp.where(lax.axis_index("seq") == 0, 0.0, in_ref[0].astype(F32))
    rate = column(heads_ref, RATE)
    def chunk(k, carry):
        lanes = pl.ds(pl.multiple_of(k * CH, CH), CH)
        writers, readers = w_ref[0, lanes, :], r_ref[0, lanes, :]
        delta = delta_ref[0, :, lanes]
        _, totals, fade, to_end, passing, barred, _ = chunk_terms(
            delta, rate, docs_ref[0, :, pl.ds(pl.multiple_of(LEAD + k * CH, CH), CH)]
        )
        columns = totals.T
        scores = nt(writers, readers)
        low_state = state[...].astype(BF16)
        start_ref[0, k] = low_state
        off[...] = nt(low_state, readers)
        for h in range(HEADS):
            rows = slice(h * HEADDIM, (h + 1) * HEADDIM)
            mixing = jnp.exp(totals[h : h + 1, :] - columns[:, h : h + 1] + barred) * scores
            scaled = val_ref[0, rows, lanes].astype(F32) * delta[h : h + 1, :]
            fresh[rows, :] = (scaled * to_end[h : h + 1, :]).astype(BF16)
            inside = nn(scaled.astype(BF16), mixing.astype(BF16))
            y_ref[0, rows, lanes] = inside + off[rows, :] * fade[h : h + 1, :]
        gained = nn(fresh[...], writers)
        for h in range(HEADS):
            rows = slice(h * HEADDIM, (h + 1) * HEADDIM)
            state[rows, :] = passing[h : h + 1, :] * state[rows, :] + gained[rows, :]
        return carry

    lax.fori_loop(0, val_ref.shape[2] // CH, chunk, 0)


def forward_scan(values, wr, delta, heads, docs, incoming):
    n, _, length = values.shape
    chunks = length // CH
    return pl.pallas_call(
        forward_kernel,
        grid=(n,),
        in_specs=[
            piece(INNER, length),
            pl.BlockSpec((1, length, STATE), lambda i: (i, 0, 0)),
            pl.BlockSpec((1, length, STATE), lambda i: (i, 0, 1)),
            piece(HP, length),
            whole(heads.shape),
            piece(*docs.shape[1:]),
            piece(INNER, STATE),
        ],
        out_specs=[piece(INNER, length), piece(chunks, INNER, STATE)],
        scratch_shapes=[
            pltpu.VMEM((INNER, STATE), F32),
            pltpu.VMEM((INNER, CH), F32),
            pltpu.VMEM((INNER, CH), BF16),
        ],
        out_shape=[
            jax.ShapeDtypeStruct((n, INNER, length), F32),
            jax.ShapeDtypeStruct((n, chunks, INNER, STATE), BF16),
        ],
        compiler_params=params(("arbitrary",)),
        name="forward_scan",
    )(values, wr, wr, delta, heads, docs, incoming)


def backward_kernel(
    val_ref, w_ref, r_ref, delta_ref, draw_ref, heads_ref, docs_ref, gy_ref, first_ref,
    start_ref, in_ref, final_ref, dsilu_ref, conv_ref, near_ref,
    gval_ref, gwr_ref, gdraw_ref, gheads_ref, ghalo_ref,
    grad, link, off, fresh, faded, gdelta, paid, sums,
):
    n, step = pl.program_id(0), pl.program_id(1)
    rate = column(heads_ref, RATE)

    @pl.when(step == 0)
    def _():
        grad[...] = in_ref[0].astype(F32)
        product = in_ref[0].astype(F32) * final_ref[0].astype(F32)
        by_head = jnp.sum(product.reshape(HEADS, HEADDIM, STATE), axis=1)
        link[0:HEADS, :] = jnp.sum(by_head, axis=1, keepdims=True)
        link[HEADS:, :] = jnp.zeros((HP - HEADS, 1), F32)

    @pl.when((n == 0) & (step == 0))
    def _():
        sums[...] = jnp.zeros_like(sums)

    writers, readers = w_ref[0], r_ref[0]
    delta = delta_ref[0]
    decay, totals, fade, to_end, passing, barred, reach = chunk_terms(delta, rate, docs_ref[0])
    columns = totals.T
    scores = nt(writers, readers)
    low_grad = grad[...].astype(BF16)
    off[...] = nt(low_grad, writers)
    gscores = jnp.zeros((CH, CH), F32)
    gdelta[HEADS:, :] = jnp.zeros((HP - HEADS, CH), F32)
    paid[HEADS:, :] = jnp.zeros((HP - HEADS, CH), F32)
    for h in range(HEADS):
        rows = slice(h * HEADDIM, (h + 1) * HEADDIM)
        spread = jnp.exp(totals[h : h + 1, :] - columns[:, h : h + 1] + barred)
        values = val_ref[0, rows, :].astype(F32)
        gy = gy_ref[0, rows, :]
        gy32 = gy.astype(F32)
        scaled = values * delta[h : h + 1, :]
        fresh[rows, :] = (scaled * to_end[h : h + 1, :]).astype(BF16)
        faded[rows, :] = (gy32 * fade[h : h + 1, :]).astype(BF16)
        gscaled = nt(gy, (spread * scores).astype(BF16)) + off[rows, :] * to_end[h : h + 1, :]
        low = scaled.astype(BF16)
        gscores = gscores + tn(low, gy) * spread
        paid[h : h + 1, :] = jnp.sum(low.astype(F32) * gscaled, axis=0, keepdims=True)
        gdelta[h : h + 1, :] = jnp.sum(values * gscaled, axis=0, keepdims=True)
        gval_ref[0, rows, :] = (
            gscaled * delta[h : h + 1, :] + gy32 * heads_ref[SKIP : SKIP + 1, h : h + 1]
        ).astype(BF16)
    low_scores = gscores.astype(BF16)
    gwr_ref[0, :, :STATE] = nn(low_scores, readers) + tn(fresh[...], low_grad)
    gwr_ref[0, :, STATE:] = tn(low_scores, writers) + tn(faded[...], start_ref[0, 0])
    off[:, :STATE] = nn(faded[...], readers)
    for h in range(HEADS):
        rows = slice(h * HEADDIM, (h + 1) * HEADDIM)
        grad[rows, :] = passing[h : h + 1, :] * grad[rows, :] + off[rows, :STATE]
    following = jnp.where(docs_ref[0, 0:1, :] == docs_ref[0, 1:2, CH - 1 :], 1.0, 0.0)
    gdecay = times_mask(first_ref[0] - paid[...], reach) + following * link[...]
    link[...] = gdecay[:, :1]
    gtotal = gdelta[...] - jnp.exp(rate) * gdecay
    gdraw = gtotal * sigmoid(draw_ref[0])
    gdraw_ref[0] = gdraw
    sums[0] += gdraw
    sums[1] += gdecay * decay

    @pl.when(step == pl.num_programs(1) - 1)
    def _():
        taps = conv_ref[...]
        near = [
            square_of(
                jnp.where(near_ref[0, j : j + 1, :] == near_ref[0, 0:1, :], 1.0, 0.0)
            )[120:, :]
            for j in range(CONV)
        ]
        for c in range(XBC // 128):
            cols = slice(c * 128, (c + 1) * 128)
            if c < INNER // 128:
                here = gval_ref[0, cols, :].astype(F32).T[:8, :]
            else:
                here = gwr_ref[0, 0:8, c * 128 - INNER : c * 128 - INNER + 128]
            left = c * 128 % TILE
            pre = here * dsilu_ref[0, c * 128 // TILE, 0:8, left : left + 128].astype(F32)
            wide = jnp.concatenate([jnp.zeros((8, 128), F32), pre], axis=0)
            total = jnp.zeros((8, 128), F32)
            for j in range(1, CONV):
                total = total + taps[3 - j : 4 - j, cols] * wide[j : j + 8] * near[j]
            ghalo_ref[0, :, cols] = total

    @pl.when((n == pl.num_programs(0) - 1) & (step == pl.num_programs(1) - 1))
    def _():
        for i in range(2):
            both = jnp.concatenate([sums[i], jnp.zeros((128 - HP, CH), F32)], axis=0)
            gheads_ref[i : i + 1, :] = jnp.sum(both.T, axis=0, keepdims=True)
        gheads_ref[2:, :] = jnp.zeros((6, 128), F32)


def backward_scan(
    values, wr, delta, draw, heads, docs, gy, first, starts, incoming, final, dsilu, conv
):
    n, _, length = values.shape
    chunks = length // CH
    back = lambda k: chunks - 1 - k
    lanes = lambda rows: pl.BlockSpec((1, rows, CH), lambda i, k: (i, 0, back(k)))
    return pl.pallas_call(
        backward_kernel,
        grid=(n, chunks),
        in_specs=[
            lanes(INNER),
            pl.BlockSpec((1, CH, STATE), lambda i, k: (i, back(k), 0)),
            pl.BlockSpec((1, CH, STATE), lambda i, k: (i, back(k), 1)),
            lanes(HP),
            lanes(HP),
            whole(heads.shape, 2),
            pl.BlockSpec((1, 8, CH), lambda i, k: (i, 0, back(k) + LEAD // CH)),
            lanes(INNER),
            lanes(HP),
            pl.BlockSpec((1, 1, INNER, STATE), lambda i, k: (i, back(k), 0, 0)),
            pl.BlockSpec((1, INNER, STATE), lambda i, k: (i, 0, 0)),
            pl.BlockSpec((1, INNER, STATE), lambda i, k: (i, 0, 0)),
            pl.BlockSpec((1, XBC // TILE, 16, TILE), lambda i, k: (i, 0, 0, 0)),
            whole(conv.shape, 2),
            pl.BlockSpec((1, 8, 128), lambda i, k: (i, 0, 0)),
        ],
        out_specs=[
            lanes(INNER),
            pl.BlockSpec((1, CH, 2 * STATE), lambda i, k: (i, back(k), 0)),
            lanes(HP),
            pl.BlockSpec((8, 128), lambda i, k: (0, 0)),
            pl.BlockSpec((1, 8, XBC), lambda i, k: (i, 0, 0)),
        ],
        scratch_shapes=[
            pltpu.VMEM((INNER, STATE), F32),
            pltpu.VMEM((HP, 1), F32),
            pltpu.VMEM((INNER, CH), F32),
            pltpu.VMEM((INNER, CH), BF16),
            pltpu.VMEM((INNER, CH), BF16),
            pltpu.VMEM((HP, CH), F32),
            pltpu.VMEM((HP, CH), F32),
            pltpu.VMEM((2, HP, CH), F32),
        ],
        out_shape=[
            jax.ShapeDtypeStruct((n, INNER, length), BF16),
            jax.ShapeDtypeStruct((n, length, 2 * STATE), F32),
            jax.ShapeDtypeStruct((n, HP, length), F32),
            jax.ShapeDtypeStruct((8, 128), F32),
            jax.ShapeDtypeStruct((n, 8, XBC), F32),
        ],
        compiler_params=params(("arbitrary", "arbitrary")),
        name="backward_scan",
    )(
        values, wr, wr, delta, draw, heads, docs, gy, first, starts, incoming, final, dsilu,
        conv, docs,
    )


def leave_kernel(group, packed, *refs):
    if packed:
        weights_ref, *refs = refs
        *refs, wgate_ref, wout_ref, loaded = refs
    else:
        wgate_ref, wout_ref, *refs = refs
    (
        normed_ref, turned_ref, cot_ref, tok_ref, y_ref, val_ref, r_ref, gain_ref, delta_ref,
        heads_ref, docs_ref,
        out_ref, gy_ref, gnorm_ref, first_ref, gstate_ref, grads_ref, ggain_ref, gskip_ref,
        gate, gated, upward, lifted, faded, flat, total_out, total_gate, products, skips, gains,
        wide_gain, fade, total_state,
    ) = refs
    n, k = pl.program_id(0), pl.program_id(1)
    begin = (n == 0) & (k == 0)
    end = (n == pl.num_programs(0) - 1) & (k == pl.num_programs(1) - 1)
    length = delta_ref.shape[2]
    rows_out, rows_in = INNER // group, D // group
    tiles = INNER // TILE
    lanes = range(0, ROWS, 128)
    down = lambda s: jnp.sum(s, axis=0, keepdims=True)

    def fold(v):
        return jnp.sum(v.reshape(v.shape[0] // 8, 8, 128), axis=0)

    def loads():
        copies = []
        for p in range(group):
            for q, ref, at, left in (
                (2, wgate_ref, p * rows_in, 0), (3, wgate_ref, p * rows_in, D),
                (0, wout_ref, p * rows_out, 0), (1, wout_ref, p * rows_out + rows_in, 0),
            ):
                copies.append(
                    pltpu.make_async_copy(
                        weights_ref.at[p, q],
                        ref.at[pl.ds(at, rows_in), pl.ds(left, D)],
                        loaded.at[len(copies)],
                    )
                )
        return copies

    @pl.when(begin)
    def _():
        if packed:
            for copy in loads():
                copy.start()
        total_out[...] = jnp.zeros_like(total_out)
        total_gate[...] = jnp.zeros_like(total_gate)
        skips[...] = jnp.zeros_like(skips)
        gains[...] = jnp.zeros_like(gains)
        for q in range(INNER // 128):
            wide_gain[q * 128 : (q + 1) * 128, :] = square_of(gain_ref[q : q + 1, :])

    @pl.when(k == 0)
    def _():
        own = docs_ref[0, 0:1, LEAD:]
        before = docs_ref[0, BEFORE + 1 : BEFORE + 2, LEAD : LEAD + 1]
        totals = times_mask(-jnp.exp(column(heads_ref, RATE)) * delta_ref[0], triangle(length))
        fade[...] = jnp.exp(totals) * jnp.where(own == before, 1.0, 0.0)
        total_state[...] = jnp.zeros_like(total_state)

    if packed:

        @pl.when(begin)
        def _():
            for copy in loads():
                copy.wait()

    here = pl.ds(pl.multiple_of(k * ROWS, ROWS), ROWS)

    def span(c):
        return slice(c * TILE, (c + 1) * TILE)

    def head_rows(h):
        return slice(h * HEADDIM, (h + 1) * HEADDIM)

    def open_tile(c):
        if c < tiles:
            gate[span(c), :] = nn(normed_ref[0], wgate_ref[:, span(c)]).T.astype(BF16)
            upward[span(c), :] = nt(wout_ref[span(c), :], cot_ref[0])

    squares = [jnp.zeros((8, 128), F32) for _ in lanes]
    dots = [jnp.zeros((8, 128), F32) for _ in lanes]
    open_tile(0)
    for c in range(tiles):
        open_tile(c + 1)
        for h in range(c * 4, c * 4 + 4):
            rows = head_rows(h)
            skip = heads_ref[SKIP : SKIP + 1, h : h + 1]
            gain = wide_gain[rows, :]
            for i, b in enumerate(lanes):
                g = gate[rows, b : b + 128].astype(F32)
                values = val_ref[0, rows, b : b + 128].astype(F32)
                v = (y_ref[0, rows, b : b + 128] + skip * values) * (g * sigmoid(g))
                gated[rows, b : b + 128] = v
                squares[i] = squares[i] + fold(v * v)
                dots[i] = dots[i] + fold(upward[rows, b : b + 128] * gain * v)
    scale = [lax.rsqrt(down(s) * (1.0 / INNER) + EPS) for s in squares]
    pull = [s * s * s * down(d) * (1.0 / INNER) for s, d in zip(scale, dots)]

    def close_tile(c):
        low = lifted[span(c), :]
        flat[:, span(c)] = low.T
        total_out[span(c), :] += nn(low, cot_ref[0])
        total_gate[:, span(c)] += nt(turned_ref[0], gate[span(c), :])
        total_state[span(c), :] += nn(faded[c % 2], r_ref[0])

    for c in range(tiles):
        if c > 0:
            close_tile(c - 1)
        for h in range(c * 4, c * 4 + 4):
            eight = slice(h * 8, h * 8 + 8)
            skip = heads_ref[SKIP : SKIP + 1, h : h + 1]
            fading = fade[h : h + 1, here]
            sums = jnp.zeros((8, 128), F32)
            product = [jnp.zeros((8, 128), F32) for _ in lanes]
            for at in range(h * HEADDIM, (h + 1) * HEADDIM, SUB):
                rows = slice(at, at + SUB)
                inner = slice(at - c * TILE, at - c * TILE + SUB)
                gain = wide_gain[rows, :]
                gain_sums = gains[rows, :]
                for i, b in enumerate(lanes):
                    v = gated[rows, b : b + 128]
                    u = upward[rows, b : b + 128]
                    normal = v * scale[i]
                    lifted[rows, b : b + 128] = (normal * gain).astype(BF16)
                    gain_sums = gain_sums + u * normal
                    gv = scale[i] * (u * gain) - pull[i] * v
                    g = gate[rows, b : b + 128].astype(F32)
                    sig = sigmoid(g)
                    silu = g * sig
                    low = (gv * silu).astype(BF16)
                    gy_ref[0, rows, b : b + 128] = low
                    gm = low.astype(F32)
                    faded[c % 2, inner, b : b + 128] = (gm * fading[:, b : b + 128]).astype(BF16)
                    values = val_ref[0, rows, b : b + 128].astype(F32)
                    sums = sums + fold(gm * values)
                    y = y_ref[0, rows, b : b + 128]
                    product[i] = product[i] + fold(gm * y)
                    gate[rows, b : b + 128] = (
                        gv * (y + skip * values) * (sig + silu * (1.0 - sig))
                    ).astype(BF16)
                gains[rows, :] = gain_sums
            for i, b in enumerate(lanes):
                products[eight, b : b + 128] = product[i]
            skips[eight, :] += sums
    close_tile(tiles - 1)
    for b in range(0, D, TILE):
        branch = nn(flat[...], wout_ref[:, b : b + TILE])
        out_ref[0, :, b : b + TILE] = (tok_ref[0, :, b : b + TILE].astype(F32) + branch).astype(BF16)
    for b in range(0, D, TILE):
        gnorm_ref[0, b : b + TILE, :] = nn(wgate_ref[b : b + TILE, :], gate[...]).astype(BF16)
    first_ref[0, 0:HEADS, :] = jnp.sum(products[...].reshape(HEADS, 8, ROWS), axis=1)
    first_ref[0, HEADS:, :] = jnp.zeros((HP - HEADS, ROWS), F32)

    @pl.when(k == pl.num_programs(1) - 1)
    def _():
        gstate_ref[0] = total_state[...].astype(BF16)

    @pl.when(end)
    def _():
        for p in range(group):
            grads_ref[p, :rows_out, :] = total_out[p * rows_out : (p + 1) * rows_out, :].astype(BF16)
            for half in range(2):
                at = rows_out + half * rows_in
                grads_ref[p, at : at + rows_in, :] = total_gate[
                    p * rows_in : (p + 1) * rows_in, half * D : (half + 1) * D
                ].astype(BF16)
        for q in range(INNER // 128):
            ggain_ref[q : q + 1, :] = down(gains[q * 128 : (q + 1) * 128, :].T)
        ggain_ref[INNER // 128 :, :] = jnp.zeros((16 - INNER // 128, 128), F32)
        by_head = jnp.sum(skips[...].reshape(HEADS, 8, 128), axis=1)
        by_head = jnp.concatenate([by_head, jnp.zeros((128 - HEADS, 128), F32)], axis=0)
        gskip_ref[0:1, :] = down(by_head.T)
        gskip_ref[1:, :] = jnp.zeros((7, 128), F32)


def leave(weights, normed, turned, cot, tokens, y, values, wr, gain, delta, heads, docs):
    n, length, _ = normed.shape
    group, _, rows_in, _ = weights.shape
    packed = rows_in % 16 == 0
    if packed:
        weights, loaded = [weights], [pl.BlockSpec(memory_space=pl.ANY)]
        scratch = [
            pltpu.VMEM((D, INNER), BF16),
            pltpu.VMEM((INNER, D), BF16),
            pltpu.SemaphoreType.DMA((4 * group,)),
        ]
    else:
        gate = jnp.concatenate([weights[:, 2], weights[:, 3]], axis=-1).reshape(D, INNER)
        weights = [gate, weights[:, :2].reshape(INNER, D)]
        loaded, scratch = [whole(a.shape, 2) for a in weights], []
    grads = (group, 4 * rows_in, D)
    rows = lambda width: pl.BlockSpec((1, ROWS, width), lambda i, k: (i, k, 0))
    lanes = lambda height: pl.BlockSpec((1, height, ROWS), lambda i, k: (i, 0, k))
    each = lambda *shape: pl.BlockSpec((1,) + shape, lambda i, k: (i, 0, 0))
    return pl.pallas_call(
        partial(leave_kernel, group, packed),
        grid=(n, length // ROWS),
        in_specs=loaded + [
            rows(D), lanes(D), rows(D), rows(D), lanes(INNER), lanes(INNER),
            pl.BlockSpec((1, ROWS, STATE), lambda i, k: (i, k, 1)),
            whole(gain.shape, 2), each(HP, length), whole(heads.shape, 2), each(*docs.shape[1:]),
        ],
        out_specs=[
            rows(D), lanes(INNER), lanes(D), lanes(HP), each(INNER, STATE), whole(grads, 2),
            whole((16, 128), 2), whole((8, 128), 2),
        ],
        scratch_shapes=[
            pltpu.VMEM((INNER, ROWS), BF16),
            pltpu.VMEM((INNER, ROWS), F32),
            pltpu.VMEM((INNER, ROWS), F32),
            pltpu.VMEM((INNER, ROWS), BF16),
            pltpu.VMEM((2, TILE, ROWS), BF16),
            pltpu.VMEM((ROWS, INNER), BF16),
            pltpu.VMEM((INNER, D), F32),
            pltpu.VMEM((D, INNER), F32),
            pltpu.VMEM((HEADS * 8, ROWS), F32),
            pltpu.VMEM((HEADS * 8, 128), F32),
            pltpu.VMEM((INNER, 128), F32),
            pltpu.VMEM((INNER, 128), F32),
            pltpu.VMEM((HP, length), F32),
            pltpu.VMEM((INNER, STATE), F32),
        ] + scratch,
        out_shape=[
            jax.ShapeDtypeStruct((n, length, D), BF16),
            jax.ShapeDtypeStruct((n, INNER, length), BF16),
            jax.ShapeDtypeStruct((n, D, length), BF16),
            jax.ShapeDtypeStruct((n, HP, length), F32),
            jax.ShapeDtypeStruct((n, INNER, STATE), BF16),
            jax.ShapeDtypeStruct(grads, BF16),
            jax.ShapeDtypeStruct((16, 128), F32),
            jax.ShapeDtypeStruct((8, 128), F32),
        ],
        compiler_params=params(("arbitrary", "arbitrary")),
        name="leave",
    )(*weights, normed, turned, cot, tokens, y, values, wr, gain, delta, heads, docs)


def exit_kernel(
    gval_ref, gwr_ref, dsilu_ref, raw_ref, docs_ref, conv_ref, back_ref, normed_ref, turned_ref,
    wraw_ref, gdraw_ref, dlow_ref, gnorm_ref, tok_ref, cot_ref, gain_ref,
    grad_ref, graw_ref, gdelta_ref, ggain_ref, gconv_ref,
    pre, low_pre, moved, halo_terms, shift, low, lifted, total, sums,
):
    n = pl.program_id(0)
    length = dsilu_ref.shape[2]
    last = n == pl.num_programs(0) - 1

    @pl.when(n == 0)
    def _():
        total[...] = jnp.zeros_like(total)
        sums[...] = jnp.zeros_like(sums)
        gdelta_ref[...] = jnp.zeros_like(gdelta_ref)
        ggain_ref[...] = jnp.zeros_like(ggain_ref)

    def shifts(rows, extent, near):
        first = lax.broadcasted_iota(jnp.int32, (rows, extent), 0)
        second = lax.broadcasted_iota(jnp.int32, (rows, extent), 1)
        return [
            jnp.where(second == first + j, near[j - 1], 0.0).astype(BF16) for j in range(1, CONV)
        ]

    near = [
        jnp.where(docs_ref[0, j : j + 1, :] == docs_ref[0, 0:1, :], 1.0, 0.0)
        for j in range(1, CONV)
    ]
    for i in range(length // 128):
        square = [square_of(v[:, LEAD + i * 128 : LEAD + i * 128 + 128]) for v in near]
        square = [jnp.concatenate([v, v[:, : SPAN - 128]], axis=1) for v in square]
        shift[i] = jnp.concatenate(shifts(128, SPAN, square), axis=0)
    square = [square_of(v[:, LEAD - 128 : LEAD])[128 - HALO :, : 2 * HALO] for v in near]
    ahead = jnp.concatenate(shifts(HALO, 2 * HALO, square), axis=0)
    for slot in range(2):
        low_pre[slot, :HALO, :] = jnp.zeros((HALO, TILE), BF16)
        low_pre[slot, HALO + length :, :] = jnp.zeros((HALO, TILE), BF16)
    tiles = XBC // TILE
    blocks = length // 128

    def span_of(c):
        return slice(c * TILE, (c + 1) * TILE)

    def open_tile(c):
        if c == tiles:
            return
        if c < INNER // TILE:
            here = gval_ref[0, span_of(c), :].astype(F32).T
        else:
            here = gwr_ref[0]
        here = here * dsilu_ref[0, c].astype(F32)
        pre[c % 2] = here
        low_pre[c % 2, HALO : HALO + length, :] = here.astype(BF16)
        halo_terms[c % 2] = nn(ahead, low_pre[c % 2, : 2 * HALO, :])
        for i in range(blocks):
            moved[c % 2 * blocks + i] = nn(
                shift[i], low_pre[c % 2, HALO + i * 128 : HALO + i * 128 + SPAN, :]
            )

    def close_tile(c):
        total[:, span_of(c)] += nn(turned_ref[0], low[c % 2])
        through = nt(low[c % 2], wraw_ref[c])
        if c == 0:
            lifted[...] = through
        else:
            lifted[...] += through

    def fold(v):
        return jnp.sum(v.reshape(v.shape[0] // 8, 8, 128), axis=0)

    open_tile(0)
    for c in range(tiles):
        slot = c % 2
        open_tile(c + 1)
        if c > 0:
            close_tile(c - 1)
        for half in range(0, TILE, 128):
            cols = slice(half, half + 128)
            wide = slice(c * TILE + half, c * TILE + half + 128)
            w = conv_ref[:, wide]
            folded = [sums[k, :, wide] for k in range(CONV + 1)]
            raw = raw_ref[0, c, :HALO, cols].astype(F32)
            for j in range(1, CONV):
                term = halo_terms[slot, (j - 1) * HALO : j * HALO, cols]
                folded[3 - j] = folded[3 - j] + fold(raw * term)
            for b in range(0, length, 64):
                raw = raw_ref[0, c, HALO + b : HALO + b + 64, cols].astype(F32)
                now = pre[slot, b : b + 64, cols]
                grad = w[3:4] * now
                folded[3] = folded[3] + fold(raw * now)
                folded[4] = folded[4] + fold(now)
                for j in range(1, CONV):
                    at = (j - 1) * 128 + b % 128
                    term = moved[slot * blocks + b // 128, at : at + 64, cols]
                    grad = grad + w[3 - j : 4 - j] * term
                    folded[3 - j] = folded[3 - j] + fold(raw * term)
                if b == length - 64:
                    grad = jnp.concatenate([grad[:56], grad[56:] + back_ref[0, :, wide]], axis=0)
                low[slot, b : b + 64, cols] = grad.astype(BF16)
            for k in range(CONV + 1):
                sums[k, :, wide] = folded[k]
    close_tile(tiles - 1)

    gdraw = gdraw_ref[0].astype(BF16)
    gdelta_ref[...] += nn(gdraw, normed_ref[0])
    gain = gain_ref[...]
    gains = jnp.zeros((8, D), F32)
    for b in range(0, length, 128):
        rows = slice(b, b + 128)
        up = lifted[rows, :] + gnorm_ref[0, :, rows].astype(F32).T + tn(gdraw[:, rows], dlow_ref[...])
        x = tok_ref[0, rows, :].astype(F32)
        scale = lax.rsqrt(jnp.mean(x * x, axis=-1, keepdims=True) + EPS)
        normal = x * scale
        gains = gains + jnp.sum((up * normal).reshape(16, 8, D), axis=0)
        up = up * gain
        inner = jnp.mean(up * normal, axis=-1, keepdims=True)
        grad = cot_ref[0, rows, :].astype(F32) + scale * (up - normal * inner)
        grad_ref[0, rows, :] = grad.astype(BF16)
    ggain_ref[0:1, :] += jnp.sum(gains, axis=0, keepdims=True)

    @pl.when(last)
    def _():
        graw_ref[...] = total[...].astype(BF16)
        gconv_ref[0 : CONV + 1, :] = jnp.sum(sums[...], axis=1)


def leave_back(
    gval, gwr, dsilu, raw, docs, conv, back, normed, turned, wraw, gdraw, dlow, gnorm, tokens,
    cotangent, gain,
):
    n, length, _ = tokens.shape
    return pl.pallas_call(
        exit_kernel,
        grid=(n,),
        in_specs=[
            piece(INNER, length), piece(length, 2 * STATE), piece(XBC // TILE, length, TILE),
            piece(XBC // TILE, length + HALO, TILE), piece(*docs.shape[1:]), whole(conv.shape), piece(8, XBC),
            piece(length, D), piece(D, length), whole(wraw.shape), piece(HP, length),
            whole(dlow.shape), piece(D, length), piece(length, D), piece(length, D),
            whole(gain.shape),
        ],
        out_specs=[
            piece(length, D), whole((D, XBC)), whole((HP, D)), whole((8, D)), whole((8, XBC)),
        ],
        out_shape=[
            jax.ShapeDtypeStruct((n, length, D), BF16),
            jax.ShapeDtypeStruct((D, XBC), BF16),
            jax.ShapeDtypeStruct((HP, D), F32),
            jax.ShapeDtypeStruct((8, D), F32),
            jax.ShapeDtypeStruct((8, XBC), F32),
        ],
        scratch_shapes=[
            pltpu.VMEM((2, length, TILE), F32),
            pltpu.VMEM((2, length + 2 * HALO, TILE), BF16),
            pltpu.VMEM((2 * (length // 128), (CONV - 1) * 128, TILE), F32),
            pltpu.VMEM((2, (CONV - 1) * HALO, TILE), F32),
            pltpu.VMEM((length // 128, (CONV - 1) * 128, SPAN), BF16),
            pltpu.VMEM((2, length, TILE), BF16),
            pltpu.VMEM((length, D), F32),
            pltpu.VMEM((D, XBC), F32),
            pltpu.VMEM((CONV + 1, 8, XBC), F32),
        ],
        compiler_params=params(("arbitrary",)),
        name="leave_back",
    )(
        gval, gwr, dsilu, raw, docs, conv, back, normed, turned, wraw, gdraw, dlow, gnorm, tokens,
        cotangent, gain,
    )


def tiles_of(extent):
    return -(-extent // 128)


def pieces_of(rows):
    return [(i, i * 128, min(128, rows - i * 128)) for i in range(tiles_of(rows))]


def split_three(v):
    high = v.astype(BF16)
    rest = v - high.astype(F32)
    middle = rest.astype(BF16)
    low = (rest - middle.astype(F32)).astype(BF16)
    return jnp.concatenate([high, middle, low], axis=0)


def join_three(v):
    return v[0:8] + v[8:16] + v[16:24]


def inverse_factor(gram):
    rows = lax.broadcasted_iota(jnp.int32, (8, 8), 0)
    cols = lax.broadcasted_iota(jnp.int32, (8, 8), 1)
    left, right = gram, jnp.where(rows == cols, 1.0, 0.0)
    for j in range(7):
        factor = jnp.where(rows[:, :1] > j, left[:, j : j + 1] / left[j : j + 1, j : j + 1], 0.0)
        left, right = left - factor * left[j : j + 1, :], right - factor * right[j : j + 1, :]
    pivots = jnp.sum(jnp.where(rows == cols, left, 0.0), axis=1, keepdims=True)
    return right * lax.rsqrt(pivots)


RIGHT_OUT = PROJ // 128
DELTA = RIGHT_OUT + D // 128
REST = DELTA + HEADS // 8 * (D // 128)
REST_ROWS = D // 128 + (CONV + 1) * (XBC // 128) + INNER // 128 + 3
SUMMED = REST + -(-REST_ROWS // 8)


class Scatter:
    def __init__(self, group, x_ref, from_core, pairs, from_far, joint, send, recv):
        self.nf = group // 2
        self.x_ref, self.from_core, self.pairs, self.from_far = x_ref, from_core, pairs, from_far
        self.joint, self.send, self.recv = joint, send, recv
        self.r, self.f, self.s = (lax.axis_index(name) for name in ("rep", "fsdp", "seq"))
        self.copies = []
        half = x_ref.shape[1] // 2
        self.parts = [slice(0, half), slice(half, 2 * half)]
        f = self.f
        if self.nf == 4:
            x, y = f + 1 - 2 * lax.rem(f, 2), lax.rem(f + 2, 4)
            self.order = [lax.rem(x + 2, 4), x, y, f]
        else:
            self.order = [lax.rem(f + 1 + j, self.nf) for j in range(self.nf)]

    def start(self, src, dst, device):
        k = len(self.copies)
        copy = pltpu.make_async_remote_copy(
            src, dst, self.send.at[k], self.recv.at[k], device_id=device, device_id_type=MESH
        )
        copy.start()
        self.copies.append(copy)
        return copy

    def begin(self):
        other = (self.r, self.f, 1 - self.s)
        self.near = [
            self.start(self.x_ref.at[f * 2 + 1 - self.s], self.from_core.at[j], other)
            for j, f in enumerate(self.order)
        ]

    def device(self, j):
        return (self.r, self.order[j], self.s)

    def cross(self):
        self.far = []
        for j, f in enumerate(self.order):
            self.near[j].wait_recv()
            total = self.x_ref[f * 2 + self.s].astype(F32) + self.from_core[j].astype(F32)
            self.pairs[j] = total.astype(BF16)
            if self.nf != 4 and j < self.nf - 1:
                self.far.append(self.start(self.pairs.at[j], self.from_far.at[j], self.device(j)))
            if self.nf == 4 and j < 3:
                for half, part in enumerate(self.parts):
                    if j == 0 or half == j - 1:
                        to = half + 1 if j == 0 else j
                        self.far.append(
                            self.start(
                                self.pairs.at[j, part], self.from_far.at[j, part], self.device(to)
                            )
                        )

    def turn(self):
        if self.nf != 4:
            return
        for half, part in enumerate(self.parts):
            self.far[half].wait_recv()
            to = 2 - half
            total = self.pairs[to, part].astype(F32) + self.from_far[0, part].astype(F32)
            self.joint[half] = total.astype(BF16)
            self.far.append(
                self.start(self.joint.at[half], self.from_far.at[to, part], self.device(to))
            )

    def end(self, o_ref):
        if self.nf == 4:
            for copy in self.far[2:]:
                copy.wait_recv()
            total = self.pairs[3].astype(F32)
            for j in (1, 2):
                total = total + self.from_far[j].astype(F32)
        else:
            total = self.pairs[self.nf - 1].astype(F32)
            for j, copy in enumerate(self.far):
                copy.wait_recv()
                total = total + self.from_far[j].astype(F32)
        o_ref[...] = total
        for copy in self.copies:
            copy.wait_send()


class Exchange:
    def __init__(self, group, replicas):
        self.group, self.replicas = group, replicas
        r, f, s = lax.axis_index("rep"), lax.axis_index("fsdp"), lax.axis_index("seq")
        self.r, self.me = r, f * 2 + s
        self.peers = []
        for j in range(1, group):
            p = lax.rem(self.me + j, group)
            self.peers.append((p, (r, lax.div(p, 2), lax.rem(p, 2))))
        self.others = [(lax.rem(r + j, replicas), f, s) for j in range(1, replicas)]

    def greet(self):
        barrier = pltpu.get_barrier_semaphore()
        for device in [d for _, d in self.peers] + self.others:
            pl.semaphore_signal(barrier, inc=1, device_id=device, device_id_type=MESH)

    def met(self):
        pl.semaphore_wait(pltpu.get_barrier_semaphore(), self.group + self.replicas - 2)

    def sum(self, x_ref, o_ref, own, from_group, from_reps, send, recv, second=None, third=None):
        group, replicas, me = self.group, self.replicas, self.me
        width = own.shape[0]
        copies = []

        def start(src, dst, device):
            k = len(copies)
            copy = pltpu.make_async_remote_copy(
                src, dst, send.at[k], recv.at[k], device_id=device, device_id_type=MESH
            )
            copy.start()
            copies.append(copy)
            return copy

        arriving = [
            start(x_ref.at[pl.ds(p * width, width)], from_group.at[j], device)
            for j, (p, device) in enumerate(self.peers)
        ]
        total = x_ref[pl.ds(me * width, width)]
        for j, copy in enumerate(arriving):
            copy.wait_recv()
            total = total + from_group[j]
        own[...] = total
        from_reps[pl.ds(self.r, 1)] = total[None]
        arriving = [start(own, from_reps.at[self.r], device) for device in self.others]
        if second is not None:
            second()
        for copy in arriving:
            copy.wait_recv()
        total = from_reps[0]
        for j in range(1, replicas):
            total = total + from_reps[j]
        mine = pl.ds(me * width, width)
        o_ref[mine] = total
        arriving = [start(o_ref.at[mine], o_ref.at[mine], device) for _, device in self.peers]
        if third is not None:
            third()
        for copy in arriving:
            copy.wait_recv()
        for copy in copies:
            copy.wait_send()


def compress_kernel(
    group, replicas,
    sin_ref, sout_ref, grads_ref, raw_ref, ein_ref, eout_ref, gdelta_ref, ggain_ref,
    gconv_ref, ggate_ref, gheads_ref, gskip_ref,
    sum_ref, left_in_ref, left_out_ref, turned_in_ref, turned_out_ref, raw_total_ref,
    lefts, left_sums, hat, rights,
    own_a, group_a, reps_a, own_b, group_b, reps_b, send_a, recv_a, send_b, recv_b,
    from_core, pairs, from_far, joint, send_c, recv_c, held_raw, held_grads, held_in, held_out,
    split_in, split_out, load,
):
    rows_in, rows_out = ein_ref.shape[0], eout_ref.shape[0]
    out_part = slice(0, rows_out)
    gate_parts = [slice(rows_out + i * rows_in, rows_out + (i + 1) * rows_in) for i in range(2)]
    ahead = tiles_of(rows_in)
    width = ahead + tiles_of(rows_out)
    exchange = Exchange(group, replicas)
    exchange.greet()
    loads = [
        pltpu.make_async_copy(src, dst, load.at[k])
        for k, (src, dst) in enumerate(
            ((ein_ref, held_in), (eout_ref, held_out), (grads_ref, held_grads), (raw_ref, held_raw))
        )
    ]
    for copy in loads:
        copy.start()
    raw_ref, grads_ref = held_raw, held_grads

    lefts[...] = jnp.zeros_like(lefts)
    mine = pl.ds(exchange.me * width, width)

    def place(index, values, rows, first):
        for i, at, n in pieces_of(rows):
            lefts[index + first + i, :, :n] += values[:, at : at + n]

    def place_own(values, rows, first):
        for i, at, n in pieces_of(rows):
            part = values[:, at : at + n]
            if n < 128:
                part = jnp.concatenate([part, jnp.zeros((8, 128 - n), F32)], axis=1)
            where = pl.ds(exchange.me * width + first + i, 1)
            lefts[where] = lefts[where] + part[None]

    s_in, s_out = split_three(sin_ref[...]), split_three(sout_ref[...])
    for k, (held, split, start, rows, first) in enumerate(
        ((held_in, split_in, s_in, rows_in, 0), (held_out, split_out, s_out, rows_out, ahead))
    ):
        loads[k].wait()
        high = held[...].astype(BF16)
        split[0] = high
        split[1] = (held[...] - high.astype(F32)).astype(BF16)
        place_own(join_three(nt(start, split[0]) + nt(start, split[1])), rows, first)
    loads[2].wait()
    for p in range(group):
        product = nt(s_in[:, :D], grads_ref[p, gate_parts[0]])
        product = product + nt(s_in[:, D:INNER], grads_ref[p, gate_parts[1]])
        place(p * width, join_three(product), rows_in, 0)
        place(p * width, join_three(nt(s_out, grads_ref[p, out_part])), rows_out, ahead)
    loads[3].wait()
    exchange.met()
    scatter = Scatter(group, raw_ref, from_core, pairs, from_far, joint, send_c, recv_c)
    scatter.begin()
    for p in range(group):
        place(p * width, join_three(nt(s_in[:, INNER:], raw_ref[p])), rows_in, 0)
    exchange.sum(
        lefts, left_sums, own_a, group_a, reps_a, send_a, recv_a, scatter.cross, scatter.turn
    )

    for first, last in ((0, ahead), (ahead, width)):
        gram = jnp.zeros((8, 8), F32)
        for p in range(group):
            for i in range(first, last):
                tile = left_sums[p * width + i] * (1.0 / replicas)
                gram = gram + nt_high(tile, tile)
        inverse = inverse_factor(gram)
        for p in range(group):
            for i in range(first, last):
                hat[p * width + i] = nn_high(inverse, left_sums[p * width + i] * (1.0 / replicas))
    own = hat[mine]
    for first, rows, left_ref, turned_ref in (
        (0, rows_in, left_in_ref, turned_in_ref), (ahead, rows_out, left_out_ref, turned_out_ref)
    ):
        for i, at, n in pieces_of(rows):
            turned_ref[:, at : at + n] = own[first + i][:, :n]
            left_ref[at : at + n, :] = own[first + i].T[:n, :]

    def joined(tiles, start, rows):
        return jnp.concatenate([tiles[start + i][:, :n] for i, _, n in pieces_of(rows)], axis=1)

    def product(matrices, rows, skipped, error, at):
        spread = [split_three(joined(hat, p * width + skipped, rows)) for p in range(group)]
        mixed = split_three(joined(own, skipped, rows))
        columns = 0
        for ref, part, extent in matrices:
            for b in range(0, extent, TILE):
                total = nn(spread[0], ref[0, part, b : b + TILE])
                for p in range(1, group):
                    total = total + nn(spread[p], ref[p, part, b : b + TILE])
                here = columns + b
                total = total + nn(mixed, error[0, :, here : here + TILE])
                total = total + nn(mixed, error[1, :, here : here + TILE])
                right = join_three(total)
                for half in range(0, TILE, 128):
                    rights[at + (here + half) // 128] = right[:, half : half + 128]
            columns += extent

    every = slice(0, rows_in)
    product(
        [(grads_ref, part, D) for part in gate_parts] + [(raw_ref, every, XBC)],
        rows_in, 0, split_in, 0,
    )
    product([(grads_ref, out_part, D)], rows_out, ahead, split_out, RIGHT_OUT)
    for g in range(HEADS // 8):
        for q in range(D // 128):
            rights[DELTA + g * (D // 128) + q] = gdelta_ref[
                g * 8 : g * 8 + 8, q * 128 : q * 128 + 128
            ]
    rights[REST:] = jnp.zeros((rights.shape[0] - REST, 8, 128), F32)
    rest = [ggain_ref[0:1, q * 128 : q * 128 + 128] for q in range(D // 128)]
    for k in range(CONV + 1):
        rest += [gconv_ref[k : k + 1, q * 128 : q * 128 + 128] for q in range(XBC // 128)]
    rest += [ggate_ref[q : q + 1, :] for q in range(INNER // 128)]
    rest += [gheads_ref[0:1, :], gheads_ref[1:2, :], gskip_ref[0:1, :]]
    for i in range(0, REST_ROWS, 8):
        eight = rest[i : i + 8]
        rights[REST + i // 8, : len(eight), :] = jnp.concatenate(eight, axis=0)
    exchange.sum(rights, sum_ref, own_b, group_b, reps_b, send_b, recv_b)
    scatter.end(raw_total_ref)


def compress(starts, grads, raw, errors, smalls):
    group = grads.shape[0]
    replicas = lax.axis_size("rep")
    raw = raw.reshape(group, D // group, XBC)
    rows_in, rows_out = errors[0].shape[0], errors[1].shape[0]
    width = tiles_of(rows_in) + tiles_of(rows_out)
    block = (rows_in, XBC)
    share = -(-SUMMED // group)
    dma = pltpu.SemaphoreType.DMA((2 * (group - 1) + replicas - 1,))
    tiles = lambda *n: pltpu.VMEM(n + (8, 128), F32)
    vmem = pl.BlockSpec(memory_space=pltpu.VMEM)
    arrays = [*starts, grads, raw, *errors, *smalls]
    return pl.pallas_call(
        partial(compress_kernel, group, replicas),
        out_shape=[
            jax.ShapeDtypeStruct((group * share, 8, 128), F32),
            jax.ShapeDtypeStruct((rows_in, 8), F32),
            jax.ShapeDtypeStruct((rows_out, 8), F32),
            jax.ShapeDtypeStruct((8, rows_in), F32),
            jax.ShapeDtypeStruct((8, rows_out), F32),
            jax.ShapeDtypeStruct((rows_in, XBC), F32),
        ],
        in_specs=[vmem] * 2 + [pl.BlockSpec(memory_space=pl.ANY)] * 4 + [vmem] * len(smalls),
        out_specs=[vmem] * 6,
        scratch_shapes=[
            tiles(group * width), tiles(group * width), tiles(group * width),
            tiles(group * share),
            tiles(width), tiles(group - 1, width), tiles(replicas, width),
            tiles(share), tiles(group - 1, share), tiles(replicas, share),
            dma, dma, dma, dma,
            pltpu.VMEM((group // 2,) + block, BF16),
            pltpu.VMEM((group // 2,) + block, BF16),
            pltpu.VMEM((group // 2 - 1,) + block, BF16),
            pltpu.VMEM((2, rows_in // 2, XBC), BF16),
            pltpu.SemaphoreType.DMA((group + 2,)),
            pltpu.SemaphoreType.DMA((group + 2,)),
            pltpu.VMEM(raw.shape, BF16),
            pltpu.VMEM(grads.shape, BF16),
            pltpu.VMEM(errors[0].shape, F32),
            pltpu.VMEM(errors[1].shape, F32),
            pltpu.VMEM((2,) + errors[0].shape, BF16),
            pltpu.VMEM((2,) + errors[1].shape, BF16),
            pltpu.SemaphoreType.DMA((4,)),
        ],
        compiler_params=pltpu.CompilerParams(
            collective_id=2, has_side_effects=True, vmem_limit_bytes=VMEM_LIMIT
        ),
        name="compress",
    )(*arrays)


def finish_kernel(
    rates, replicas, rights_ref, tin_ref, tout_ref, lin_ref, lout_ref,
    win_ref, min_ref, ein_ref, raw_ref, wout_ref, mout_ref, eout_ref, out_ref, low_ref, high_ref,
    nwin_ref, nmin_ref, nein_ref, nwout_ref, nmout_ref, neout_ref,
    rin_ref, rout_ref, ntin_ref, ntout_ref,
):
    @pl.when(pl.program_id(0) == 0)
    def _():
        for ref, at, extent in ((rin_ref, 0, PROJ), (rout_ref, RIGHT_OUT, D)):
            for q in range(extent // 128):
                ref[:, q * 128 : q * 128 + 128] = rights_ref[at + q] * (1.0 / replicas)
        ntin_ref[...] = tin_ref[...]
        ntout_ref[...] = tout_ref[...]

    def update(w, m, e, nw, nm, ne, left_ref, grads, at, rate):
        rows = w.shape[0]
        left = [jnp.broadcast_to(left_ref[:, k : k + 1], (rows, 128)) for k in range(8)]
        begin = 0
        for grad in grads:
            for b in range(0, grad.shape[1], 128):
                cols = slice(begin + b, begin + b + 128)
                right = rights_ref[at + (begin + b) // 128] * (1.0 / replicas)
                approx = left[0] * right[0:1]
                for k in range(1, 8):
                    approx = approx + left[k] * right[k : k + 1]
                momentum = MOMENTUM * m[:, cols] + approx
                nm[:, cols] = momentum
                nw[:, cols] = w[:, cols] - rate * momentum
                ne[:, cols] = (grad[:, b : b + 128].astype(F32) + e[:, cols]) - approx
            begin += grad.shape[1]

    update(
        win_ref, min_ref, ein_ref, nwin_ref, nmin_ref, nein_ref, lin_ref, (low_ref, high_ref, raw_ref), 0,
        rates[0],
    )
    update(
        wout_ref, mout_ref, eout_ref, nwout_ref, nmout_ref, neout_ref, lout_ref, (out_ref,),
        RIGHT_OUT, rates[1],
    )


def finish(rates, replicas, rights, turned_in, turned_out, left_in, left_out, wide, narrow, grads):
    rows_in, rows_out = left_in.shape[0], left_out.shape[0]
    steps = 3 if rows_in % 48 == 0 else 1
    block = lambda a: pl.BlockSpec((a.shape[0] // steps, a.shape[1]), lambda i: (i, 0))
    like = lambda a: jax.ShapeDtypeStruct(a.shape, F32)
    step_in, step_out = rows_in // steps, rows_out // steps
    parts = [pl.BlockSpec((step_out, D), lambda i: (i, 0))] + [
        pl.BlockSpec((step_in, D), lambda i, k=k: ((rows_out + k * rows_in) // step_in + i, 0))
        for k in range(2)
    ]
    arrays = [*wide, *narrow]
    outs = [*wide[:3], *narrow[:3]]
    extra = [(8, PROJ), (8, D), turned_in.shape, turned_out.shape]
    return pl.pallas_call(
        partial(finish_kernel, rates, replicas),
        grid=(steps,),
        in_specs=[
            whole(rights.shape), whole(turned_in.shape), whole(turned_out.shape),
            block(left_in), block(left_out), *map(block, arrays), *parts,
        ],
        out_specs=[*map(block, outs), *map(whole, extra)],
        out_shape=[*map(like, outs), *(jax.ShapeDtypeStruct(e, F32) for e in extra)],
        compiler_params=params(("arbitrary",)),
        name="finish",
    )(rights, turned_in, turned_out, left_in, left_out, *arrays, grads, grads, grads)


def step_rates(tokens_replica):
    grad_scale = 0.3 * math.sqrt(tokens_replica)
    return (
        0.5 / (math.sqrt(D) * grad_scale),
        0.5 / (math.sqrt(INNER) * grad_scale),
        0.1 / grad_scale,
    )


def to_later(block):
    return lax.ppermute(block, "seq", [(i, i + 1) for i in range(lax.axis_size("seq") - 1)])


def to_earlier(block):
    return lax.ppermute(block, "seq", [(i + 1, i) for i in range(lax.axis_size("seq") - 1)])


def gather_rows(shard):
    return lax.all_gather(shard, ("fsdp", "seq"), axis=0, tiled=True)


def scatter_rows(total):
    return lax.psum_scatter(total, ("fsdp", "seq"), scatter_dimension=0, tiled=True)


def body(
    tokens,
    cotangent,
    segments,
    input_weight,
    output_weight,
    small_values,
    input_momentum,
    output_momentum,
    small_momentum,
    input_error,
    output_error,
    input_start,
    output_start,
):
    shape = tokens.shape
    pieces = shape[0] * shape[1]
    length = shape[2]
    replicas = lax.axis_size("rep")
    tokens_replica = pieces * length * lax.axis_size("fsdp") * lax.axis_size("seq")
    rate_in, rate_out, rate_small = step_rates(tokens_replica)

    tokens = tokens.reshape(pieces, length, D)
    cotangent = cotangent.reshape(pieces, length, D)
    small_rows = jnp.pad(small_values, (0, -small_values.shape[0] % 1024)).reshape(-1, 128)
    group = lax.axis_size("fsdp") * lax.axis_size("seq")
    weights = jnp.concatenate(
        [output_weight, input_weight[:, :D], input_weight[:, D:INNER]], axis=0
    ).astype(BF16)
    weights = gather_rows(weights).reshape(group, 4, -1, D)
    delta_rows = small_values[D:AT_CONV].reshape(D, HEADS).astype(BF16).T
    delta_rows = jnp.pad(delta_rows, ((0, HP - HEADS), (0, 0)))
    segments = segments.reshape(pieces, 1, segments.shape[2])
    norm_gain = small_values[:D].reshape(1, D)
    if lax.axis_size("fsdp") == 4 and input_weight.shape[0] % 16 == 0:
        (
            raw_full, normed, turned, raw, dsilu, values, wr, draw, delta, send, come,
            conv, gate_gain, heads, docs,
        ) = front(input_weight, tokens, small_rows, segments, delta_rows)
        raw_full = raw_full.reshape(XBC // TILE, D, TILE)
    else:
        raw_full, halo, _, conv, gate_gain, heads, docs = gather_raw(
            input_weight, tokens, small_rows, segments
        )
        raw_full = raw_full.reshape(D, XBC // TILE, TILE).transpose(1, 0, 2)
        normed, turned, raw, dsilu, values, wr, draw, delta, send = enter(
            tokens, halo, norm_gain, raw_full, delta_rows, conv, heads, docs
        )
        come = to_later(send)
    y, starts = forward_scan(values, wr, delta, heads, docs, come)
    output, gy, gnorm, first, gstate, grads, ggate, gskip = leave(
        weights, normed, turned, cotangent, tokens, y, values, wr, gate_gain, delta, heads, docs
    )
    total = scatter_rows(grads.reshape(-1, D))
    gval, gwr, gdraw, gheads, ghalo = backward_scan(
        values, wr, delta, draw, heads, docs, gy, first, starts, to_earlier(gstate), send, dsilu,
        conv,
    )
    input_grad, grad_raw, gdelta, ggain, gconv = leave_back(
        gval, gwr, dsilu, raw, docs, conv, to_earlier(ghalo), normed, turned, raw_full, gdraw,
        delta_rows, gnorm, tokens, cotangent, norm_gain,
    )
    rights, left_in, left_out, turned_in, turned_out, raw_total = compress(
        (input_start.T, output_start.T),
        grads,
        grad_raw,
        (input_error[0], output_error[0]),
        (gdelta, ggain, gconv, ggate, gheads, gskip),
    )
    (
        new_input_weight, new_input_momentum, new_input_error,
        new_output_weight, new_output_momentum, new_output_error,
        input_right, output_right, input_left, output_left,
    ) = finish(
        (rate_in, rate_out), replicas, rights, turned_in, turned_out, left_in, left_out,
        (input_weight, input_momentum, input_error[0], raw_total),
        (output_weight, output_momentum, output_error[0]),
        total,
    )
    rest = rights[REST:SUMMED].reshape(-1, 128)[:REST_ROWS]
    turned_delta = rights[DELTA:REST].reshape(HEADS // 8, D // 128, 8, 128)
    small_sum = jnp.concatenate(
        [
            rest[: D // 128].reshape(-1),
            turned_delta.transpose(1, 3, 0, 2).reshape(-1),
            rest[D // 128 : -3].reshape(-1),
            rest[-3:, :HEADS].reshape(-1),
        ]
    )
    new_small_momentum = MOMENTUM * small_momentum + small_sum / replicas
    new_small_values = small_values - rate_small * new_small_momentum
    return (
        output.reshape(shape),
        input_grad.reshape(shape),
        new_input_weight,
        new_output_weight,
        new_input_momentum,
        new_output_momentum,
        new_small_values,
        new_small_momentum,
        input_left.T,
        input_right.T,
        output_left.T,
        output_right.T,
        new_input_error[None],
        new_output_error[None],
    )


def solution(mesh):
    return jax.shard_map(
        body,
        mesh=mesh,
        in_specs=(
            P(None, ("rep", "fsdp"), "seq", None),
            P(None, ("rep", "fsdp"), "seq", None),
            P(None, ("rep", "fsdp"), None),
            P(("fsdp", "seq"), None),
            P(("fsdp", "seq"), None),
            P(),
            P(("fsdp", "seq"), None),
            P(("fsdp", "seq"), None),
            P(),
            P("rep", ("fsdp", "seq"), None),
            P("rep", ("fsdp", "seq"), None),
            P(),
            P(),
        ),
        out_specs=(
            P(None, ("rep", "fsdp"), "seq", None),
            P(None, ("rep", "fsdp"), "seq", None),
            P(("fsdp", "seq"), None),
            P(("fsdp", "seq"), None),
            P(("fsdp", "seq"), None),
            P(("fsdp", "seq"), None),
            P(),
            P(),
            P(("fsdp", "seq"), None),
            P(),
            P(("fsdp", "seq"), None),
            P(),
            P("rep", ("fsdp", "seq"), None),
            P("rep", ("fsdp", "seq"), None),
        ),
        check_vma=False,
    )
```
